32 devices in a mesh: seq: 8 (over z, y), batch: 4 (over x, core).
Axes of the slice: x: 2, y: 2, z: 4, core: 2. Of those that a mesh axis runs over, the one named last changes fastest.
Arguments:
- inputs: bfloat16 [16, 1024, 768], P('batch', 'seq'), may hold values from -6 to 6
- cotangent: bfloat16 [16, 1024, 768], P('batch', 'seq'), may hold values from -6 to 6
- doc_lengths: int32 [16, 8], P('batch'), may hold values from 1 to 512, 1024 in all within a row
- qkv_weight: float32 [896, 768], P('seq'), may hold values from -0.3125 to 0.3125
- out_weight: float32 [768, 768], P('seq'), may hold values from -0.625 to 0.625
- up_weight: float32 [3072, 768], P('seq'), may hold values from -0.21875 to 0.21875
- down_weight: float32 [768, 3072], P(None, 'seq'), may hold values from -0.109375 to 0.109375
- vectors: float32 [8576], P('seq'), may hold values from -0.9 to 1.6, as said below
- bases: float32 [4, 768, 768], replicated, may hold values from -1 to 1, as said below
- qkv_first: float32 [896, 768], P('seq'), may hold values from -64 to 64
- out_first: float32 [768, 768], P('seq'), may hold values from -20 to 20
- up_first: float32 [3072, 768], P('seq'), may hold values from -24 to 24
- down_first: float32 [768, 3072], P(None, 'seq'), may hold values from -40 to 40
- vector_first: float32 [8576], P('seq'), may hold values from -64 to 64
- qkv_second: float32 [896, 768], P('seq'), may hold values from 819.2 to 8192
- out_second: float32 [768, 768], P('seq'), may hold values from 81.92 to 1310.72
- up_second: float32 [3072, 768], P('seq'), may hold values from 131.072 to 1966.08
- down_second: float32 [768, 3072], P(None, 'seq'), may hold values from 409.6 to 6553.6
- vector_second: float32 [8576], P('seq'), may hold values from 327.68 to 16384
Outputs:
- outputs: bfloat16 [16, 1024, 768], P('batch', 'seq')
- input_grad: bfloat16 [16, 1024, 768], P('batch', 'seq')
- qkv_grad: float32 [896, 768], P('seq')
- out_grad: float32 [768, 768], P('seq')
- up_grad: float32 [3072, 768], P('seq')
- down_grad: float32 [768, 3072], P(None, 'seq')
- vector_grad: float32 [8576], P('seq')
- qkv_first_new: float32 [896, 768], P('seq')
- out_first_new: float32 [768, 768], P('seq')
- up_first_new: float32 [3072, 768], P('seq')
- down_first_new: float32 [768, 3072], P(None, 'seq')
- vector_first_new: float32 [8576], P('seq')
- qkv_second_new: float32 [896, 768], P('seq')
- out_second_new: float32 [768, 768], P('seq')
- up_second_new: float32 [3072, 768], P('seq')
- down_second_new: float32 [768, 3072], P(None, 'seq')
- vector_second_new: float32 [8576], P('seq')
- qkv_new: float32 [896, 768], P('seq')
- out_new: float32 [768, 768], P('seq')
- up_new: float32 [3072, 768], P('seq')
- down_new: float32 [768, 3072], P(None, 'seq')
- vector_new: float32 [8576], P('seq')
The draws below stay inside these ranges and needn't reach their ends.
Inputs may be any that keep to these rules, and one draw needn't show every extreme that they name: `doc_lengths`: the 8 lengths of a row sum to 1024, and in every row the longest document has exactly half of 1024 positions. `vectors`: entries 0 to 767 and 1536 to 2303 are the two norms' gains, all others shifts and biases. `bases`: each of the four matrices is orthogonal.
All inputs are finite; a program needn't handle non-finite values.
Results may differ from the reference program's by a relative error of at most 0.006.
The reference program's roundings to bfloat16 on the way count: a program that leaves them out, or rounds other values in their place, can miss the bound.
Values may be sent and summed in bfloat16 or wider, within the bound.
No kernel may reach another device: no remote copies, remote signals or barrier semaphores. Data moves between devices by JAX's collectives and lax.ppermute only.
A program may use at most 192 MiB of HBM per device.

```python
import math
import jax
import jax.numpy as jnp
import numpy as np
from jax import lax

D = 768
HEADS = 12
HEAD = 64
ROT = 16
FF = 3072
DOCS = 8
STEP = 10
SEQ_LEN = 1024
ROWS = 16
TOKENS = 16384
NVEC = 8576


def draw_vectors(key, part):
    position = jnp.arange(NVEC)
    is_gain = (position < D) | (position >= 2 * D) & (position < 3 * D)
    random_part = jnp.clip(jax.random.normal(key, (NVEC,), jnp.float32), -3.0, 3.0)
    return jnp.where(is_gain, 1.0 + 0.2 * random_part, 0.3 * random_part)


def one_basis(basis_key):
    keys_split = jax.random.split(basis_key, 4)
    column_freq = jax.random.permutation(keys_split[0], D).astype(jnp.int32)
    row_order = jax.random.permutation(keys_split[1], D).astype(jnp.int32)
    column_sign = (2 * jax.random.randint(keys_split[2], (D,), 0, 2) - 1).astype(jnp.float32)
    row_sign = (2 * jax.random.randint(keys_split[3], (D,), 0, 2) - 1).astype(jnp.float32)
    phase_index = (2 * row_order[:, None] + 1) * column_freq[None, :] % (4 * D)
    angles = jnp.pi * phase_index.astype(jnp.float32) / (2.0 * D)
    column_scale = jnp.where(column_freq == 0, (1.0 / D) ** 0.5, (2.0 / D) ** 0.5)
    matrix = jnp.cos(angles) * column_scale[None, :]
    return matrix * row_sign[:, None] * column_sign[None, :]


def draw_bases(key, part):
    return jax.vmap(one_basis)(jax.random.split(key, 4))


def levels(own_key, dims, cuts, smallest, high):
    level = 1.0
    for dim, shards_of in cuts:
        draws = jax.random.uniform(jax.random.fold_in(jax.random.fold_in(own_key, 6), dim), (shards_of,), jnp.float32, smallest / len(cuts), high / len(cuts))
        level = level * jnp.repeat(jnp.exp(draws), dims[dim] // shards_of).reshape((-1,) + (1,) * (len(dims) - 1 - dim))
    return level


def split_up(amount, total, limit, slope):
    loads = [(1 << 20) // math.isqrt(grade ** slope) + 1 for grade in range(2, amount + 1)]
    surplus, counts = total - limit - (amount - 1), [1] * (amount - 1)
    while surplus > 0:
        candidates = [i for i in range(amount - 1) if counts[i] < limit]
        mass, left = sum([loads[i] for i in candidates]), surplus
        for i in candidates:
            more = min(limit - counts[i], max(1, left * loads[i] // mass), surplus)
            counts[i] = counts[i] + more
            surplus = surplus - more
    return np.array([limit] + counts)


def ragged(stream_key, amount, total, most, slope):
    if amount == 2:
        one = jax.random.randint(stream_key, (), max(1, total - most), min(most, total - 1) + 1)
        return jnp.stack([one, total - one])
    sizes = jnp.asarray(split_up(amount, total, most, slope), jnp.int32)
    couples = (amount - 1) // 2
    source_of, sink = sizes[1:1 + 2 * couples:2], sizes[2:2 + 2 * couples:2]
    margin = jnp.minimum(source_of - 1, most - sink)
    moved = jax.random.randint(jax.random.fold_in(stream_key, 1), (couples,), 0, 1 << 20) % (margin + 1)
    sizes = sizes.at[1:1 + 2 * couples:2].set(source_of - moved).at[2:2 + 2 * couples:2].set(sink + moved)
    return sizes[jax.random.permutation(jax.random.fold_in(stream_key, 2), amount)]


def noise(rng, extent, scale, reach, cuts=(), kind=jnp.bfloat16):
    array = jax.random.normal(rng, extent, jnp.float32) * scale
    if len(cuts) > 0:
        array = levels(rng, extent, cuts, -0.22, 0.18) * array
    return jnp.clip(array, min=-reach, max=reach).astype(kind)


def setup_inputs(seed: int = 0) -> dict:
    arg_keys = jax.random.split(jax.random.key(seed), 20)
    return {
        "inputs": noise(arg_keys[0], (ROWS, SEQ_LEN, D), 1.0, 6.0, ((0, 4), (1, 8))),
        "cotangent": noise(arg_keys[1], (ROWS, SEQ_LEN, D), 1.0, 6.0, ((0, 4), (1, 8))),
        "doc_lengths": jax.vmap(lambda own: ragged(own, DOCS, SEQ_LEN, SEQ_LEN // 2, 2))(jax.random.split(arg_keys[2], ROWS)).reshape((ROWS, DOCS)).astype(jnp.int32),
        "qkv_weight": noise(arg_keys[3], (D + 2 * HEAD, D), (D // 2) ** -0.5, 0.3125, ((0, 8),), jnp.float32),
        "out_weight": noise(arg_keys[4], (D, D), (D // 8) ** -0.5, 0.625, ((0, 8),), jnp.float32),
        "up_weight": noise(arg_keys[5], (FF, D), D ** -0.5, 0.21875, ((0, 8),), jnp.float32),
        "down_weight": noise(arg_keys[6], (D, FF), FF ** -0.5, 0.109375, ((1, 8),), jnp.float32),
        "vectors": draw_vectors(jax.random.fold_in(arg_keys[19], 71), 0),
        "bases": draw_bases(jax.random.fold_in(arg_keys[19], 71), 0),
        "qkv_first": noise(arg_keys[9], (D + 2 * HEAD, D), (0.08 * TOKENS ** 0.5), 64.0, ((0, 8),), jnp.float32),
        "out_first": noise(arg_keys[10], (D, D), (0.025 * TOKENS ** 0.5), 20.0, ((0, 8),), jnp.float32),
        "up_first": noise(arg_keys[11], (FF, D), (0.03 * TOKENS ** 0.5), 24.0, ((0, 8),), jnp.float32),
        "down_first": noise(arg_keys[12], (D, FF), (0.05 * TOKENS ** 0.5), 40.0, ((1, 8),), jnp.float32),
        "vector_first": noise(arg_keys[13], (NVEC,), (0.08 * TOKENS ** 0.5), 64.0, ((0, 8),), jnp.float32),
        "qkv_second": jnp.clip(jnp.exp(math.log(8192.0) - 2.3025851 * jax.random.uniform(arg_keys[14], (D + 2 * HEAD, D), jnp.float32) ** levels(arg_keys[14], (D + 2 * HEAD, D), ((0, 8),), -0.2, 0.2)), 819.2, 8192.0),
        "out_second": jnp.clip(jnp.exp(math.log(1310.72) - 2.7725887 * jax.random.uniform(arg_keys[15], (D, D), jnp.float32) ** levels(arg_keys[15], (D, D), ((0, 8),), -0.2, 0.2)), 81.92, 1310.72),
        "up_second": jnp.clip(jnp.exp(math.log(1966.08) - 2.70805 * jax.random.uniform(arg_keys[16], (FF, D), jnp.float32) ** levels(arg_keys[16], (FF, D), ((0, 8),), -0.2, 0.2)), 131.072, 1966.08),
        "down_second": jnp.clip(jnp.exp(math.log(6553.6) - 2.7725887 * jax.random.uniform(arg_keys[17], (D, FF), jnp.float32) ** levels(arg_keys[17], (D, FF), ((1, 8),), -0.2, 0.2)), 409.6, 6553.6),
        "vector_second": jnp.clip(jnp.exp(math.log(16384.0) - 3.912023 * jax.random.uniform(arg_keys[18], (NVEC,), jnp.float32) ** levels(arg_keys[18], (NVEC,), ((0, 8),), -0.2, 0.2)), 327.68, 16384.0),
    }


@jax.custom_vjp
def low(v):
    return lax.optimization_barrier(v.astype(jnp.bfloat16)).astype(jnp.float32)

@jax.custom_vjp
def low_back(v):
    return v

def low_keep(v):
    return (low(v), None)

def low_pass(kept, grad):
    return (grad,)

def back_keep(v):
    return (v, None)

def back_low(kept, grad):
    return (low(grad),)
low.defvjp(low_keep, low_pass)
low_back.defvjp(back_keep, back_low)
layer_eps = 1e-05
adam_eps = 1e-08
beta_first = 0.95
beta_second = 0.95
matrix_rate = 0.08
vector_rate = 0.3
rope_base = 10000.0
masked_score = -1e+30

def matmul(left, right):
    return jnp.dot(left, right, precision=lax.Precision.HIGHEST, preferred_element_type=jnp.float32)

def layer_norm(values, gain, shift):
    center = values - lax.optimization_barrier(jnp.mean(values, axis=-1, keepdims=True))
    spread = lax.optimization_barrier(jnp.mean(center * center, axis=-1, keepdims=True))
    return center * lax.rsqrt(spread + layer_eps) * gain + shift

def split_vectors(vectors):
    widths = [D, D, D, D, D + 2 * HEAD, D, FF, D]
    pieces = []
    offset = 0
    for piece_width in widths:
        pieces.append(vectors[offset:offset + piece_width])
        offset = offset + piece_width
    return pieces

def rotary_tables(offsets):
    freq_steps = jnp.arange(0, ROT, 2).astype(jnp.float32)
    inverse = 1.0 / rope_base ** (freq_steps / ROT)
    angles = offsets.astype(jnp.float32)[..., None] * inverse
    angles = jnp.concatenate([angles, angles], axis=-1)
    return (jnp.cos(angles), jnp.sin(angles))

def rotate(values, cosine, sine):
    turned = values[..., :ROT]
    half_rot = ROT // 2
    swapped = jnp.concatenate([-turned[..., half_rot:], turned[..., :half_rot]], axis=-1)
    return jnp.concatenate([turned * cosine + swapped * sine, values[..., ROT:]], axis=-1)

def doc_layout(lengths, positions):
    starts = (jnp.cumsum(lengths) - lengths).astype(jnp.int32)
    before = starts[None, :] <= positions[:, None]
    doc_ident = lax.optimization_barrier(jnp.sum(before.astype(jnp.int32), axis=1)) - 1
    doc_begin = lax.optimization_barrier(jnp.max(jnp.where(before, starts[None, :], 0), axis=1))
    return (doc_ident.astype(jnp.int32), (positions - doc_begin).astype(jnp.int32))

def attend_block(block_item, key_rows, value_rows, key_doc, key_pos):
    query_rows, query_doc, query_pos = block_item
    scores = jnp.einsum('qhd,kd->hqk', query_rows, key_rows, precision=lax.Precision.HIGHEST) * HEAD ** (-0.5)
    scores = low_back(scores)
    allowed = (query_doc[:, None] == key_doc[None, :]) & (key_pos[None, :] <= query_pos[:, None])
    scores = jnp.where(allowed[None], scores, masked_score)
    row_max = lax.optimization_barrier(jnp.max(scores, axis=-1, keepdims=True))
    weights = jnp.exp(scores - row_max)
    probs = weights / lax.optimization_barrier(jnp.sum(weights, axis=-1, keepdims=True))
    probs = low(probs)
    return jnp.einsum('hqk,kd->qhd', probs, value_rows, precision=lax.Precision.HIGHEST)

def row_forward(row_values, qkv_w, out_w, up_w, down_w, vec_w, row_lengths):
    pieces = split_vectors(low(vec_w))
    gain_one, shift_one, gain_two, shift_two, qkv_bias, out_bias, up_bias, down_bias = pieces
    positions = jnp.arange(SEQ_LEN).astype(jnp.int32)
    doc_ident, offsets = doc_layout(row_lengths, positions)
    cosine, sine = rotary_tables(offsets)
    normed_one = layer_norm(row_values, gain_one, shift_one)
    normed_two = layer_norm(row_values, gain_two, shift_two)
    projected = matmul(low(normed_one), low(qkv_w).T) + qkv_bias
    projected = low_back(projected)
    queries = rotate(projected[:, :D].reshape(SEQ_LEN, HEADS, HEAD), cosine[:, None, :], sine[:, None, :])
    key_rows = rotate(projected[:, D:D + HEAD], cosine, sine)
    value_rows = projected[:, D + HEAD:]
    queries = low(queries)
    key_rows = low(key_rows)
    value_rows = low(value_rows)
    block_rows = min(512, SEQ_LEN)
    block_count = SEQ_LEN // block_rows
    attend = jax.checkpoint(lambda block_item: attend_block(block_item, key_rows, value_rows, doc_ident, positions))
    context = lax.map(attend, (queries.reshape(block_count, block_rows, HEADS, HEAD), doc_ident.reshape(block_count, block_rows), positions.reshape(block_count, block_rows)))
    context = context.reshape(SEQ_LEN, D)
    context = low(low_back(context))
    attn_out = matmul(context, low(out_w).T) + out_bias
    hidden = low_back(matmul(low(normed_two), low(up_w).T) + up_bias)
    active = low(jax.nn.gelu(hidden, approximate=False))
    mlp_out = matmul(active, low(down_w).T) + down_bias
    return row_values + attn_out + mlp_out

def soap_step(weight, grad, first, second, basis, on_right):
    if on_right:
        rotated = matmul(grad, basis)
    else:
        rotated = matmul(basis.T, grad)
    new_first = beta_first * first + (1.0 - beta_first) * rotated
    new_second = beta_second * second + (1.0 - beta_second) * rotated * rotated
    ratio = new_first / (1.0 - beta_first ** STEP) / (jnp.sqrt(new_second / (1.0 - beta_second ** STEP)) + adam_eps)
    if on_right:
        unrotated = matmul(ratio, basis.T)
    else:
        unrotated = matmul(basis, ratio)
    return (weight - matrix_rate * unrotated, new_first, new_second)

def adam_step(weight, grad, first, second):
    new_first = beta_first * first + (1.0 - beta_first) * grad
    new_second = beta_second * second + (1.0 - beta_second) * grad * grad
    ratio = new_first / (1.0 - beta_first ** STEP) / (jnp.sqrt(new_second / (1.0 - beta_second ** STEP)) + adam_eps)
    return (weight - vector_rate * ratio, new_first, new_second)

def reference(inputs, cotangent, doc_lengths, qkv_weight, out_weight, up_weight, down_weight, vectors, bases, qkv_first, out_first, up_first, down_first, vector_first, qkv_second, out_second, up_second, down_second, vector_second):
    params = (qkv_weight, out_weight, up_weight, down_weight, vectors)

    def scan_row(totals, row_item):
        row_in, row_cot, row_lengths = row_item

        def forward_row(row_values, qkv_w, out_w, up_w, down_w, vec_w):
            return row_forward(row_values, qkv_w, out_w, up_w, down_w, vec_w, row_lengths)
        result, pullback = jax.vjp(forward_row, row_in.astype(jnp.float32), *params)
        gradients = pullback(row_cot.astype(jnp.float32))
        totals = tuple((total_now + grad_now for total_now, grad_now in zip(totals, gradients[1:])))
        return (totals, (result.astype(jnp.bfloat16), gradients[0].astype(jnp.bfloat16)))
    zero_totals = tuple((jnp.zeros(param.shape, jnp.float32) for param in params))
    totals, (outputs, input_grad) = lax.scan(scan_row, zero_totals, (inputs, cotangent, doc_lengths))
    qkv_grad, out_grad, up_grad, down_grad, vector_grad = totals
    qkv_new, qkv_first_new, qkv_second_new = soap_step(qkv_weight, qkv_grad, qkv_first, qkv_second, bases[0], True)
    out_new, out_first_new, out_second_new = soap_step(out_weight, out_grad, out_first, out_second, bases[1], True)
    up_new, up_first_new, up_second_new = soap_step(up_weight, up_grad, up_first, up_second, bases[2], True)
    down_new, down_first_new, down_second_new = soap_step(down_weight, down_grad, down_first, down_second, bases[3], False)
    vector_new, vector_first_new, vector_second_new = adam_step(vectors, vector_grad, vector_first, vector_second)
    return (outputs, input_grad, qkv_grad, out_grad, up_grad, down_grad, vector_grad, qkv_first_new, out_first_new, up_first_new, down_first_new, vector_first_new, qkv_second_new, out_second_new, up_second_new, down_second_new, vector_second_new, qkv_new, out_new, up_new, down_new, vector_new)
```

```python
import functools

import jax
import jax.numpy as jnp
from jax import lax
from jax.experimental import pallas as pl
from jax.experimental.pallas import tpu as pltpu
from jax.sharding import PartitionSpec as P

D = 768
HEADS = 12
HEAD = 64
ROT = 16
FF = 3072
STEP = 10

layer_eps = 1e-05
adam_eps = 1e-08
beta_first = 0.95
beta_second = 0.95
matrix_rate = 0.08
vector_rate = 0.3
rope_base = 10000.0
masked_score = -1e30
low = jnp.bfloat16
f32 = jnp.float32
VMEM_LIMIT = 56 * 1024 * 1024


def swap(value, bit):
    axis, step = bit
    return lax.ppermute(value, axis, [(i, i ^ step) for i in range(lax.axis_size(axis))])


def mine(bit):
    axis, step = bit
    return lax.rem(lax.axis_index(axis) // step, 2)


def place(have, bit, canon):
    return sum(1 for other in have if canon.index(other) < canon.index(bit))


def gather_bits(piece, order, canon, absolute):
    have = []
    value = piece
    for bit in order:
        got = swap(value, bit)
        if absolute:
            upper = mine(bit) == 1
            pair = [jnp.where(upper, got, value), jnp.where(upper, value, got)]
        else:
            pair = [value, got]
        value = jnp.stack(pair, axis=place(have, bit, canon))
        have.append(bit)
    return value


def sum_bits(value, order, canon, absolute):
    left = list(order)
    for bit in order:
        axis = place([b for b in left if b != bit], bit, canon)
        if absolute:
            own = mine(bit)
            kept = lax.dynamic_index_in_dim(value, own, axis, keepdims=False)
            sent = lax.dynamic_index_in_dim(value, 1 - own, axis, keepdims=False)
        else:
            kept = lax.index_in_dim(value, 0, axis, keepdims=False)
            sent = lax.index_in_dim(value, 1, axis, keepdims=False)
        value = kept.astype(f32) + swap(sent.astype(low), bit).astype(f32)
        left.remove(bit)
    return value


def bit_names(axis, size):
    return [(axis, 1 << k) for k in range(size.bit_length() - 1)]


def matmul_exact(left, right):
    return jnp.dot(left, right, precision=lax.Precision.HIGHEST, preferred_element_type=f32)


def split_vectors(vectors):
    widths = [D, D, D, D, D + 2 * HEAD, D, FF, D]
    pieces = []
    offset = 0
    for piece_width in widths:
        pieces.append(vectors[offset : offset + piece_width])
        offset = offset + piece_width
    return pieces


def moments(rotated, first, second):
    new_first = beta_first * first + (1.0 - beta_first) * rotated
    new_second = beta_second * second + (1.0 - beta_second) * rotated * rotated
    ratio = (
        new_first
        / (1.0 - beta_first**STEP)
        / (jnp.sqrt(new_second / (1.0 - beta_second**STEP)) + adam_eps)
    )
    return ratio, new_first, new_second


def soap_step(weight, grad, first, second, basis, on_right):
    rotated = matmul_exact(grad, basis) if on_right else matmul_exact(basis.T, grad)
    ratio, new_first, new_second = moments(rotated, first, second)
    unrotated = matmul_exact(ratio, basis.T) if on_right else matmul_exact(basis, ratio)
    return (weight - matrix_rate * unrotated, new_first, new_second)


def adam_step(weight, grad, first, second):
    ratio, new_first, new_second = moments(grad, first, second)
    return (weight - vector_rate * ratio, new_first, new_second)


def turn(values, cosine, sine, back):
    half = ROT // 2
    heads = values.reshape(-1, HEAD, values.shape[-1])
    a, b = heads[:, :half], heads[:, half:ROT]
    if back:
        pair = [a * cosine + b * sine, b * cosine - a * sine]
    else:
        pair = [a * cosine - b * sine, b * cosine + a * sine]
    return jnp.concatenate(pair + [heads[:, ROT:]], axis=1).reshape(values.shape)


def attention_kernel(blocks, width, q_ref, do_ref, start_ref, cos_ref, sin_ref, *refs):
    kv_refs = refs[:blocks]
    context_ref, dq_ref, dkv_own_ref, dkv_ref = refs[blocks:]
    length = q_ref.shape[1]
    keys = blocks * length
    key_t = jnp.concatenate([ref[:HEAD, :] for ref in reversed(kv_refs)], axis=1)
    value_t = jnp.concatenate([ref[HEAD:, :] for ref in reversed(kv_refs)], axis=1)
    key = key_t.astype(f32).T.astype(low)
    value = value_t.astype(f32).T.astype(low)
    key_pos = lax.broadcasted_iota(jnp.int32, (keys, length), 0) - (blocks - 1) * length
    query_pos = lax.broadcasted_iota(jnp.int32, (keys, length), 1)
    allowed = (key_pos >= start_ref[0]) & (key_pos <= query_pos)
    bias = jnp.where(allowed, 0.0, masked_score)
    cosine, sine = cos_ref[...], sin_ref[...]
    d_key = jnp.zeros((keys, HEAD), f32)
    d_value = jnp.zeros((keys, HEAD), f32)
    last = (((1,), (1,)), ((), ()))
    for first in range(0, HEADS, width):
        heads = range(first, first + width)
        query = jnp.concatenate([q_ref[h * HEAD : (h + 1) * HEAD, :] for h in heads], axis=1)
        d_out = jnp.concatenate([do_ref[h * HEAD : (h + 1) * HEAD, :] for h in heads], axis=1)
        scores = jnp.dot(key, query, preferred_element_type=f32)
        scores = scores + jnp.concatenate([bias] * width, axis=1)
        weights = jnp.exp(scores - jnp.max(scores, axis=0, keepdims=True))
        probs = weights * (1.0 / jnp.sum(weights, axis=0, keepdims=True))
        probs_low = probs.astype(low)
        context_t = jnp.dot(value_t, probs_low, preferred_element_type=f32)
        d_probs = jnp.dot(value, d_out, preferred_element_type=f32)
        inner = jnp.sum(probs * d_probs, axis=0, keepdims=True)
        d_scores = (probs * (d_probs - inner)).astype(low)
        d_query = jnp.dot(key_t, d_scores, preferred_element_type=f32) * HEAD ** (-0.5)
        d_value = d_value + lax.dot_general(probs_low, d_out, last, preferred_element_type=f32)
        d_key = d_key + lax.dot_general(d_scores, query, last, preferred_element_type=f32)
        for k, h in enumerate(heads):
            lanes = slice(k * length, (k + 1) * length)
            part = d_query[:, lanes]
            a, b = part[: ROT // 2], part[ROT // 2 : ROT]
            turned = jnp.concatenate([a * cosine + b * sine, b * cosine - a * sine, part[ROT:]], axis=0)
            dq_ref[h * HEAD : (h + 1) * HEAD, :] = turned.astype(low)
        for k in range(0, width, 2):
            h = first + k
            two = jnp.concatenate(
                [context_t[:, k * length : (k + 1) * length], context_t[:, (k + 1) * length : (k + 2) * length]], axis=0
            )
            context_ref[:, h * HEAD : (h + 2) * HEAD] = two.T.astype(low)
    d_kv = jnp.concatenate([d_key, d_value], axis=1).T
    for k in range(blocks):
        part = d_kv[:, (blocks - 1 - k) * length : (blocks - k) * length]
        if k == 0:
            dkv_own_ref[...] = part
        else:
            dkv_ref[k - 1] = part.astype(low)


def attention(q_t, do_t, start, cosine, sine, kv):
    rows, _, length = start.shape
    blocks = len(kv)
    tokens = q_t.shape[1]
    by_row = lambda height: pl.BlockSpec((height, length), lambda r: (0, r))
    return pl.pallas_call(
        functools.partial(attention_kernel, blocks, 4),
        grid=(rows,),
        in_specs=[by_row(D), by_row(D), pl.BlockSpec((1, 1, length), lambda r: (r, 0, 0)), by_row(ROT // 2), by_row(ROT // 2)]
        + [by_row(2 * HEAD)] * blocks,
        out_specs=[
            pl.BlockSpec((length, D), lambda r: (r, 0)),
            by_row(D),
            by_row(2 * HEAD),
            pl.BlockSpec((blocks - 1, 2 * HEAD, length), lambda r: (0, 0, r)),
        ],
        out_shape=[
            jax.ShapeDtypeStruct((tokens, D), low),
            jax.ShapeDtypeStruct((D, tokens), low),
            jax.ShapeDtypeStruct((2 * HEAD, tokens), f32),
            jax.ShapeDtypeStruct((blocks - 1, 2 * HEAD, tokens), low),
        ],
        compiler_params=pltpu.CompilerParams(vmem_limit_bytes=VMEM_LIMIT),
        cost_estimate=pl.CostEstimate(
            flops=4 * 7 * tokens * HEADS * blocks * length * HEAD * 2, bytes_accessed=8 << 20, transcendentals=0
        ),
        name="attention",
    )(q_t, do_t, start, cosine, sine, *kv)


def feed_kernel(n_ref, dy_ref, up_ref, down_ref, bias_ref, out_ref, dn_ref, up_grad_ref, down_grad_ref, bias_grad_ref):
    last = (((1,), (1,)), ((), ()))
    first = (((0,), (0,)), ((), ()))
    normed, d_out = n_ref[...], dy_ref[...]
    up, down = up_ref[...], down_ref[...]
    hidden = lax.dot_general(normed, up, last, preferred_element_type=f32) + bias_ref[...]
    share = 0.5 * (1.0 + lax.erf(hidden * (0.5**0.5)))
    slope = share + hidden * (jnp.exp(-0.5 * hidden * hidden) * (0.5 / 3.141592653589793) ** 0.5)
    active = (hidden * share).astype(low)
    d_active = lax.dot_general(d_out, down, last, preferred_element_type=f32)
    d_hidden = (d_active * slope).astype(low)
    out = jnp.dot(active, down, preferred_element_type=f32)
    d_normed = jnp.dot(d_hidden, up, preferred_element_type=f32)

    @pl.when(pl.program_id(0) == 0)
    def _():
        out_ref[...] = out
        dn_ref[...] = d_normed

    @pl.when(pl.program_id(0) > 0)
    def _():
        out_ref[...] += out
        dn_ref[...] += d_normed

    up_grad_ref[...] = lax.dot_general(d_hidden, normed, first, preferred_element_type=f32).astype(up_grad_ref.dtype)
    down_grad_ref[...] = lax.dot_general(active, d_out, first, preferred_element_type=f32).astype(down_grad_ref.dtype)
    bias_grad_ref[...] = jnp.sum(d_hidden.astype(f32), axis=0, keepdims=True)


def feed(normed, d_out, up, down, bias, grad_type):
    tokens = normed.shape[0]
    units = up.shape[0]
    step = 512 if units % 512 == 0 else units
    whole = pl.BlockSpec((tokens, D), lambda i: (0, 0))
    part = pl.BlockSpec((step, D), lambda i: (i, 0))
    row = pl.BlockSpec((1, step), lambda i: (0, i))
    return pl.pallas_call(
        feed_kernel,
        grid=(units // step,),
        in_specs=[whole, whole, part, part, row],
        out_specs=[whole, whole, part, part, row],
        out_shape=[
            jax.ShapeDtypeStruct((tokens, D), f32),
            jax.ShapeDtypeStruct((tokens, D), f32),
            jax.ShapeDtypeStruct((units, D), grad_type),
            jax.ShapeDtypeStruct((units, D), grad_type),
            jax.ShapeDtypeStruct((1, units), f32),
        ],
        compiler_params=pltpu.CompilerParams(vmem_limit_bytes=VMEM_LIMIT),
        cost_estimate=pl.CostEstimate(flops=12 * tokens * units * D, bytes_accessed=8 << 20, transcendentals=0),
        name="feed",
    )(normed, d_out, up, down, bias)


def shards(
    inputs,
    cotangent,
    doc_lengths,
    qkv_weight,
    out_weight,
    up_weight,
    down_weight,
    vectors,
    bases,
    qkv_first,
    out_first,
    up_first,
    down_first,
    vector_first,
    qkv_second,
    out_second,
    up_second,
    down_second,
    vector_second,
):
    seq_count, batch_count = lax.axis_size("seq"), lax.axis_size("batch")
    seq_index, batch_index = lax.axis_index("seq"), lax.axis_index("batch")
    row_count, shard_len = inputs.shape[:2]
    tokens = row_count * shard_len
    y_bit, *z_bits = bit_names("seq", seq_count)
    core_bit, *x_bits = bit_names("batch", batch_count)
    canon = z_bits[::-1] + [y_bit] + x_bits[::-1] + [core_bit]
    near = [core_bit] + x_bits[::-1] + [y_bit] + z_bits[::-1]
    y_then_x = z_bits + [y_bit] + x_bits
    x_then_y = z_bits + x_bits + [y_bit]

    qkv_rows, out_rows, up_rows, vec_len = qkv_weight.shape[0], out_weight.shape[0], up_weight.shape[0], vectors.shape[0]
    vec_rows = -(-vec_len // D)
    used = qkv_rows + vec_rows
    head_rows = -(-used // (8 * batch_count)) * 8 * batch_count
    vec_pad = vec_rows * D - vec_len

    def own_part(rows):
        size = rows.shape[0] // batch_count
        return lax.dynamic_slice_in_dim(rows, batch_index * size, size, axis=0)

    head_shard = jnp.concatenate(
        [qkv_weight, jnp.pad(vectors, (0, vec_pad)).reshape(vec_rows, D), jnp.zeros((head_rows - used, D), f32)], axis=0
    ).astype(low)
    head_full = gather_bits(own_part(head_shard), y_then_x + [core_bit], canon, True).reshape(seq_count, head_rows, D)
    out_full = gather_bits(own_part(out_weight.astype(low)), x_then_y + [core_bit], canon, True).reshape(D, D)
    up_near = gather_bits(own_part(up_weight.astype(low)), y_then_x, near, False).reshape(-1, D)
    down_near = gather_bits(own_part(down_weight.T.astype(low)), x_then_y, near, False).reshape(-1, D)
    up_far = swap(up_near, core_bit)
    down_far = swap(down_near, core_bit)

    qkv_full = head_full[:, :qkv_rows].reshape(D + 2 * HEAD, D)
    vector_full = head_full[:, qkv_rows:used].reshape(seq_count, vec_rows * D)[:, :vec_len].reshape(-1)
    pieces = split_vectors(vector_full.astype(f32))
    gain_one, shift_one, gain_two, shift_two, qkv_bias, out_bias, up_bias, down_bias = pieces
    unit_count = up_rows // batch_count
    device = jnp.arange(seq_count * batch_count)
    entry = jnp.zeros_like(device)
    for axis_name, index, number in (("seq", seq_index, device // batch_count), ("batch", batch_index, device % batch_count)):
        differs = number ^ index
        for place_from_end, bit in enumerate(near[::-1]):
            if bit[0] == axis_name:
                entry = entry + ((differs // bit[1]) % 2) * (1 << place_from_end)
    is_entry = entry[None, :] == device[:, None]
    bias_near = lax.dot_general(
        is_entry.astype(f32), up_bias.reshape(-1, unit_count), (((1,), (0,)), ((), ())), preferred_element_type=f32
    ).reshape(2, 1, FF // 2)

    first_pos = seq_index * shard_len
    query_pos = first_pos + jnp.arange(shard_len, dtype=jnp.int32)
    docs = doc_lengths.shape[1]
    earlier = jnp.arange(docs)[:, None] < jnp.arange(docs)[None, :]
    doc_starts = jnp.sum(jnp.where(earlier[None], doc_lengths[:, :, None], 0), axis=1)
    start = jnp.max(
        jnp.where(doc_starts[:, None, :] <= query_pos[None, :, None], doc_starts[:, None, :], 0), axis=-1
    )
    offsets = (query_pos[None, :] - start).reshape(tokens)
    inverse = 1.0 / rope_base ** (jnp.arange(0, ROT, 2).astype(f32) / ROT)
    angles = offsets.astype(f32)[None, :] * inverse[:, None]
    cosine, sine = jnp.cos(angles), jnp.sin(angles)
    start_here = (start - first_pos).astype(jnp.int32)[:, None, :]

    flat_in = inputs.astype(f32).reshape(tokens, D)
    center = flat_in - jnp.mean(flat_in, axis=-1, keepdims=True)
    inv_sigma = lax.rsqrt(jnp.mean(center * center, axis=-1, keepdims=True) + layer_eps)
    xhat = center * inv_sigma
    normed_one = (xhat * gain_one + shift_one).astype(low)
    normed_two = (xhat * gain_two + shift_two).astype(low)
    dy = cotangent.reshape(tokens, D)
    last = (((1,), (1,)), ((), ()))
    projected = lax.dot_general(qkv_full, normed_one, last, preferred_element_type=f32) + qkv_bias[:, None]
    turned = turn(projected[: D + HEAD], cosine, sine, False).astype(low)
    q_t = turned[:D] * jnp.asarray(HEAD ** (-0.5), low)
    kv_own = jnp.concatenate([turned[D:], projected[D + HEAD :].astype(low)], axis=0)
    reach = seq_count // 2
    kv = [kv_own] + [
        lax.ppermute(kv_own, "seq", [(j, j + i) for j in range(seq_count - i)]) for i in range(1, reach + 1)
    ]
    do_t = lax.dot_general(out_full, dy, (((0,), (1,)), ((), ())), preferred_element_type=f32).astype(low)
    context, dq_t, dkv_own, dkv_sent = attention(q_t, do_t, start_here, cosine, sine, kv)
    dkv = dkv_own
    for i in range(1, reach + 1):
        dkv = dkv + lax.ppermute(dkv_sent[i - 1], "seq", [(j + i, j) for j in range(seq_count - i)]).astype(f32)

    out_one, dn_one, up_grad_far, down_grad_far, bias_grad_far = feed(normed_two, dy, up_far, down_far, bias_near[1], low)
    out_two, dn_two, up_grad_near, down_grad_near, bias_grad_near = feed(
        normed_two, dy, up_near, down_near, bias_near[0], f32
    )

    attn_out = lax.dot_general(context, out_full, last, preferred_element_type=f32)
    outputs = (flat_in + attn_out + (out_one + out_two) + (out_bias + down_bias)).astype(low)

    def reduce_near(near_half, far_half, order):
        value = near_half + swap(far_half, core_bit).astype(f32)
        bits = near[1:]
        value = value.reshape((2,) * len(bits) + (-1, D))
        return sum_bits(value, order[::-1], bits, False)

    up_sum = reduce_near(up_grad_near, up_grad_far, y_then_x)
    down_sum = reduce_near(down_grad_near, down_grad_far, x_then_y)

    out_grad_part = lax.dot_general(dy, context, (((0,), (0,)), ((), ())), preferred_element_type=f32)
    bit_shape = (2,) * len(canon)
    out_sum = sum_bits(
        out_grad_part.reshape(bit_shape + (-1, D)), [core_bit] + x_then_y[::-1], canon, True
    )

    d_proj = jnp.concatenate([dq_t, turn(dkv[:HEAD], cosine, sine, True).astype(low), dkv[HEAD:].astype(low)], axis=0)
    qkv_grad_part = jnp.dot(d_proj, normed_one, preferred_element_type=f32)
    d_normed_one = lax.dot_general(d_proj, qkv_full, (((0,), (0,)), ((), ())), preferred_element_type=f32)
    d_normed_two = dn_one + dn_two
    d_hat = d_normed_one * gain_one + d_normed_two * gain_two
    d_in = (
        d_hat - jnp.mean(d_hat, axis=-1, keepdims=True) - xhat * jnp.mean(d_hat * xhat, axis=-1, keepdims=True)
    ) * inv_sigma
    input_grad = (dy.astype(f32) + d_in).astype(low)
    dy_column = jnp.sum(dy.astype(f32), axis=0)
    bias_grad = jnp.concatenate([bias_grad_near, bias_grad_far], axis=0).reshape(-1, unit_count)
    bias_grad = lax.dot_general(
        is_entry.astype(f32), bias_grad, (((0,), (0,)), ((), ())), precision=lax.Precision.HIGHEST, preferred_element_type=f32
    ).reshape(FF)
    vector_part = jnp.concatenate(
        [
            jnp.sum(d_normed_one * xhat, axis=0),
            jnp.sum(d_normed_one, axis=0),
            jnp.sum(d_normed_two * xhat, axis=0),
            jnp.sum(d_normed_two, axis=0),
            jnp.sum(d_proj.astype(f32), axis=1),
            dy_column,
            bias_grad,
            dy_column,
        ]
    )
    head_part = jnp.concatenate(
        [
            qkv_grad_part.reshape(seq_count, qkv_rows, D),
            jnp.pad(vector_part.reshape(seq_count, vec_len), ((0, 0), (0, vec_pad))).reshape(seq_count, vec_rows, D),
            jnp.zeros((seq_count, head_rows - used, D), f32),
        ],
        axis=1,
    )
    head_sum = sum_bits(head_part.reshape(bit_shape + (-1, D)), [core_bit] + y_then_x[::-1], canon, True)

    batch_canon = x_bits[::-1] + [core_bit]

    def spread(part):
        return gather_bits(part.astype(low), x_bits + [core_bit], batch_canon, True).reshape(-1, D).astype(f32)

    head_grad, out_grad, up_grad, down_grad = spread(head_sum), spread(out_sum), spread(up_sum), spread(down_sum).T
    qkv_grad = head_grad[:qkv_rows]
    vector_grad = head_grad[qkv_rows:used].reshape(-1)[:vec_len]
    qkv_states = soap_step(qkv_weight, qkv_grad, qkv_first, qkv_second, bases[0], True)
    out_states = soap_step(out_weight, out_grad, out_first, out_second, bases[1], True)
    up_states = soap_step(up_weight, up_grad, up_first, up_second, bases[2], True)
    down_states = soap_step(down_weight, down_grad, down_first, down_second, bases[3], False)
    vector_states = adam_step(vectors, vector_grad, vector_first, vector_second)
    states = (qkv_states, out_states, up_states, down_states, vector_states)
    return (
        outputs.reshape(inputs.shape),
        input_grad.reshape(inputs.shape),
        qkv_grad,
        out_grad,
        up_grad,
        down_grad,
        vector_grad,
        *(state[1] for state in states),
        *(state[2] for state in states),
        *(state[0] for state in states),
    )


def solution(mesh):
    tokens = P("batch", "seq", None)
    rows, columns, flat = P("seq", None), P(None, "seq"), P("seq")
    params = (rows, rows, rows, columns, flat)
    return jax.shard_map(
        shards,
        mesh=mesh,
        in_specs=(tokens, tokens, P("batch", None)) + params + (P(),) + params + params,
        out_specs=(tokens, tokens) + params * 4,
        check_vma=False,
    )
```

```python
import functools

import jax
import jax.numpy as jnp
from jax import lax
from jax.experimental import pallas as pl
from jax.experimental.pallas import tpu as pltpu
from jax.sharding import PartitionSpec as P

D = 768
HEADS = 12
HEAD = 64
ROT = 16
FF = 3072
STEP = 10

layer_eps = 1e-05
adam_eps = 1e-08
beta_first = 0.95
beta_second = 0.95
matrix_rate = 0.08
vector_rate = 0.3
rope_base = 10000.0
masked_score = -1e30
low = jnp.bfloat16
f32 = jnp.float32
VMEM_LIMIT = 56 * 1024 * 1024
GROUPS = 2


def swap(value, bit):
    axis, step = bit
    return lax.ppermute(value, axis, [(i, i ^ step) for i in range(lax.axis_size(axis))])


def mine(bit):
    axis, step = bit
    return lax.rem(lax.axis_index(axis) // step, 2)


def flow(first, *others):
    return lax.optimization_barrier((first, *others))[0]


def swap_z(value, step):
    size = lax.axis_size("seq")
    return lax.ppermute(value, "seq", [(i, i ^ (2 * step)) for i in range(size)])


def z_index():
    return lax.axis_index("seq") // 2


def gather_z(piece):
    return [piece] + [swap_z(piece, k) for k in range(1, lax.axis_size("seq") // 2)]


def by_z(parts):
    count = len(parts)
    step = 1
    while step < count:
        upper = lax.rem(z_index() // step, 2) == 1
        parts = [jnp.where(upper, parts[k ^ step], parts[k]) for k in range(count)]
        step *= 2
    return jnp.stack(parts)


def gather_bit(value, bit, axis, absolute=False):
    got = swap(value, bit)
    if absolute:
        upper = mine(bit) == 1
        return jnp.stack([jnp.where(upper, got, value), jnp.where(upper, value, got)], axis=axis)
    return jnp.stack([value, got], axis=axis)


def split_bit(value, bit, axis, absolute=False):
    if absolute:
        own = mine(bit)
        return (
            lax.dynamic_index_in_dim(value, own, axis, keepdims=False),
            lax.dynamic_index_in_dim(value, 1 - own, axis, keepdims=False).astype(low),
        )
    return lax.index_in_dim(value, 0, axis, keepdims=False), lax.index_in_dim(value, 1, axis, keepdims=False).astype(low)


def sum_bit(value, bit, axis, absolute=False):
    kept, sent = split_bit(value, bit, axis, absolute)
    return kept.astype(f32) + swap(sent, bit).astype(f32)


def sum_z(value, absolute=False):
    count = value.shape[0]
    own = z_index() if absolute else 0
    pick = lambda k: lax.dynamic_index_in_dim(value, own ^ k, 0, keepdims=False) if absolute else value[k]
    total = pick(0).astype(f32)
    for k in range(1, count):
        total = total + swap_z(pick(k).astype(low), k).astype(f32)
    return total


def bit_names(axis, size):
    return [(axis, 1 << k) for k in range(size.bit_length() - 1)]


def split_vectors(vectors):
    widths = [D, D, D, D, D + 2 * HEAD, D, FF, D]
    pieces = []
    offset = 0
    for piece_width in widths:
        pieces.append(vectors[offset : offset + piece_width])
        offset = offset + piece_width
    return pieces


def moments(rotated, first, second):
    new_first = beta_first * first + (1.0 - beta_first) * rotated
    new_second = beta_second * second + (1.0 - beta_second) * rotated * rotated
    ratio = (
        new_first
        / (1.0 - beta_first**STEP)
        / (jnp.sqrt(new_second / (1.0 - beta_second**STEP)) + adam_eps)
    )
    return ratio, new_first, new_second


def adam_step(weight, grad, first, second):
    ratio, new_first, new_second = moments(grad, first, second)
    return (weight - vector_rate * ratio, new_first, new_second)


def turn(values, cosine, sine, back):
    half = ROT // 2
    heads = values.reshape(-1, HEAD, values.shape[-1])
    a, b = heads[:, :half], heads[:, half:ROT]
    if back:
        pair = [a * cosine + b * sine, b * cosine - a * sine]
    else:
        pair = [a * cosine - b * sine, b * cosine + a * sine]
    return jnp.concatenate(pair + [heads[:, ROT:]], axis=1).reshape(values.shape)


def attention_kernel(blocks, width, q_ref, do_ref, start_ref, cos_ref, sin_ref, *refs):
    kv_refs = refs[:blocks]
    context_ref, dq_ref, dkv_own_ref, dkv_ref = refs[blocks:]
    length = q_ref.shape[1]
    keys = blocks * length
    key_t = jnp.concatenate([ref[:HEAD, :] for ref in reversed(kv_refs)], axis=1)
    value_t = jnp.concatenate([ref[HEAD:, :] for ref in reversed(kv_refs)], axis=1)
    key = key_t.astype(f32).T.astype(low)
    value = value_t.astype(f32).T.astype(low)
    key_pos = lax.broadcasted_iota(jnp.int32, (keys, length), 0) - (blocks - 1) * length
    query_pos = lax.broadcasted_iota(jnp.int32, (keys, length), 1)
    allowed = (key_pos >= start_ref[0]) & (key_pos <= query_pos)
    bias = jnp.where(allowed, 0.0, masked_score)
    cosine, sine = cos_ref[...], sin_ref[...]
    d_key = jnp.zeros((keys, HEAD), f32)
    d_value = jnp.zeros((keys, HEAD), f32)
    last = (((1,), (1,)), ((), ()))
    for first in range(0, HEADS, width):
        heads = range(first, first + width)
        query = jnp.concatenate([q_ref[h * HEAD : (h + 1) * HEAD, :] for h in heads], axis=1)
        d_out = jnp.concatenate([do_ref[h * HEAD : (h + 1) * HEAD, :] for h in heads], axis=1)
        scores = jnp.dot(key, query, preferred_element_type=f32)
        scores = scores + jnp.concatenate([bias] * width, axis=1)
        weights = jnp.exp(scores - jnp.max(scores, axis=0, keepdims=True))
        probs = weights * (1.0 / jnp.sum(weights, axis=0, keepdims=True))
        probs_low = probs.astype(low)
        context_t = jnp.dot(value_t, probs_low, preferred_element_type=f32)
        d_probs = jnp.dot(value, d_out, preferred_element_type=f32)
        inner = jnp.sum(probs * d_probs, axis=0, keepdims=True)
        d_scores = (probs * (d_probs - inner)).astype(low)
        d_query = jnp.dot(key_t, d_scores, preferred_element_type=f32) * HEAD ** (-0.5)
        d_value = d_value + lax.dot_general(probs_low, d_out, last, preferred_element_type=f32)
        d_key = d_key + lax.dot_general(d_scores, query, last, preferred_element_type=f32)
        for k, h in enumerate(heads):
            lanes = slice(k * length, (k + 1) * length)
            part = d_query[:, lanes]
            a, b = part[: ROT // 2], part[ROT // 2 : ROT]
            turned = jnp.concatenate([a * cosine + b * sine, b * cosine - a * sine, part[ROT:]], axis=0)
            dq_ref[h * HEAD : (h + 1) * HEAD, :] = turned.astype(low)
        for k in range(0, width, 2):
            h = first + k
            two = jnp.concatenate(
                [context_t[:, k * length : (k + 1) * length], context_t[:, (k + 1) * length : (k + 2) * length]], axis=0
            )
            context_ref[:, h * HEAD : (h + 2) * HEAD] = two.T.astype(low)
    d_kv = jnp.concatenate([d_key, d_value], axis=1).T
    for k in range(blocks):
        part = d_kv[:, (blocks - 1 - k) * length : (blocks - k) * length]
        if k == 0:
            dkv_own_ref[...] = part
        else:
            dkv_ref[k - 1] = part.astype(low)


def attention(q_t, do_t, start, cosine, sine, kv):
    rows, _, length = start.shape
    blocks = len(kv)
    tokens = q_t.shape[1]
    by_row = lambda height: pl.BlockSpec((height, length), lambda r: (0, r))
    return pl.pallas_call(
        functools.partial(attention_kernel, blocks, 4),
        grid=(rows,),
        in_specs=[by_row(D), by_row(D), pl.BlockSpec((1, 1, length), lambda r: (r, 0, 0)), by_row(ROT // 2), by_row(ROT // 2)]
        + [by_row(2 * HEAD)] * blocks,
        out_specs=[
            pl.BlockSpec((length, D), lambda r: (r, 0)),
            by_row(D),
            by_row(2 * HEAD),
            pl.BlockSpec((blocks - 1, 2 * HEAD, length), lambda r: (0, 0, r)),
        ],
        out_shape=[
            jax.ShapeDtypeStruct((tokens, D), low),
            jax.ShapeDtypeStruct((D, tokens), low),
            jax.ShapeDtypeStruct((2 * HEAD, tokens), f32),
            jax.ShapeDtypeStruct((blocks - 1, 2 * HEAD, tokens), low),
        ],
        compiler_params=pltpu.CompilerParams(vmem_limit_bytes=VMEM_LIMIT),
        cost_estimate=pl.CostEstimate(
            flops=4 * 7 * tokens * HEADS * blocks * length * HEAD * 2, bytes_accessed=8 << 20, transcendentals=0
        ),
        name="attention",
    )(q_t, do_t, start, cosine, sine, *kv)


def feed_kernel(n_ref, dy_ref, up_ref, down_ref, bias_ref, *refs):
    out_ref, dn_ref, up_grad_ref, down_grad_ref, bias_grad_ref = refs[-5:]
    before = refs[:-5]
    last = (((1,), (1,)), ((), ()))
    first = (((0,), (0,)), ((), ()))
    normed, d_out = n_ref[...], dy_ref[...]
    up, down = up_ref[...], down_ref[...]
    hidden = lax.dot_general(normed, up, last, preferred_element_type=f32) + bias_ref[...]
    share = 0.5 * (1.0 + lax.erf(hidden * (0.5**0.5)))
    slope = share + hidden * (jnp.exp(-0.5 * hidden * hidden) * (0.5 / 3.141592653589793) ** 0.5)
    active = (hidden * share).astype(low)
    d_active = lax.dot_general(d_out, down, last, preferred_element_type=f32)
    d_hidden = (d_active * slope).astype(low)
    out = jnp.dot(active, down, preferred_element_type=f32)
    d_normed = jnp.dot(d_hidden, up, preferred_element_type=f32)

    @pl.when(pl.program_id(0) == 0)
    def _():
        out_ref[...] = before[0][...] + out if before else out
        dn_ref[...] = before[1][...] + d_normed if before else d_normed

    @pl.when(pl.program_id(0) > 0)
    def _():
        out_ref[...] += out
        dn_ref[...] += d_normed

    up_grad_ref[...] = lax.dot_general(d_hidden, normed, first, preferred_element_type=f32).astype(up_grad_ref.dtype)
    down_grad_ref[...] = lax.dot_general(active, d_out, first, preferred_element_type=f32).astype(down_grad_ref.dtype)
    bias_grad_ref[...] = jnp.sum(d_hidden.astype(f32), axis=0, keepdims=True)


def feed(normed, d_out, up, down, bias, before, grad_type):
    tokens = normed.shape[0]
    units = up.shape[0]
    step = 256 if units % 256 == 0 else units
    whole = pl.BlockSpec((tokens, D), lambda i: (0, 0))
    part = pl.BlockSpec((step, D), lambda i: (i, 0))
    row = pl.BlockSpec((1, step), lambda i: (0, i))
    before = before or []
    return pl.pallas_call(
        feed_kernel,
        grid=(units // step,),
        in_specs=[whole, whole, part, part, row] + [whole] * len(before),
        out_specs=[whole, whole, part, part, row],
        out_shape=[
            jax.ShapeDtypeStruct((tokens, D), f32),
            jax.ShapeDtypeStruct((tokens, D), f32),
            jax.ShapeDtypeStruct((units, D), grad_type),
            jax.ShapeDtypeStruct((units, D), grad_type),
            jax.ShapeDtypeStruct((1, units), f32),
        ],
        compiler_params=pltpu.CompilerParams(vmem_limit_bytes=VMEM_LIMIT),
        cost_estimate=pl.CostEstimate(flops=12 * tokens * units * D, bytes_accessed=8 << 20, transcendentals=0),
        name="feed",
    )(normed, d_out, up, down, bias, *before)


def tail_kernel(
    vec_len, x_ref, dy_ref, dq_ref, dkv_ref, cos_ref, sin_ref, w_ref, n_ref, dn_ref, gain_ref, bias_ref,
    in_grad_ref, part_ref, flat,
):
    shards_of, rows = w_ref.shape[:2]
    d_kv = dkv_ref[...]
    a, b = d_kv[: ROT // 2], d_kv[ROT // 2 : ROT]
    cosine, sine = cos_ref[...], sin_ref[...]
    d_kv = jnp.concatenate([a * cosine + b * sine, b * cosine - a * sine, d_kv[ROT:]], axis=0).astype(low)
    d_proj = jnp.concatenate([dq_ref[...], d_kv], axis=0)
    first = (((0,), (0,)), ((), ()))
    weight = w_ref[...].reshape(shards_of * rows, D)
    qkv_grad = jnp.dot(d_proj, n_ref[...], preferred_element_type=f32)
    d_one = lax.dot_general(d_proj, weight, first, preferred_element_type=f32)
    d_two = dn_ref[...]
    x = x_ref[...].astype(f32)
    dy = dy_ref[...].astype(f32)
    center = x - jnp.mean(x, axis=-1, keepdims=True)
    inv_sigma = lax.rsqrt(jnp.mean(center * center, axis=-1, keepdims=True) + layer_eps)
    xhat = center * inv_sigma
    d_hat = d_one * gain_ref[0:1] + d_two * gain_ref[1:2]
    d_in = (
        d_hat - jnp.mean(d_hat, axis=-1, keepdims=True) - xhat * jnp.mean(d_hat * xhat, axis=-1, keepdims=True)
    ) * inv_sigma
    in_grad_ref[...] = (dy + d_in).astype(low)
    columns = lambda v: jnp.sum(v, axis=0, keepdims=True)
    dy_column = columns(dy)
    ones = jnp.ones((8, d_proj.shape[1]), low)
    proj_sum = lax.dot_general(ones, d_proj, (((1,), (1,)), ((), ())), preferred_element_type=f32)[0:1]
    pieces = [columns(d_one * xhat), columns(d_one), columns(d_two * xhat), columns(d_two)]
    pieces += [proj_sum, dy_column, bias_ref[...], dy_column]
    offset = 0
    for piece in pieces:
        flat[:, offset : offset + piece.shape[1]] = piece
        offset += piece.shape[1]
    part_ref[...] = jnp.zeros_like(part_ref)
    for s in range(shards_of):
        part_ref[s, :rows, :] = qkv_grad[s * rows : (s + 1) * rows]
        left = vec_len
        row = rows
        while left > 0:
            size = min(left, D)
            begin = s * vec_len + (row - rows) * D
            part_ref[s, row : row + 1, :size] = flat[:, begin : begin + size]
            left -= size
            row += 1


def tail(x, dy, dq_t, dkv, cosine, sine, weight, normed, d_normed, gains, bias_grad, head_rows, vec_len):
    tokens = x.shape[0]
    shards_of = weight.shape[0]
    total = shards_of * vec_len
    return pl.pallas_call(
        functools.partial(tail_kernel, vec_len),
        out_shape=[
            jax.ShapeDtypeStruct((tokens, D), low),
            jax.ShapeDtypeStruct((shards_of, head_rows, D), f32),
        ],
        scratch_shapes=[pltpu.VMEM((1, total), f32)],
        compiler_params=pltpu.CompilerParams(vmem_limit_bytes=VMEM_LIMIT),
        cost_estimate=pl.CostEstimate(flops=4 * tokens * 896 * D, bytes_accessed=8 << 20, transcendentals=0),
        name="tail",
    )(x, dy, dq_t, dkv, cosine, sine, weight, normed, d_normed, gains, bias_grad)


def split_low(value):
    high = value.astype(low)
    return high, (value - high.astype(f32)).astype(low)


def update_kernel(
    across, g_ref, basis_ref, w_ref, first_ref, second_ref, grad_ref, first_new_ref, second_new_ref, w_new_ref, b_high, b_low
):
    @pl.when(pl.program_id(0) == 0)
    def _():
        high, rest = split_low(basis_ref[...])
        b_high[...] = high
        b_low[...] = rest

    high, rest = b_high[...], b_low[...]
    grad = g_ref[...]
    rotated = jnp.dot(grad, high, preferred_element_type=f32) + jnp.dot(grad, rest, preferred_element_type=f32)
    grad = grad.astype(f32)
    if across:
        rotated, grad = rotated.T, grad.T
    grad_ref[...] = grad
    ratio, first_new, second_new = moments(rotated, first_ref[...], second_ref[...])
    first_new_ref[...] = first_new
    second_new_ref[...] = second_new
    r_high, r_rest = split_low(ratio)
    if across:
        product = lambda r, b: jnp.dot(b, r, preferred_element_type=f32)
    else:
        product = lambda r, b: lax.dot_general(r, b, (((1,), (1,)), ((), ())), preferred_element_type=f32)
    unrotated = product(r_high, high) + (product(r_high, rest) + product(r_rest, high))
    w_new_ref[...] = w_ref[...] - matrix_rate * unrotated


def update(grad, bases, number, weight, first, second, across=False):
    count = grad.shape[0]
    step = 128 if count % 128 == 0 else count
    block = pl.BlockSpec((D, step), lambda i: (0, i)) if across else pl.BlockSpec((step, D), lambda i: (i, 0))
    return pl.pallas_call(
        functools.partial(update_kernel, across),
        grid=(count // step,),
        in_specs=[pl.BlockSpec((step, D), lambda i: (i, 0)), pl.BlockSpec((None, D, D), lambda i: (number, 0, 0)), block, block, block],
        out_specs=[block] * 4,
        out_shape=[jax.ShapeDtypeStruct(weight.shape, f32)] * 4,
        scratch_shapes=[pltpu.VMEM((D, D), low), pltpu.VMEM((D, D), low)],
        compiler_params=pltpu.CompilerParams(vmem_limit_bytes=VMEM_LIMIT),
        cost_estimate=pl.CostEstimate(flops=10 * count * D * D, bytes_accessed=8 << 20, transcendentals=0),
        name="update",
    )(grad, bases, weight, first, second)


def shards(
    inputs,
    cotangent,
    doc_lengths,
    qkv_weight,
    out_weight,
    up_weight,
    down_weight,
    vectors,
    bases,
    qkv_first,
    out_first,
    up_first,
    down_first,
    vector_first,
    qkv_second,
    out_second,
    up_second,
    down_second,
    vector_second,
):
    seq_count, batch_count = lax.axis_size("seq"), lax.axis_size("batch")
    seq_index, batch_index = lax.axis_index("seq"), lax.axis_index("batch")
    row_count, shard_len = inputs.shape[:2]
    tokens = row_count * shard_len
    y_bit, *z_bits = bit_names("seq", seq_count)
    core_bit, *x_bits = bit_names("batch", batch_count)
    near = [core_bit] + x_bits[::-1] + [y_bit] + z_bits[::-1]

    qkv_rows, out_rows, up_rows, vec_len = qkv_weight.shape[0], out_weight.shape[0], up_weight.shape[0], vectors.shape[0]
    vec_rows = -(-vec_len // D)
    used = qkv_rows + vec_rows
    head_rows = -(-used // (8 * batch_count)) * 8 * batch_count
    vec_pad = vec_rows * D - vec_len

    def own_part(rows):
        size = rows.shape[0] // batch_count
        return lax.dynamic_slice_in_dim(rows, batch_index * size, size, axis=0)

    head_shard = jnp.concatenate(
        [qkv_weight, jnp.pad(vectors, (0, vec_pad)).reshape(vec_rows, D), jnp.zeros((head_rows - used, D), f32)], axis=0
    ).astype(low)
    out_part = own_part(out_weight.astype(low))
    head_part_rows = head_rows // batch_count
    first_group = gather_z(jnp.concatenate([own_part(head_shard), out_part], axis=0))
    by_depth = by_z(first_group)
    head_full, out_full = by_depth[:, :head_part_rows], by_depth[:, head_part_rows:]
    head_full = gather_bit(head_full, y_bit, 1, True)
    for bit in x_bits:
        out_full = gather_bit(out_full, bit, 1, True)
    for bit in x_bits:
        head_full = gather_bit(head_full, bit, 2, True)
    out_full = gather_bit(out_full, y_bit, 1, True)
    order = 2 + len(x_bits)
    head_full = gather_bit(head_full, core_bit, order, True).reshape(seq_count, head_rows, D)
    out_full = gather_bit(out_full, core_bit, order, True).reshape(D, D)

    up_part, down_part = own_part(up_weight.astype(low)), own_part(down_weight.T.astype(low))
    unit_rows = up_part.shape[0] // GROUPS
    earlier_z = first_group[1]
    feed_weights = []
    for g in range(GROUPS):
        rows = slice(g * unit_rows, (g + 1) * unit_rows)
        both = flow(jnp.concatenate([up_part[rows], down_part[rows]], axis=0), earlier_z)
        parts = gather_z(both)
        earlier_z = parts[1]
        parts = jnp.stack(parts)
        up_near, down_near = parts[:, :unit_rows], parts[:, unit_rows:]
        up_near = gather_bit(up_near, y_bit, 0)
        for bit in x_bits:
            down_near = gather_bit(down_near, bit, 0)
        for bit in x_bits:
            up_near = gather_bit(up_near, bit, 0)
        down_near = gather_bit(down_near, y_bit, len(x_bits))
        up_near, down_near = up_near.reshape(-1, D), down_near.reshape(-1, D)
        feed_weights.append((up_near, down_near, swap(up_near, core_bit), swap(down_near, core_bit)))

    qkv_rows_full = head_full[:, :qkv_rows]
    qkv_full = qkv_rows_full.reshape(D + 2 * HEAD, D)
    vector_full = head_full[:, qkv_rows:used].reshape(seq_count, vec_rows * D)[:, :vec_len].reshape(-1)
    pieces = split_vectors(vector_full.astype(f32))
    gain_one, shift_one, gain_two, shift_two, qkv_bias, out_bias, up_bias, down_bias = pieces
    unit_count = up_rows // batch_count
    device = jnp.arange(seq_count * batch_count)
    entry = jnp.zeros_like(device)
    for axis_name, index, number in (("seq", seq_index, device // batch_count), ("batch", batch_index, device % batch_count)):
        differs = number ^ index
        for place_from_end, bit in enumerate(near[::-1]):
            if bit[0] == axis_name:
                entry = entry + ((differs // bit[1]) % 2) * (1 << place_from_end)
    is_entry = entry[None, :] == device[:, None]
    bias_near = lax.dot_general(
        is_entry.astype(f32), up_bias.reshape(-1, unit_count), (((1,), (0,)), ((), ())), preferred_element_type=f32
    )
    bias_near = bias_near.reshape(2, -1, GROUPS, unit_rows).transpose(0, 2, 1, 3).reshape(2, GROUPS, 1, -1)

    first_pos = seq_index * shard_len
    query_pos = first_pos + jnp.arange(shard_len, dtype=jnp.int32)
    docs = doc_lengths.shape[1]
    earlier = jnp.arange(docs)[:, None] < jnp.arange(docs)[None, :]
    doc_starts = jnp.sum(jnp.where(earlier[None], doc_lengths[:, :, None], 0), axis=1)
    start = jnp.max(
        jnp.where(doc_starts[:, None, :] <= query_pos[None, :, None], doc_starts[:, None, :], 0), axis=-1
    )
    offsets = (query_pos[None, :] - start).reshape(tokens)
    inverse = 1.0 / rope_base ** (jnp.arange(0, ROT, 2).astype(f32) / ROT)
    angles = offsets.astype(f32)[None, :] * inverse[:, None]
    cosine, sine = jnp.cos(angles), jnp.sin(angles)
    start_here = (start - first_pos).astype(jnp.int32)[:, None, :]

    flat_in = inputs.astype(f32).reshape(tokens, D)
    center = flat_in - jnp.mean(flat_in, axis=-1, keepdims=True)
    inv_sigma = lax.rsqrt(jnp.mean(center * center, axis=-1, keepdims=True) + layer_eps)
    xhat = center * inv_sigma
    normed_one = (xhat * gain_one + shift_one).astype(low)
    normed_two = (xhat * gain_two + shift_two).astype(low)
    dy = cotangent.reshape(tokens, D)
    last = (((1,), (1,)), ((), ()))
    projected = lax.dot_general(qkv_full, normed_one, last, preferred_element_type=f32) + qkv_bias[:, None]
    turned = turn(projected[: D + HEAD], cosine, sine, False).astype(low)
    q_t = turned[:D] * jnp.asarray(HEAD ** (-0.5), low)
    kv_own = jnp.concatenate([turned[D:], projected[D + HEAD :].astype(low)], axis=0)
    reach = seq_count // 2
    kv = [kv_own] + [
        lax.ppermute(kv_own, "seq", [(j, j + i) for j in range(seq_count - i)]) for i in range(1, reach + 1)
    ]
    do_t = lax.dot_general(out_full, dy, (((0,), (1,)), ((), ())), preferred_element_type=f32).astype(low)
    context, dq_t, dkv_own, dkv_sent = attention(q_t, do_t, start_here, cosine, sine, kv)
    dkv = dkv_own
    for i in range(1, reach + 1):
        dkv = dkv + lax.ppermute(dkv_sent[i - 1], "seq", [(j + i, j) for j in range(seq_count - i)]).astype(f32)

    d_hidden_sums, up_sums, down_sums = [[], []], [], []
    sums = None
    for g, (up_near, down_near, up_far, down_far) in enumerate(feed_weights):
        *sums, up_grad_far, down_grad_far, bias_far = feed(normed_two, dy, up_far, down_far, bias_near[1, g], sums, low)
        up_got, down_got = swap(up_grad_far, core_bit), swap(down_grad_far, core_bit)
        *sums, up_grad, down_grad, bias_here = feed(normed_two, dy, up_near, down_near, bias_near[0, g], sums, f32)
        d_hidden_sums[0].append(bias_here)
        d_hidden_sums[1].append(bias_far)
        shape = (2,) * len(x_bits) + (2, seq_count // 2, unit_rows, D)
        up_sum = (up_grad + up_got.astype(f32)).reshape(shape)
        down_sum = (down_grad + down_got.astype(f32)).reshape(shape)
        for bit in x_bits[::-1]:
            up_sum = sum_bit(up_sum, bit, 0)
        down_sum = sum_bit(down_sum, y_bit, len(x_bits))
        up_sum = sum_bit(up_sum, y_bit, 0)
        for bit in x_bits[::-1]:
            down_sum = sum_bit(down_sum, bit, 0)
        both = sum_z(jnp.concatenate([up_sum, down_sum], axis=1))
        up_sums.append(both[:unit_rows])
        down_sums.append(both[unit_rows:])
    mlp_out, d_normed_two = sums

    attn_out = lax.dot_general(context, out_full, last, preferred_element_type=f32)
    outputs = (flat_in + attn_out + mlp_out + (out_bias + down_bias)).astype(low)

    out_grad_part = lax.dot_general(dy, context, (((0,), (0,)), ((), ())), preferred_element_type=f32)
    bias_grad = jnp.stack([jnp.concatenate(side, axis=0) for side in d_hidden_sums])
    bias_grad = bias_grad.reshape(2, GROUPS, -1, unit_rows).transpose(0, 2, 1, 3).reshape(-1, unit_count)
    bias_grad = lax.dot_general(
        is_entry.astype(f32), bias_grad, (((0,), (0,)), ((), ())), precision=lax.Precision.HIGHEST, preferred_element_type=f32
    ).reshape(1, FF)
    input_grad, head_part = tail(
        inputs.reshape(tokens, D), dy, dq_t, dkv, cosine, sine, qkv_rows_full, normed_one, d_normed_two,
        jnp.stack([gain_one, gain_two]), bias_grad, head_rows, vec_len,
    )
    shape = (seq_count // 2, 2) + (2,) * len(x_bits) + (2, -1, D)
    both = jnp.concatenate([head_part.reshape(shape), out_grad_part.reshape(shape)], axis=len(shape) - 2)
    both = sum_bit(both, core_bit, len(shape) - 3, True)
    head_sum, out_sum = both[..., :head_part_rows, :], both[..., head_part_rows:, :]
    for bit in x_bits[::-1]:
        head_sum = sum_bit(head_sum, bit, 2, True)
    out_sum = sum_bit(out_sum, y_bit, 1, True)
    head_sum = sum_bit(head_sum, y_bit, 1, True)
    for bit in x_bits[::-1]:
        out_sum = sum_bit(out_sum, bit, 1, True)
    both = sum_z(jnp.concatenate([head_sum, out_sum], axis=1), True)

    def spread(part):
        value = part.astype(low)
        for k, bit in enumerate(x_bits):
            value = gather_bit(value, bit, 0, True)
        value = gather_bit(value, core_bit, len(x_bits), True)
        return value.reshape(batch_count, -1, D)

    feed_grads = spread(jnp.concatenate(up_sums + down_sums, axis=0))
    up_low = feed_grads[:, : GROUPS * unit_rows].reshape(-1, D)
    down_low = feed_grads[:, GROUPS * unit_rows :].reshape(-1, D)
    others = spread(both)
    head_low = others[:, :head_part_rows].reshape(-1, D)
    out_low = others[:, head_part_rows:].reshape(-1, D)
    up_grad, *up_states = update(up_low, bases, 2, up_weight, up_first, up_second)
    down_grad, *down_states = update(down_low, bases, 3, down_weight, down_first, down_second, True)
    out_grad, *out_states = update(out_low, bases, 1, out_weight, out_first, out_second)
    qkv_grad, *qkv_states = update(head_low[:qkv_rows], bases, 0, qkv_weight, qkv_first, qkv_second)
    vector_grad = head_low[qkv_rows:used].astype(f32).reshape(-1)[:vec_len]
    vector_new, *vector_states = adam_step(vectors, vector_grad, vector_first, vector_second)
    states = (qkv_states, out_states, up_states, down_states, (*vector_states, vector_new))
    return (
        outputs.reshape(inputs.shape),
        input_grad.reshape(inputs.shape),
        qkv_grad,
        out_grad,
        up_grad,
        down_grad,
        vector_grad,
        *(state[0] for state in states),
        *(state[1] for state in states),
        *(state[2] for state in states),
    )


def solution(mesh):
    tokens = P("batch", "seq", None)
    rows, columns, flat = P("seq", None), P(None, "seq"), P("seq")
    params = (rows, rows, rows, columns, flat)
    return jax.shard_map(
        shards,
        mesh=mesh,
        in_specs=(tokens, tokens, P("batch", None)) + params + (P(),) + params + params,
        out_specs=(tokens, tokens) + params * 4,
        check_vma=False,
    )
```

```python
import functools

import jax
import jax.numpy as jnp
from jax import lax
from jax.experimental import pallas as pl
from jax.experimental.pallas import tpu as pltpu
from jax.sharding import PartitionSpec as P

D = 768
HEADS = 12
HEAD = 64
ROT = 16
FF = 3072
STEP = 10

layer_eps = 1e-05
adam_eps = 1e-08
beta_first = 0.95
beta_second = 0.95
matrix_rate = 0.08
vector_rate = 0.3
rope_base = 10000.0
masked_score = -1e30
low = jnp.bfloat16
f32 = jnp.float32
VMEM_LIMIT = 56 * 1024 * 1024
GROUPS = 2
FEED_VMEM = 36 * 1024 * 1024
UPDATE_VMEM = 24 * 1024 * 1024


def swap(value, bit):
    axis, step = bit
    return lax.ppermute(value, axis, [(i, i ^ step) for i in range(lax.axis_size(axis))])


def mine(bit):
    axis, step = bit
    return lax.rem(lax.axis_index(axis) // step, 2)


def flow(first, *others):
    return lax.optimization_barrier((first, *others))[0]


def swap_z(value, step):
    size = lax.axis_size("seq")
    return lax.ppermute(value, "seq", [(i, i ^ (2 * step)) for i in range(size)])


def z_index():
    return lax.axis_index("seq") // 2


def gather_z(piece):
    return [piece] + [swap_z(piece, k) for k in range(1, lax.axis_size("seq") // 2)]


def by_z(parts):
    count = len(parts)
    step = 1
    while step < count:
        upper = lax.rem(z_index() // step, 2) == 1
        parts = [jnp.where(upper, parts[k ^ step], parts[k]) for k in range(count)]
        step *= 2
    return jnp.stack(parts)


def gather_bit(value, bit, axis, absolute=False):
    got = swap(value, bit)
    if absolute:
        upper = mine(bit) == 1
        return jnp.stack([jnp.where(upper, got, value), jnp.where(upper, value, got)], axis=axis)
    return jnp.stack([value, got], axis=axis)


def split_bit(value, bit, axis, absolute=False):
    if absolute:
        own = mine(bit)
        return (
            lax.dynamic_index_in_dim(value, own, axis, keepdims=False),
            lax.dynamic_index_in_dim(value, 1 - own, axis, keepdims=False).astype(low),
        )
    return lax.index_in_dim(value, 0, axis, keepdims=False), lax.index_in_dim(value, 1, axis, keepdims=False).astype(low)


def sum_bit(value, bit, axis, absolute=False):
    kept, sent = split_bit(value, bit, axis, absolute)
    return kept.astype(f32) + swap(sent, bit).astype(f32)


def sum_z(value, absolute=False):
    count = value.shape[0]
    own = z_index() if absolute else 0
    pick = lambda k: lax.dynamic_index_in_dim(value, own ^ k, 0, keepdims=False) if absolute else value[k]
    total = pick(0).astype(f32)
    for k in range(1, count):
        total = total + swap_z(pick(k).astype(low), k).astype(f32)
    return total


def bit_names(axis, size):
    return [(axis, 1 << k) for k in range(size.bit_length() - 1)]


def split_vectors(vectors):
    widths = [D, D, D, D, D + 2 * HEAD, D, FF, D]
    pieces = []
    offset = 0
    for piece_width in widths:
        pieces.append(vectors[offset : offset + piece_width])
        offset = offset + piece_width
    return pieces


def moments(rotated, first, second):
    new_first = beta_first * first + (1.0 - beta_first) * rotated
    new_second = beta_second * second + (1.0 - beta_second) * rotated * rotated
    ratio = (
        new_first
        / (1.0 - beta_first**STEP)
        / (jnp.sqrt(new_second / (1.0 - beta_second**STEP)) + adam_eps)
    )
    return ratio, new_first, new_second


def adam_step(weight, grad, first, second):
    ratio, new_first, new_second = moments(grad, first, second)
    return (weight - vector_rate * ratio, new_first, new_second)


def turn(values, cosine, sine, back):
    half = ROT // 2
    heads = values.reshape(-1, HEAD, values.shape[-1])
    a, b = heads[:, :half], heads[:, half:ROT]
    if back:
        pair = [a * cosine + b * sine, b * cosine - a * sine]
    else:
        pair = [a * cosine - b * sine, b * cosine + a * sine]
    return jnp.concatenate(pair + [heads[:, ROT:]], axis=1).reshape(values.shape)


def attention_kernel(blocks, width, q_ref, do_ref, start_ref, cos_ref, sin_ref, *refs):
    kv_refs = refs[:blocks]
    context_ref, dq_ref, dkv_own_ref, dkv_ref = refs[blocks:]
    length = q_ref.shape[1]
    keys = blocks * length
    key_t = jnp.concatenate([ref[:HEAD, :] for ref in reversed(kv_refs)], axis=1)
    value_t = jnp.concatenate([ref[HEAD:, :] for ref in reversed(kv_refs)], axis=1)
    key = key_t.astype(f32).T.astype(low)
    value = value_t.astype(f32).T.astype(low)
    key_pos = lax.broadcasted_iota(jnp.int32, (keys, length), 0) - (blocks - 1) * length
    query_pos = lax.broadcasted_iota(jnp.int32, (keys, length), 1)
    allowed = (key_pos >= start_ref[0]) & (key_pos <= query_pos)
    bias = jnp.where(allowed, 0.0, masked_score)
    cosine, sine = cos_ref[...], sin_ref[...]
    d_key = jnp.zeros((keys, HEAD), f32)
    d_value = jnp.zeros((keys, HEAD), f32)
    last = (((1,), (1,)), ((), ()))
    for first in range(0, HEADS, width):
        heads = range(first, first + width)
        query = jnp.concatenate([q_ref[h * HEAD : (h + 1) * HEAD, :] for h in heads], axis=1)
        d_out = jnp.concatenate([do_ref[h * HEAD : (h + 1) * HEAD, :] for h in heads], axis=1)
        scores = jnp.dot(key, query, preferred_element_type=f32)
        scores = scores + jnp.concatenate([bias] * width, axis=1)
        weights = jnp.exp(scores - jnp.max(scores, axis=0, keepdims=True))
        probs = weights * (1.0 / jnp.sum(weights, axis=0, keepdims=True))
        probs_low = probs.astype(low)
        context_t = jnp.dot(value_t, probs_low, preferred_element_type=f32)
        d_probs = jnp.dot(value, d_out, preferred_element_type=f32)
        inner = jnp.sum(probs * d_probs, axis=0, keepdims=True)
        d_scores = (probs * (d_probs - inner)).astype(low)
        d_query = jnp.dot(key_t, d_scores, preferred_element_type=f32) * HEAD ** (-0.5)
        d_value = d_value + lax.dot_general(probs_low, d_out, last, preferred_element_type=f32)
        d_key = d_key + lax.dot_general(d_scores, query, last, preferred_element_type=f32)
        for k, h in enumerate(heads):
            lanes = slice(k * length, (k + 1) * length)
            part = d_query[:, lanes]
            a, b = part[: ROT // 2], part[ROT // 2 : ROT]
            turned = jnp.concatenate([a * cosine + b * sine, b * cosine - a * sine, part[ROT:]], axis=0)
            dq_ref[h * HEAD : (h + 1) * HEAD, :] = turned.astype(low)
        for k in range(0, width, 2):
            h = first + k
            two = jnp.concatenate(
                [context_t[:, k * length : (k + 1) * length], context_t[:, (k + 1) * length : (k + 2) * length]], axis=0
            )
            context_ref[:, h * HEAD : (h + 2) * HEAD] = two.T.astype(low)
    d_kv = jnp.concatenate([d_key, d_value], axis=1).T
    for k in range(blocks):
        part = d_kv[:, (blocks - 1 - k) * length : (blocks - k) * length]
        if k == 0:
            dkv_own_ref[...] = part
        else:
            dkv_ref[k - 1] = part.astype(low)


def attention(q_t, do_t, start, cosine, sine, kv):
    rows, _, length = start.shape
    blocks = len(kv)
    tokens = q_t.shape[1]
    by_row = lambda height: pl.BlockSpec((height, length), lambda r: (0, r))
    return pl.pallas_call(
        functools.partial(attention_kernel, blocks, HEADS),
        grid=(rows,),
        in_specs=[by_row(D), by_row(D), pl.BlockSpec((1, 1, length), lambda r: (r, 0, 0)), by_row(ROT // 2), by_row(ROT // 2)]
        + [by_row(2 * HEAD)] * blocks,
        out_specs=[
            pl.BlockSpec((length, D), lambda r: (r, 0)),
            by_row(D),
            by_row(2 * HEAD),
            pl.BlockSpec((blocks - 1, 2 * HEAD, length), lambda r: (0, 0, r)),
        ],
        out_shape=[
            jax.ShapeDtypeStruct((tokens, D), low),
            jax.ShapeDtypeStruct((D, tokens), low),
            jax.ShapeDtypeStruct((2 * HEAD, tokens), f32),
            jax.ShapeDtypeStruct((blocks - 1, 2 * HEAD, tokens), low),
        ],
        compiler_params=pltpu.CompilerParams(vmem_limit_bytes=VMEM_LIMIT),
        cost_estimate=pl.CostEstimate(
            flops=4 * 7 * tokens * HEADS * blocks * length * HEAD * 2, bytes_accessed=8 << 20, transcendentals=0
        ),
        name="attention",
    )(q_t, do_t, start, cosine, sine, *kv)


def feed_kernel(n_ref, dy_ref, far_ref, near_ref, bias_far_ref, bias_near_ref, *refs):
    out_ref, dn_ref, far_grad_ref, near_grad_ref, bias_far_grad_ref, bias_near_grad_ref = refs[-6:]
    before = refs[:-6]
    last = (((1,), (1,)), ((), ()))
    first = (((0,), (0,)), ((), ()))
    normed, d_out = n_ref[...], dy_ref[...]
    units = far_ref.shape[0] // 2
    out, d_normed = 0.0, 0.0
    for weight_ref, bias_ref, grad_ref, bias_grad_ref in (
        (far_ref, bias_far_ref, far_grad_ref, bias_far_grad_ref),
        (near_ref, bias_near_ref, near_grad_ref, bias_near_grad_ref),
    ):
        up, down = weight_ref[:units], weight_ref[units:]
        hidden = lax.dot_general(normed, up, last, preferred_element_type=f32) + bias_ref[...]
        share = 0.5 * (1.0 + lax.erf(hidden * (0.5**0.5)))
        slope = share + hidden * (jnp.exp(-0.5 * hidden * hidden) * (0.5 / 3.141592653589793) ** 0.5)
        active = (hidden * share).astype(low)
        d_active = lax.dot_general(d_out, down, last, preferred_element_type=f32)
        d_hidden = (d_active * slope).astype(low)
        grad_ref[:units] = lax.dot_general(d_hidden, normed, first, preferred_element_type=f32).astype(grad_ref.dtype)
        grad_ref[units:] = lax.dot_general(active, d_out, first, preferred_element_type=f32).astype(grad_ref.dtype)
        bias_grad_ref[...] = jnp.sum(d_hidden.astype(f32), axis=0, keepdims=True)
        out = out + jnp.dot(active, down, preferred_element_type=f32)
        d_normed = d_normed + jnp.dot(d_hidden, up, preferred_element_type=f32)
    out_ref[...] = before[0][...] + out if before else out
    dn_ref[...] = before[1][...] + d_normed if before else d_normed


def feed(normed, d_out, far, near, bias_far, bias_near, before):
    tokens = normed.shape[0]
    units = far.shape[0] // 2
    return pl.pallas_call(
        feed_kernel,
        out_shape=[
            jax.ShapeDtypeStruct((tokens, D), f32),
            jax.ShapeDtypeStruct((tokens, D), f32),
            jax.ShapeDtypeStruct((2 * units, D), low),
            jax.ShapeDtypeStruct((2 * units, D), f32),
            jax.ShapeDtypeStruct((1, units), f32),
            jax.ShapeDtypeStruct((1, units), f32),
        ],
        compiler_params=pltpu.CompilerParams(vmem_limit_bytes=FEED_VMEM),
        cost_estimate=pl.CostEstimate(flops=24 * tokens * units * D, bytes_accessed=8 << 20, transcendentals=0),
        name="feed",
    )(normed, d_out, far, near, bias_far, bias_near, *(before or []))


def tail_kernel(
    vec_len, sides, entry_ref, x_ref, dy_ref, dq_ref, dkv_ref, cos_ref, sin_ref, w_ref, n_ref, dn_ref, gain_ref, *refs,
):
    bias_refs, (in_grad_ref, part_ref, flat, units) = refs[:-4], refs[-4:]
    shards_of, rows = w_ref.shape[:2]
    d_kv = dkv_ref[...]
    a, b = d_kv[: ROT // 2], d_kv[ROT // 2 : ROT]
    cosine, sine = cos_ref[...], sin_ref[...]
    d_kv = jnp.concatenate([a * cosine + b * sine, b * cosine - a * sine, d_kv[ROT:]], axis=0).astype(low)
    d_proj = jnp.concatenate([dq_ref[...], d_kv], axis=0)
    first = (((0,), (0,)), ((), ()))
    weight = w_ref[...].reshape(shards_of * rows, D)
    qkv_grad = jnp.dot(d_proj, n_ref[...], preferred_element_type=f32)
    d_one = lax.dot_general(d_proj, weight, first, preferred_element_type=f32)
    d_two = dn_ref[...]
    x = x_ref[...].astype(f32)
    dy = dy_ref[...].astype(f32)
    center = x - jnp.mean(x, axis=-1, keepdims=True)
    inv_sigma = lax.rsqrt(jnp.mean(center * center, axis=-1, keepdims=True) + layer_eps)
    xhat = center * inv_sigma
    d_hat = d_one * gain_ref[0:1] + d_two * gain_ref[1:2]
    d_in = (
        d_hat - jnp.mean(d_hat, axis=-1, keepdims=True) - xhat * jnp.mean(d_hat * xhat, axis=-1, keepdims=True)
    ) * inv_sigma
    in_grad_ref[...] = (dy + d_in).astype(low)
    columns = lambda v: jnp.sum(v, axis=0, keepdims=True)
    dy_column = columns(dy)
    ones = jnp.ones((8, d_proj.shape[1]), low)
    proj_sum = lax.dot_general(ones, d_proj, (((1,), (1,)), ((), ())), preferred_element_type=f32)[0:1]
    pieces = [columns(d_one * xhat), columns(d_one), columns(d_two * xhat), columns(d_two)]
    pieces += [proj_sum, dy_column, None, dy_column]
    count, size = units.shape
    groups = len(bias_refs) // sides
    width = size // groups
    for k, ref in enumerate(bias_refs):
        side, g = k // groups, k % groups
        for i in range(count // sides):
            entry = side * (count // sides) + i
            units[entry : entry + 1, g * width : (g + 1) * width] = ref[:, i * width : (i + 1) * width]
    offset = 0
    for piece in pieces:
        if piece is None:
            for k in range(count):
                flat[:, offset : offset + size] = units[pl.ds(entry_ref[k], 1), :]
                offset += size
        else:
            flat[:, offset : offset + piece.shape[1]] = piece
            offset += piece.shape[1]
    part_ref[...] = jnp.zeros_like(part_ref)
    for s in range(shards_of):
        part_ref[s, :rows, :] = qkv_grad[s * rows : (s + 1) * rows]
        left = vec_len
        row = rows
        while left > 0:
            size = min(left, D)
            begin = s * vec_len + (row - rows) * D
            part_ref[s, row : row + 1, :size] = flat[:, begin : begin + size]
            left -= size
            row += 1


def tail(entry, x, dy, dq_t, dkv, cosine, sine, weight, normed, d_normed, gains, bias_grads, head_rows, vec_len):
    tokens = x.shape[0]
    shards_of = weight.shape[0]
    total = shards_of * vec_len
    sides = len(bias_grads)
    count = entry.shape[0]
    operands = (entry, x, dy, dq_t, dkv, cosine, sine, weight, normed, d_normed, gains, *sum(bias_grads, []))
    return pl.pallas_call(
        functools.partial(tail_kernel, vec_len, sides),
        in_specs=[pl.BlockSpec(memory_space=pltpu.SMEM)] + [pl.BlockSpec(memory_space=pltpu.VMEM)] * (len(operands) - 1),
        out_shape=[
            jax.ShapeDtypeStruct((tokens, D), low),
            jax.ShapeDtypeStruct((shards_of, head_rows, D), f32),
        ],
        scratch_shapes=[pltpu.VMEM((1, total), f32), pltpu.VMEM((count, FF // count), f32)],
        compiler_params=pltpu.CompilerParams(vmem_limit_bytes=VMEM_LIMIT),
        cost_estimate=pl.CostEstimate(flops=4 * tokens * 896 * D, bytes_accessed=8 << 20, transcendentals=0),
        name="tail",
    )(*operands)


def split_low(value):
    high = value.astype(low)
    return high, (value - high.astype(f32)).astype(low)


def update_kernel(
    across, g_ref, high_ref, rest_ref, w_ref, first_ref, second_ref, grad_ref, first_new_ref, second_new_ref, w_new_ref
):
    high, rest = high_ref[...], rest_ref[...]
    grad = g_ref[...]
    rotated = jnp.dot(grad, high, preferred_element_type=f32) + jnp.dot(grad, rest, preferred_element_type=f32)
    grad = grad.astype(f32)
    if across:
        rotated, grad = rotated.T, grad.T
    grad_ref[...] = grad
    ratio, first_new, second_new = moments(rotated, first_ref[...], second_ref[...])
    first_new_ref[...] = first_new
    second_new_ref[...] = second_new
    r_high, r_rest = split_low(ratio)
    if across:
        product = lambda r, b: jnp.dot(b, r, preferred_element_type=f32)
    else:
        product = lambda r, b: lax.dot_general(r, b, (((1,), (1,)), ((), ())), preferred_element_type=f32)
    unrotated = product(r_high, high) + (product(r_high, rest) + product(r_rest, high))
    w_new_ref[...] = w_ref[...] - matrix_rate * unrotated


def update(grad, bases, number, weight, first, second, across=False):
    count = grad.shape[0]
    step = 128 if count % 128 == 0 else count
    basis = pl.BlockSpec((None, D, D), lambda i: (number, 0, 0))
    block = pl.BlockSpec((D, step), lambda i: (0, i)) if across else pl.BlockSpec((step, D), lambda i: (i, 0))
    return pl.pallas_call(
        functools.partial(update_kernel, across),
        grid=(count // step,),
        in_specs=[pl.BlockSpec((step, D), lambda i: (i, 0)), basis, basis, block, block, block],
        out_specs=[block] * 4,
        out_shape=[jax.ShapeDtypeStruct(weight.shape, f32)] * 4,
        compiler_params=pltpu.CompilerParams(vmem_limit_bytes=UPDATE_VMEM),
        cost_estimate=pl.CostEstimate(flops=10 * count * D * D, bytes_accessed=8 << 20, transcendentals=0),
        name="update",
    )(grad, *bases, weight, first, second)


def shards(
    inputs,
    cotangent,
    doc_lengths,
    qkv_weight,
    out_weight,
    up_weight,
    down_weight,
    vectors,
    bases,
    qkv_first,
    out_first,
    up_first,
    down_first,
    vector_first,
    qkv_second,
    out_second,
    up_second,
    down_second,
    vector_second,
):
    seq_count, batch_count = lax.axis_size("seq"), lax.axis_size("batch")
    seq_index, batch_index = lax.axis_index("seq"), lax.axis_index("batch")
    row_count, shard_len = inputs.shape[:2]
    tokens = row_count * shard_len
    y_bit, *z_bits = bit_names("seq", seq_count)
    core_bit, *x_bits = bit_names("batch", batch_count)
    near = [core_bit] + x_bits[::-1] + [y_bit] + z_bits[::-1]

    qkv_rows, out_rows, up_rows, vec_len = qkv_weight.shape[0], out_weight.shape[0], up_weight.shape[0], vectors.shape[0]
    vec_rows = -(-vec_len // D)
    used = qkv_rows + vec_rows
    head_rows = -(-used // (8 * batch_count)) * 8 * batch_count
    vec_pad = vec_rows * D - vec_len

    def own_part(rows):
        size = rows.shape[0] // batch_count
        return lax.dynamic_slice_in_dim(rows, batch_index * size, size, axis=0)

    head_shard = jnp.concatenate(
        [qkv_weight, jnp.pad(vectors, (0, vec_pad)).reshape(vec_rows, D), jnp.zeros((head_rows - used, D), f32)], axis=0
    ).astype(low)
    out_part = own_part(out_weight.astype(low))
    head_part_rows = head_rows // batch_count
    first_group = gather_z(jnp.concatenate([own_part(head_shard), out_part], axis=0))
    bases_high = bases.astype(low)
    bases_split = (bases_high, (bases - bases_high.astype(f32)).astype(low))
    by_depth = flow(by_z(first_group), *bases_split)
    head_full, out_full = by_depth[:, :head_part_rows], by_depth[:, head_part_rows:]
    head_full = gather_bit(head_full, y_bit, 1, True)
    for bit in x_bits:
        out_full = gather_bit(out_full, bit, 1, True)
    half_way = (head_full, out_full)
    for bit in x_bits:
        head_full = gather_bit(head_full, bit, 2, True)
    out_full = gather_bit(out_full, y_bit, 1, True)
    order = 2 + len(x_bits)
    both = gather_bit(jnp.concatenate([head_full, out_full], axis=order), core_bit, order, True)
    head_full = both[..., :head_part_rows, :].reshape(seq_count, head_rows, D)
    out_full = both[..., head_part_rows:, :].reshape(D, D)

    up_part, down_part = own_part(up_weight.astype(low)), own_part(down_weight.T.astype(low))
    unit_rows = up_part.shape[0] // GROUPS
    feed_parts = []
    for g in range(GROUPS):
        rows = slice(g * unit_rows, (g + 1) * unit_rows)
        parts = gather_z(flow(jnp.concatenate([up_part[rows], down_part[rows]], axis=0), *half_way))
        half_way = half_way + (parts[0],)
        feed_parts.append(parts)

    qkv_rows_full = head_full[:, :qkv_rows]
    qkv_full = qkv_rows_full.reshape(D + 2 * HEAD, D)
    vector_full = head_full[:, qkv_rows:used].reshape(seq_count, vec_rows * D)[:, :vec_len].reshape(-1)
    pieces = split_vectors(vector_full.astype(f32))
    gain_one, shift_one, gain_two, shift_two, qkv_bias, out_bias, up_bias, down_bias = pieces
    unit_count = up_rows // batch_count
    device = jnp.arange(seq_count * batch_count)
    entry = jnp.zeros_like(device)
    for axis_name, index, number in (("seq", seq_index, device // batch_count), ("batch", batch_index, device % batch_count)):
        differs = number ^ index
        for place_from_end, bit in enumerate(near[::-1]):
            if bit[0] == axis_name:
                entry = entry + ((differs // bit[1]) % 2) * (1 << place_from_end)
    is_entry = entry[None, :] == device[:, None]
    bias_near = lax.dot_general(
        is_entry.astype(f32), up_bias.reshape(-1, unit_count), (((1,), (0,)), ((), ())), preferred_element_type=f32
    )
    bias_near = bias_near.reshape(2, -1, GROUPS, unit_rows).transpose(0, 2, 1, 3).reshape(2, GROUPS, 1, -1)

    first_pos = seq_index * shard_len
    query_pos = first_pos + jnp.arange(shard_len, dtype=jnp.int32)
    docs = doc_lengths.shape[1]
    earlier = jnp.arange(docs)[:, None] < jnp.arange(docs)[None, :]
    doc_starts = jnp.sum(jnp.where(earlier[None], doc_lengths[:, :, None], 0), axis=1)
    start = jnp.max(
        jnp.where(doc_starts[:, None, :] <= query_pos[None, :, None], doc_starts[:, None, :], 0), axis=-1
    )
    offsets = (query_pos[None, :] - start).reshape(tokens)
    inverse = 1.0 / rope_base ** (jnp.arange(0, ROT, 2).astype(f32) / ROT)
    angles = offsets.astype(f32)[None, :] * inverse[:, None]
    cosine, sine = jnp.cos(angles), jnp.sin(angles)
    start_here = (start - first_pos).astype(jnp.int32)[:, None, :]

    flat_in = inputs.astype(f32).reshape(tokens, D)
    center = flat_in - jnp.mean(flat_in, axis=-1, keepdims=True)
    inv_sigma = lax.rsqrt(jnp.mean(center * center, axis=-1, keepdims=True) + layer_eps)
    xhat = center * inv_sigma
    normed_one = (xhat * gain_one + shift_one).astype(low)
    normed_two = (xhat * gain_two + shift_two).astype(low)
    dy = cotangent.reshape(tokens, D)
    last = (((1,), (1,)), ((), ()))
    projected = lax.dot_general(qkv_full, normed_one, last, preferred_element_type=f32) + qkv_bias[:, None]
    turned = turn(projected[: D + HEAD], cosine, sine, False).astype(low)
    q_t = turned[:D] * jnp.asarray(HEAD ** (-0.5), low)
    kv_own = jnp.concatenate([turned[D:], projected[D + HEAD :].astype(low)], axis=0)
    reach = seq_count // 2
    kv = [kv_own] + [
        lax.ppermute(kv_own, "seq", [(j, j + i) for j in range(seq_count - i)]) for i in range(1, reach + 1)
    ]
    feed_weights = []
    first_phase = ()
    for parts in feed_parts:
        parts = flow(jnp.stack(parts), kv[min(2, reach)])
        up_near, down_near = parts[:, :unit_rows], parts[:, unit_rows:]
        up_near = gather_bit(up_near, y_bit, 0)
        for bit in x_bits:
            down_near = gather_bit(down_near, bit, 0)
        first_phase = (up_near, down_near)
        for bit in x_bits:
            up_near = gather_bit(up_near, bit, 0)
        down_near = gather_bit(down_near, y_bit, len(x_bits))
        both = jnp.concatenate([up_near.reshape(-1, D), down_near.reshape(-1, D)], axis=0)
        feed_weights.append((both, swap(both, core_bit)))
    do_t = lax.dot_general(out_full, dy, (((0,), (1,)), ((), ())), preferred_element_type=f32).astype(low)
    context, dq_t, dkv_own, dkv_sent = attention(q_t, do_t, start_here, cosine, sine, kv)
    dkv = dkv_own
    for i in range(1, reach + 1):
        dkv = dkv + lax.ppermute(dkv_sent[i - 1], "seq", [(j + i, j) for j in range(seq_count - i)]).astype(f32)

    bias_grads, grad_sums = [[], []], []
    sums = None
    earlier = (dq_t, *first_phase)
    for g, (near_weight, far_weight) in enumerate(feed_weights):
        far_weight = flow(far_weight, *earlier)
        *sums, far_grad, near_grad, bias_far, bias_here = feed(
            normed_two, dy, far_weight, near_weight, bias_near[1, g], bias_near[0, g], sums
        )
        bias_grads[0].append(bias_here)
        bias_grads[1].append(bias_far)
        grad_sums.append(near_grad + swap(far_grad, core_bit).astype(f32))
        earlier = (grad_sums[-1], dkv)
    mlp_out, d_normed_two = sums

    attn_out = lax.dot_general(context, out_full, last, preferred_element_type=f32)
    outputs = (flat_in + attn_out + mlp_out + (out_bias + down_bias)).astype(low)

    out_grad_part = lax.dot_general(dy, context, (((0,), (0,)), ((), ())), preferred_element_type=f32)
    input_grad, head_part = tail(
        entry.astype(jnp.int32), inputs.reshape(tokens, D), dy, dq_t, dkv, cosine, sine, qkv_rows_full, normed_one, d_normed_two,
        jnp.stack([gain_one, gain_two]), bias_grads, head_rows, vec_len,
    )
    def feed_first(both):
        units = both.shape[0] // 2
        shape = (2,) * len(x_bits) + (2, seq_count // 2, unit_rows, D)
        up_sum, down_sum = both[:units].reshape(shape), both[units:].reshape(shape)
        for bit in x_bits[::-1]:
            up_sum = sum_bit(up_sum, bit, 0)
        return up_sum, sum_bit(down_sum, y_bit, len(x_bits))

    def feed_second(up_sum, down_sum):
        up_sum = sum_bit(up_sum, y_bit, 0)
        for bit in x_bits[::-1]:
            down_sum = sum_bit(down_sum, bit, 0)
        return jnp.concatenate([up_sum, down_sum], axis=1)

    shape = (seq_count // 2, 2) + (2,) * len(x_bits) + (2, -1, D)
    feed_sums = []
    for g, grad_sum in enumerate(grad_sums):
        up_sum, down_sum = feed_first(grad_sum)
        if g == GROUPS - 1:
            both = jnp.concatenate([head_part.reshape(shape), out_grad_part.reshape(shape)], axis=len(shape) - 2)
            both = sum_bit(flow(both, grad_sum), core_bit, len(shape) - 3, True)
            up_sum = flow(up_sum, both)
        last_step = feed_second(up_sum, down_sum)
        if g == GROUPS - 1:
            head_sum, out_sum = both[..., :head_part_rows, :], both[..., head_part_rows:, :]
            for bit in x_bits[::-1]:
                head_sum = sum_bit(head_sum, bit, 2, True)
            out_sum = sum_bit(out_sum, y_bit, 1, True)
            last_step = flow(last_step, head_sum, out_sum)
        else:
            last_step = flow(last_step, head_part)
        feed_sums.append(sum_z(last_step))
    head_sum = sum_bit(head_sum, y_bit, 1, True)
    for bit in x_bits[::-1]:
        out_sum = sum_bit(out_sum, bit, 1, True)
    both = jnp.concatenate([head_sum, out_sum], axis=1)
    feed_sums[-1] = flow(feed_sums[-1], both)
    both = sum_z(both, True)

    def spread(part):
        value = part.astype(low)
        for k, bit in enumerate(x_bits):
            value = gather_bit(value, bit, 0, True)
        value = gather_bit(value, core_bit, len(x_bits), True)
        return value.reshape(batch_count, -1, D)

    feed_grads = spread(
        jnp.concatenate([part[:unit_rows] for part in feed_sums] + [part[unit_rows:] for part in feed_sums], axis=0)
    )
    up_low = feed_grads[:, : GROUPS * unit_rows].reshape(-1, D)
    down_low = feed_grads[:, GROUPS * unit_rows :].reshape(-1, D)
    others = spread(both)
    head_low = others[:, :head_part_rows].reshape(-1, D)
    out_low = others[:, head_part_rows:].reshape(-1, D)
    up_grad, *up_states = update(up_low, bases_split, 2, up_weight, up_first, up_second)
    down_grad, *down_states = update(down_low, bases_split, 3, down_weight, down_first, down_second, True)
    out_grad, *out_states = update(out_low, bases_split, 1, out_weight, out_first, out_second)
    qkv_grad, *qkv_states = update(head_low[:qkv_rows], bases_split, 0, qkv_weight, qkv_first, qkv_second)
    vector_grad = head_low[qkv_rows:used].astype(f32).reshape(-1)[:vec_len]
    vector_new, *vector_states = adam_step(vectors, vector_grad, vector_first, vector_second)
    states = (qkv_states, out_states, up_states, down_states, (*vector_states, vector_new))
    return (
        outputs.reshape(inputs.shape),
        input_grad.reshape(inputs.shape),
        qkv_grad,
        out_grad,
        up_grad,
        down_grad,
        vector_grad,
        *(state[0] for state in states),
        *(state[1] for state in states),
        *(state[2] for state in states),
    )


def solution(mesh):
    tokens = P("batch", "seq", None)
    rows, columns, flat = P("seq", None), P(None, "seq"), P("seq")
    params = (rows, rows, rows, columns, flat)
    return jax.shard_map(
        shards,
        mesh=mesh,
        in_specs=(tokens, tokens, P("batch", None)) + params + (P(),) + params + params,
        out_specs=(tokens, tokens) + params * 4,
        check_vma=False,
    )
```

```python
import functools

import jax
import jax.numpy as jnp
from jax import lax
from jax.experimental import pallas as pl
from jax.experimental.pallas import tpu as pltpu
from jax.sharding import PartitionSpec as P

D = 768
HEADS = 12
HEAD = 64
ROT = 16
FF = 3072
STEP = 10

layer_eps = 1e-05
adam_eps = 1e-08
beta_first = 0.95
beta_second = 0.95
matrix_rate = 0.08
vector_rate = 0.3
rope_base = 10000.0
masked_score = -1e30
low = jnp.bfloat16
f32 = jnp.float32
VMEM_LIMIT = 56 * 1024 * 1024
FEED_VMEM = 36 * 1024 * 1024
UPDATE_VMEM = 24 * 1024 * 1024


def swap(value, bit):
    axis, step = bit
    return lax.ppermute(value, axis, [(i, i ^ step) for i in range(lax.axis_size(axis))])


def mine(bit):
    axis, step = bit
    return lax.rem(lax.axis_index(axis) // step, 2)


def flow(first, *others):
    return lax.optimization_barrier((first, *others))[0]


def swap_z(value, step):
    size = lax.axis_size("seq")
    return lax.ppermute(value, "seq", [(i, i ^ (2 * step)) for i in range(size)])


def z_index():
    return lax.axis_index("seq") // 2


def gather_z(piece):
    return [piece] + [swap_z(piece, k) for k in range(1, lax.axis_size("seq") // 2)]


def gather_bit(value, bit, axis, absolute=False):
    got = swap(value, bit)
    if absolute:
        upper = mine(bit) == 1
        return jnp.stack([jnp.where(upper, got, value), jnp.where(upper, value, got)], axis=axis)
    return jnp.stack([value, got], axis=axis)


def split_bit(value, bit, axis, absolute=False):
    if absolute:
        own = mine(bit)
        return (
            lax.dynamic_index_in_dim(value, own, axis, keepdims=False),
            lax.dynamic_index_in_dim(value, 1 - own, axis, keepdims=False).astype(low),
        )
    return lax.index_in_dim(value, 0, axis, keepdims=False), lax.index_in_dim(value, 1, axis, keepdims=False).astype(low)


def sum_bit(value, bit, axis, absolute=False):
    kept, sent = split_bit(value, bit, axis, absolute)
    return kept.astype(f32) + swap(sent, bit).astype(f32)


def sum_z(value, absolute=False):
    count = value.shape[0]
    own = z_index() if absolute else 0
    pick = lambda k: lax.dynamic_index_in_dim(value, own ^ k, 0, keepdims=False) if absolute else value[k]
    total = pick(0).astype(f32)
    for k in range(1, count):
        total = total + swap_z(pick(k).astype(low), k).astype(f32)
    return total


def bit_names(axis, size):
    return [(axis, 1 << k) for k in range(size.bit_length() - 1)]


def moments(rotated, first, second):
    new_first = beta_first * first + (1.0 - beta_first) * rotated
    new_second = beta_second * second + (1.0 - beta_second) * rotated * rotated
    ratio = (
        new_first
        / (1.0 - beta_first**STEP)
        / (jnp.sqrt(new_second / (1.0 - beta_second**STEP)) + adam_eps)
    )
    return ratio, new_first, new_second


def adam_step(weight, grad, first, second):
    ratio, new_first, new_second = moments(grad, first, second)
    return (weight - vector_rate * ratio, new_first, new_second)


def attention_kernel(blocks, width, q_ref, do_ref, start_ref, cos_ref, sin_ref, kv_ref, context_ref, dq_ref, dkv_own_ref, dkv_ref):
    length = q_ref.shape[1]
    keys = blocks * length
    key_t = jnp.concatenate([kv_ref[k, :HEAD, :] for k in reversed(range(blocks))], axis=1)
    value_t = jnp.concatenate([kv_ref[k, HEAD:, :] for k in reversed(range(blocks))], axis=1)
    key = key_t.astype(f32).T.astype(low)
    value = value_t.astype(f32).T.astype(low)
    key_pos = lax.broadcasted_iota(jnp.int32, (keys, length), 0) - (blocks - 1) * length
    query_pos = lax.broadcasted_iota(jnp.int32, (keys, length), 1)
    allowed = (key_pos >= start_ref[0]) & (key_pos <= query_pos)
    bias = jnp.where(allowed, 0.0, masked_score)
    cosine, sine = cos_ref[...], sin_ref[...]
    d_key = jnp.zeros((keys, HEAD), f32)
    d_value = jnp.zeros((keys, HEAD), f32)
    last = (((1,), (1,)), ((), ()))
    for first in range(0, HEADS, width):
        heads = range(first, first + width)
        query = jnp.concatenate([q_ref[h * HEAD : (h + 1) * HEAD, :] for h in heads], axis=1)
        d_out = jnp.concatenate([do_ref[h * HEAD : (h + 1) * HEAD, :] for h in heads], axis=1)
        scores = jnp.dot(key, query, preferred_element_type=f32)
        scores = scores + jnp.concatenate([bias] * width, axis=1)
        weights = jnp.exp(scores - jnp.max(scores, axis=0, keepdims=True))
        probs = weights * (1.0 / jnp.sum(weights, axis=0, keepdims=True))
        probs_low = probs.astype(low)
        context_t = jnp.dot(value_t, probs_low, preferred_element_type=f32)
        d_probs = jnp.dot(value, d_out, preferred_element_type=f32)
        inner = jnp.sum(probs * d_probs, axis=0, keepdims=True)
        d_scores = (probs * (d_probs - inner)).astype(low)
        d_query = jnp.dot(key_t, d_scores, preferred_element_type=f32) * HEAD ** (-0.5)
        d_value = d_value + lax.dot_general(probs_low, d_out, last, preferred_element_type=f32)
        d_key = d_key + lax.dot_general(d_scores, query, last, preferred_element_type=f32)
        for k, h in enumerate(heads):
            lanes = slice(k * length, (k + 1) * length)
            part = d_query[:, lanes]
            a, b = part[: ROT // 2], part[ROT // 2 : ROT]
            turned = jnp.concatenate([a * cosine + b * sine, b * cosine - a * sine, part[ROT:]], axis=0)
            dq_ref[h * HEAD : (h + 1) * HEAD, :] = turned.astype(low)
        for k in range(0, width, 2):
            h = first + k
            two = jnp.concatenate(
                [context_t[:, k * length : (k + 1) * length], context_t[:, (k + 1) * length : (k + 2) * length]], axis=0
            )
            context_ref[:, h * HEAD : (h + 2) * HEAD] = two.T.astype(low)
    d_kv = jnp.concatenate([d_key, d_value], axis=1).T
    for k in range(blocks):
        part = d_kv[:, (blocks - 1 - k) * length : (blocks - k) * length]
        if k == 0:
            dkv_own_ref[...] = part
        else:
            dkv_ref[k - 1] = part.astype(low)


def attention(q_t, do_t, start, cosine, sine, kv):
    rows, _, length = start.shape
    blocks = kv.shape[0]
    tokens = q_t.shape[1]
    by_row = lambda height: pl.BlockSpec((height, length), lambda r: (0, r))
    return pl.pallas_call(
        functools.partial(attention_kernel, blocks, HEADS),
        grid=(rows,),
        in_specs=[by_row(D), by_row(D), pl.BlockSpec((1, 1, length), lambda r: (r, 0, 0)), by_row(ROT // 2), by_row(ROT // 2)]
        + [pl.BlockSpec((blocks, 2 * HEAD, length), lambda r: (0, 0, r))],
        out_specs=[
            pl.BlockSpec((length, D), lambda r: (r, 0)),
            by_row(D),
            by_row(2 * HEAD),
            pl.BlockSpec((blocks - 1, 2 * HEAD, length), lambda r: (0, 0, r)),
        ],
        out_shape=[
            jax.ShapeDtypeStruct((tokens, D), low),
            jax.ShapeDtypeStruct((D, tokens), low),
            jax.ShapeDtypeStruct((2 * HEAD, tokens), f32),
            jax.ShapeDtypeStruct((blocks - 1, 2 * HEAD, tokens), low),
        ],
        compiler_params=pltpu.CompilerParams(vmem_limit_bytes=VMEM_LIMIT),
        cost_estimate=pl.CostEstimate(
            flops=4 * 7 * tokens * HEADS * blocks * length * HEAD * 2, bytes_accessed=8 << 20, transcendentals=0
        ),
        name="attention",
    )(q_t, do_t, start, cosine, sine, kv)


def feed_kernel(pieces, n_ref, dy_ref, far_ref, near_ref, bias_far_ref, bias_near_ref, *refs):
    out_ref, dn_ref, far_grad_ref, near_grad_ref, bias_far_grad_ref, bias_near_grad_ref = refs[-6:]
    before = refs[:-6]
    last = (((1,), (1,)), ((), ()))
    first = (((0,), (0,)), ((), ()))
    normed, d_out = n_ref[...], dy_ref[...]
    units = far_grad_ref.shape[1]
    out, d_normed = 0.0, 0.0
    for weight_ref, bias_ref, grad_ref, bias_grad_ref in (
        (far_ref, bias_far_ref, far_grad_ref, bias_far_grad_ref),
        (near_ref, bias_near_ref, near_grad_ref, bias_near_grad_ref),
    ):
        up = jnp.concatenate([weight_ref[0, k] for k in pieces], axis=0)
        down = jnp.concatenate([weight_ref[1, k] for k in pieces], axis=0)
        hidden = lax.dot_general(normed, up, last, preferred_element_type=f32) + bias_ref[...]
        share = 0.5 * (1.0 + lax.erf(hidden * (0.5**0.5)))
        slope = share + hidden * (jnp.exp(-0.5 * hidden * hidden) * (0.5 / 3.141592653589793) ** 0.5)
        active = (hidden * share).astype(low)
        d_active = lax.dot_general(d_out, down, last, preferred_element_type=f32)
        d_hidden = (d_active * slope).astype(low)
        grad_ref[0] = lax.dot_general(d_hidden, normed, first, preferred_element_type=f32).astype(grad_ref.dtype)
        grad_ref[1] = lax.dot_general(active, d_out, first, preferred_element_type=f32).astype(grad_ref.dtype)
        bias_grad_ref[...] = jnp.sum(d_hidden.astype(f32), axis=0, keepdims=True)
        out = out + jnp.dot(active, down, preferred_element_type=f32)
        d_normed = d_normed + jnp.dot(d_hidden, up, preferred_element_type=f32)
    out_ref[...] = before[0][...] + out if before else out
    dn_ref[...] = before[1][...] + d_normed if before else d_normed


def feed(normed, d_out, far, near, bias_far, bias_near, pieces, before):
    tokens = normed.shape[0]
    units = len(pieces) * far.shape[2]
    return pl.pallas_call(
        functools.partial(feed_kernel, pieces),
        out_shape=[
            jax.ShapeDtypeStruct((tokens, D), f32),
            jax.ShapeDtypeStruct((tokens, D), f32),
            jax.ShapeDtypeStruct((2, units, D), low),
            jax.ShapeDtypeStruct((2, units, D), f32),
            jax.ShapeDtypeStruct((1, units), f32),
            jax.ShapeDtypeStruct((1, units), f32),
        ],
        compiler_params=pltpu.CompilerParams(vmem_limit_bytes=FEED_VMEM),
        cost_estimate=pl.CostEstimate(flops=24 * tokens * units * D, bytes_accessed=8 << 20, transcendentals=0),
        name="feed",
    )(normed, d_out, far, near, bias_far, bias_near, *(before or []))


def head_kernel(
    vec_len, group_pieces, device_ref, x_ref, head_ref, cos_ref, sin_ref, n_one_ref, n_two_ref, q_ref, kv_ref, gain_ref,
    bias_ref, *refs
):
    bias_refs, (flat, units) = refs[:-2], refs[-2:]
    shards_of = head_ref.shape[0]
    rows = (D + 2 * HEAD) // shards_of
    for s in range(shards_of):
        left, row = vec_len, rows
        tile = head_ref[s, rows:, :].astype(f32)
        while left > 0:
            size = min(left, D)
            begin = s * vec_len + (row - rows) * D
            flat[:, begin : begin + size] = tile[row - rows : row - rows + 1, :size]
            left -= size
            row += 1
    vector = lambda begin, size: flat[:, begin : begin + size]
    gain_one, shift_one, gain_two, shift_two = [vector(k * D, D) for k in range(4)]
    gain_ref[0:1] = gain_one
    gain_ref[1:2] = gain_two
    qkv_bias = vector(4 * D, D + 2 * HEAD)
    offset = 4 * D + D + 2 * HEAD
    bias_ref[...] = vector(offset, D) + vector(offset + D + FF, D)
    count, size = units.shape
    for k in range(count):
        units[k : k + 1, :] = vector(offset + D + k * size, size)
    sides = len(bias_refs) // len(group_pieces)
    for k, ref in enumerate(bias_refs):
        side, pieces = k // len(group_pieces), group_pieces[k % len(group_pieces)]
        for i, piece in enumerate(pieces):
            ref[:, i * size : (i + 1) * size] = units[pl.ds(device_ref[side * (count // sides) + piece], 1), :]
    x = x_ref[...].astype(f32)
    center = x - jnp.mean(x, axis=-1, keepdims=True)
    xhat = center * lax.rsqrt(jnp.mean(center * center, axis=-1, keepdims=True) + layer_eps)
    n_one = (xhat * gain_one + shift_one).astype(low)
    n_one_ref[...] = n_one
    n_two_ref[...] = (xhat * gain_two + shift_two).astype(low)
    weight = head_ref[:, :rows, :].reshape(shards_of * rows, D)
    column = jnp.broadcast_to(qkv_bias, (8, qkv_bias.shape[1])).T[:, 0:1]
    projected = lax.dot_general(weight, n_one, (((1,), (1,)), ((), ())), preferred_element_type=f32) + column
    cosine, sine = cos_ref[...], sin_ref[...]
    half = ROT // 2

    def turned(first):
        a, b = projected[first : first + half], projected[first + half : first + ROT]
        rest = projected[first + ROT : first + HEAD]
        return jnp.concatenate([a * cosine - b * sine, b * cosine + a * sine, rest], axis=0).astype(low)

    for h in range(HEADS):
        q_ref[h * HEAD : (h + 1) * HEAD, :] = turned(h * HEAD) * jnp.asarray(HEAD ** (-0.5), low)
    kv_ref[:HEAD, :] = turned(D)
    kv_ref[HEAD:, :] = projected[D + HEAD :].astype(low)


def head(device, x, head_full, cosine, sine, group_pieces, sides, vec_len):
    tokens = x.shape[0]
    shards_of = head_full.shape[0]
    count = device.shape[0]
    bias_rows = [jax.ShapeDtypeStruct((1, len(pieces) * (FF // count)), f32) for pieces in group_pieces] * sides
    return pl.pallas_call(
        functools.partial(head_kernel, vec_len, group_pieces),
        in_specs=[pl.BlockSpec(memory_space=pltpu.SMEM)] + [pl.BlockSpec(memory_space=pltpu.VMEM)] * 4,
        out_shape=[
            jax.ShapeDtypeStruct((tokens, D), low),
            jax.ShapeDtypeStruct((tokens, D), low),
            jax.ShapeDtypeStruct((D, tokens), low),
            jax.ShapeDtypeStruct((2 * HEAD, tokens), low),
            jax.ShapeDtypeStruct((2, D), f32),
            jax.ShapeDtypeStruct((1, D), f32),
            *bias_rows,
        ],
        scratch_shapes=[pltpu.VMEM((1, shards_of * vec_len), f32), pltpu.VMEM((count, FF // count), f32)],
        compiler_params=pltpu.CompilerParams(vmem_limit_bytes=FEED_VMEM),
        cost_estimate=pl.CostEstimate(flops=2 * tokens * 896 * D, bytes_accessed=8 << 20, transcendentals=0),
        name="head",
    )(device, x, head_full, cosine, sine)


def tail_kernel(
    vec_len, group_pieces, entry_ref, x_ref, dy_ref, dq_ref, dkv_ref, cos_ref, sin_ref, w_ref, n_ref, dn_ref, gain_ref, *refs,
):
    bias_refs, (in_grad_ref, part_ref, flat, units) = refs[:-4], refs[-4:]
    shards_of = w_ref.shape[0]
    rows = (D + 2 * HEAD) // shards_of
    d_kv = dkv_ref[...]
    a, b = d_kv[: ROT // 2], d_kv[ROT // 2 : ROT]
    cosine, sine = cos_ref[...], sin_ref[...]
    d_kv = jnp.concatenate([a * cosine + b * sine, b * cosine - a * sine, d_kv[ROT:]], axis=0).astype(low)
    d_proj = jnp.concatenate([dq_ref[...], d_kv], axis=0)
    first = (((0,), (0,)), ((), ()))
    weight = w_ref[:, :rows, :].reshape(shards_of * rows, D)
    qkv_grad = jnp.dot(d_proj, n_ref[...], preferred_element_type=f32)
    d_one = lax.dot_general(d_proj, weight, first, preferred_element_type=f32)
    d_two = dn_ref[...]
    x = x_ref[...].astype(f32)
    dy = dy_ref[...].astype(f32)
    center = x - jnp.mean(x, axis=-1, keepdims=True)
    inv_sigma = lax.rsqrt(jnp.mean(center * center, axis=-1, keepdims=True) + layer_eps)
    xhat = center * inv_sigma
    d_hat = d_one * gain_ref[0:1] + d_two * gain_ref[1:2]
    d_in = (
        d_hat - jnp.mean(d_hat, axis=-1, keepdims=True) - xhat * jnp.mean(d_hat * xhat, axis=-1, keepdims=True)
    ) * inv_sigma
    in_grad_ref[...] = (dy + d_in).astype(low)
    columns = lambda v: jnp.sum(v, axis=0, keepdims=True)
    dy_column = columns(dy)
    ones = jnp.ones((8, d_proj.shape[1]), low)
    proj_sum = lax.dot_general(ones, d_proj, (((1,), (1,)), ((), ())), preferred_element_type=f32)[0:1]
    pieces = [columns(d_one * xhat), columns(d_one), columns(d_two * xhat), columns(d_two)]
    pieces += [proj_sum, dy_column, None, dy_column]
    count, size = units.shape
    sides = len(bias_refs) // len(group_pieces)
    for k, ref in enumerate(bias_refs):
        side, members = k // len(group_pieces), group_pieces[k % len(group_pieces)]
        for i, member in enumerate(members):
            entry = side * (count // sides) + member
            units[entry : entry + 1, :] = ref[:, i * size : (i + 1) * size]
    offset = 0
    for piece in pieces:
        if piece is None:
            for k in range(count):
                flat[:, offset : offset + size] = units[pl.ds(entry_ref[k], 1), :]
                offset += size
        else:
            flat[:, offset : offset + piece.shape[1]] = piece
            offset += piece.shape[1]
    part_ref[...] = jnp.zeros_like(part_ref)
    for s in range(shards_of):
        part_ref[s, :rows, :] = qkv_grad[s * rows : (s + 1) * rows]
        left = vec_len
        row = rows
        while left > 0:
            size = min(left, D)
            begin = s * vec_len + (row - rows) * D
            part_ref[s, row : row + 1, :size] = flat[:, begin : begin + size]
            left -= size
            row += 1


def tail(entry, x, dy, dq_t, dkv, cosine, sine, weight, normed, d_normed, gains, bias_grads, group_pieces, head_rows, vec_len):
    tokens = x.shape[0]
    shards_of = weight.shape[0]
    total = shards_of * vec_len
    count = entry.shape[0]
    operands = (entry, x, dy, dq_t, dkv, cosine, sine, weight, normed, d_normed, gains, *sum(bias_grads, []))
    return pl.pallas_call(
        functools.partial(tail_kernel, vec_len, group_pieces),
        in_specs=[pl.BlockSpec(memory_space=pltpu.SMEM)] + [pl.BlockSpec(memory_space=pltpu.VMEM)] * (len(operands) - 1),
        out_shape=[
            jax.ShapeDtypeStruct((tokens, D), low),
            jax.ShapeDtypeStruct((shards_of, head_rows, D), f32),
        ],
        scratch_shapes=[pltpu.VMEM((1, total), f32), pltpu.VMEM((count, FF // count), f32)],
        compiler_params=pltpu.CompilerParams(vmem_limit_bytes=VMEM_LIMIT),
        cost_estimate=pl.CostEstimate(flops=4 * tokens * 896 * D, bytes_accessed=8 << 20, transcendentals=0),
        name="tail",
    )(*operands)


def split_low(value):
    high = value.astype(low)
    return high, (value - high.astype(f32)).astype(low)


def update_kernel(
    across, g_ref, high_ref, rest_ref, w_ref, first_ref, second_ref, grad_ref, first_new_ref, second_new_ref, w_new_ref
):
    high, rest = high_ref[...], rest_ref[...]
    grad = g_ref[...]
    rotated = jnp.dot(grad, high, preferred_element_type=f32) + jnp.dot(grad, rest, preferred_element_type=f32)
    grad = grad.astype(f32)
    if across:
        rotated, grad = rotated.T, grad.T
    grad_ref[...] = grad
    ratio, first_new, second_new = moments(rotated, first_ref[...], second_ref[...])
    first_new_ref[...] = first_new
    second_new_ref[...] = second_new
    r_high, r_rest = split_low(ratio)
    if across:
        product = lambda r, b: jnp.dot(b, r, preferred_element_type=f32)
    else:
        product = lambda r, b: lax.dot_general(r, b, (((1,), (1,)), ((), ())), preferred_element_type=f32)
    unrotated = product(r_high, high) + (product(r_high, rest) + product(r_rest, high))
    w_new_ref[...] = w_ref[...] - matrix_rate * unrotated


def update(grad, bases, number, weight, first, second, across=False):
    count = grad.shape[0]
    step = 128 if count % 128 == 0 else count
    basis = pl.BlockSpec((None, D, D), lambda i: (number, 0, 0))
    block = pl.BlockSpec((D, step), lambda i: (0, i)) if across else pl.BlockSpec((step, D), lambda i: (i, 0))
    return pl.pallas_call(
        functools.partial(update_kernel, across),
        grid=(count // step,),
        in_specs=[pl.BlockSpec((step, D), lambda i: (i, 0)), basis, basis, block, block, block],
        out_specs=[block] * 4,
        out_shape=[jax.ShapeDtypeStruct(weight.shape, f32)] * 4,
        compiler_params=pltpu.CompilerParams(vmem_limit_bytes=UPDATE_VMEM),
        cost_estimate=pl.CostEstimate(flops=10 * count * D * D, bytes_accessed=8 << 20, transcendentals=0),
        name="update",
    )(grad, *bases, weight, first, second)


def shards(
    inputs,
    cotangent,
    doc_lengths,
    qkv_weight,
    out_weight,
    up_weight,
    down_weight,
    vectors,
    bases,
    qkv_first,
    out_first,
    up_first,
    down_first,
    vector_first,
    qkv_second,
    out_second,
    up_second,
    down_second,
    vector_second,
):
    seq_count, batch_count = lax.axis_size("seq"), lax.axis_size("batch")
    seq_index, batch_index = lax.axis_index("seq"), lax.axis_index("batch")
    row_count, shard_len = inputs.shape[:2]
    tokens = row_count * shard_len
    y_bit, *z_bits = bit_names("seq", seq_count)
    core_bit, *x_bits = bit_names("batch", batch_count)
    near = [core_bit] + x_bits[::-1] + [y_bit] + z_bits[::-1]
    depth = seq_count // 2
    plane = 2 ** (len(x_bits) + 1)
    group_depths = (range(depth // 2, depth), range(depth // 2))
    group_pieces = [[k * depth + z for k in range(plane) for z in depths] for depths in group_depths]
    x_low = inputs.reshape(tokens, D)
    dy = cotangent.reshape(tokens, D)

    first_pos = seq_index * shard_len
    query_pos = first_pos + jnp.arange(shard_len, dtype=jnp.int32)
    docs = doc_lengths.shape[1]
    earlier = jnp.arange(docs)[:, None] < jnp.arange(docs)[None, :]
    doc_starts = jnp.sum(jnp.where(earlier[None], doc_lengths[:, :, None], 0), axis=1)
    start = jnp.max(
        jnp.where(doc_starts[:, None, :] <= query_pos[None, :, None], doc_starts[:, None, :], 0), axis=-1
    )
    offsets = (query_pos[None, :] - start).reshape(tokens)
    inverse = 1.0 / rope_base ** (jnp.arange(0, ROT, 2).astype(f32) / ROT)
    angles = offsets.astype(f32)[None, :] * inverse[:, None]
    cosine, sine = jnp.cos(angles), jnp.sin(angles)
    start_here = (start - first_pos).astype(jnp.int32)[:, None, :]
    number = jnp.arange(seq_count * batch_count, dtype=jnp.int32)

    def bits_of(value, place_of):
        total = 0
        for k, (axis_name, step) in enumerate(near[::-1]):
            total = total + place_of(value, k, axis_name, step)
        return total

    differs = {"seq": (number // batch_count) ^ seq_index, "batch": (number % batch_count) ^ batch_index}
    entry = bits_of(number, lambda v, k, name, step: (differs[name] // step) % 2 << k).astype(jnp.int32)
    xor_of = lambda name: sum((number >> k) % 2 * step for k, (axis_name, step) in enumerate(near[::-1]) if axis_name == name)
    device = ((xor_of("seq") ^ seq_index) * batch_count + (xor_of("batch") ^ batch_index)).astype(jnp.int32)

    qkv_rows, out_rows, up_rows, vec_len = qkv_weight.shape[0], out_weight.shape[0], up_weight.shape[0], vectors.shape[0]
    vec_rows = -(-vec_len // D)
    used = qkv_rows + vec_rows
    head_rows = -(-used // (8 * batch_count)) * 8 * batch_count
    vec_pad = vec_rows * D - vec_len

    def own_part(rows):
        size = rows.shape[0] // batch_count
        return lax.dynamic_slice_in_dim(rows, batch_index * size, size, axis=0)

    head_shard = jnp.concatenate(
        [qkv_weight, jnp.pad(vectors, (0, vec_pad)).reshape(vec_rows, D), jnp.zeros((head_rows - used, D), f32)], axis=0
    ).astype(low)
    head_part_rows = head_rows // batch_count
    value = jnp.concatenate([own_part(head_shard), own_part(out_weight.astype(low))], axis=0)
    unit_rows = up_rows // batch_count
    feed_parts = gather_z(
        jnp.concatenate([own_part(up_weight.astype(low)), own_part(down_weight.T.astype(low))], axis=0)
    )
    for bit in z_bits:
        value = gather_bit(value, bit, 0, True)
    value = value.reshape(depth, -1, D)
    value, cosine, sine, start_here, entry, device = lax.optimization_barrier((value, cosine, sine, start_here, entry, device))
    head_full, out_full = value[:, :head_part_rows], value[:, head_part_rows:]
    head_full = gather_bit(head_full, y_bit, 1, True)
    for bit in x_bits:
        out_full = gather_bit(out_full, bit, 1, True)
    half_way = (head_full, out_full)
    for bit in x_bits:
        head_full = gather_bit(head_full, bit, 2, True)
    out_full = gather_bit(out_full, y_bit, 1, True)
    order = 2 + len(x_bits)
    both = gather_bit(jnp.concatenate([head_full, out_full], axis=order), core_bit, order, True)
    head_full = both[..., :head_part_rows, :].reshape(seq_count, head_rows, D)
    out_full = both[..., head_part_rows:, :].reshape(D, D)

    normed_one, normed_two, q_t, kv_own, gains, out_bias, *bias_rows = head(
        device, x_low, head_full, cosine, sine, group_pieces, 2, vec_len
    )
    bias_rows = [bias_rows[: len(group_pieces)], bias_rows[len(group_pieces) :]]
    reach = seq_count // 2

    def shifted(value, step, back=False):
        pairs = [(j, j + step) for j in range(seq_count - step)]
        return lax.ppermute(value, "seq", [(b, a) for a, b in pairs] if back else pairs)

    kv = kv_own[None]
    farthest = shifted(kv_own, reach)
    pair = shifted(kv, 1)
    kv = jnp.concatenate([kv, pair], axis=0)
    while kv.shape[0] < reach:
        kv = jnp.concatenate([kv, shifted(kv, kv.shape[0])], axis=0)
    kv = jnp.concatenate([kv, farthest[None]], axis=0)

    parts = flow(jnp.stack(feed_parts), pair, farthest)
    up_near, down_near = parts[:, :unit_rows], parts[:, unit_rows:]
    up_near = gather_bit(up_near, y_bit, 0)
    for bit in x_bits:
        down_near = gather_bit(down_near, bit, 0)
    up_near, down_near, kv = lax.optimization_barrier((up_near, down_near, kv))
    for bit in x_bits:
        up_near = gather_bit(up_near, bit, 0)
    down_near = gather_bit(down_near, y_bit, len(x_bits))
    last = (((1,), (1,)), ((), ()))
    do_t = lax.dot_general(out_full, dy, (((0,), (1,)), ((), ())), preferred_element_type=f32).astype(low)
    context, dq_t, dkv_own, dkv_sent = attention(q_t, do_t, start_here, cosine, sine, kv)
    shape = (1, plane * depth, unit_rows, D)
    near_weight = jnp.concatenate([up_near.reshape(shape), down_near.reshape(shape)], axis=0)
    near_weight = flow(near_weight, dq_t)
    far_weight = swap(near_weight, core_bit)

    dkv_far = shifted(dkv_sent[reach - 1], reach, True)
    dkv = jnp.concatenate([dkv_own[None], dkv_sent[: reach - 1].astype(f32)], axis=0)
    dkv_steps = []
    while dkv.shape[0] > 1:
        half = dkv.shape[0] // 2
        dkv = dkv[:half] + shifted(dkv[half:].astype(low), half, True).astype(f32)
        dkv_steps.append(dkv)
    dkv = dkv[0] + dkv_far.astype(f32)
    bias_grads, grad_sums = [[], []], []
    sums = None
    earlier = (dkv_steps[0],)
    for g, pieces in enumerate(group_pieces):
        *sums, far_grad, near_grad, bias_far, bias_here = feed(
            normed_two, dy, flow(far_weight, *earlier), near_weight, bias_rows[1][g], bias_rows[0][g], pieces, sums
        )
        bias_grads[0].append(bias_here)
        bias_grads[1].append(bias_far)
        grad_sums.append(near_grad + swap(far_grad, core_bit).astype(f32))
        earlier = (grad_sums[-1], dkv)
    mlp_out, d_normed_two = sums
    bases_late = flow(bases, d_normed_two)
    bases_high = bases_late.astype(low)
    bases_split = (bases_high, (bases_late - bases_high.astype(f32)).astype(low))

    attn_out = lax.dot_general(context, out_full, last, preferred_element_type=f32)
    outputs = (x_low.astype(f32) + attn_out + mlp_out + out_bias).astype(low)
    out_grad_part = lax.dot_general(dy, context, (((0,), (0,)), ((), ())), preferred_element_type=f32)
    input_grad, head_part = tail(
        entry, x_low, dy, dq_t, dkv, cosine, sine, head_full, normed_one, d_normed_two, gains, bias_grads, group_pieces,
        head_rows, vec_len,
    )

    def feed_first(both, size):
        shape = (2,) * len(x_bits) + (2, size, unit_rows, D)
        up_sum, down_sum = both[0].reshape(shape), both[1].reshape(shape)
        for bit in x_bits[::-1]:
            up_sum = sum_bit(up_sum, bit, 0)
        return up_sum, sum_bit(down_sum, y_bit, len(x_bits))

    def feed_second(up_sum, down_sum):
        up_sum = sum_bit(up_sum, y_bit, 0)
        for bit in x_bits[::-1]:
            down_sum = sum_bit(down_sum, bit, 0)
        return jnp.concatenate([up_sum, down_sum], axis=1)

    shape = (depth, 2) + (2,) * len(x_bits) + (2, -1, D)
    feed_sum = 0.0
    for g, (grad_sum, depths) in enumerate(zip(grad_sums, group_depths)):
        final = g == len(grad_sums) - 1
        up_sum, down_sum = feed_first(grad_sum, len(depths))
        if final:
            both = jnp.concatenate([head_part.reshape(shape), out_grad_part.reshape(shape)], axis=len(shape) - 2)
            both = sum_bit(flow(both, grad_sum), core_bit, len(shape) - 3, True)
            up_sum = flow(up_sum, both)
        last_step = feed_second(up_sum, down_sum)
        if final:
            head_sum, out_sum = both[..., :head_part_rows, :], both[..., head_part_rows:, :]
            for bit in x_bits[::-1]:
                head_sum = sum_bit(head_sum, bit, 2, True)
            out_sum = sum_bit(out_sum, y_bit, 1, True)
            last_step = flow(last_step, head_sum, out_sum)
        else:
            last_step = flow(last_step, head_part)
        for k, z in enumerate(depths):
            feed_sum = feed_sum + (last_step[k] if z == 0 else swap_z(last_step[k].astype(low), z).astype(f32))
    head_sum = sum_bit(head_sum, y_bit, 1, True)
    for bit in x_bits[::-1]:
        out_sum = sum_bit(out_sum, bit, 1, True)
    both = jnp.concatenate([head_sum, out_sum], axis=1)
    feed_sum = flow(feed_sum, both)
    both = sum_z(both, True)

    def spread(part):
        value = part.astype(low)
        for k, bit in enumerate(x_bits):
            value = gather_bit(value, bit, 0, True)
        value = gather_bit(value, core_bit, len(x_bits), True)
        return value.reshape(batch_count, -1, D)

    feed_grads = spread(feed_sum)
    up_low = feed_grads[:, :unit_rows].reshape(-1, D)
    down_low = feed_grads[:, unit_rows:].reshape(-1, D)
    others = spread(both)
    head_low = others[:, :head_part_rows].reshape(-1, D)
    out_low = others[:, head_part_rows:].reshape(-1, D)
    up_grad, *up_states = update(up_low, bases_split, 2, up_weight, up_first, up_second)
    down_grad, *down_states = update(down_low, bases_split, 3, down_weight, down_first, down_second, True)
    out_grad, *out_states = update(out_low, bases_split, 1, out_weight, out_first, out_second)
    qkv_grad, *qkv_states = update(head_low[:qkv_rows], bases_split, 0, qkv_weight, qkv_first, qkv_second)
    vector_grad = head_low[qkv_rows:used].astype(f32).reshape(-1)[:vec_len]
    vector_new, *vector_states = adam_step(vectors, vector_grad, vector_first, vector_second)
    states = (qkv_states, out_states, up_states, down_states, (*vector_states, vector_new))
    return (
        outputs.reshape(inputs.shape),
        input_grad.reshape(inputs.shape),
        qkv_grad,
        out_grad,
        up_grad,
        down_grad,
        vector_grad,
        *(state[0] for state in states),
        *(state[1] for state in states),
        *(state[2] for state in states),
    )


def solution(mesh):
    tokens = P("batch", "seq", None)
    rows, columns, flat = P("seq", None), P(None, "seq"), P("seq")
    params = (rows, rows, rows, columns, flat)
    return jax.shard_map(
        shards,
        mesh=mesh,
        in_specs=(tokens, tokens, P("batch", None)) + params + (P(),) + params + params,
        out_specs=(tokens, tokens) + params * 4,
        check_vma=False,
    )
```

```python
import functools

import jax
import jax.numpy as jnp
from jax import lax
from jax.experimental import pallas as pl
from jax.experimental.pallas import tpu as pltpu
from jax.sharding import PartitionSpec as P

D = 768
HEADS = 12
HEAD = 64
ROT = 16
FF = 3072
STEP = 10

layer_eps = 1e-05
adam_eps = 1e-08
beta_first = 0.95
beta_second = 0.95
matrix_rate = 0.08
vector_rate = 0.3
rope_base = 10000.0
masked_score = -1e30
low = jnp.bfloat16
f32 = jnp.float32
VMEM_LIMIT = 56 * 1024 * 1024
FEED_VMEM = 56 * 1024 * 1024
UPDATE_VMEM = 56 * 1024 * 1024


def swap(value, bit):
    axis, step = bit
    return lax.ppermute(value, axis, [(i, i ^ step) for i in range(lax.axis_size(axis))])


def mine(bit):
    axis, step = bit
    return lax.rem(lax.axis_index(axis) // step, 2)


def flow(first, *others):
    return lax.optimization_barrier((first, *others))[0]


def swap_z(value, step):
    size = lax.axis_size("seq")
    return lax.ppermute(value, "seq", [(i, i ^ (2 * step)) for i in range(size)])


def z_index():
    return lax.axis_index("seq") // 2


def gather_z(piece):
    return [piece] + [swap_z(piece, k) for k in range(1, lax.axis_size("seq") // 2)]


def gather_bit(value, bit, axis, absolute=False, after=()):
    got = swap(value, bit)
    if after:
        got = flow(got, *after)
    if absolute:
        upper = mine(bit) == 1
        return jnp.stack([jnp.where(upper, got, value), jnp.where(upper, value, got)], axis=axis)
    return jnp.stack([value, got], axis=axis)


def split_bit(value, bit, axis, absolute=False):
    if absolute:
        own = mine(bit)
        return (
            lax.dynamic_index_in_dim(value, own, axis, keepdims=False),
            lax.dynamic_index_in_dim(value, 1 - own, axis, keepdims=False).astype(low),
        )
    return lax.index_in_dim(value, 0, axis, keepdims=False), lax.index_in_dim(value, 1, axis, keepdims=False).astype(low)


def sum_bit(value, bit, axis, absolute=False):
    kept, sent = split_bit(value, bit, axis, absolute)
    return kept.astype(f32) + swap(sent, bit).astype(f32)


def sum_z(value, absolute=False):
    count = value.shape[0]
    own = z_index() if absolute else 0
    pick = lambda k: lax.dynamic_index_in_dim(value, own ^ k, 0, keepdims=False) if absolute else value[k]
    total = pick(0).astype(f32)
    for k in range(1, count):
        total = total + swap_z(pick(k).astype(low), k).astype(f32)
    return total


def bit_names(axis, size):
    return [(axis, 1 << k) for k in range(size.bit_length() - 1)]


def moments(rotated, first, second):
    new_first = beta_first * first + (1.0 - beta_first) * rotated
    new_second = beta_second * second + (1.0 - beta_second) * rotated * rotated
    ratio = (
        new_first
        / (1.0 - beta_first**STEP)
        / (jnp.sqrt(new_second / (1.0 - beta_second**STEP)) + adam_eps)
    )
    return ratio, new_first, new_second


def adam_step(weight, grad, first, second):
    ratio, new_first, new_second = moments(grad, first, second)
    return (weight - vector_rate * ratio, new_first, new_second)


def attention_kernel(blocks, width, q_ref, do_ref, start_ref, cos_ref, sin_ref, kv_ref, context_ref, dq_ref, dkv_own_ref, dkv_ref):
    length = q_ref.shape[1]
    keys = blocks * length
    key_t = jnp.concatenate([kv_ref[k, :HEAD, :] for k in reversed(range(blocks))], axis=1)
    value_t = jnp.concatenate([kv_ref[k, HEAD:, :] for k in reversed(range(blocks))], axis=1)
    key = key_t.astype(f32).T.astype(low)
    value = value_t.astype(f32).T.astype(low)
    key_pos = lax.broadcasted_iota(jnp.int32, (keys, length), 0) - (blocks - 1) * length
    query_pos = lax.broadcasted_iota(jnp.int32, (keys, length), 1)
    allowed = (key_pos >= start_ref[0]) & (key_pos <= query_pos)
    bias = jnp.where(allowed, 0.0, masked_score)
    cosine, sine = cos_ref[...], sin_ref[...]
    d_key = jnp.zeros((keys, HEAD), f32)
    d_value = jnp.zeros((keys, HEAD), f32)
    last = (((1,), (1,)), ((), ()))
    for first in range(0, HEADS, width):
        heads = range(first, first + width)
        query = jnp.concatenate([q_ref[h * HEAD : (h + 1) * HEAD, :] for h in heads], axis=1)
        d_out = jnp.concatenate([do_ref[h * HEAD : (h + 1) * HEAD, :] for h in heads], axis=1)
        scores = jnp.dot(key, query, preferred_element_type=f32)
        scores = scores + jnp.concatenate([bias] * width, axis=1)
        weights = jnp.exp(scores - jnp.max(scores, axis=0, keepdims=True))
        probs = weights * (1.0 / jnp.sum(weights, axis=0, keepdims=True))
        probs_low = probs.astype(low)
        context_t = jnp.dot(value_t, probs_low, preferred_element_type=f32)
        d_probs = jnp.dot(value, d_out, preferred_element_type=f32)
        inner = jnp.sum(probs * d_probs, axis=0, keepdims=True)
        d_scores = (probs * (d_probs - inner)).astype(low)
        d_query = jnp.dot(key_t, d_scores, preferred_element_type=f32) * HEAD ** (-0.5)
        d_value = d_value + lax.dot_general(probs_low, d_out, last, preferred_element_type=f32)
        d_key = d_key + lax.dot_general(d_scores, query, last, preferred_element_type=f32)
        for k, h in enumerate(heads):
            lanes = slice(k * length, (k + 1) * length)
            part = d_query[:, lanes]
            a, b = part[: ROT // 2], part[ROT // 2 : ROT]
            turned = jnp.concatenate([a * cosine + b * sine, b * cosine - a * sine, part[ROT:]], axis=0)
            dq_ref[h * HEAD : (h + 1) * HEAD, :] = turned.astype(low)
        for k in range(0, width, 2):
            h = first + k
            two = jnp.concatenate(
                [context_t[:, k * length : (k + 1) * length], context_t[:, (k + 1) * length : (k + 2) * length]], axis=0
            )
            context_ref[:, h * HEAD : (h + 2) * HEAD] = two.T.astype(low)
    d_kv = jnp.concatenate([d_key, d_value], axis=1).T
    for k in range(blocks):
        part = d_kv[:, (blocks - 1 - k) * length : (blocks - k) * length]
        if k == 0:
            dkv_own_ref[...] = part
        else:
            dkv_ref[k - 1] = part.astype(low)


def attention(q_t, do_t, start, cosine, sine, kv):
    rows, _, length = start.shape
    blocks = kv.shape[0]
    tokens = q_t.shape[1]
    by_row = lambda height: pl.BlockSpec((height, length), lambda r: (0, r))
    return pl.pallas_call(
        functools.partial(attention_kernel, blocks, HEADS),
        grid=(rows,),
        in_specs=[by_row(D), by_row(D), pl.BlockSpec((1, 1, length), lambda r: (r, 0, 0)), by_row(ROT // 2), by_row(ROT // 2)]
        + [pl.BlockSpec((blocks, 2 * HEAD, length), lambda r: (0, 0, r))],
        out_specs=[
            pl.BlockSpec((length, D), lambda r: (r, 0)),
            by_row(D),
            by_row(2 * HEAD),
            pl.BlockSpec((blocks - 1, 2 * HEAD, length), lambda r: (0, 0, r)),
        ],
        out_shape=[
            jax.ShapeDtypeStruct((tokens, D), low),
            jax.ShapeDtypeStruct((D, tokens), low),
            jax.ShapeDtypeStruct((2 * HEAD, tokens), f32),
            jax.ShapeDtypeStruct((blocks - 1, 2 * HEAD, tokens), low),
        ],
        compiler_params=pltpu.CompilerParams(vmem_limit_bytes=VMEM_LIMIT),
        cost_estimate=pl.CostEstimate(
            flops=4 * 7 * tokens * HEADS * blocks * length * HEAD * 2, bytes_accessed=8 << 20, transcendentals=0
        ),
        name="attention",
    )(q_t, do_t, start, cosine, sine, kv)


def feed_kernel(depths, n_ref, dy_ref, far_ref, near_ref, bias_far_ref, bias_near_ref, *refs):
    before = refs[: len(refs) - 11]
    out_ref, dn_ref, far_grad_ref, near_grad_ref, bias_far_grad_ref, bias_near_grad_ref = refs[-11:-5]
    weights, far_sum, near_sum, held, sems = refs[-5:]
    plane = weights.shape[2]
    last = (((1,), (1,)), ((), ()))
    first = (((0,), (0,)), ((), ()))
    loads = []
    for side, ref in enumerate((far_ref, near_ref)):
        loads.append(
            [
                pltpu.make_async_copy(
                    ref.at[:, k, pl.ds(depths[0], len(depths))], weights.at[side, :, k], sems.at[side, k]
                )
                for k in range(plane)
            ]
        )
    fetches = [pltpu.make_async_copy(ref, held.at[k], sems.at[2, k]) for k, ref in enumerate(before)]
    for copy in loads[0] + loads[1] + fetches:
        copy.start()
    normed, d_out = n_ref[...], dy_ref[...]
    units = far_sum.shape[1]
    out, d_normed = 0.0, 0.0
    stores = []
    for side, (bias_ref, bias_grad_ref, buffer, grad_ref) in enumerate(
        (
            (bias_far_ref, bias_far_grad_ref, far_sum, far_grad_ref),
            (bias_near_ref, bias_near_grad_ref, near_sum, near_grad_ref),
        )
    ):
        for copy in loads[side]:
            copy.wait()
        up, down = weights[side, 0].reshape(units, D), weights[side, 1].reshape(units, D)
        hidden = lax.dot_general(normed, up, last, preferred_element_type=f32) + bias_ref[...]
        share = 0.5 * (1.0 + lax.erf(hidden * (0.5**0.5)))
        slope = share + hidden * (jnp.exp(-0.5 * hidden * hidden) * (0.5 / 3.141592653589793) ** 0.5)
        active = (hidden * share).astype(low)
        d_active = lax.dot_general(d_out, down, last, preferred_element_type=f32)
        d_hidden = (d_active * slope).astype(low)
        for k, part in enumerate(
            (
                lax.dot_general(d_hidden, normed, first, preferred_element_type=f32),
                lax.dot_general(active, d_out, first, preferred_element_type=f32),
            )
        ):
            buffer[k] = part.astype(buffer.dtype)
            copy = pltpu.make_async_copy(buffer.at[k], grad_ref.at[k], sems.at[3, 2 * side + k])
            copy.start()
            stores.append(copy)
        bias_grad_ref[...] = jnp.sum(d_hidden.astype(f32), axis=0, keepdims=True)
        out = out + jnp.dot(active, down, preferred_element_type=f32)
        d_normed = d_normed + jnp.dot(d_hidden, up, preferred_element_type=f32)
    for copy in fetches:
        copy.wait()
    out_ref[...] = held[0] + out if before else out
    dn_ref[...] = held[1] + d_normed if before else d_normed
    for copy in stores:
        copy.wait()


def feed(normed, d_out, far, near, bias_far, bias_near, depths, before):
    tokens = normed.shape[0]
    plane, rows = far.shape[1], far.shape[3]
    units = plane * len(depths) * rows
    before = before or []
    vmem, hbm = pl.BlockSpec(memory_space=pltpu.VMEM), pl.BlockSpec(memory_space=pl.ANY)
    return pl.pallas_call(
        functools.partial(feed_kernel, depths),
        in_specs=[vmem, vmem, hbm, hbm, vmem, vmem] + [hbm] * len(before),
        out_specs=[vmem, vmem, hbm, hbm, vmem, vmem],
        out_shape=[
            jax.ShapeDtypeStruct((tokens, D), f32),
            jax.ShapeDtypeStruct((tokens, D), f32),
            jax.ShapeDtypeStruct((2, units, D), low),
            jax.ShapeDtypeStruct((2, units, D), f32),
            jax.ShapeDtypeStruct((1, units), f32),
            jax.ShapeDtypeStruct((1, units), f32),
        ],
        scratch_shapes=[
            pltpu.VMEM((2, 2, plane, len(depths), rows, D), low),
            pltpu.VMEM((2, units, D), low),
            pltpu.VMEM((2, units, D), f32),
            pltpu.VMEM((2, tokens, D), f32),
            pltpu.SemaphoreType.DMA((4, max(plane, 4))),
        ],
        compiler_params=pltpu.CompilerParams(vmem_limit_bytes=FEED_VMEM),
        cost_estimate=pl.CostEstimate(flops=4 * 24 * tokens * units * D, bytes_accessed=8 << 20, transcendentals=0),
        name="feed",
    )(normed, d_out, far, near, bias_far, bias_near, *before)


def head_kernel(
    vec_len, group_pieces, device_ref, x_ref, head_ref, cos_ref, sin_ref, n_one_ref, n_two_ref, q_ref, kv_ref, gain_ref,
    bias_ref, *refs
):
    bias_refs, (flat, units) = refs[:-2], refs[-2:]
    shards_of = head_ref.shape[0]
    rows = (D + 2 * HEAD) // shards_of
    for s in range(shards_of):
        left, row = vec_len, rows
        tile = head_ref[s, rows:, :].astype(f32)
        while left > 0:
            size = min(left, D)
            begin = s * vec_len + (row - rows) * D
            flat[:, begin : begin + size] = tile[row - rows : row - rows + 1, :size]
            left -= size
            row += 1
    vector = lambda begin, size: flat[:, begin : begin + size]
    gain_one, shift_one, gain_two, shift_two = [vector(k * D, D) for k in range(4)]
    gain_ref[0:1] = gain_one
    gain_ref[1:2] = gain_two
    qkv_bias = vector(4 * D, D + 2 * HEAD)
    offset = 4 * D + D + 2 * HEAD
    bias_ref[...] = vector(offset, D) + vector(offset + D + FF, D)
    count, size = units.shape
    for k in range(count):
        units[k : k + 1, :] = vector(offset + D + k * size, size)
    sides = len(bias_refs) // len(group_pieces)
    for k, ref in enumerate(bias_refs):
        side, pieces = k // len(group_pieces), group_pieces[k % len(group_pieces)]
        for i, piece in enumerate(pieces):
            ref[:, i * size : (i + 1) * size] = units[pl.ds(device_ref[side * (count // sides) + piece], 1), :]
    x = x_ref[...].astype(f32)
    center = x - jnp.mean(x, axis=-1, keepdims=True)
    xhat = center * lax.rsqrt(jnp.mean(center * center, axis=-1, keepdims=True) + layer_eps)
    n_one = (xhat * gain_one + shift_one).astype(low)
    n_one_ref[...] = n_one
    n_two_ref[...] = (xhat * gain_two + shift_two).astype(low)
    weight = head_ref[:, :rows, :].reshape(shards_of * rows, D)
    column = jnp.broadcast_to(qkv_bias, (8, qkv_bias.shape[1])).T[:, 0:1]
    projected = lax.dot_general(weight, n_one, (((1,), (1,)), ((), ())), preferred_element_type=f32) + column
    cosine, sine = cos_ref[...], sin_ref[...]
    half = ROT // 2

    def turned(first):
        a, b = projected[first : first + half], projected[first + half : first + ROT]
        rest = projected[first + ROT : first + HEAD]
        return jnp.concatenate([a * cosine - b * sine, b * cosine + a * sine, rest], axis=0).astype(low)

    for h in range(HEADS):
        q_ref[h * HEAD : (h + 1) * HEAD, :] = turned(h * HEAD) * jnp.asarray(HEAD ** (-0.5), low)
    kv_ref[:HEAD, :] = turned(D)
    kv_ref[HEAD:, :] = projected[D + HEAD :].astype(low)


def head(device, x, head_full, cosine, sine, group_pieces, sides, vec_len):
    tokens = x.shape[0]
    shards_of = head_full.shape[0]
    count = device.shape[0]
    bias_rows = [jax.ShapeDtypeStruct((1, len(pieces) * (FF // count)), f32) for pieces in group_pieces] * sides
    return pl.pallas_call(
        functools.partial(head_kernel, vec_len, group_pieces),
        in_specs=[pl.BlockSpec(memory_space=pltpu.SMEM)] + [pl.BlockSpec(memory_space=pltpu.VMEM)] * 4,
        out_shape=[
            jax.ShapeDtypeStruct((tokens, D), low),
            jax.ShapeDtypeStruct((tokens, D), low),
            jax.ShapeDtypeStruct((D, tokens), low),
            jax.ShapeDtypeStruct((2 * HEAD, tokens), low),
            jax.ShapeDtypeStruct((2, D), f32),
            jax.ShapeDtypeStruct((1, D), f32),
            *bias_rows,
        ],
        scratch_shapes=[pltpu.VMEM((1, shards_of * vec_len), f32), pltpu.VMEM((count, FF // count), f32)],
        compiler_params=pltpu.CompilerParams(vmem_limit_bytes=FEED_VMEM),
        cost_estimate=pl.CostEstimate(flops=4 * 2 * tokens * 896 * D, bytes_accessed=8 << 20, transcendentals=0),
        name="head",
    )(device, x, head_full, cosine, sine)


def tail_kernel(
    vec_len, group_pieces, entry_ref, x_ref, dy_ref, dq_ref, dkv_ref, cos_ref, sin_ref, w_ref, n_ref, dn_ref, gain_ref, *refs,
):
    bias_refs, (in_grad_ref, part_ref, flat, units) = refs[:-4], refs[-4:]
    shards_of = w_ref.shape[0]
    rows = (D + 2 * HEAD) // shards_of
    d_kv = dkv_ref[...]
    a, b = d_kv[: ROT // 2], d_kv[ROT // 2 : ROT]
    cosine, sine = cos_ref[...], sin_ref[...]
    d_kv = jnp.concatenate([a * cosine + b * sine, b * cosine - a * sine, d_kv[ROT:]], axis=0).astype(low)
    d_proj = jnp.concatenate([dq_ref[...], d_kv], axis=0)
    first = (((0,), (0,)), ((), ()))
    weight = w_ref[:, :rows, :].reshape(shards_of * rows, D)
    qkv_grad = jnp.dot(d_proj, n_ref[...], preferred_element_type=f32)
    d_one = lax.dot_general(d_proj, weight, first, preferred_element_type=f32)
    d_two = dn_ref[...]
    x = x_ref[...].astype(f32)
    dy = dy_ref[...].astype(f32)
    center = x - jnp.mean(x, axis=-1, keepdims=True)
    inv_sigma = lax.rsqrt(jnp.mean(center * center, axis=-1, keepdims=True) + layer_eps)
    xhat = center * inv_sigma
    d_hat = d_one * gain_ref[0:1] + d_two * gain_ref[1:2]
    d_in = (
        d_hat - jnp.mean(d_hat, axis=-1, keepdims=True) - xhat * jnp.mean(d_hat * xhat, axis=-1, keepdims=True)
    ) * inv_sigma
    in_grad_ref[...] = (dy + d_in).astype(low)
    columns = lambda v: jnp.sum(v, axis=0, keepdims=True)
    dy_column = columns(dy)
    ones = jnp.ones((8, d_proj.shape[1]), low)
    proj_sum = lax.dot_general(ones, d_proj, (((1,), (1,)), ((), ())), preferred_element_type=f32)[0:1]
    pieces = [columns(d_one * xhat), columns(d_one), columns(d_two * xhat), columns(d_two)]
    pieces += [proj_sum, dy_column, None, dy_column]
    count, size = units.shape
    sides = len(bias_refs) // len(group_pieces)
    for k, ref in enumerate(bias_refs):
        side, members = k // len(group_pieces), group_pieces[k % len(group_pieces)]
        for i, member in enumerate(members):
            entry = side * (count // sides) + member
            units[entry : entry + 1, :] = ref[:, i * size : (i + 1) * size]
    offset = 0
    for piece in pieces:
        if piece is None:
            for k in range(count):
                flat[:, offset : offset + size] = units[pl.ds(entry_ref[k], 1), :]
                offset += size
        else:
            flat[:, offset : offset + piece.shape[1]] = piece
            offset += piece.shape[1]
    part_ref[...] = jnp.zeros_like(part_ref)
    for s in range(shards_of):
        part_ref[s, :rows, :] = qkv_grad[s * rows : (s + 1) * rows]
        left = vec_len
        row = rows
        while left > 0:
            size = min(left, D)
            begin = s * vec_len + (row - rows) * D
            part_ref[s, row : row + 1, :size] = flat[:, begin : begin + size]
            left -= size
            row += 1


def tail(entry, x, dy, dq_t, dkv, cosine, sine, weight, normed, d_normed, gains, bias_grads, group_pieces, head_rows, vec_len):
    tokens = x.shape[0]
    shards_of = weight.shape[0]
    total = shards_of * vec_len
    count = entry.shape[0]
    operands = (entry, x, dy, dq_t, dkv, cosine, sine, weight, normed, d_normed, gains, *sum(bias_grads, []))
    return pl.pallas_call(
        functools.partial(tail_kernel, vec_len, group_pieces),
        in_specs=[pl.BlockSpec(memory_space=pltpu.SMEM)] + [pl.BlockSpec(memory_space=pltpu.VMEM)] * (len(operands) - 1),
        out_shape=[
            jax.ShapeDtypeStruct((tokens, D), low),
            jax.ShapeDtypeStruct((shards_of, head_rows, D), f32),
        ],
        scratch_shapes=[pltpu.VMEM((1, total), f32), pltpu.VMEM((count, FF // count), f32)],
        compiler_params=pltpu.CompilerParams(vmem_limit_bytes=VMEM_LIMIT),
        cost_estimate=pl.CostEstimate(flops=4 * 4 * tokens * 896 * D, bytes_accessed=8 << 20, transcendentals=0),
        name="tail",
    )(*operands)


def split_low(value):
    high = value.astype(low)
    return high, (value - high.astype(f32)).astype(low)


def update_step(across, grad, high, rest, w_ref, first_ref, second_ref, grad_ref, first_new_ref, second_new_ref, w_new_ref):
    rotated = jnp.dot(grad, high, preferred_element_type=f32) + jnp.dot(grad, rest, preferred_element_type=f32)
    grad = grad.astype(f32)
    if across:
        rotated, grad = rotated.T, grad.T
    grad_ref[...] = grad
    ratio, first_new, second_new = moments(rotated, first_ref[...], second_ref[...])
    first_new_ref[...] = first_new
    second_new_ref[...] = second_new
    r_high, r_rest = split_low(ratio)
    if across:
        product = lambda r, b: jnp.dot(b, r, preferred_element_type=f32)
    else:
        product = lambda r, b: lax.dot_general(r, b, (((1,), (1,)), ((), ())), preferred_element_type=f32)
    unrotated = product(r_high, high) + (product(r_high, rest) + product(r_rest, high))
    w_new_ref[...] = w_ref[...] - matrix_rate * unrotated


def update_kernel(plan, *refs):
    count = len(plan)
    ins, outs, splits = refs[: 5 * count], refs[5 * count : 9 * count], refs[9 * count :]
    for k, (across, begin, steps) in enumerate(plan):
        grad_ref, basis_ref, *state = ins[5 * k : 5 * k + 5]

        @pl.when(pl.program_id(0) == begin)
        def _():
            splits[0][...], splits[1][...] = split_low(basis_ref[...])

        @pl.when((pl.program_id(0) >= begin) & (pl.program_id(0) < begin + steps))
        def _():
            update_step(across, grad_ref[...], splits[0][...], splits[1][...], *state, *outs[4 * k : 4 * k + 4])


def update(bases, *matrices):
    plan, in_specs, out_specs, out_shape, operands = [], [], [], [], []
    begin = 0
    for grad, number, weight, first, second, across in matrices:
        count = grad.shape[0]
        step = 128 if count % 128 == 0 else count
        steps = count // step
        at = lambda i, begin=begin, steps=steps: jnp.clip(i - begin, 0, steps - 1)
        if across:
            block = pl.BlockSpec((D, step), lambda i, at=at: (0, at(i)))
        else:
            block = pl.BlockSpec((step, D), lambda i, at=at: (at(i), 0))
        in_specs += [
            pl.BlockSpec((step, D), lambda i, at=at: (at(i), 0)),
            pl.BlockSpec((None, D, D), lambda i, number=number: (number, 0, 0)),
            block, block, block,
        ]
        out_specs += [block] * 4
        out_shape += [jax.ShapeDtypeStruct(weight.shape, f32)] * 4
        operands += [grad, bases, weight, first, second]
        plan.append((across, begin, steps))
        begin += steps
    out = pl.pallas_call(
        functools.partial(update_kernel, plan),
        grid=(begin,),
        in_specs=in_specs,
        out_specs=out_specs,
        out_shape=out_shape,
        scratch_shapes=[pltpu.VMEM((D, D), low), pltpu.VMEM((D, D), low)],
        compiler_params=pltpu.CompilerParams(vmem_limit_bytes=UPDATE_VMEM),
        cost_estimate=pl.CostEstimate(flops=4 * 10 * 128 * begin * D * D, bytes_accessed=8 << 20, transcendentals=0),
        name="update",
    )(*operands)
    return [out[4 * k : 4 * k + 4] for k in range(len(matrices))]


def shards(
    inputs,
    cotangent,
    doc_lengths,
    qkv_weight,
    out_weight,
    up_weight,
    down_weight,
    vectors,
    bases,
    qkv_first,
    out_first,
    up_first,
    down_first,
    vector_first,
    qkv_second,
    out_second,
    up_second,
    down_second,
    vector_second,
):
    seq_count, batch_count = lax.axis_size("seq"), lax.axis_size("batch")
    seq_index, batch_index = lax.axis_index("seq"), lax.axis_index("batch")
    row_count, shard_len = inputs.shape[:2]
    tokens = row_count * shard_len
    y_bit, *z_bits = bit_names("seq", seq_count)
    core_bit, *x_bits = bit_names("batch", batch_count)
    near = [core_bit] + x_bits[::-1] + [y_bit] + z_bits[::-1]
    depth = seq_count // 2
    plane = 2 ** (len(x_bits) + 1)
    group_depths = (range(depth // 2, depth), range(depth // 2))
    group_pieces = [[k * depth + z for k in range(plane) for z in depths] for depths in group_depths]
    x_low = inputs.reshape(tokens, D)
    dy = cotangent.reshape(tokens, D)

    first_pos = seq_index * shard_len
    query_pos = first_pos + jnp.arange(shard_len, dtype=jnp.int32)
    docs = doc_lengths.shape[1]
    earlier = jnp.arange(docs)[:, None] < jnp.arange(docs)[None, :]
    doc_starts = jnp.sum(jnp.where(earlier[None], doc_lengths[:, :, None], 0), axis=1)
    start = jnp.max(
        jnp.where(doc_starts[:, None, :] <= query_pos[None, :, None], doc_starts[:, None, :], 0), axis=-1
    )
    offsets = (query_pos[None, :] - start).reshape(tokens)
    inverse = 1.0 / rope_base ** (jnp.arange(0, ROT, 2).astype(f32) / ROT)
    angles = offsets.astype(f32)[None, :] * inverse[:, None]
    cosine, sine = jnp.cos(angles), jnp.sin(angles)
    start_here = (start - first_pos).astype(jnp.int32)[:, None, :]
    number = jnp.arange(seq_count * batch_count, dtype=jnp.int32)

    def bits_of(value, place_of):
        total = 0
        for k, (axis_name, step) in enumerate(near[::-1]):
            total = total + place_of(value, k, axis_name, step)
        return total

    differs = {"seq": (number // batch_count) ^ seq_index, "batch": (number % batch_count) ^ batch_index}
    entry = bits_of(number, lambda v, k, name, step: (differs[name] // step) % 2 << k).astype(jnp.int32)
    xor_of = lambda name: sum((number >> k) % 2 * step for k, (axis_name, step) in enumerate(near[::-1]) if axis_name == name)
    device = ((xor_of("seq") ^ seq_index) * batch_count + (xor_of("batch") ^ batch_index)).astype(jnp.int32)

    qkv_rows, out_rows, up_rows, vec_len = qkv_weight.shape[0], out_weight.shape[0], up_weight.shape[0], vectors.shape[0]
    vec_rows = -(-vec_len // D)
    used = qkv_rows + vec_rows
    head_rows = -(-used // (8 * batch_count)) * 8 * batch_count
    vec_pad = vec_rows * D - vec_len

    def own_part(rows):
        size = rows.shape[0] // batch_count
        return lax.dynamic_slice_in_dim(rows, batch_index * size, size, axis=0)

    head_shard = jnp.concatenate(
        [qkv_weight, jnp.pad(vectors, (0, vec_pad)).reshape(vec_rows, D), jnp.zeros((head_rows - used, D), f32)], axis=0
    ).astype(low)
    head_part_rows = head_rows // batch_count
    value = jnp.concatenate([own_part(head_shard), own_part(out_weight.astype(low))], axis=0)
    unit_rows = up_rows // batch_count
    feed_parts = gather_z(
        jnp.concatenate([own_part(up_weight.astype(low)), own_part(down_weight.T.astype(low))], axis=0)
    )
    for bit in z_bits:
        value = gather_bit(value, bit, 0, True)
        if bit == z_bits[0]:
            value = flow(value, feed_parts[1])
    value = value.reshape(depth, -1, D)
    value, cosine, sine, start_here, entry, device, _ = lax.optimization_barrier(
        (value, cosine, sine, start_here, entry, device, feed_parts[min(2, depth - 1)])
    )
    head_full, out_full = value[:, :head_part_rows], value[:, head_part_rows:]
    head_full = gather_bit(head_full, y_bit, 1, True)
    for bit in x_bits:
        out_full = gather_bit(out_full, bit, 1, True)
    head_full, out_full, *_ = lax.optimization_barrier((head_full, out_full, *feed_parts[3:]))
    for bit in x_bits:
        head_full = gather_bit(head_full, bit, 2, True)
    out_full = gather_bit(out_full, y_bit, 1, True)
    order = 2 + len(x_bits)
    half_way = (head_full, out_full)
    both = gather_bit(jnp.concatenate([head_full, out_full], axis=order), core_bit, order, True)
    head_full = both[..., :head_part_rows, :].reshape(seq_count, head_rows, D)
    out_full = both[..., head_part_rows:, :].reshape(D, D)

    normed_one, normed_two, q_t, kv_own, gains, out_bias, *bias_rows = head(
        device, x_low, head_full, cosine, sine, group_pieces, 2, vec_len
    )
    bias_rows = [bias_rows[: len(group_pieces)], bias_rows[len(group_pieces) :]]
    reach = seq_count // 2

    def shifted(value, step, back=False):
        pairs = [(j, j + step) for j in range(seq_count - step)]
        return lax.ppermute(value, "seq", [(b, a) for a, b in pairs] if back else pairs)

    kv = kv_own[None]
    farthest = shifted(kv_own, reach)
    pair = shifted(kv, 1)
    kv = jnp.concatenate([kv, pair], axis=0)
    while kv.shape[0] < reach:
        kv = jnp.concatenate([kv, shifted(kv, kv.shape[0])], axis=0)
    kv = jnp.concatenate([kv, farthest[None]], axis=0)

    last = (((1,), (1,)), ((), ()))
    do_t = lax.dot_general(out_full, dy, (((0,), (1,)), ((), ())), preferred_element_type=f32).astype(low)
    context, dq_t, dkv_own, dkv_sent = attention(q_t, do_t, start_here, cosine, sine, kv)
    parts = flow(jnp.stack(feed_parts), *half_way)
    up_near, down_near = parts[:, :unit_rows], parts[:, unit_rows:]
    up_near = gather_bit(up_near, y_bit, 0, after=(pair, farthest))
    for bit in x_bits:
        down_near = gather_bit(down_near, bit, 0, after=(pair, farthest))
    for bit in x_bits:
        up_near = gather_bit(up_near, bit, 0, after=(dq_t,))
    down_near = gather_bit(down_near, y_bit, len(x_bits), after=(dq_t,))
    shape = (1, plane, depth, unit_rows, D)
    near_weight = jnp.concatenate([up_near.reshape(shape), down_near.reshape(shape)], axis=0)
    near_weight = flow(near_weight, dq_t)
    far_weight = swap(near_weight, core_bit)

    dkv_far = shifted(dkv_sent[reach - 1], reach, True)
    dkv = jnp.concatenate([dkv_own[None], dkv_sent[: reach - 1].astype(f32)], axis=0)
    dkv_steps = []
    while dkv.shape[0] > 1:
        half = dkv.shape[0] // 2
        dkv = dkv[:half] + shifted(dkv[half:].astype(low), half, True).astype(f32)
        dkv_steps.append(dkv)
    dkv = dkv[0] + dkv_far.astype(f32)
    bias_grads, grad_sums = [[], []], []
    sums = None
    earlier = (dkv_steps[0],)
    for g, depths in enumerate(group_depths):
        *sums, far_grad, near_grad, bias_far, bias_here = feed(
            normed_two, dy, flow(far_weight, *earlier), near_weight, bias_rows[1][g], bias_rows[0][g], depths, sums
        )
        bias_grads[0].append(bias_here)
        bias_grads[1].append(bias_far)
        grad_sums.append(near_grad + swap(far_grad, core_bit).astype(f32))
        shape = (2,) * len(x_bits) + (2, len(group_depths[g]), unit_rows, D)
        halves = [
            split_bit(grad_sums[-1][0].reshape(shape), x_bits[-1], 0),
            split_bit(grad_sums[-1][1].reshape(shape), y_bit, len(x_bits)),
        ]
        grad_sums[-1] = halves
        earlier = (halves[0][1], halves[1][1], dkv)
    mlp_out, d_normed_two = sums

    attn_out = lax.dot_general(context, out_full, last, preferred_element_type=f32)
    outputs = (x_low.astype(f32) + attn_out + mlp_out + out_bias).astype(low)
    out_grad_part = lax.dot_general(dy, context, (((0,), (0,)), ((), ())), preferred_element_type=f32)
    def feed_first(halves):
        (up_kept, up_sent), (down_kept, down_sent) = halves
        up_sum = up_kept + swap(up_sent, x_bits[-1]).astype(f32)
        for bit in x_bits[-2::-1]:
            up_sum = sum_bit(up_sum, bit, 0)
        return up_sum, down_kept + swap(down_sent, y_bit).astype(f32)

    def feed_second(up_sum, down_sum):
        up_sum = sum_bit(up_sum, y_bit, 0)
        for bit in x_bits[::-1]:
            down_sum = sum_bit(down_sum, bit, 0)
        return jnp.concatenate([up_sum, down_sum], axis=1)

    shape = (depth, 2) + (2,) * len(x_bits) + (2, -1, D)
    feed_sum = 0.0
    for g, (grad_sum, depths) in enumerate(zip(grad_sums, group_depths)):
        final = g == len(grad_sums) - 1
        up_sum, down_sum = feed_first(grad_sum)
        if g == 0:
            input_grad, head_part = tail(
                entry, x_low, dy, dq_t, dkv, cosine, sine, head_full, normed_one, flow(d_normed_two, up_sum, down_sum), gains, bias_grads, group_pieces,
                head_rows, vec_len,
            )
        if final:
            both = jnp.concatenate([head_part.reshape(shape), out_grad_part.reshape(shape)], axis=len(shape) - 2)
            both = sum_bit(flow(both, grad_sum[0][1], grad_sum[1][1]), core_bit, len(shape) - 3, True)
            up_sum = flow(up_sum, both)
        last_step = feed_second(up_sum, down_sum)
        if final:
            head_sum, out_sum = both[..., :head_part_rows, :], both[..., head_part_rows:, :]
            for bit in x_bits[::-1]:
                head_sum = sum_bit(head_sum, bit, 2, True)
            out_sum = sum_bit(out_sum, y_bit, 1, True)
            last_step = flow(last_step, head_sum, out_sum)
        for k, z in enumerate(depths):
            feed_sum = feed_sum + (last_step[k] if z == 0 else swap_z(last_step[k].astype(low), z).astype(f32))
    head_sum = sum_bit(head_sum, y_bit, 1, True)
    for bit in x_bits[::-1]:
        out_sum = sum_bit(out_sum, bit, 1, True)
    both = jnp.concatenate([head_sum, out_sum], axis=1)
    feed_sum = flow(feed_sum, both)
    both = sum_z(both, True)

    def spread(part):
        value = part.astype(low)
        for k, bit in enumerate(x_bits):
            value = gather_bit(value, bit, 0, True)
        value = gather_bit(value, core_bit, len(x_bits), True)
        return value.reshape(batch_count, -1, D)

    feed_grads = spread(feed_sum)
    up_low = feed_grads[:, :unit_rows].reshape(-1, D)
    down_low = feed_grads[:, unit_rows:].reshape(-1, D)
    others = spread(both)
    head_low = others[:, :head_part_rows].reshape(-1, D)
    out_low = others[:, head_part_rows:].reshape(-1, D)
    (up_grad, *up_states), (down_grad, *down_states) = update(
        bases,
        (up_low, 2, up_weight, up_first, up_second, False),
        (down_low, 3, down_weight, down_first, down_second, True),
    )
    (out_grad, *out_states), (qkv_grad, *qkv_states) = update(
        bases,
        (out_low, 1, out_weight, out_first, out_second, False),
        (head_low[:qkv_rows], 0, qkv_weight, qkv_first, qkv_second, False),
    )
    vector_grad = head_low[qkv_rows:used].astype(f32).reshape(-1)[:vec_len]
    vector_new, *vector_states = adam_step(vectors, vector_grad, vector_first, vector_second)
    states = (qkv_states, out_states, up_states, down_states, (*vector_states, vector_new))
    return (
        outputs.reshape(inputs.shape),
        input_grad.reshape(inputs.shape),
        qkv_grad,
        out_grad,
        up_grad,
        down_grad,
        vector_grad,
        *(state[0] for state in states),
        *(state[1] for state in states),
        *(state[2] for state in states),
    )


def solution(mesh):
    tokens = P("batch", "seq", None)
    rows, columns, flat = P("seq", None), P(None, "seq"), P("seq")
    params = (rows, rows, rows, columns, flat)
    return jax.shard_map(
        shards,
        mesh=mesh,
        in_specs=(tokens, tokens, P("batch", None)) + params + (P(),) + params + params,
        out_specs=(tokens, tokens) + params * 4,
        check_vma=False,
    )
```

```python
import functools

import jax
import jax.numpy as jnp
from jax import lax
from jax.experimental import pallas as pl
from jax.experimental.pallas import tpu as pltpu
from jax.sharding import PartitionSpec as P

D = 768
HEADS = 12
HEAD = 64
ROT = 16
FF = 3072
STEP = 10

layer_eps = 1e-05
adam_eps = 1e-08
beta_first = 0.95
beta_second = 0.95
matrix_rate = 0.08
vector_rate = 0.3
rope_base = 10000.0
masked_score = -1e30
low = jnp.bfloat16
f32 = jnp.float32
VMEM_LIMIT = 56 * 1024 * 1024
FEED_VMEM = 56 * 1024 * 1024
UPDATE_VMEM = 28 * 1024 * 1024


def swap(value, bit):
    axis, step = bit
    return lax.ppermute(value, axis, [(i, i ^ step) for i in range(lax.axis_size(axis))])


def mine(bit):
    axis, step = bit
    return lax.rem(lax.axis_index(axis) // step, 2)


def flow(first, *others):
    return lax.optimization_barrier((first, *others))[0]


def swap_z(value, step):
    size = lax.axis_size("seq")
    return lax.ppermute(value, "seq", [(i, i ^ (2 * step)) for i in range(size)])


def z_index():
    return lax.axis_index("seq") // 2


def gather_z(piece):
    return [piece] + [swap_z(piece, k) for k in range(1, lax.axis_size("seq") // 2)]


def gather_bit(value, bit, axis, absolute=False, after=()):
    got = swap(value, bit)
    if after:
        got = flow(got, *after)
    if absolute:
        upper = mine(bit) == 1
        return jnp.stack([jnp.where(upper, got, value), jnp.where(upper, value, got)], axis=axis)
    return jnp.stack([value, got], axis=axis)


def split_bit(value, bit, axis, absolute=False):
    if absolute:
        own = mine(bit)
        return (
            lax.dynamic_index_in_dim(value, own, axis, keepdims=False),
            lax.dynamic_index_in_dim(value, 1 - own, axis, keepdims=False).astype(low),
        )
    return lax.index_in_dim(value, 0, axis, keepdims=False), lax.index_in_dim(value, 1, axis, keepdims=False).astype(low)


def sum_bit(value, bit, axis, absolute=False, after=()):
    kept, sent = split_bit(value, bit, axis, absolute)
    got = swap(sent, bit)
    if after:
        got = flow(got, *after)
    return kept.astype(f32) + got.astype(f32)


def sum_z(value, absolute=False):
    count = value.shape[0]
    own = z_index() if absolute else 0
    pick = lambda k: lax.dynamic_index_in_dim(value, own ^ k, 0, keepdims=False) if absolute else value[k]
    total = pick(0).astype(f32)
    for k in range(1, count):
        total = total + swap_z(pick(k).astype(low), k).astype(f32)
    return total


def bit_names(axis, size):
    return [(axis, 1 << k) for k in range(size.bit_length() - 1)]


def moments(rotated, first, second):
    new_first = beta_first * first + (1.0 - beta_first) * rotated
    new_second = beta_second * second + (1.0 - beta_second) * rotated * rotated
    first_scale, second_scale = 1.0 / (1.0 - beta_first**STEP), 1.0 / (1.0 - beta_second**STEP)
    ratio = new_first * first_scale / (jnp.sqrt(new_second * second_scale) + adam_eps)
    return ratio, new_first, new_second


def adam_step(weight, grad, first, second):
    ratio, new_first, new_second = moments(grad, first, second)
    return (weight - vector_rate * ratio, new_first, new_second)


def attention_kernel(blocks, width, q_ref, do_ref, start_ref, cos_ref, sin_ref, kv_ref, context_ref, dq_ref, dkv_own_ref, dkv_ref):
    length = q_ref.shape[1]
    keys = blocks * length
    key_t = jnp.concatenate([kv_ref[k, :HEAD, :] for k in reversed(range(blocks))], axis=1)
    value_t = jnp.concatenate([kv_ref[k, HEAD:, :] for k in reversed(range(blocks))], axis=1)
    key = key_t.astype(f32).T.astype(low)
    value = value_t.astype(f32).T.astype(low)
    key_pos = lax.broadcasted_iota(jnp.int32, (keys, length), 0) - (blocks - 1) * length
    query_pos = lax.broadcasted_iota(jnp.int32, (keys, length), 1)
    allowed = (key_pos >= start_ref[0]) & (key_pos <= query_pos)
    bias = jnp.where(allowed, 0.0, masked_score)
    cosine, sine = cos_ref[...], sin_ref[...]
    d_key = jnp.zeros((keys, HEAD), f32)
    d_value = jnp.zeros((keys, HEAD), f32)
    last = (((1,), (1,)), ((), ()))
    for first in range(0, HEADS, width):
        heads = range(first, first + width)
        query = jnp.concatenate([q_ref[h * HEAD : (h + 1) * HEAD, :] for h in heads], axis=1)
        d_out = jnp.concatenate([do_ref[h * HEAD : (h + 1) * HEAD, :] for h in heads], axis=1)
        scores = jnp.dot(key, query, preferred_element_type=f32)
        scores = scores + jnp.concatenate([bias] * width, axis=1)
        weights = jnp.exp(scores - jnp.max(scores, axis=0, keepdims=True))
        probs = weights * (1.0 / jnp.sum(weights, axis=0, keepdims=True))
        probs_low = probs.astype(low)
        context_t = jnp.dot(value_t, probs_low, preferred_element_type=f32)
        d_probs = jnp.dot(value, d_out, preferred_element_type=f32)
        inner = jnp.sum(probs * d_probs, axis=0, keepdims=True)
        d_scores = (probs * (d_probs - inner)).astype(low)
        d_query = jnp.dot(key_t, d_scores, preferred_element_type=f32) * HEAD ** (-0.5)
        d_value = d_value + lax.dot_general(probs_low, d_out, last, preferred_element_type=f32)
        d_key = d_key + lax.dot_general(d_scores, query, last, preferred_element_type=f32)
        for k, h in enumerate(heads):
            lanes = slice(k * length, (k + 1) * length)
            part = d_query[:, lanes]
            a, b = part[: ROT // 2], part[ROT // 2 : ROT]
            turned = jnp.concatenate([a * cosine + b * sine, b * cosine - a * sine, part[ROT:]], axis=0)
            dq_ref[h * HEAD : (h + 1) * HEAD, :] = turned.astype(low)
        for k in range(0, width, 2):
            h = first + k
            two = jnp.concatenate(
                [context_t[:, k * length : (k + 1) * length], context_t[:, (k + 1) * length : (k + 2) * length]], axis=0
            )
            context_ref[:, h * HEAD : (h + 2) * HEAD] = two.T.astype(low)
    d_kv = jnp.concatenate([d_key, d_value], axis=1).T
    for k in range(blocks):
        part = d_kv[:, (blocks - 1 - k) * length : (blocks - k) * length]
        if k == 0:
            dkv_own_ref[...] = part
        else:
            dkv_ref[k - 1] = part.astype(low)


def attention(q_t, do_t, start, cosine, sine, kv):
    rows, _, length = start.shape
    blocks = kv.shape[0]
    tokens = q_t.shape[1]
    by_row = lambda height: pl.BlockSpec((height, length), lambda r: (0, r))
    return pl.pallas_call(
        functools.partial(attention_kernel, blocks, HEADS),
        grid=(rows,),
        in_specs=[by_row(D), by_row(D), pl.BlockSpec((1, 1, length), lambda r: (r, 0, 0)), by_row(ROT // 2), by_row(ROT // 2)]
        + [pl.BlockSpec((blocks, 2 * HEAD, length), lambda r: (0, 0, r))],
        out_specs=[
            pl.BlockSpec((length, D), lambda r: (r, 0)),
            by_row(D),
            by_row(2 * HEAD),
            pl.BlockSpec((blocks - 1, 2 * HEAD, length), lambda r: (0, 0, r)),
        ],
        out_shape=[
            jax.ShapeDtypeStruct((tokens, D), low),
            jax.ShapeDtypeStruct((D, tokens), low),
            jax.ShapeDtypeStruct((2 * HEAD, tokens), f32),
            jax.ShapeDtypeStruct((blocks - 1, 2 * HEAD, tokens), low),
        ],
        compiler_params=pltpu.CompilerParams(vmem_limit_bytes=VMEM_LIMIT),
        cost_estimate=pl.CostEstimate(
            flops=4 * 7 * tokens * HEADS * blocks * length * HEAD * 2, bytes_accessed=8 << 20, transcendentals=0
        ),
        name="attention",
    )(q_t, do_t, start, cosine, sine, kv)


def feed_kernel(depths, n_ref, dy_ref, far_ref, near_ref, bias_far_ref, bias_near_ref, *refs):
    before = refs[: len(refs) - 11]
    out_ref, dn_ref, far_grad_ref, near_grad_ref, bias_far_grad_ref, bias_near_grad_ref = refs[-11:-5]
    weights, far_sum, near_sum, held, sems = refs[-5:]
    plane = weights.shape[2]
    last = (((1,), (1,)), ((), ()))
    first = (((0,), (0,)), ((), ()))
    loads = []
    for side, ref in enumerate((far_ref, near_ref)):
        loads.append(
            [
                pltpu.make_async_copy(
                    ref.at[:, k, pl.ds(depths[0], len(depths))], weights.at[side, :, k], sems.at[side, k]
                )
                for k in range(plane)
            ]
        )
    fetches = [pltpu.make_async_copy(ref, held.at[k], sems.at[2, k]) for k, ref in enumerate(before)]
    for copy in loads[0] + loads[1] + fetches:
        copy.start()
    normed, d_out = n_ref[...], dy_ref[...]
    units = far_sum.shape[1]
    out, d_normed = 0.0, 0.0
    stores = []
    for side, (bias_ref, bias_grad_ref, buffer, grad_ref) in enumerate(
        (
            (bias_far_ref, bias_far_grad_ref, far_sum, far_grad_ref),
            (bias_near_ref, bias_near_grad_ref, near_sum, near_grad_ref),
        )
    ):
        for copy in loads[side]:
            copy.wait()
        up, down = weights[side, 0].reshape(units, D), weights[side, 1].reshape(units, D)
        hidden = lax.dot_general(normed, up, last, preferred_element_type=f32) + bias_ref[...]
        share = 0.5 * (1.0 + lax.erf(hidden * (0.5**0.5)))
        slope = share + hidden * (jnp.exp(-0.5 * hidden * hidden) * (0.5 / 3.141592653589793) ** 0.5)
        active = (hidden * share).astype(low)
        d_active = lax.dot_general(d_out, down, last, preferred_element_type=f32)
        d_hidden = (d_active * slope).astype(low)
        for k, part in enumerate(
            (
                lax.dot_general(d_hidden, normed, first, preferred_element_type=f32),
                lax.dot_general(active, d_out, first, preferred_element_type=f32),
            )
        ):
            buffer[k] = part.astype(buffer.dtype)
            copy = pltpu.make_async_copy(buffer.at[k], grad_ref.at[k], sems.at[3, 2 * side + k])
            copy.start()
            stores.append(copy)
        bias_grad_ref[...] = jnp.sum(d_hidden.astype(f32), axis=0, keepdims=True)
        out = out + jnp.dot(active, down, preferred_element_type=f32)
        d_normed = d_normed + jnp.dot(d_hidden, up, preferred_element_type=f32)
    for copy in fetches:
        copy.wait()
    out_ref[...] = held[0] + out if before else out
    dn_ref[...] = held[1] + d_normed if before else d_normed
    for copy in stores:
        copy.wait()


def feed(normed, d_out, far, near, bias_far, bias_near, depths, before):
    tokens = normed.shape[0]
    plane, rows = far.shape[1], far.shape[3]
    units = plane * len(depths) * rows
    before = before or []
    vmem, hbm = pl.BlockSpec(memory_space=pltpu.VMEM), pl.BlockSpec(memory_space=pl.ANY)
    return pl.pallas_call(
        functools.partial(feed_kernel, depths),
        in_specs=[vmem, vmem, hbm, hbm, vmem, vmem] + [hbm] * len(before),
        out_specs=[vmem, vmem, hbm, hbm, vmem, vmem],
        out_shape=[
            jax.ShapeDtypeStruct((tokens, D), f32),
            jax.ShapeDtypeStruct((tokens, D), f32),
            jax.ShapeDtypeStruct((2, units, D), low),
            jax.ShapeDtypeStruct((2, units, D), f32),
            jax.ShapeDtypeStruct((1, units), f32),
            jax.ShapeDtypeStruct((1, units), f32),
        ],
        scratch_shapes=[
            pltpu.VMEM((2, 2, plane, len(depths), rows, D), low),
            pltpu.VMEM((2, units, D), low),
            pltpu.VMEM((2, units, D), f32),
            pltpu.VMEM((2, tokens, D), f32),
            pltpu.SemaphoreType.DMA((4, max(plane, 4))),
        ],
        compiler_params=pltpu.CompilerParams(vmem_limit_bytes=FEED_VMEM),
        cost_estimate=pl.CostEstimate(flops=4 * 24 * tokens * units * D, bytes_accessed=8 << 20, transcendentals=0),
        name="feed",
    )(normed, d_out, far, near, bias_far, bias_near, *before)


def head_kernel(
    vec_len, group_pieces, device_ref, x_ref, head_ref, cos_ref, sin_ref, n_one_ref, n_two_ref, q_ref, kv_ref, gain_ref,
    bias_ref, *refs
):
    bias_refs, (flat, units) = refs[:-2], refs[-2:]
    shards_of = head_ref.shape[0]
    rows = (D + 2 * HEAD) // shards_of
    for s in range(shards_of):
        left, row = vec_len, rows
        tile = head_ref[s, rows:, :].astype(f32)
        while left > 0:
            size = min(left, D)
            begin = s * vec_len + (row - rows) * D
            flat[:, begin : begin + size] = tile[row - rows : row - rows + 1, :size]
            left -= size
            row += 1
    vector = lambda begin, size: flat[:, begin : begin + size]
    gain_one, shift_one, gain_two, shift_two = [vector(k * D, D) for k in range(4)]
    gain_ref[0:1] = gain_one
    gain_ref[1:2] = gain_two
    qkv_bias = vector(4 * D, D + 2 * HEAD)
    offset = 4 * D + D + 2 * HEAD
    bias_ref[...] = vector(offset, D) + vector(offset + D + FF, D)
    count, size = units.shape
    for k in range(count):
        units[k : k + 1, :] = vector(offset + D + k * size, size)
    sides = len(bias_refs) // len(group_pieces)
    for k, ref in enumerate(bias_refs):
        side, pieces = k // len(group_pieces), group_pieces[k % len(group_pieces)]
        for i, piece in enumerate(pieces):
            ref[:, i * size : (i + 1) * size] = units[pl.ds(device_ref[side * (count // sides) + piece], 1), :]
    x = x_ref[...].astype(f32)
    center = x - jnp.mean(x, axis=-1, keepdims=True)
    xhat = center * lax.rsqrt(jnp.mean(center * center, axis=-1, keepdims=True) + layer_eps)
    n_one = (xhat * gain_one + shift_one).astype(low)
    n_one_ref[...] = n_one
    n_two_ref[...] = (xhat * gain_two + shift_two).astype(low)
    weight = head_ref[:, :rows, :].reshape(shards_of * rows, D)
    column = jnp.broadcast_to(qkv_bias, (8, qkv_bias.shape[1])).T[:, 0:1]
    projected = lax.dot_general(weight, n_one, (((1,), (1,)), ((), ())), preferred_element_type=f32) + column
    cosine, sine = cos_ref[...], sin_ref[...]
    half = ROT // 2

    def turned(first):
        a, b = projected[first : first + half], projected[first + half : first + ROT]
        rest = projected[first + ROT : first + HEAD]
        return jnp.concatenate([a * cosine - b * sine, b * cosine + a * sine, rest], axis=0).astype(low)

    for h in range(HEADS):
        q_ref[h * HEAD : (h + 1) * HEAD, :] = turned(h * HEAD) * jnp.asarray(HEAD ** (-0.5), low)
    kv_ref[:HEAD, :] = turned(D)
    kv_ref[HEAD:, :] = projected[D + HEAD :].astype(low)


def head(device, x, head_full, cosine, sine, group_pieces, sides, vec_len):
    tokens = x.shape[0]
    shards_of = head_full.shape[0]
    count = device.shape[0]
    bias_rows = [jax.ShapeDtypeStruct((1, len(pieces) * (FF // count)), f32) for pieces in group_pieces] * sides
    return pl.pallas_call(
        functools.partial(head_kernel, vec_len, group_pieces),
        in_specs=[pl.BlockSpec(memory_space=pltpu.SMEM)] + [pl.BlockSpec(memory_space=pltpu.VMEM)] * 4,
        out_shape=[
            jax.ShapeDtypeStruct((tokens, D), low),
            jax.ShapeDtypeStruct((tokens, D), low),
            jax.ShapeDtypeStruct((D, tokens), low),
            jax.ShapeDtypeStruct((2 * HEAD, tokens), low),
            jax.ShapeDtypeStruct((2, D), f32),
            jax.ShapeDtypeStruct((1, D), f32),
            *bias_rows,
        ],
        scratch_shapes=[pltpu.VMEM((1, shards_of * vec_len), f32), pltpu.VMEM((count, FF // count), f32)],
        compiler_params=pltpu.CompilerParams(vmem_limit_bytes=FEED_VMEM),
        cost_estimate=pl.CostEstimate(flops=4 * 2 * tokens * 896 * D, bytes_accessed=8 << 20, transcendentals=0),
        name="head",
    )(device, x, head_full, cosine, sine)


def tail_kernel(
    vec_len, group_pieces, entry_ref, x_ref, dy_ref, dq_ref, dkv_ref, cos_ref, sin_ref, w_ref, n_ref, dn_ref, gain_ref, *refs,
):
    bias_refs, (in_grad_ref, part_ref, flat, units) = refs[:-4], refs[-4:]
    shards_of = w_ref.shape[0]
    rows = (D + 2 * HEAD) // shards_of
    d_kv = dkv_ref[...]
    a, b = d_kv[: ROT // 2], d_kv[ROT // 2 : ROT]
    cosine, sine = cos_ref[...], sin_ref[...]
    d_kv = jnp.concatenate([a * cosine + b * sine, b * cosine - a * sine, d_kv[ROT:]], axis=0).astype(low)
    d_proj = jnp.concatenate([dq_ref[...], d_kv], axis=0)
    first = (((0,), (0,)), ((), ()))
    weight = w_ref[:, :rows, :].reshape(shards_of * rows, D)
    qkv_grad = jnp.dot(d_proj, n_ref[...], preferred_element_type=f32)
    d_one = lax.dot_general(d_proj, weight, first, preferred_element_type=f32)
    d_two = dn_ref[...]
    x = x_ref[...].astype(f32)
    dy = dy_ref[...].astype(f32)
    center = x - jnp.mean(x, axis=-1, keepdims=True)
    inv_sigma = lax.rsqrt(jnp.mean(center * center, axis=-1, keepdims=True) + layer_eps)
    xhat = center * inv_sigma
    d_hat = d_one * gain_ref[0:1] + d_two * gain_ref[1:2]
    d_in = (
        d_hat - jnp.mean(d_hat, axis=-1, keepdims=True) - xhat * jnp.mean(d_hat * xhat, axis=-1, keepdims=True)
    ) * inv_sigma
    in_grad_ref[...] = (dy + d_in).astype(low)
    columns = lambda v: jnp.sum(v, axis=0, keepdims=True)
    dy_column = columns(dy)
    ones = jnp.ones((8, d_proj.shape[1]), low)
    proj_sum = lax.dot_general(ones, d_proj, (((1,), (1,)), ((), ())), preferred_element_type=f32)[0:1]
    pieces = [columns(d_one * xhat), columns(d_one), columns(d_two * xhat), columns(d_two)]
    pieces += [proj_sum, dy_column, None, dy_column]
    count, size = units.shape
    sides = len(bias_refs) // len(group_pieces)
    for k, ref in enumerate(bias_refs):
        side, members = k // len(group_pieces), group_pieces[k % len(group_pieces)]
        for i, member in enumerate(members):
            entry = side * (count // sides) + member
            units[entry : entry + 1, :] = ref[:, i * size : (i + 1) * size]
    offset = 0
    for piece in pieces:
        if piece is None:
            for k in range(count):
                flat[:, offset : offset + size] = units[pl.ds(entry_ref[k], 1), :]
                offset += size
        else:
            flat[:, offset : offset + piece.shape[1]] = piece
            offset += piece.shape[1]
    part_ref[...] = jnp.zeros_like(part_ref)
    for s in range(shards_of):
        part_ref[s, :rows, :] = qkv_grad[s * rows : (s + 1) * rows]
        left = vec_len
        row = rows
        while left > 0:
            size = min(left, D)
            begin = s * vec_len + (row - rows) * D
            part_ref[s, row : row + 1, :size] = flat[:, begin : begin + size]
            left -= size
            row += 1


def tail(entry, x, dy, dq_t, dkv, cosine, sine, weight, normed, d_normed, gains, bias_grads, group_pieces, head_rows, vec_len):
    tokens = x.shape[0]
    shards_of = weight.shape[0]
    total = shards_of * vec_len
    count = entry.shape[0]
    operands = (entry, x, dy, dq_t, dkv, cosine, sine, weight, normed, d_normed, gains, *sum(bias_grads, []))
    return pl.pallas_call(
        functools.partial(tail_kernel, vec_len, group_pieces),
        in_specs=[pl.BlockSpec(memory_space=pltpu.SMEM)] + [pl.BlockSpec(memory_space=pltpu.VMEM)] * (len(operands) - 1),
        out_shape=[
            jax.ShapeDtypeStruct((tokens, D), low),
            jax.ShapeDtypeStruct((shards_of, head_rows, D), f32),
        ],
        scratch_shapes=[pltpu.VMEM((1, total), f32), pltpu.VMEM((count, FF // count), f32)],
        compiler_params=pltpu.CompilerParams(vmem_limit_bytes=VMEM_LIMIT),
        cost_estimate=pl.CostEstimate(flops=4 * 4 * tokens * 896 * D, bytes_accessed=8 << 20, transcendentals=0),
        name="tail",
    )(*operands)


def split_low(value):
    high = value.astype(low)
    return high, (value - high.astype(f32)).astype(low)


def update_step(across, grad, high, rest, w_ref, first_ref, second_ref, grad_ref, first_new_ref, second_new_ref, w_new_ref):
    rotated = jnp.dot(grad, high, preferred_element_type=f32) + jnp.dot(grad, rest, preferred_element_type=f32)
    grad = grad.astype(f32)
    if across:
        rotated, grad = rotated.T, grad.T
    grad_ref[...] = grad
    ratio, first_new, second_new = moments(rotated, first_ref[...], second_ref[...])
    first_new_ref[...] = first_new
    second_new_ref[...] = second_new
    r_high, r_rest = split_low(ratio)
    if across:
        product = lambda r, b: jnp.dot(b, r, preferred_element_type=f32)
    else:
        product = lambda r, b: lax.dot_general(r, b, (((1,), (1,)), ((), ())), preferred_element_type=f32)
    unrotated = product(r_high, high) + (product(r_high, rest) + product(r_rest, high))
    w_new_ref[...] = w_ref[...] - matrix_rate * unrotated


def update_kernel(across, grad_ref, basis_ref, *refs):
    high, rest = split_low(basis_ref[...])
    update_step(across, grad_ref[...], high, rest, *refs)


def update(grad, basis, weight, first, second, across=False):
    return pl.pallas_call(
        functools.partial(update_kernel, across),
        out_shape=[jax.ShapeDtypeStruct(weight.shape, f32)] * 4,
        compiler_params=pltpu.CompilerParams(vmem_limit_bytes=UPDATE_VMEM),
        cost_estimate=pl.CostEstimate(flops=10 * grad.shape[0] * D * D, bytes_accessed=8 << 20, transcendentals=0),
        name="update",
    )(grad, basis, weight, first, second)


def shards(
    inputs,
    cotangent,
    doc_lengths,
    qkv_weight,
    out_weight,
    up_weight,
    down_weight,
    vectors,
    bases,
    qkv_first,
    out_first,
    up_first,
    down_first,
    vector_first,
    qkv_second,
    out_second,
    up_second,
    down_second,
    vector_second,
):
    seq_count, batch_count = lax.axis_size("seq"), lax.axis_size("batch")
    seq_index, batch_index = lax.axis_index("seq"), lax.axis_index("batch")
    row_count, shard_len = inputs.shape[:2]
    tokens = row_count * shard_len
    y_bit, *z_bits = bit_names("seq", seq_count)
    core_bit, *x_bits = bit_names("batch", batch_count)
    near = [core_bit] + x_bits[::-1] + [y_bit] + z_bits[::-1]
    depth = seq_count // 2
    plane = 2 ** (len(x_bits) + 1)
    group_depths = (range(depth // 2, depth), range(depth // 2))
    group_pieces = [[k * depth + z for k in range(plane) for z in depths] for depths in group_depths]
    x_low = inputs.reshape(tokens, D)
    dy = cotangent.reshape(tokens, D)

    first_pos = seq_index * shard_len
    query_pos = first_pos + jnp.arange(shard_len, dtype=jnp.int32)
    docs = doc_lengths.shape[1]
    earlier = jnp.arange(docs)[:, None] < jnp.arange(docs)[None, :]
    doc_starts = jnp.sum(jnp.where(earlier[None], doc_lengths[:, :, None], 0), axis=1)
    start = jnp.max(
        jnp.where(doc_starts[:, None, :] <= query_pos[None, :, None], doc_starts[:, None, :], 0), axis=-1
    )
    offsets = (query_pos[None, :] - start).reshape(tokens)
    inverse = 1.0 / rope_base ** (jnp.arange(0, ROT, 2).astype(f32) / ROT)
    angles = offsets.astype(f32)[None, :] * inverse[:, None]
    cosine, sine = jnp.cos(angles), jnp.sin(angles)
    start_here = (start - first_pos).astype(jnp.int32)[:, None, :]
    number = jnp.arange(seq_count * batch_count, dtype=jnp.int32)

    def bits_of(value, place_of):
        total = 0
        for k, (axis_name, step) in enumerate(near[::-1]):
            total = total + place_of(value, k, axis_name, step)
        return total

    differs = {"seq": (number // batch_count) ^ seq_index, "batch": (number % batch_count) ^ batch_index}
    entry = bits_of(number, lambda v, k, name, step: (differs[name] // step) % 2 << k).astype(jnp.int32)
    xor_of = lambda name: sum((number >> k) % 2 * step for k, (axis_name, step) in enumerate(near[::-1]) if axis_name == name)
    device = ((xor_of("seq") ^ seq_index) * batch_count + (xor_of("batch") ^ batch_index)).astype(jnp.int32)

    qkv_rows, out_rows, up_rows, vec_len = qkv_weight.shape[0], out_weight.shape[0], up_weight.shape[0], vectors.shape[0]
    vec_rows = -(-vec_len // D)
    used = qkv_rows + vec_rows
    head_rows = -(-used // (8 * batch_count)) * 8 * batch_count
    vec_pad = vec_rows * D - vec_len

    def own_part(rows):
        size = rows.shape[0] // batch_count
        return lax.dynamic_slice_in_dim(rows, batch_index * size, size, axis=0)

    head_shard = jnp.concatenate(
        [qkv_weight, jnp.pad(vectors, (0, vec_pad)).reshape(vec_rows, D), jnp.zeros((head_rows - used, D), f32)], axis=0
    ).astype(low)
    head_part_rows = head_rows // batch_count
    value = jnp.concatenate([own_part(head_shard), own_part(out_weight.astype(low))], axis=0)
    unit_rows = up_rows // batch_count
    feed_part = jnp.concatenate([own_part(up_weight.astype(low)), own_part(down_weight.T.astype(low))], axis=0)
    for bit in z_bits:
        value = gather_bit(value, bit, 0, True)
        if bit == z_bits[0]:
            feed_parts = gather_z(flow(feed_part, value))
    value = value.reshape(depth, -1, D)
    value, cosine, sine, start_here, entry, device, _ = lax.optimization_barrier(
        (value, cosine, sine, start_here, entry, device, feed_parts[1])
    )
    head_full, out_full = value[:, :head_part_rows], value[:, head_part_rows:]
    head_full = gather_bit(head_full, y_bit, 1, True)
    for bit in x_bits:
        out_full = gather_bit(out_full, bit, 1, True)
    head_full, out_full, _ = lax.optimization_barrier((head_full, out_full, feed_parts[min(2, depth - 1)]))
    for bit in x_bits:
        head_full = gather_bit(head_full, bit, 2, True)
    out_full = gather_bit(out_full, y_bit, 1, True)
    order = 2 + len(x_bits)
    head_full, out_full, *_ = lax.optimization_barrier((head_full, out_full, *feed_parts[3:]))
    half_way = (head_full, out_full)
    both = gather_bit(jnp.concatenate([head_full, out_full], axis=order), core_bit, order, True)
    head_full = both[..., :head_part_rows, :].reshape(seq_count, head_rows, D)
    out_full = both[..., head_part_rows:, :].reshape(D, D)

    normed_one, normed_two, q_t, kv_own, gains, out_bias, *bias_rows = head(
        device, x_low, head_full, cosine, sine, group_pieces, 2, vec_len
    )
    bias_rows = [bias_rows[: len(group_pieces)], bias_rows[len(group_pieces) :]]
    reach = seq_count // 2

    def shifted(value, step, back=False):
        pairs = [(j, j + step) for j in range(seq_count - step)]
        return lax.ppermute(value, "seq", [(b, a) for a, b in pairs] if back else pairs)

    kv = kv_own[None]
    farthest = shifted(kv_own, reach)
    pair = shifted(kv, 1)
    kv = jnp.concatenate([kv, pair], axis=0)
    while kv.shape[0] < reach:
        kv = jnp.concatenate([kv, shifted(kv, kv.shape[0])], axis=0)
    kv = jnp.concatenate([kv, farthest[None]], axis=0)

    last = (((1,), (1,)), ((), ()))
    do_t = lax.dot_general(out_full, dy, (((0,), (1,)), ((), ())), preferred_element_type=f32).astype(low)
    context, dq_t, dkv_own, dkv_sent = attention(q_t, do_t, start_here, cosine, sine, kv)
    parts = flow(jnp.stack(feed_parts), *half_way)
    up_near, down_near = parts[:, :unit_rows], parts[:, unit_rows:]
    up_near = gather_bit(up_near, y_bit, 0, after=(pair, farthest))
    for bit in x_bits:
        down_near = gather_bit(down_near, bit, 0, after=(pair, farthest))
    for bit in x_bits:
        up_near = gather_bit(up_near, bit, 0, after=(dq_t,))
    down_near = gather_bit(down_near, y_bit, len(x_bits), after=(dq_t,))
    shape = (1, plane, depth, unit_rows, D)
    near_weight = jnp.concatenate([up_near.reshape(shape), down_near.reshape(shape)], axis=0)
    near_weight = flow(near_weight, dq_t)
    far_weight = swap(near_weight, core_bit)

    dkv_far = shifted(dkv_sent[reach - 1], reach, True)
    dkv = jnp.concatenate([dkv_own[None], dkv_sent[: reach - 1].astype(f32)], axis=0)
    dkv_steps = []
    while dkv.shape[0] > 1:
        half = dkv.shape[0] // 2
        dkv = dkv[:half] + shifted(dkv[half:].astype(low), half, True).astype(f32)
        dkv_steps.append(dkv)
    dkv = dkv[0] + dkv_far.astype(f32)
    bias_grads, grad_sums = [[], []], []
    sums = None
    earlier = (dkv_steps[0],)
    for g, depths in enumerate(group_depths):
        *sums, far_grad, near_grad, bias_far, bias_here = feed(
            normed_two, dy, flow(far_weight, *earlier), near_weight, bias_rows[1][g], bias_rows[0][g], depths, sums
        )
        bias_grads[0].append(bias_here)
        bias_grads[1].append(bias_far)
        grad_sums.append(near_grad + swap(far_grad, core_bit).astype(f32))
        shape = (2,) * len(x_bits) + (2, len(group_depths[g]), unit_rows, D)
        halves = [
            split_bit(grad_sums[-1][0].reshape(shape), x_bits[-1], 0),
            split_bit(grad_sums[-1][1].reshape(shape), y_bit, len(x_bits)),
        ]
        grad_sums[-1] = halves
        earlier = (halves[0][1], halves[1][1], dkv)
    mlp_out, d_normed_two = sums

    attn_out = lax.dot_general(context, out_full, last, preferred_element_type=f32)
    out_grad_part = lax.dot_general(dy, context, (((0,), (0,)), ((), ())), preferred_element_type=f32)
    def feed_first(halves):
        (up_kept, up_sent), (down_kept, down_sent) = halves
        up_sum = up_kept + swap(up_sent, x_bits[-1]).astype(f32)
        for bit in x_bits[-2::-1]:
            up_sum = sum_bit(up_sum, bit, 0)
        return up_sum, down_kept + swap(down_sent, y_bit).astype(f32)

    def feed_second(up_sum, down_sum, after):
        up_sum = sum_bit(up_sum, y_bit, 0, after=after)
        for bit in x_bits[::-1]:
            down_sum = sum_bit(down_sum, bit, 0, after=after)
        return jnp.concatenate([up_sum, down_sum], axis=1)

    shape = (depth, 2) + (2,) * len(x_bits) + (2, -1, D)
    feed_sum = 0.0
    for g, (grad_sum, depths) in enumerate(zip(grad_sums, group_depths)):
        final = g == len(grad_sums) - 1
        up_sum, down_sum = feed_first(grad_sum)
        if g == 0:
            input_grad, head_part = tail(
                entry, x_low, dy, dq_t, dkv, cosine, sine, head_full, normed_one, flow(d_normed_two, up_sum, down_sum), gains, bias_grads, group_pieces,
                head_rows, vec_len,
            )
        if final:
            both = jnp.concatenate([head_part.reshape(shape), out_grad_part.reshape(shape)], axis=len(shape) - 2)
            both = sum_bit(flow(both, grad_sum[0][1], grad_sum[1][1]), core_bit, len(shape) - 3, True)
            up_sum = flow(up_sum, both)
        last_step = feed_second(up_sum, down_sum, () if final else (grad_sums[-1][0][1], grad_sums[-1][1][1]))
        if final:
            head_sum, out_sum = both[..., :head_part_rows, :], both[..., head_part_rows:, :]
            for bit in x_bits[::-1]:
                head_sum = sum_bit(head_sum, bit, 2, True)
            out_sum = sum_bit(out_sum, y_bit, 1, True)
        for k, z in enumerate(depths):
            feed_sum = feed_sum + (last_step[k] if z == 0 else swap_z(last_step[k].astype(low), z).astype(f32))
    head_sum = sum_bit(head_sum, y_bit, 1, True)
    for bit in x_bits[::-1]:
        out_sum = sum_bit(out_sum, bit, 1, True)
    both = jnp.concatenate([head_sum, out_sum], axis=1)
    both = sum_z(both, True)

    outputs = (x_low.astype(f32) + attn_out + flow(mlp_out, head_part) + out_bias).astype(low)

    def spread(part):
        value = part.astype(low)
        for k, bit in enumerate(x_bits):
            value = gather_bit(value, bit, 0, True)
        value = gather_bit(value, core_bit, len(x_bits), True)
        return value.reshape(batch_count, -1, D)

    feed_grads = spread(feed_sum)
    up_low = feed_grads[:, :unit_rows].reshape(-1, D)
    down_low = feed_grads[:, unit_rows:].reshape(-1, D)
    others = spread(both)
    head_low = others[:, :head_part_rows].reshape(-1, D)
    out_low = others[:, head_part_rows:].reshape(-1, D)
    up_grad, *up_states = update(up_low, bases[2], up_weight, up_first, up_second)
    down_grad, *down_states = update(down_low, bases[3], down_weight, down_first, down_second, True)
    out_grad, *out_states = update(out_low, bases[1], out_weight, out_first, out_second)
    qkv_grad, *qkv_states = update(head_low[:qkv_rows], bases[0], qkv_weight, qkv_first, qkv_second)
    vector_grad = head_low[qkv_rows:used].astype(f32).reshape(-1)[:vec_len]
    vector_new, *vector_states = adam_step(vectors, vector_grad, vector_first, vector_second)
    states = (qkv_states, out_states, up_states, down_states, (*vector_states, vector_new))
    return (
        outputs.reshape(inputs.shape),
        input_grad.reshape(inputs.shape),
        qkv_grad,
        out_grad,
        up_grad,
        down_grad,
        vector_grad,
        *(state[0] for state in states),
        *(state[1] for state in states),
        *(state[2] for state in states),
    )


def solution(mesh):
    tokens = P("batch", "seq", None)
    rows, columns, flat = P("seq", None), P(None, "seq"), P("seq")
    params = (rows, rows, rows, columns, flat)
    return jax.shard_map(
        shards,
        mesh=mesh,
        in_specs=(tokens, tokens, P("batch", None)) + params + (P(),) + params + params,
        out_specs=(tokens, tokens) + params * 4,
        check_vma=False,
    )
```

```python
import functools

import jax
import jax.numpy as jnp
from jax import lax
from jax.experimental import pallas as pl
from jax.experimental.pallas import tpu as pltpu
from jax.sharding import PartitionSpec as P

D = 768
HEADS = 12
HEAD = 64
ROT = 16
FF = 3072
STEP = 10

layer_eps = 1e-05
adam_eps = 1e-08
beta_first = 0.95
beta_second = 0.95
matrix_rate = 0.08
vector_rate = 0.3
rope_base = 10000.0
masked_score = -1e30
low = jnp.bfloat16
f32 = jnp.float32
VMEM_LIMIT = 56 * 1024 * 1024
FEED_VMEM = 56 * 1024 * 1024
UPDATE_VMEM = 28 * 1024 * 1024


def swap(value, bit):
    axis, step = bit
    return lax.ppermute(value, axis, [(i, i ^ step) for i in range(lax.axis_size(axis))])


def mine(bit):
    axis, step = bit
    return lax.rem(lax.axis_index(axis) // step, 2)


def flow(first, *others):
    return lax.optimization_barrier((first, *others))[0]


def swap_z(value, step):
    size = lax.axis_size("seq")
    return lax.ppermute(value, "seq", [(i, i ^ (2 * step)) for i in range(size)])


def z_index():
    return lax.axis_index("seq") // 2


def gather_z(piece):
    return [piece] + [swap_z(piece, k) for k in range(1, lax.axis_size("seq") // 2)]


def gather_bit(value, bit, axis, absolute=False, after=()):
    got = swap(value, bit)
    if after:
        got = flow(got, *after)
    if absolute:
        upper = mine(bit) == 1
        return jnp.stack([jnp.where(upper, got, value), jnp.where(upper, value, got)], axis=axis)
    return jnp.stack([value, got], axis=axis)


def split_bit(value, bit, axis, absolute=False):
    if absolute:
        own = mine(bit)
        return (
            lax.dynamic_index_in_dim(value, own, axis, keepdims=False),
            lax.dynamic_index_in_dim(value, 1 - own, axis, keepdims=False).astype(low),
        )
    return lax.index_in_dim(value, 0, axis, keepdims=False), lax.index_in_dim(value, 1, axis, keepdims=False).astype(low)


def sum_bit(value, bit, axis, absolute=False, after=()):
    kept, sent = split_bit(value, bit, axis, absolute)
    got = swap(sent, bit)
    if after:
        got = flow(got, *after)
    return kept.astype(f32) + got.astype(f32)


def sum_z(value, absolute=False):
    count = value.shape[0]
    own = z_index() if absolute else 0
    pick = lambda k: lax.dynamic_index_in_dim(value, own ^ k, 0, keepdims=False) if absolute else value[k]
    total = pick(0).astype(f32)
    for k in range(1, count):
        total = total + swap_z(pick(k).astype(low), k).astype(f32)
    return total


def bit_names(axis, size):
    return [(axis, 1 << k) for k in range(size.bit_length() - 1)]


def moments(rotated, first, second):
    new_first = beta_first * first + (1.0 - beta_first) * rotated
    new_second = beta_second * second + (1.0 - beta_second) * rotated * rotated
    first_scale, second_scale = 1.0 / (1.0 - beta_first**STEP), 1.0 / (1.0 - beta_second**STEP)
    ratio = new_first * first_scale / (jnp.sqrt(new_second * second_scale) + adam_eps)
    return ratio, new_first, new_second


def adam_step(weight, grad, first, second):
    ratio, new_first, new_second = moments(grad, first, second)
    return (weight - vector_rate * ratio, new_first, new_second)


def attention_kernel(blocks, width, q_ref, do_ref, start_ref, cos_ref, sin_ref, kv_ref, context_ref, dq_ref, dkv_own_ref, dkv_ref):
    length = q_ref.shape[1]
    keys = blocks * length
    key_t = jnp.concatenate([kv_ref[k, :HEAD, :] for k in reversed(range(blocks))], axis=1)
    value_t = jnp.concatenate([kv_ref[k, HEAD:, :] for k in reversed(range(blocks))], axis=1)
    key = key_t.astype(f32).T.astype(low)
    value = value_t.astype(f32).T.astype(low)
    key_pos = lax.broadcasted_iota(jnp.int32, (keys, length), 0) - (blocks - 1) * length
    query_pos = lax.broadcasted_iota(jnp.int32, (keys, length), 1)
    allowed = (key_pos >= start_ref[0]) & (key_pos <= query_pos)
    bias = jnp.where(allowed, 0.0, masked_score)
    cosine, sine = cos_ref[...], sin_ref[...]
    d_key = jnp.zeros((keys, HEAD), f32)
    d_value = jnp.zeros((keys, HEAD), f32)
    last = (((1,), (1,)), ((), ()))
    for first in range(0, HEADS, width):
        heads = range(first, first + width)
        query = jnp.concatenate([q_ref[h * HEAD : (h + 1) * HEAD, :] for h in heads], axis=1)
        d_out = jnp.concatenate([do_ref[h * HEAD : (h + 1) * HEAD, :] for h in heads], axis=1)
        scores = jnp.dot(key, query, preferred_element_type=f32)
        scores = scores + jnp.concatenate([bias] * width, axis=1)
        weights = jnp.exp(scores - jnp.max(scores, axis=0, keepdims=True))
        probs = weights * (1.0 / jnp.sum(weights, axis=0, keepdims=True))
        probs_low = probs.astype(low)
        context_t = jnp.dot(value_t, probs_low, preferred_element_type=f32)
        d_probs = jnp.dot(value, d_out, preferred_element_type=f32)
        inner = jnp.sum(probs * d_probs, axis=0, keepdims=True)
        d_scores = (probs * (d_probs - inner)).astype(low)
        d_query = jnp.dot(key_t, d_scores, preferred_element_type=f32) * HEAD ** (-0.5)
        d_value = d_value + lax.dot_general(probs_low, d_out, last, preferred_element_type=f32)
        d_key = d_key + lax.dot_general(d_scores, query, last, preferred_element_type=f32)
        for k, h in enumerate(heads):
            lanes = slice(k * length, (k + 1) * length)
            part = d_query[:, lanes]
            a, b = part[: ROT // 2], part[ROT // 2 : ROT]
            turned = jnp.concatenate([a * cosine + b * sine, b * cosine - a * sine, part[ROT:]], axis=0)
            dq_ref[h * HEAD : (h + 1) * HEAD, :] = turned.astype(low)
        for k in range(0, width, 2):
            h = first + k
            two = jnp.concatenate(
                [context_t[:, k * length : (k + 1) * length], context_t[:, (k + 1) * length : (k + 2) * length]], axis=0
            )
            context_ref[:, h * HEAD : (h + 2) * HEAD] = two.T.astype(low)
    d_kv = jnp.concatenate([d_key, d_value], axis=1).T
    for k in range(blocks):
        part = d_kv[:, (blocks - 1 - k) * length : (blocks - k) * length]
        if k == 0:
            dkv_own_ref[...] = part
        else:
            dkv_ref[k - 1] = part.astype(low)


def attention(q_t, do_t, start, cosine, sine, kv):
    rows, _, length = start.shape
    blocks = kv.shape[0]
    tokens = q_t.shape[1]
    by_row = lambda height: pl.BlockSpec((height, length), lambda r: (0, r))
    return pl.pallas_call(
        functools.partial(attention_kernel, blocks, HEADS),
        grid=(rows,),
        in_specs=[by_row(D), by_row(D), pl.BlockSpec((1, 1, length), lambda r: (r, 0, 0)), by_row(ROT // 2), by_row(ROT // 2)]
        + [pl.BlockSpec((blocks, 2 * HEAD, length), lambda r: (0, 0, r))],
        out_specs=[
            pl.BlockSpec((length, D), lambda r: (r, 0)),
            by_row(D),
            by_row(2 * HEAD),
            pl.BlockSpec((blocks - 1, 2 * HEAD, length), lambda r: (0, 0, r)),
        ],
        out_shape=[
            jax.ShapeDtypeStruct((tokens, D), low),
            jax.ShapeDtypeStruct((D, tokens), low),
            jax.ShapeDtypeStruct((2 * HEAD, tokens), f32),
            jax.ShapeDtypeStruct((blocks - 1, 2 * HEAD, tokens), low),
        ],
        compiler_params=pltpu.CompilerParams(vmem_limit_bytes=VMEM_LIMIT),
        cost_estimate=pl.CostEstimate(
            flops=4 * 7 * tokens * HEADS * blocks * length * HEAD * 2, bytes_accessed=8 << 20, transcendentals=0
        ),
        name="attention",
    )(q_t, do_t, start, cosine, sine, kv)


def feed_kernel(depths, n_ref, dy_ref, far_ref, near_ref, bias_far_ref, bias_near_ref, *refs):
    before = refs[: len(refs) - 11]
    out_ref, dn_ref, far_grad_ref, near_grad_ref, bias_far_grad_ref, bias_near_grad_ref = refs[-11:-5]
    weights, far_sum, near_sum, held, sems = refs[-5:]
    plane = weights.shape[2]
    last = (((1,), (1,)), ((), ()))
    first = (((0,), (0,)), ((), ()))
    loads = []
    for side, ref in enumerate((far_ref, near_ref)):
        loads.append(
            [
                pltpu.make_async_copy(
                    ref.at[:, k, pl.ds(depths[0], len(depths))], weights.at[side, :, k], sems.at[side, k]
                )
                for k in range(plane)
            ]
        )
    fetches = [pltpu.make_async_copy(ref, held.at[k], sems.at[2, k]) for k, ref in enumerate(before)]
    for copy in loads[0] + loads[1] + fetches:
        copy.start()
    normed, d_out = n_ref[...], dy_ref[...]
    units = far_sum.shape[1]
    out, d_normed = 0.0, 0.0
    stores = []
    for side, (bias_ref, bias_grad_ref, buffer, grad_ref) in enumerate(
        (
            (bias_far_ref, bias_far_grad_ref, far_sum, far_grad_ref),
            (bias_near_ref, bias_near_grad_ref, near_sum, near_grad_ref),
        )
    ):
        for copy in loads[side]:
            copy.wait()
        up, down = weights[side, 0].reshape(units, D), weights[side, 1].reshape(units, D)
        hidden = lax.dot_general(normed, up, last, preferred_element_type=f32) + bias_ref[...]
        share = 0.5 * (1.0 + lax.erf(hidden * (0.5**0.5)))
        slope = share + hidden * (jnp.exp(-0.5 * hidden * hidden) * (0.5 / 3.141592653589793) ** 0.5)
        active = (hidden * share).astype(low)
        d_active = lax.dot_general(d_out, down, last, preferred_element_type=f32)
        d_hidden = (d_active * slope).astype(low)
        for k, part in enumerate(
            (
                lax.dot_general(d_hidden, normed, first, preferred_element_type=f32),
                lax.dot_general(active, d_out, first, preferred_element_type=f32),
            )
        ):
            buffer[k] = part.astype(buffer.dtype)
            copy = pltpu.make_async_copy(buffer.at[k], grad_ref.at[k], sems.at[3, 2 * side + k])
            copy.start()
            stores.append(copy)
        bias_grad_ref[...] = jnp.sum(d_hidden.astype(f32), axis=0, keepdims=True)
        out = out + jnp.dot(active, down, preferred_element_type=f32)
        d_normed = d_normed + jnp.dot(d_hidden, up, preferred_element_type=f32)
    for copy in fetches:
        copy.wait()
    out_ref[...] = held[0] + out if before else out
    dn_ref[...] = held[1] + d_normed if before else d_normed
    for copy in stores:
        copy.wait()


def feed(normed, d_out, far, near, bias_far, bias_near, depths, before):
    tokens = normed.shape[0]
    plane, rows = far.shape[1], far.shape[3]
    units = plane * len(depths) * rows
    before = before or []
    vmem, hbm = pl.BlockSpec(memory_space=pltpu.VMEM), pl.BlockSpec(memory_space=pl.ANY)
    return pl.pallas_call(
        functools.partial(feed_kernel, depths),
        in_specs=[vmem, vmem, hbm, hbm, vmem, vmem] + [hbm] * len(before),
        out_specs=[vmem, vmem, hbm, hbm, vmem, vmem],
        out_shape=[
            jax.ShapeDtypeStruct((tokens, D), f32),
            jax.ShapeDtypeStruct((tokens, D), f32),
            jax.ShapeDtypeStruct((2, units, D), low),
            jax.ShapeDtypeStruct((2, units, D), f32),
            jax.ShapeDtypeStruct((1, units), f32),
            jax.ShapeDtypeStruct((1, units), f32),
        ],
        scratch_shapes=[
            pltpu.VMEM((2, 2, plane, len(depths), rows, D), low),
            pltpu.VMEM((2, units, D), low),
            pltpu.VMEM((2, units, D), f32),
            pltpu.VMEM((2, tokens, D), f32),
            pltpu.SemaphoreType.DMA((4, max(plane, 4))),
        ],
        compiler_params=pltpu.CompilerParams(vmem_limit_bytes=FEED_VMEM),
        cost_estimate=pl.CostEstimate(flops=4 * 24 * tokens * units * D, bytes_accessed=8 << 20, transcendentals=0),
        name="feed",
    )(normed, d_out, far, near, bias_far, bias_near, *before)


def head_kernel(
    vec_len, group_pieces, device_ref, x_ref, head_ref, cos_ref, sin_ref, n_one_ref, n_two_ref, q_ref, kv_ref, gain_ref,
    bias_ref, *refs
):
    bias_refs, (flat, units) = refs[:-2], refs[-2:]
    shards_of = head_ref.shape[0]
    rows = (D + 2 * HEAD) // shards_of
    for s in range(shards_of):
        left, row = vec_len, rows
        tile = head_ref[s, rows:, :].astype(f32)
        while left > 0:
            size = min(left, D)
            begin = s * vec_len + (row - rows) * D
            flat[:, begin : begin + size] = tile[row - rows : row - rows + 1, :size]
            left -= size
            row += 1
    vector = lambda begin, size: flat[:, begin : begin + size]
    gain_one, shift_one, gain_two, shift_two = [vector(k * D, D) for k in range(4)]
    gain_ref[0:1] = gain_one
    gain_ref[1:2] = gain_two
    qkv_bias = vector(4 * D, D + 2 * HEAD)
    offset = 4 * D + D + 2 * HEAD
    bias_ref[...] = vector(offset, D) + vector(offset + D + FF, D)
    count, size = units.shape
    for k in range(count):
        units[k : k + 1, :] = vector(offset + D + k * size, size)
    sides = len(bias_refs) // len(group_pieces)
    for k, ref in enumerate(bias_refs):
        side, pieces = k // len(group_pieces), group_pieces[k % len(group_pieces)]
        for i, piece in enumerate(pieces):
            ref[:, i * size : (i + 1) * size] = units[pl.ds(device_ref[side * (count // sides) + piece], 1), :]
    x = x_ref[...].astype(f32)
    center = x - jnp.mean(x, axis=-1, keepdims=True)
    xhat = center * lax.rsqrt(jnp.mean(center * center, axis=-1, keepdims=True) + layer_eps)
    n_one = (xhat * gain_one + shift_one).astype(low)
    n_one_ref[...] = n_one
    n_two_ref[...] = (xhat * gain_two + shift_two).astype(low)
    weight = head_ref[:, :rows, :].reshape(shards_of * rows, D)
    column = jnp.broadcast_to(qkv_bias, (8, qkv_bias.shape[1])).T[:, 0:1]
    projected = lax.dot_general(weight, n_one, (((1,), (1,)), ((), ())), preferred_element_type=f32) + column
    cosine, sine = cos_ref[...], sin_ref[...]
    half = ROT // 2

    def turned(first):
        a, b = projected[first : first + half], projected[first + half : first + ROT]
        rest = projected[first + ROT : first + HEAD]
        return jnp.concatenate([a * cosine - b * sine, b * cosine + a * sine, rest], axis=0).astype(low)

    for h in range(HEADS):
        q_ref[h * HEAD : (h + 1) * HEAD, :] = turned(h * HEAD) * jnp.asarray(HEAD ** (-0.5), low)
    kv_ref[:HEAD, :] = turned(D)
    kv_ref[HEAD:, :] = projected[D + HEAD :].astype(low)


def head(device, x, head_full, cosine, sine, group_pieces, sides, vec_len):
    tokens = x.shape[0]
    shards_of = head_full.shape[0]
    count = device.shape[0]
    bias_rows = [jax.ShapeDtypeStruct((1, len(pieces) * (FF // count)), f32) for pieces in group_pieces] * sides
    return pl.pallas_call(
        functools.partial(head_kernel, vec_len, group_pieces),
        in_specs=[pl.BlockSpec(memory_space=pltpu.SMEM)] + [pl.BlockSpec(memory_space=pltpu.VMEM)] * 4,
        out_shape=[
            jax.ShapeDtypeStruct((tokens, D), low),
            jax.ShapeDtypeStruct((tokens, D), low),
            jax.ShapeDtypeStruct((D, tokens), low),
            jax.ShapeDtypeStruct((2 * HEAD, tokens), low),
            jax.ShapeDtypeStruct((2, D), f32),
            jax.ShapeDtypeStruct((1, D), f32),
            *bias_rows,
        ],
        scratch_shapes=[pltpu.VMEM((1, shards_of * vec_len), f32), pltpu.VMEM((count, FF // count), f32)],
        compiler_params=pltpu.CompilerParams(vmem_limit_bytes=FEED_VMEM),
        cost_estimate=pl.CostEstimate(flops=4 * 2 * tokens * 896 * D, bytes_accessed=8 << 20, transcendentals=0),
        name="head",
    )(device, x, head_full, cosine, sine)


def back_kernel(dq_ref, dkv_ref, cos_ref, sin_ref, head_ref, n_ref, grad_ref, dn_ref, sum_ref):
    shards_of = head_ref.shape[0]
    rows = (D + 2 * HEAD) // shards_of
    d_kv = dkv_ref[...]
    a, b = d_kv[: ROT // 2], d_kv[ROT // 2 : ROT]
    cosine, sine = cos_ref[...], sin_ref[...]
    d_kv = jnp.concatenate([a * cosine + b * sine, b * cosine - a * sine, d_kv[ROT:]], axis=0).astype(low)
    d_proj = jnp.concatenate([dq_ref[...], d_kv], axis=0)
    weight = head_ref[:, :rows, :].reshape(shards_of * rows, D)
    grad = jnp.dot(d_proj, n_ref[...], preferred_element_type=f32)
    grad_ref[...] = jnp.zeros_like(grad_ref)
    for s in range(shards_of):
        grad_ref[s, :rows, :] = grad[s * rows : (s + 1) * rows]
    dn_ref[...] = lax.dot_general(d_proj, weight, (((0,), (0,)), ((), ())), preferred_element_type=f32)
    ones = jnp.ones((8, d_proj.shape[1]), low)
    sum_ref[...] = lax.dot_general(ones, d_proj, (((1,), (1,)), ((), ())), preferred_element_type=f32)[0:1]


def back(dq_t, dkv, cosine, sine, head_full, normed, padded):
    tokens = normed.shape[0]
    width = D + 2 * HEAD
    return pl.pallas_call(
        back_kernel,
        out_shape=[
            jax.ShapeDtypeStruct((head_full.shape[0], padded, D), f32),
            jax.ShapeDtypeStruct((tokens, D), f32),
            jax.ShapeDtypeStruct((1, width), f32),
        ],
        compiler_params=pltpu.CompilerParams(vmem_limit_bytes=VMEM_LIMIT),
        cost_estimate=pl.CostEstimate(flops=4 * 4 * tokens * 896 * D, bytes_accessed=8 << 20, transcendentals=0),
        name="back",
    )(dq_t, dkv, cosine, sine, head_full, normed)


def tail_kernel(group_pieces, entry_ref, x_ref, dy_ref, d_one_ref, d_two_ref, gain_ref, sum_ref, *refs):
    bias_refs, (in_grad_ref, flat, units) = refs[:-3], refs[-3:]
    d_one, d_two = d_one_ref[...], d_two_ref[...]
    x = x_ref[...].astype(f32)
    dy = dy_ref[...].astype(f32)
    center = x - jnp.mean(x, axis=-1, keepdims=True)
    inv_sigma = lax.rsqrt(jnp.mean(center * center, axis=-1, keepdims=True) + layer_eps)
    xhat = center * inv_sigma
    d_hat = d_one * gain_ref[0:1] + d_two * gain_ref[1:2]
    d_in = (
        d_hat - jnp.mean(d_hat, axis=-1, keepdims=True) - xhat * jnp.mean(d_hat * xhat, axis=-1, keepdims=True)
    ) * inv_sigma
    in_grad_ref[...] = (dy + d_in).astype(low)
    columns = lambda v: jnp.sum(v, axis=0, keepdims=True)
    dy_column = columns(dy)
    pieces = [columns(d_one * xhat), columns(d_one), columns(d_two * xhat), columns(d_two)]
    pieces += [sum_ref[...], dy_column, None, dy_column]
    count, size = units.shape
    sides = len(bias_refs) // len(group_pieces)
    for k, ref in enumerate(bias_refs):
        side, members = k // len(group_pieces), group_pieces[k % len(group_pieces)]
        for i, member in enumerate(members):
            place = side * (count // sides) + member
            units[place : place + 1, :] = ref[:, i * size : (i + 1) * size]
    offset = 0
    for piece in pieces:
        if piece is None:
            for k in range(count):
                flat[:, offset : offset + size] = units[pl.ds(entry_ref[k], 1), :]
                offset += size
        else:
            flat[:, offset : offset + piece.shape[1]] = piece
            offset += piece.shape[1]


def tail(entry, x, dy, d_one, d_two, gains, proj_sum, bias_grads, group_pieces, total):
    tokens = x.shape[0]
    count = entry.shape[0]
    operands = (entry, x, dy, d_one, d_two, gains, proj_sum, *sum(bias_grads, []))
    return pl.pallas_call(
        functools.partial(tail_kernel, group_pieces),
        in_specs=[pl.BlockSpec(memory_space=pltpu.SMEM)] + [pl.BlockSpec(memory_space=pltpu.VMEM)] * (len(operands) - 1),
        out_shape=[jax.ShapeDtypeStruct((tokens, D), low), jax.ShapeDtypeStruct((1, total), f32)],
        scratch_shapes=[pltpu.VMEM((count, FF // count), f32)],
        compiler_params=pltpu.CompilerParams(vmem_limit_bytes=VMEM_LIMIT),
        cost_estimate=pl.CostEstimate(flops=4 * tokens * 896 * D, bytes_accessed=8 << 20, transcendentals=0),
        name="tail",
    )(*operands)


def split_low(value):
    high = value.astype(low)
    return high, (value - high.astype(f32)).astype(low)


def update_step(across, grad, high, rest, w_ref, first_ref, second_ref, grad_ref, first_new_ref, second_new_ref, w_new_ref):
    rotated = jnp.dot(grad, high, preferred_element_type=f32) + jnp.dot(grad, rest, preferred_element_type=f32)
    grad = grad.astype(f32)
    if across:
        rotated, grad = rotated.T, grad.T
    grad_ref[...] = grad
    ratio, first_new, second_new = moments(rotated, first_ref[...], second_ref[...])
    first_new_ref[...] = first_new
    second_new_ref[...] = second_new
    r_high, r_rest = split_low(ratio)
    if across:
        product = lambda r, b: jnp.dot(b, r, preferred_element_type=f32)
    else:
        product = lambda r, b: lax.dot_general(r, b, (((1,), (1,)), ((), ())), preferred_element_type=f32)
    unrotated = product(r_high, high) + (product(r_high, rest) + product(r_rest, high))
    w_new_ref[...] = w_ref[...] - matrix_rate * unrotated


def update_kernel(across, number, grad_ref, bases_ref, *refs):
    *refs, basis, sem = refs
    copy = pltpu.make_async_copy(bases_ref.at[number], basis, sem)
    copy.start()
    copy.wait()
    high, rest = split_low(basis[...])
    update_step(across, grad_ref[...], high, rest, *refs)


def update(grad, bases, number, weight, first, second, across=False):
    vmem = pl.BlockSpec(memory_space=pltpu.VMEM)
    return pl.pallas_call(
        functools.partial(update_kernel, across, number),
        in_specs=[vmem, pl.BlockSpec(memory_space=pl.ANY), vmem, vmem, vmem],
        out_shape=[jax.ShapeDtypeStruct(weight.shape, f32)] * 4,
        scratch_shapes=[pltpu.VMEM((D, D), f32), pltpu.SemaphoreType.DMA(())],
        compiler_params=pltpu.CompilerParams(vmem_limit_bytes=UPDATE_VMEM),
        cost_estimate=pl.CostEstimate(flops=10 * grad.shape[0] * D * D, bytes_accessed=8 << 20, transcendentals=0),
        name="update",
    )(grad, bases, weight, first, second)


def shards(
    inputs,
    cotangent,
    doc_lengths,
    qkv_weight,
    out_weight,
    up_weight,
    down_weight,
    vectors,
    bases,
    qkv_first,
    out_first,
    up_first,
    down_first,
    vector_first,
    qkv_second,
    out_second,
    up_second,
    down_second,
    vector_second,
):
    seq_count, batch_count = lax.axis_size("seq"), lax.axis_size("batch")
    seq_index, batch_index = lax.axis_index("seq"), lax.axis_index("batch")
    row_count, shard_len = inputs.shape[:2]
    tokens = row_count * shard_len
    y_bit, *z_bits = bit_names("seq", seq_count)
    core_bit, *x_bits = bit_names("batch", batch_count)
    near = [core_bit] + x_bits[::-1] + [y_bit] + z_bits[::-1]
    depth = seq_count // 2
    plane = 2 ** (len(x_bits) + 1)
    group_depths = (range(depth // 2, depth), range(depth // 2))
    group_pieces = [[k * depth + z for k in range(plane) for z in depths] for depths in group_depths]
    x_low = inputs.reshape(tokens, D)
    dy = cotangent.reshape(tokens, D)

    first_pos = seq_index * shard_len
    query_pos = first_pos + jnp.arange(shard_len, dtype=jnp.int32)
    docs = doc_lengths.shape[1]
    earlier = jnp.arange(docs)[:, None] < jnp.arange(docs)[None, :]
    doc_starts = jnp.sum(jnp.where(earlier[None], doc_lengths[:, :, None], 0), axis=1)
    start = jnp.max(
        jnp.where(doc_starts[:, None, :] <= query_pos[None, :, None], doc_starts[:, None, :], 0), axis=-1
    )
    offsets = (query_pos[None, :] - start).reshape(tokens)
    inverse = 1.0 / rope_base ** (jnp.arange(0, ROT, 2).astype(f32) / ROT)
    angles = offsets.astype(f32)[None, :] * inverse[:, None]
    cosine, sine = jnp.cos(angles), jnp.sin(angles)
    start_here = (start - first_pos).astype(jnp.int32)[:, None, :]
    number = jnp.arange(seq_count * batch_count, dtype=jnp.int32)

    def bits_of(value, place_of):
        total = 0
        for k, (axis_name, step) in enumerate(near[::-1]):
            total = total + place_of(value, k, axis_name, step)
        return total

    differs = {"seq": (number // batch_count) ^ seq_index, "batch": (number % batch_count) ^ batch_index}
    entry = bits_of(number, lambda v, k, name, step: (differs[name] // step) % 2 << k).astype(jnp.int32)
    xor_of = lambda name: sum((number >> k) % 2 * step for k, (axis_name, step) in enumerate(near[::-1]) if axis_name == name)
    device = ((xor_of("seq") ^ seq_index) * batch_count + (xor_of("batch") ^ batch_index)).astype(jnp.int32)

    qkv_rows, out_rows, up_rows, vec_len = qkv_weight.shape[0], out_weight.shape[0], up_weight.shape[0], vectors.shape[0]
    vec_rows = -(-vec_len // D)
    used = qkv_rows + vec_rows
    head_rows = -(-used // (8 * batch_count)) * 8 * batch_count
    vec_pad = vec_rows * D - vec_len

    def own_part(rows):
        size = rows.shape[0] // batch_count
        return lax.dynamic_slice_in_dim(rows, batch_index * size, size, axis=0)

    head_shard = jnp.concatenate(
        [qkv_weight, jnp.pad(vectors, (0, vec_pad)).reshape(vec_rows, D), jnp.zeros((head_rows - used, D), f32)], axis=0
    ).astype(low)
    head_part_rows = head_rows // batch_count
    value = jnp.concatenate([own_part(head_shard), own_part(out_weight.astype(low))], axis=0)
    unit_rows = up_rows // batch_count
    feed_part = jnp.concatenate([own_part(up_weight.astype(low)), own_part(down_weight.T.astype(low))], axis=0)
    for bit in z_bits:
        value = gather_bit(value, bit, 0, True)
        if bit == z_bits[0]:
            feed_parts = gather_z(flow(feed_part, value))
    value = value.reshape(depth, -1, D)
    value, cosine, sine, start_here, entry, device, _ = lax.optimization_barrier(
        (value, cosine, sine, start_here, entry, device, feed_parts[1])
    )
    head_full, out_full = value[:, :head_part_rows], value[:, head_part_rows:]
    head_full = gather_bit(head_full, y_bit, 1, True)
    for bit in x_bits:
        out_full = gather_bit(out_full, bit, 1, True)
    head_full, out_full, _ = lax.optimization_barrier((head_full, out_full, feed_parts[min(2, depth - 1)]))
    for bit in x_bits:
        head_full = gather_bit(head_full, bit, 2, True)
    out_full = gather_bit(out_full, y_bit, 1, True)
    order = 2 + len(x_bits)
    head_full, out_full, *_ = lax.optimization_barrier((head_full, out_full, *feed_parts[3:]))
    half_way = (head_full, out_full)
    both = gather_bit(jnp.concatenate([head_full, out_full], axis=order), core_bit, order, True)
    head_full = both[..., :head_part_rows, :].reshape(seq_count, head_rows, D)
    out_full = both[..., head_part_rows:, :].reshape(D, D)

    normed_one, normed_two, q_t, kv_own, gains, out_bias, *bias_rows = head(
        device, x_low, head_full, cosine, sine, group_pieces, 2, vec_len
    )
    bias_rows = [bias_rows[: len(group_pieces)], bias_rows[len(group_pieces) :]]
    reach = seq_count // 2

    def shifted(value, step, back=False):
        pairs = [(j, j + step) for j in range(seq_count - step)]
        return lax.ppermute(value, "seq", [(b, a) for a, b in pairs] if back else pairs)

    kv = kv_own[None]
    farthest = shifted(kv_own, reach)
    pair = shifted(kv, 1)
    kv = jnp.concatenate([kv, pair], axis=0)
    while kv.shape[0] < reach:
        kv = jnp.concatenate([kv, shifted(kv, kv.shape[0])], axis=0)
    kv = jnp.concatenate([kv, farthest[None]], axis=0)

    last = (((1,), (1,)), ((), ()))
    do_t = lax.dot_general(out_full, dy, (((0,), (1,)), ((), ())), preferred_element_type=f32).astype(low)
    context, dq_t, dkv_own, dkv_sent = attention(q_t, do_t, start_here, cosine, sine, kv)
    parts = flow(jnp.stack(feed_parts), *half_way)
    up_near, down_near = parts[:, :unit_rows], parts[:, unit_rows:]
    up_near = gather_bit(up_near, y_bit, 0, after=(pair, farthest))
    for bit in x_bits:
        down_near = gather_bit(down_near, bit, 0, after=(pair, farthest))
    for bit in x_bits:
        up_near = gather_bit(up_near, bit, 0, after=(dq_t,))
    down_near = gather_bit(down_near, y_bit, len(x_bits), after=(dq_t,))
    shape = (1, plane, depth, unit_rows, D)
    near_weight = jnp.concatenate([up_near.reshape(shape), down_near.reshape(shape)], axis=0)
    near_weight = flow(near_weight, dq_t)
    far_weight = swap(near_weight, core_bit)

    dkv_far = shifted(dkv_sent[reach - 1], reach, True)
    dkv = jnp.concatenate([dkv_own[None], dkv_sent[: reach - 1].astype(f32)], axis=0)
    dkv_steps = []
    while dkv.shape[0] > 1:
        half = dkv.shape[0] // 2
        dkv = dkv[:half] + shifted(dkv[half:].astype(low), half, True).astype(f32)
        dkv_steps.append(dkv)
    dkv = dkv[0] + dkv_far.astype(f32)
    bias_grads, halves_of = [[], []], []
    qkv_own = -(-qkv_rows // (8 * batch_count)) * 8
    sums = None
    earlier = (dkv_steps[0],)
    shape = (depth, 2) + (2,) * len(x_bits) + (2, -1, D)
    for g, depths in enumerate(group_depths):
        *sums, far_grad, near_grad, bias_far, bias_here = feed(
            normed_two, dy, flow(far_weight, *earlier), near_weight, bias_rows[1][g], bias_rows[0][g], depths, sums
        )
        bias_grads[0].append(bias_here)
        bias_grads[1].append(bias_far)
        grad_sum = near_grad + swap(far_grad, core_bit).astype(f32)
        half_shape = (2,) * len(x_bits) + (2, len(depths), unit_rows, D)
        halves = [
            split_bit(grad_sum[0].reshape(half_shape), x_bits[-1], 0),
            split_bit(grad_sum[1].reshape(half_shape), y_bit, len(x_bits)),
        ]
        halves_of.append(halves)
        if g == 0:
            qkv_part, d_normed_one, proj_sum = back(
                dq_t, dkv, cosine, sine, head_full, normed_one, qkv_own * batch_count
            )
            out_part = lax.dot_general(dy, context, (((0,), (0,)), ((), ())), preferred_element_type=f32)
            both = jnp.concatenate([qkv_part.reshape(shape), out_part.reshape(shape)], axis=len(shape) - 2)
            both = sum_bit(both, core_bit, len(shape) - 3, True)
            earlier = (halves[0][1], halves[1][1], both)
    mlp_out, d_normed_two = sums

    def feed_first(halves):
        (up_kept, up_sent), (down_kept, down_sent) = halves
        up_sum = up_kept + swap(up_sent, x_bits[-1]).astype(f32)
        for bit in x_bits[-2::-1]:
            up_sum = sum_bit(up_sum, bit, 0)
        return up_sum, down_kept + swap(down_sent, y_bit).astype(f32)

    def feed_second(up_sum, down_sum, after):
        up_sum = sum_bit(up_sum, y_bit, 0, after=after)
        for bit in x_bits[::-1]:
            down_sum = sum_bit(down_sum, bit, 0, after=after)
        return jnp.concatenate([up_sum, down_sum], axis=1)

    def spread(part):
        value = part.astype(low)
        for k, bit in enumerate(x_bits):
            value = gather_bit(value, bit, 0, True)
        value = gather_bit(value, core_bit, len(x_bits), True)
        return value.reshape(batch_count, -1, D)

    first_sums = feed_first(halves_of[0])
    qkv_sum, out_sum = both[..., :qkv_own, :], both[..., qkv_own:, :]
    for bit in x_bits[::-1]:
        qkv_sum = sum_bit(qkv_sum, bit, 2, True)
    out_sum = sum_bit(out_sum, y_bit, 1, True)
    sent = (halves_of[1][0][1], halves_of[1][1][1])
    input_grad, vector_part = tail(
        entry, x_low, dy, d_normed_one, flow(d_normed_two, *first_sums), gains, proj_sum, bias_grads, group_pieces,
        seq_count * vec_len,
    )
    vector_parts = lax.all_gather(vector_part[0], ("seq", "batch"))
    last_steps = [feed_second(*first_sums, sent)]
    qkv_sum = sum_bit(qkv_sum, y_bit, 1, True, after=sent)
    for bit in x_bits[::-1]:
        out_sum = sum_bit(out_sum, bit, 1, True, after=sent)
    both = sum_z(jnp.concatenate([qkv_sum, out_sum], axis=1), True)
    second_sums = feed_first(halves_of[1])
    last_steps.append(feed_second(*second_sums, (both,)))
    feed_sum = 0.0
    for depths, last_step in zip(group_depths, last_steps):
        for k, z in enumerate(depths):
            feed_sum = feed_sum + (last_step[k] if z == 0 else swap_z(last_step[k].astype(low), z).astype(f32))
    others = spread(both)
    qkv_low = others[:, :qkv_own].reshape(-1, D)[:qkv_rows]
    out_low = others[:, qkv_own:].reshape(-1, D)
    out_grad, *out_states = update(out_low, bases, 1, out_weight, out_first, out_second)
    qkv_grad, *qkv_states = update(qkv_low, bases, 0, qkv_weight, qkv_first, qkv_second)
    attn_out = lax.dot_general(context, out_full, last, preferred_element_type=f32)
    outputs = (x_low.astype(f32) + attn_out + flow(mlp_out, both) + out_bias).astype(low)
    feed_grads = spread(flow(feed_sum, out_grad, qkv_grad, outputs))
    up_low = feed_grads[:, :unit_rows].reshape(-1, D)
    down_low = feed_grads[:, unit_rows:].reshape(-1, D)
    up_grad, *up_states = update(up_low, bases, 2, up_weight, up_first, up_second)
    down_grad, *down_states = update(down_low, bases, 3, down_weight, down_first, down_second, True)
    vector_grad = jnp.sum(lax.dynamic_slice_in_dim(vector_parts, seq_index * vec_len, vec_len, axis=1), axis=0)
    vector_new, *vector_states = adam_step(vectors, vector_grad, vector_first, vector_second)
    states = (qkv_states, out_states, up_states, down_states, (*vector_states, vector_new))
    return (
        outputs.reshape(inputs.shape),
        input_grad.reshape(inputs.shape),
        qkv_grad,
        out_grad,
        up_grad,
        down_grad,
        vector_grad,
        *(state[0] for state in states),
        *(state[1] for state in states),
        *(state[2] for state in states),
    )


def solution(mesh):
    tokens = P("batch", "seq", None)
    rows, columns, flat = P("seq", None), P(None, "seq"), P("seq")
    params = (rows, rows, rows, columns, flat)
    return jax.shard_map(
        shards,
        mesh=mesh,
        in_specs=(tokens, tokens, P("batch", None)) + params + (P(),) + params + params,
        out_specs=(tokens, tokens) + params * 4,
        check_vma=False,
    )
```

```python
import functools

import jax
import jax.numpy as jnp
from jax import lax
from jax.experimental import pallas as pl
from jax.experimental.pallas import tpu as pltpu
from jax.sharding import PartitionSpec as P

D = 768
HEADS = 12
HEAD = 64
ROT = 16
FF = 3072
STEP = 10

layer_eps = 1e-05
adam_eps = 1e-08
beta_first = 0.95
beta_second = 0.95
matrix_rate = 0.08
vector_rate = 0.3
rope_base = 10000.0
masked_score = -1e30
low = jnp.bfloat16
f32 = jnp.float32
VMEM_LIMIT = 56 * 1024 * 1024
FEED_VMEM = 56 * 1024 * 1024
UPDATE_VMEM = 28 * 1024 * 1024


def swap(value, bit):
    axis, step = bit
    return lax.ppermute(value, axis, [(i, i ^ step) for i in range(lax.axis_size(axis))])


def mine(bit):
    axis, step = bit
    return lax.rem(lax.axis_index(axis) // step, 2)


def flow(first, *others):
    return lax.optimization_barrier((first, *others))[0]


def swap_z(value, step):
    size = lax.axis_size("seq")
    return lax.ppermute(value, "seq", [(i, i ^ (2 * step)) for i in range(size)])


def z_index():
    return lax.axis_index("seq") // 2


def gather_z(piece):
    return [piece] + [swap_z(piece, k) for k in range(1, lax.axis_size("seq") // 2)]


def gather_bit(value, bit, axis, absolute=False, after=()):
    got = swap(value, bit)
    if after:
        got = flow(got, *after)
    if absolute:
        upper = mine(bit) == 1
        return jnp.stack([jnp.where(upper, got, value), jnp.where(upper, value, got)], axis=axis)
    return jnp.stack([value, got], axis=axis)


def split_bit(value, bit, axis, absolute=False):
    if absolute:
        own = mine(bit)
        return (
            lax.dynamic_index_in_dim(value, own, axis, keepdims=False),
            lax.dynamic_index_in_dim(value, 1 - own, axis, keepdims=False).astype(low),
        )
    return lax.index_in_dim(value, 0, axis, keepdims=False), lax.index_in_dim(value, 1, axis, keepdims=False).astype(low)


def sum_bit(value, bit, axis, absolute=False, after=()):
    kept, sent = split_bit(value, bit, axis, absolute)
    got = swap(sent, bit)
    if after:
        got = flow(got, *after)
    return kept.astype(f32) + got.astype(f32)


def sum_z(value, absolute=False):
    count = value.shape[0]
    own = z_index() if absolute else 0
    pick = lambda k: lax.dynamic_index_in_dim(value, own ^ k, 0, keepdims=False) if absolute else value[k]
    total = pick(0).astype(f32)
    for k in range(1, count):
        total = total + swap_z(pick(k).astype(low), k).astype(f32)
    return total


def bit_names(axis, size):
    return [(axis, 1 << k) for k in range(size.bit_length() - 1)]


def moments(rotated, first, second):
    new_first = beta_first * first + (1.0 - beta_first) * rotated
    new_second = beta_second * second + (1.0 - beta_second) * rotated * rotated
    first_scale, second_scale = 1.0 / (1.0 - beta_first**STEP), 1.0 / (1.0 - beta_second**STEP)
    ratio = new_first * first_scale / (jnp.sqrt(new_second * second_scale) + adam_eps)
    return ratio, new_first, new_second


def adam_step(weight, grad, first, second):
    ratio, new_first, new_second = moments(grad, first, second)
    return (weight - vector_rate * ratio, new_first, new_second)


def attention_kernel(blocks, width, q_ref, do_ref, start_ref, cos_ref, sin_ref, kv_ref, context_ref, dq_ref, dkv_own_ref, dkv_ref):
    length = q_ref.shape[1]
    keys = blocks * length
    key_t = jnp.concatenate([kv_ref[k, :HEAD, :] for k in reversed(range(blocks))], axis=1)
    value_t = jnp.concatenate([kv_ref[k, HEAD:, :] for k in reversed(range(blocks))], axis=1)
    key = key_t.astype(f32).T.astype(low)
    value = value_t.astype(f32).T.astype(low)
    key_pos = lax.broadcasted_iota(jnp.int32, (keys, length), 0) - (blocks - 1) * length
    query_pos = lax.broadcasted_iota(jnp.int32, (keys, length), 1)
    allowed = (key_pos >= start_ref[0]) & (key_pos <= query_pos)
    bias = jnp.where(allowed, 0.0, masked_score)
    cosine, sine = cos_ref[...], sin_ref[...]
    d_key = jnp.zeros((keys, HEAD), f32)
    d_value = jnp.zeros((keys, HEAD), f32)
    last = (((1,), (1,)), ((), ()))
    for first in range(0, HEADS, width):
        heads = range(first, first + width)
        query = jnp.concatenate([q_ref[h * HEAD : (h + 1) * HEAD, :] for h in heads], axis=1)
        d_out = jnp.concatenate([do_ref[h * HEAD : (h + 1) * HEAD, :] for h in heads], axis=1)
        scores = jnp.dot(key, query, preferred_element_type=f32)
        scores = scores + jnp.concatenate([bias] * width, axis=1)
        weights = jnp.exp(scores - jnp.max(scores, axis=0, keepdims=True))
        probs = weights * (1.0 / jnp.sum(weights, axis=0, keepdims=True))
        probs_low = probs.astype(low)
        context_t = jnp.dot(value_t, probs_low, preferred_element_type=f32)
        d_probs = jnp.dot(value, d_out, preferred_element_type=f32)
        inner = jnp.sum(probs * d_probs, axis=0, keepdims=True)
        d_scores = (probs * (d_probs - inner)).astype(low)
        d_query = jnp.dot(key_t, d_scores, preferred_element_type=f32) * HEAD ** (-0.5)
        d_value = d_value + lax.dot_general(probs_low, d_out, last, preferred_element_type=f32)
        d_key = d_key + lax.dot_general(d_scores, query, last, preferred_element_type=f32)
        for k, h in enumerate(heads):
            lanes = slice(k * length, (k + 1) * length)
            part = d_query[:, lanes]
            a, b = part[: ROT // 2], part[ROT // 2 : ROT]
            turned = jnp.concatenate([a * cosine + b * sine, b * cosine - a * sine, part[ROT:]], axis=0)
            dq_ref[h * HEAD : (h + 1) * HEAD, :] = turned.astype(low)
        for k in range(0, width, 2):
            h = first + k
            two = jnp.concatenate(
                [context_t[:, k * length : (k + 1) * length], context_t[:, (k + 1) * length : (k + 2) * length]], axis=0
            )
            context_ref[:, h * HEAD : (h + 2) * HEAD] = two.T.astype(low)
    d_kv = jnp.concatenate([d_key, d_value], axis=1).T
    for k in range(blocks):
        part = d_kv[:, (blocks - 1 - k) * length : (blocks - k) * length]
        if k == 0:
            dkv_own_ref[...] = part
        else:
            dkv_ref[k - 1] = part.astype(low)


def attention(q_t, do_t, start, cosine, sine, kv):
    rows, _, length = start.shape
    blocks = kv.shape[0]
    tokens = q_t.shape[1]
    by_row = lambda height: pl.BlockSpec((height, length), lambda r: (0, r))
    return pl.pallas_call(
        functools.partial(attention_kernel, blocks, HEADS),
        grid=(rows,),
        in_specs=[by_row(D), by_row(D), pl.BlockSpec((1, 1, length), lambda r: (r, 0, 0)), by_row(ROT // 2), by_row(ROT // 2)]
        + [pl.BlockSpec((blocks, 2 * HEAD, length), lambda r: (0, 0, r))],
        out_specs=[
            pl.BlockSpec((length, D), lambda r: (r, 0)),
            by_row(D),
            by_row(2 * HEAD),
            pl.BlockSpec((blocks - 1, 2 * HEAD, length), lambda r: (0, 0, r)),
        ],
        out_shape=[
            jax.ShapeDtypeStruct((tokens, D), low),
            jax.ShapeDtypeStruct((D, tokens), low),
            jax.ShapeDtypeStruct((2 * HEAD, tokens), f32),
            jax.ShapeDtypeStruct((blocks - 1, 2 * HEAD, tokens), low),
        ],
        compiler_params=pltpu.CompilerParams(vmem_limit_bytes=VMEM_LIMIT),
        cost_estimate=pl.CostEstimate(
            flops=4 * 7 * tokens * HEADS * blocks * length * HEAD * 2, bytes_accessed=8 << 20, transcendentals=0
        ),
        name="attention",
    )(q_t, do_t, start, cosine, sine, kv)


def feed_kernel(depths, n_ref, dy_ref, far_ref, near_ref, bias_far_ref, bias_near_ref, *refs):
    before = refs[: len(refs) - 11]
    out_ref, dn_ref, far_grad_ref, near_grad_ref, bias_far_grad_ref, bias_near_grad_ref = refs[-11:-5]
    weights, far_sum, near_sum, held, sems = refs[-5:]
    plane = weights.shape[2]
    last = (((1,), (1,)), ((), ()))
    first = (((0,), (0,)), ((), ()))
    loads = []
    for side, ref in enumerate((far_ref, near_ref)):
        loads.append(
            [
                pltpu.make_async_copy(
                    ref.at[:, k, pl.ds(depths[0], len(depths)), pl.ds(0, weights.shape[4])], weights.at[side, :, k], sems.at[side, k]
                )
                for k in range(plane)
            ]
        )
    fetches = [pltpu.make_async_copy(ref, held.at[k], sems.at[2, k]) for k, ref in enumerate(before)]
    for copy in loads[0] + loads[1] + fetches:
        copy.start()
    normed, d_out = n_ref[...], dy_ref[...]
    units = far_sum.shape[1]
    out, d_normed = 0.0, 0.0
    stores = []
    for side, (bias_ref, bias_grad_ref, buffer, grad_ref) in enumerate(
        (
            (bias_far_ref, bias_far_grad_ref, far_sum, far_grad_ref),
            (bias_near_ref, bias_near_grad_ref, near_sum, near_grad_ref),
        )
    ):
        for copy in loads[side]:
            copy.wait()
        up, down = weights[side, 0].reshape(units, D), weights[side, 1].reshape(units, D)
        hidden = lax.dot_general(normed, up, last, preferred_element_type=f32) + bias_ref[...]
        share = 0.5 * (1.0 + lax.erf(hidden * (0.5**0.5)))
        slope = share + hidden * (jnp.exp(-0.5 * hidden * hidden) * (0.5 / 3.141592653589793) ** 0.5)
        active = (hidden * share).astype(low)
        d_active = lax.dot_general(d_out, down, last, preferred_element_type=f32)
        d_hidden = (d_active * slope).astype(low)
        for k, part in enumerate(
            (
                lax.dot_general(d_hidden, normed, first, preferred_element_type=f32),
                lax.dot_general(active, d_out, first, preferred_element_type=f32),
            )
        ):
            buffer[k] = part.astype(buffer.dtype)
            copy = pltpu.make_async_copy(buffer.at[k], grad_ref.at[k], sems.at[3, 2 * side + k])
            copy.start()
            stores.append(copy)
        bias_grad_ref[...] = jnp.sum(d_hidden.astype(f32), axis=0, keepdims=True)
        out = out + jnp.dot(active, down, preferred_element_type=f32)
        d_normed = d_normed + jnp.dot(d_hidden, up, preferred_element_type=f32)
    for copy in fetches:
        copy.wait()
    out_ref[...] = held[0] + out if before else out
    dn_ref[...] = held[1] + d_normed if before else d_normed
    for copy in stores:
        copy.wait()


def feed(normed, d_out, far, near, bias_far, bias_near, depths, rows, before):
    tokens = normed.shape[0]
    plane = far.shape[1]
    units = plane * len(depths) * rows
    before = before or []
    vmem, hbm = pl.BlockSpec(memory_space=pltpu.VMEM), pl.BlockSpec(memory_space=pl.ANY)
    return pl.pallas_call(
        functools.partial(feed_kernel, depths),
        in_specs=[vmem, vmem, hbm, hbm, vmem, vmem] + [hbm] * len(before),
        out_specs=[vmem, vmem, hbm, hbm, vmem, vmem],
        out_shape=[
            jax.ShapeDtypeStruct((tokens, D), f32),
            jax.ShapeDtypeStruct((tokens, D), f32),
            jax.ShapeDtypeStruct((2, units, D), low),
            jax.ShapeDtypeStruct((2, units, D), f32),
            jax.ShapeDtypeStruct((1, units), f32),
            jax.ShapeDtypeStruct((1, units), f32),
        ],
        scratch_shapes=[
            pltpu.VMEM((2, 2, plane, len(depths), rows, D), low),
            pltpu.VMEM((2, units, D), low),
            pltpu.VMEM((2, units, D), f32),
            pltpu.VMEM((2, tokens, D), f32),
            pltpu.SemaphoreType.DMA((4, max(plane, 4))),
        ],
        compiler_params=pltpu.CompilerParams(vmem_limit_bytes=FEED_VMEM),
        cost_estimate=pl.CostEstimate(flops=4 * 24 * tokens * units * D, bytes_accessed=8 << 20, transcendentals=0),
        name="feed",
    )(normed, d_out, far, near, bias_far, bias_near, *before)


def head_kernel(
    vec_len, group_pieces, offset, out_rows, device_ref, x_ref, near_ref, far_ref, cos_ref, sin_ref, n_one_ref, n_two_ref,
    q_ref, kv_ref, w_ref, gain_ref, bias_ref, *refs
):
    *bias_refs, out_ref, flat, units, held, pieces_of, outs_of, sems = refs if out_rows else (*refs[:-6], None, *refs[-6:])
    _, _, plane, depth, size, _ = held.shape
    copies = [
        pltpu.make_async_copy(ref.at[:, :, :, pl.ds(offset, size)], held.at[side], sems.at[side])
        for side, ref in enumerate((near_ref, far_ref))
    ]
    for copy in copies:
        copy.start()
    x = x_ref[...].astype(f32)
    center = x - jnp.mean(x, axis=-1, keepdims=True)
    xhat = center * lax.rsqrt(jnp.mean(center * center, axis=-1, keepdims=True) + layer_eps)
    for copy in copies:
        copy.wait()
    for side in range(2):
        for k in range(plane):
            for z in range(depth):
                number = device_ref[(side * plane + k) * depth + z]
                pieces_of[number] = held[side, 0, k, z].astype(f32)
                if out_rows:
                    outs_of[number] = held[side, 1, k, z][:out_rows].astype(f32)
    if out_rows:
        out_ref[...] = outs_of[...].reshape(out_ref.shape).astype(low)
    shards_of = (flat.shape[1]) // vec_len
    rows = (D + 2 * HEAD) // shards_of
    whole = pieces_of[...].reshape(shards_of, -1, D)
    for s in range(shards_of):
        left, row = vec_len, rows
        while left > 0:
            size = min(left, D)
            begin = s * vec_len + (row - rows) * D
            flat[:, begin : begin + size] = whole[s, row : row + 1, :size]
            left -= size
            row += 1
    vector = lambda begin, size: flat[:, begin : begin + size]
    gain_one, shift_one, gain_two, shift_two = [vector(k * D, D) for k in range(4)]
    gain_ref[0:1] = gain_one
    gain_ref[1:2] = gain_two
    qkv_bias = vector(4 * D, D + 2 * HEAD)
    offset = 4 * D + D + 2 * HEAD
    bias_ref[...] = vector(offset, D) + vector(offset + D + FF, D)
    count, size = units.shape
    for k in range(count):
        units[k : k + 1, :] = vector(offset + D + k * size, size)
    sides = len(bias_refs) // len(group_pieces)
    for k, ref in enumerate(bias_refs):
        side, pieces = k // len(group_pieces), group_pieces[k % len(group_pieces)]
        for i, piece in enumerate(pieces):
            ref[:, i * size : (i + 1) * size] = units[pl.ds(device_ref[side * (count // sides) + piece], 1), :]
    n_one = (xhat * gain_one + shift_one).astype(low)
    n_one_ref[...] = n_one
    n_two_ref[...] = (xhat * gain_two + shift_two).astype(low)
    weight = whole[:, :rows].reshape(shards_of * rows, D).astype(low)
    w_ref[...] = weight
    column = jnp.broadcast_to(qkv_bias, (8, qkv_bias.shape[1])).T[:, 0:1]
    projected = lax.dot_general(weight, n_one, (((1,), (1,)), ((), ())), preferred_element_type=f32) + column
    cosine, sine = cos_ref[...], sin_ref[...]
    half = ROT // 2

    def turned(first):
        a, b = projected[first : first + half], projected[first + half : first + ROT]
        rest = projected[first + ROT : first + HEAD]
        return jnp.concatenate([a * cosine - b * sine, b * cosine + a * sine, rest], axis=0).astype(low)

    for h in range(HEADS):
        q_ref[h * HEAD : (h + 1) * HEAD, :] = turned(h * HEAD) * jnp.asarray(HEAD ** (-0.5), low)
    kv_ref[:HEAD, :] = turned(D)
    kv_ref[HEAD:, :] = projected[D + HEAD :].astype(low)


def head(device, x, near, far, offset, size, out_rows, cosine, sine, group_pieces, vec_len, shards_of):
    tokens = x.shape[0]
    count = device.shape[0]
    _, plane, depth = near.shape[:3]
    width = FF // count
    vmem, hbm = pl.BlockSpec(memory_space=pltpu.VMEM), pl.BlockSpec(memory_space=pl.ANY)
    bias_rows = [jax.ShapeDtypeStruct((1, len(pieces) * width), f32) for pieces in group_pieces] * 2
    return pl.pallas_call(
        functools.partial(head_kernel, vec_len, group_pieces, offset, out_rows),
        in_specs=[pl.BlockSpec(memory_space=pltpu.SMEM), vmem, hbm, hbm, vmem, vmem],
        out_shape=[
            jax.ShapeDtypeStruct((tokens, D), low),
            jax.ShapeDtypeStruct((tokens, D), low),
            jax.ShapeDtypeStruct((D, tokens), low),
            jax.ShapeDtypeStruct((2 * HEAD, tokens), low),
            jax.ShapeDtypeStruct((D + 2 * HEAD, D), low),
            jax.ShapeDtypeStruct((2, D), f32),
            jax.ShapeDtypeStruct((1, D), f32),
            *bias_rows,
        ]
        + [jax.ShapeDtypeStruct((D, D), low)] * (out_rows > 0),
        scratch_shapes=[
            pltpu.VMEM((1, shards_of * vec_len), f32),
            pltpu.VMEM((count, width), f32),
            pltpu.VMEM((2, 2, plane, depth, size, D), low),
            pltpu.VMEM((count, size, D), f32),
            pltpu.VMEM((count, max(out_rows, 8), D), f32),
            pltpu.SemaphoreType.DMA((2,)),
        ],
        compiler_params=pltpu.CompilerParams(vmem_limit_bytes=FEED_VMEM),
        cost_estimate=pl.CostEstimate(flops=4 * 2 * tokens * 896 * D, bytes_accessed=8 << 20, transcendentals=0),
        name="head",
    )(device, x, near, far, cosine, sine)


def back_kernel(dq_ref, dkv_ref, cos_ref, sin_ref, w_ref, n_ref, grad_ref, dn_ref, sum_ref):
    shards_of = grad_ref.shape[0]
    rows = (D + 2 * HEAD) // shards_of
    d_kv = dkv_ref[...]
    a, b = d_kv[: ROT // 2], d_kv[ROT // 2 : ROT]
    cosine, sine = cos_ref[...], sin_ref[...]
    d_kv = jnp.concatenate([a * cosine + b * sine, b * cosine - a * sine, d_kv[ROT:]], axis=0).astype(low)
    d_proj = jnp.concatenate([dq_ref[...], d_kv], axis=0)
    weight = w_ref[...]
    grad = jnp.dot(d_proj, n_ref[...], preferred_element_type=f32)
    grad_ref[...] = jnp.zeros_like(grad_ref)
    for s in range(shards_of):
        grad_ref[s, :rows, :] = grad[s * rows : (s + 1) * rows]
    dn_ref[...] = lax.dot_general(d_proj, weight, (((0,), (0,)), ((), ())), preferred_element_type=f32)
    ones = jnp.ones((8, d_proj.shape[1]), low)
    sum_ref[...] = lax.dot_general(ones, d_proj, (((1,), (1,)), ((), ())), preferred_element_type=f32)[0:1]


def back(dq_t, dkv, cosine, sine, weight, normed, shards_of, padded):
    tokens = normed.shape[0]
    width = D + 2 * HEAD
    return pl.pallas_call(
        back_kernel,
        out_shape=[
            jax.ShapeDtypeStruct((shards_of, padded, D), f32),
            jax.ShapeDtypeStruct((tokens, D), f32),
            jax.ShapeDtypeStruct((1, width), f32),
        ],
        compiler_params=pltpu.CompilerParams(vmem_limit_bytes=VMEM_LIMIT),
        cost_estimate=pl.CostEstimate(flops=4 * 4 * tokens * 896 * D, bytes_accessed=8 << 20, transcendentals=0),
        name="back",
    )(dq_t, dkv, cosine, sine, weight, normed)


def tail_kernel(group_pieces, entry_ref, x_ref, dy_ref, d_one_ref, d_two_ref, gain_ref, sum_ref, *refs):
    bias_refs, (in_grad_ref, flat, units) = refs[:-3], refs[-3:]
    d_one, d_two = d_one_ref[...], d_two_ref[...]
    x = x_ref[...].astype(f32)
    dy = dy_ref[...].astype(f32)
    center = x - jnp.mean(x, axis=-1, keepdims=True)
    inv_sigma = lax.rsqrt(jnp.mean(center * center, axis=-1, keepdims=True) + layer_eps)
    xhat = center * inv_sigma
    d_hat = d_one * gain_ref[0:1] + d_two * gain_ref[1:2]
    d_in = (
        d_hat - jnp.mean(d_hat, axis=-1, keepdims=True) - xhat * jnp.mean(d_hat * xhat, axis=-1, keepdims=True)
    ) * inv_sigma
    in_grad_ref[...] = (dy + d_in).astype(low)
    columns = lambda v: jnp.sum(v, axis=0, keepdims=True)
    dy_column = columns(dy)
    pieces = [columns(d_one * xhat), columns(d_one), columns(d_two * xhat), columns(d_two)]
    pieces += [sum_ref[...], dy_column, None, dy_column]
    count, size = units.shape
    sides = len(bias_refs) // len(group_pieces)
    for k, ref in enumerate(bias_refs):
        side, members = k // len(group_pieces), group_pieces[k % len(group_pieces)]
        for i, member in enumerate(members):
            place = side * (count // sides) + member
            units[place : place + 1, :] = ref[:, i * size : (i + 1) * size]
    offset = 0
    for piece in pieces:
        if piece is None:
            for k in range(count):
                flat[:, offset : offset + size] = units[pl.ds(entry_ref[k], 1), :]
                offset += size
        else:
            flat[:, offset : offset + piece.shape[1]] = piece
            offset += piece.shape[1]


def tail(entry, x, dy, d_one, d_two, gains, proj_sum, bias_grads, group_pieces, total):
    tokens = x.shape[0]
    count = entry.shape[0]
    operands = (entry, x, dy, d_one, d_two, gains, proj_sum, *sum(bias_grads, []))
    return pl.pallas_call(
        functools.partial(tail_kernel, group_pieces),
        in_specs=[pl.BlockSpec(memory_space=pltpu.SMEM)] + [pl.BlockSpec(memory_space=pltpu.VMEM)] * (len(operands) - 1),
        out_shape=[jax.ShapeDtypeStruct((tokens, D), low), jax.ShapeDtypeStruct((1, total), f32)],
        scratch_shapes=[pltpu.VMEM((count, FF // count), f32)],
        compiler_params=pltpu.CompilerParams(vmem_limit_bytes=VMEM_LIMIT),
        cost_estimate=pl.CostEstimate(flops=4 * tokens * 896 * D, bytes_accessed=8 << 20, transcendentals=0),
        name="tail",
    )(*operands)


def split_low(value):
    high = value.astype(low)
    return high, (value - high.astype(f32)).astype(low)


def update_step(across, grad, high, rest, w_ref, first_ref, second_ref, grad_ref, first_new_ref, second_new_ref, w_new_ref):
    rotated = jnp.dot(grad, high, preferred_element_type=f32) + jnp.dot(grad, rest, preferred_element_type=f32)
    grad = grad.astype(f32)
    if across:
        rotated, grad = rotated.T, grad.T
    grad_ref[...] = grad
    ratio, first_new, second_new = moments(rotated, first_ref[...], second_ref[...])
    first_new_ref[...] = first_new
    second_new_ref[...] = second_new
    r_high, r_rest = split_low(ratio)
    if across:
        product = lambda r, b: jnp.dot(b, r, preferred_element_type=f32)
    else:
        product = lambda r, b: lax.dot_general(r, b, (((1,), (1,)), ((), ())), preferred_element_type=f32)
    unrotated = product(r_high, high) + (product(r_high, rest) + product(r_rest, high))
    w_new_ref[...] = w_ref[...] - matrix_rate * unrotated


def update_kernel(across, number, grad_ref, bases_ref, *refs):
    *refs, basis, sem = refs
    copy = pltpu.make_async_copy(bases_ref.at[number], basis, sem)
    copy.start()
    copy.wait()
    high, rest = split_low(basis[...])
    update_step(across, grad_ref[...], high, rest, *refs)


def update(grad, bases, number, weight, first, second, across=False):
    vmem = pl.BlockSpec(memory_space=pltpu.VMEM)
    return pl.pallas_call(
        functools.partial(update_kernel, across, number),
        in_specs=[vmem, pl.BlockSpec(memory_space=pl.ANY), vmem, vmem, vmem],
        out_shape=[jax.ShapeDtypeStruct(weight.shape, f32)] * 4,
        scratch_shapes=[pltpu.VMEM((D, D), f32), pltpu.SemaphoreType.DMA(())],
        compiler_params=pltpu.CompilerParams(vmem_limit_bytes=UPDATE_VMEM),
        cost_estimate=pl.CostEstimate(flops=10 * grad.shape[0] * D * D, bytes_accessed=8 << 20, transcendentals=0),
        name="update",
    )(grad, bases, weight, first, second)


def shards(
    inputs,
    cotangent,
    doc_lengths,
    qkv_weight,
    out_weight,
    up_weight,
    down_weight,
    vectors,
    bases,
    qkv_first,
    out_first,
    up_first,
    down_first,
    vector_first,
    qkv_second,
    out_second,
    up_second,
    down_second,
    vector_second,
):
    seq_count, batch_count = lax.axis_size("seq"), lax.axis_size("batch")
    seq_index, batch_index = lax.axis_index("seq"), lax.axis_index("batch")
    row_count, shard_len = inputs.shape[:2]
    tokens = row_count * shard_len
    y_bit, *z_bits = bit_names("seq", seq_count)
    core_bit, *x_bits = bit_names("batch", batch_count)
    near = [core_bit] + x_bits[::-1] + [y_bit] + z_bits[::-1]
    depth = seq_count // 2
    plane = 2 ** (len(x_bits) + 1)
    group_depths = (range(depth // 2, depth), range(depth // 2))
    group_pieces = [[k * depth + z for k in range(plane) for z in depths] for depths in group_depths]
    x_low = inputs.reshape(tokens, D)
    dy = cotangent.reshape(tokens, D)

    first_pos = seq_index * shard_len
    query_pos = first_pos + jnp.arange(shard_len, dtype=jnp.int32)
    docs = doc_lengths.shape[1]
    earlier = jnp.arange(docs)[:, None] < jnp.arange(docs)[None, :]
    doc_starts = jnp.sum(jnp.where(earlier[None], doc_lengths[:, :, None], 0), axis=1)
    start = jnp.max(
        jnp.where(doc_starts[:, None, :] <= query_pos[None, :, None], doc_starts[:, None, :], 0), axis=-1
    )
    offsets = (query_pos[None, :] - start).reshape(tokens)
    inverse = 1.0 / rope_base ** (jnp.arange(0, ROT, 2).astype(f32) / ROT)
    angles = offsets.astype(f32)[None, :] * inverse[:, None]
    cosine, sine = jnp.cos(angles), jnp.sin(angles)
    start_here = (start - first_pos).astype(jnp.int32)[:, None, :]
    number = jnp.arange(seq_count * batch_count, dtype=jnp.int32)

    def bits_of(value, place_of):
        total = 0
        for k, (axis_name, step) in enumerate(near[::-1]):
            total = total + place_of(value, k, axis_name, step)
        return total

    differs = {"seq": (number // batch_count) ^ seq_index, "batch": (number % batch_count) ^ batch_index}
    entry = bits_of(number, lambda v, k, name, step: (differs[name] // step) % 2 << k).astype(jnp.int32)
    xor_of = lambda name: sum((number >> k) % 2 * step for k, (axis_name, step) in enumerate(near[::-1]) if axis_name == name)
    device = ((xor_of("seq") ^ seq_index) * batch_count + (xor_of("batch") ^ batch_index)).astype(jnp.int32)

    qkv_rows, out_rows, up_rows, vec_len = qkv_weight.shape[0], out_weight.shape[0], up_weight.shape[0], vectors.shape[0]
    vec_rows = -(-vec_len // D)
    used = qkv_rows + vec_rows
    head_rows = -(-used // (8 * batch_count)) * 8 * batch_count
    vec_pad = vec_rows * D - vec_len

    def own_part(rows):
        size = rows.shape[0] // batch_count
        return lax.dynamic_slice_in_dim(rows, batch_index * size, size, axis=0)

    head_shard = jnp.concatenate(
        [qkv_weight, jnp.pad(vectors, (0, vec_pad)).reshape(vec_rows, D), jnp.zeros((head_rows - used, D), f32)], axis=0
    ).astype(low)
    head_part_rows = head_rows // batch_count
    unit_rows = up_rows // batch_count
    out_own = out_rows // batch_count
    part = jnp.concatenate(
        [
            own_part(up_weight.astype(low)),
            own_part(head_shard),
            own_part(down_weight.T.astype(low)),
            own_part(out_weight.astype(low)),
            jnp.zeros((head_part_rows - out_own, D), low),
        ],
        axis=0,
    )
    parts, cosine, sine, start_here, entry, device = lax.optimization_barrier(
        (jnp.stack(gather_z(part)), cosine, sine, start_here, entry, device)
    )
    half = part.shape[0] // 2
    up_near, down_near = parts[:, :half], parts[:, half:]
    up_near = gather_bit(up_near, y_bit, 0)
    for bit in x_bits:
        down_near = gather_bit(down_near, bit, 0)
    for bit in x_bits:
        up_near = gather_bit(up_near, bit, 0)
    down_near = gather_bit(down_near, y_bit, len(x_bits))
    near_all = jnp.stack([up_near, down_near]).reshape(2, plane, depth, half, D)
    far_all = swap(near_all, core_bit)
    aligned = unit_rows % 16 == 0 and head_part_rows % 16 == 0
    trim = lambda value, begin, end: value if aligned else value[..., begin:end, :]
    near_weight, far_weight = trim(near_all, 0, unit_rows), trim(far_all, 0, unit_rows)

    inside = out_own % 8 == 0
    normed_one, normed_two, q_t, kv_own, qkv_full, gains, out_bias, *bias_rows = head(
        device, x_low, trim(near_all, unit_rows, half), trim(far_all, unit_rows, half), unit_rows if aligned else 0,
        head_part_rows, out_own if inside else 0, cosine, sine, group_pieces, vec_len, seq_count,
    )
    if inside:
        out_full = bias_rows.pop()
    else:
        out_full = jnp.concatenate([v[1, ..., unit_rows : unit_rows + out_own, :] for v in (near_all, far_all)], axis=0)
        chosen = (entry[:, None] == number[None, :]).astype(low)
        out_full = jnp.dot(chosen, out_full.reshape(-1, out_own * D), preferred_element_type=f32).astype(low).reshape(D, D)
    bias_rows = [bias_rows[: len(group_pieces)], bias_rows[len(group_pieces) :]]
    reach = seq_count // 2

    def shifted(value, step, back=False):
        pairs = [(j, j + step) for j in range(seq_count - step)]
        return lax.ppermute(value, "seq", [(b, a) for a, b in pairs] if back else pairs)

    kv = kv_own[None]
    farthest = shifted(kv_own, reach)
    pair = shifted(kv, 1)
    kv = jnp.concatenate([kv, pair], axis=0)
    while kv.shape[0] < reach:
        kv = jnp.concatenate([kv, shifted(kv, kv.shape[0])], axis=0)
    kv = jnp.concatenate([kv, farthest[None]], axis=0)

    last = (((1,), (1,)), ((), ()))
    bias_grads, halves_of = [[], []], []

    def feed_group(g, sums, *earlier):
        depths = group_depths[g]
        *sums, far_grad, near_grad, bias_far, bias_here = feed(
            flow(normed_two, *earlier), dy, far_weight, near_weight, bias_rows[1][g], bias_rows[0][g], depths, unit_rows, sums
        )
        bias_grads[0].append(bias_here)
        bias_grads[1].append(bias_far)
        grad_sum = near_grad + swap(far_grad, core_bit).astype(f32)
        half_shape = (2,) * len(x_bits) + (2, len(depths), unit_rows, D)
        halves_of.append(
            [
                split_bit(grad_sum[0].reshape(half_shape), x_bits[-1], 0),
                split_bit(grad_sum[1].reshape(half_shape), y_bit, len(x_bits)),
            ]
        )
        return sums

    def feed_first(halves):
        (up_kept, up_sent), (down_kept, down_sent) = halves
        up_sum = up_kept + swap(up_sent, x_bits[-1]).astype(f32)
        for bit in x_bits[-2::-1]:
            up_sum = sum_bit(up_sum, bit, 0)
        return up_sum, down_kept + swap(down_sent, y_bit).astype(f32)

    def feed_halves(up_sum, down_sum):
        return split_bit(up_sum, y_bit, 0), split_bit(down_sum, x_bits[-1], 0)

    def feed_second(halves, after):
        (up_kept, up_sent), (down_kept, down_sent) = halves
        up_sum = up_kept + flow(swap(up_sent, y_bit), *after).astype(f32)
        down_sum = down_kept + flow(swap(down_sent, x_bits[-1]), *after).astype(f32)
        for bit in x_bits[-2::-1]:
            down_sum = sum_bit(down_sum, bit, 0, after=after)
        return jnp.concatenate([up_sum, down_sum], axis=1)

    sums = feed_group(0, None, pair, farthest)
    first_sent = (halves_of[0][0][1], halves_of[0][1][1])

    do_t = lax.dot_general(out_full, dy, (((0,), (1,)), ((), ())), preferred_element_type=f32).astype(low)
    context, dq_t, dkv_own, dkv_sent = attention(flow(q_t, *first_sent), do_t, start_here, cosine, sine, kv)
    first_halves = feed_halves(*feed_first(halves_of[0]))
    mlp_out, d_normed_two = feed_group(1, sums, dq_t, first_halves[0][1], first_halves[1][1])

    dkv_far = flow(shifted(dkv_sent[reach - 1], reach, True), d_normed_two)
    dkv = jnp.concatenate([dkv_own[None], dkv_sent[: reach - 1].astype(f32)], axis=0)
    while dkv.shape[0] > 1:
        both = dkv.shape[0] // 2
        dkv = dkv[:both] + flow(shifted(dkv[both:].astype(low), both, True), d_normed_two).astype(f32)
    dkv = dkv[0] + dkv_far.astype(f32)

    last_step = feed_second(first_halves, (d_normed_two,))
    dkv, last_step = lax.optimization_barrier((dkv, last_step))
    last_steps = [last_step]

    shape = (depth, 2) + (2,) * len(x_bits) + (2, -1, D)
    qkv_own = -(-qkv_rows // (8 * batch_count)) * 8
    qkv_part, d_normed_one, proj_sum = back(
        dq_t, dkv, cosine, sine, qkv_full, normed_one, seq_count, qkv_own * batch_count
    )
    out_part = lax.dot_general(dy, context, (((0,), (0,)), ((), ())), preferred_element_type=f32)
    both = jnp.concatenate([qkv_part.reshape(shape), out_part.reshape(shape)], axis=len(shape) - 2)
    both = sum_bit(both, core_bit, len(shape) - 3, True)

    def spread(part):
        value = part.astype(low)
        for k, bit in enumerate(x_bits):
            value = gather_bit(value, bit, 0, True)
        value = gather_bit(value, core_bit, len(x_bits), True)
        return value.reshape(batch_count, -1, D)

    qkv_sum, out_sum = both[..., :qkv_own, :], both[..., qkv_own:, :]
    for bit in x_bits[::-1]:
        qkv_sum = sum_bit(qkv_sum, bit, 2, True)
    out_sum = sum_bit(out_sum, y_bit, 1, True)
    sent = (halves_of[1][0][1], halves_of[1][1][1])
    input_grad, vector_part = tail(
        entry, x_low, dy, d_normed_one, flow(d_normed_two, *sent), gains, proj_sum, bias_grads, group_pieces,
        seq_count * vec_len,
    )
    vector_parts = lax.all_gather(vector_part[0], ("seq", "batch"))
    qkv_sum = sum_bit(qkv_sum, y_bit, 1, True, after=sent)
    for bit in x_bits[::-1]:
        out_sum = sum_bit(out_sum, bit, 1, True, after=sent)
    both = sum_z(jnp.concatenate([qkv_sum, out_sum], axis=1), True)
    second_halves = feed_halves(*feed_first(halves_of[1]))
    last_steps.append(feed_second(second_halves, (both, vector_part)))
    feed_sum = 0.0
    for depths, last_step in zip(group_depths, last_steps):
        for k, z in enumerate(depths):
            feed_sum = feed_sum + (last_step[k] if z == 0 else swap_z(last_step[k].astype(low), z).astype(f32))
    others = spread(both)
    qkv_low = others[:, :qkv_own].reshape(-1, D)[:qkv_rows]
    out_low = others[:, qkv_own:].reshape(-1, D)
    out_grad, *out_states = update(out_low, bases, 1, out_weight, out_first, out_second)
    qkv_grad, *qkv_states = update(qkv_low, bases, 0, qkv_weight, qkv_first, qkv_second)
    attn_out = lax.dot_general(context, out_full, last, preferred_element_type=f32)
    outputs = (x_low.astype(f32) + attn_out + flow(mlp_out, both) + out_bias).astype(low)
    feed_grads = spread(flow(feed_sum, out_grad, qkv_grad, outputs))
    up_low = feed_grads[:, :unit_rows].reshape(-1, D)
    down_low = feed_grads[:, unit_rows:].reshape(-1, D)
    up_grad, *up_states = update(up_low, bases, 2, up_weight, up_first, up_second)
    down_grad, *down_states = update(down_low, bases, 3, down_weight, down_first, down_second, True)
    vector_grad = jnp.sum(lax.dynamic_slice_in_dim(vector_parts, seq_index * vec_len, vec_len, axis=1), axis=0)
    vector_new, *vector_states = adam_step(vectors, vector_grad, vector_first, vector_second)
    states = (qkv_states, out_states, up_states, down_states, (*vector_states, vector_new))
    return (
        outputs.reshape(inputs.shape),
        input_grad.reshape(inputs.shape),
        qkv_grad,
        out_grad,
        up_grad,
        down_grad,
        vector_grad,
        *(state[0] for state in states),
        *(state[1] for state in states),
        *(state[2] for state in states),
    )


def solution(mesh):
    tokens = P("batch", "seq", None)
    rows, columns, flat = P("seq", None), P(None, "seq"), P("seq")
    params = (rows, rows, rows, columns, flat)
    return jax.shard_map(
        shards,
        mesh=mesh,
        in_specs=(tokens, tokens, P("batch", None)) + params + (P(),) + params + params,
        out_specs=(tokens, tokens) + params * 4,
        check_vma=False,
    )
```

```python
import functools

import jax
import jax.numpy as jnp
from jax import lax
from jax.experimental import pallas as pl
from jax.experimental.pallas import tpu as pltpu
from jax.sharding import PartitionSpec as P

D = 768
HEADS = 12
HEAD = 64
ROT = 16
FF = 3072
STEP = 10

layer_eps = 1e-05
adam_eps = 1e-08
beta_first = 0.95
beta_second = 0.95
matrix_rate = 0.08
vector_rate = 0.3
rope_base = 10000.0
masked_score = -1e30
low = jnp.bfloat16
f32 = jnp.float32
VMEM_LIMIT = 56 * 1024 * 1024
GROUPS = 2
FEED_VMEM = 56 * 1024 * 1024
UPDATE_VMEM = 28 * 1024 * 1024


def swap(value, bit):
    axis, step = bit
    return lax.ppermute(value, axis, [(i, i ^ step) for i in range(lax.axis_size(axis))])


def mine(bit):
    axis, step = bit
    return lax.rem(lax.axis_index(axis) // step, 2)


def hold(*values):
    return lax.optimization_barrier(values)


def swap_z(value, step):
    size = lax.axis_size("seq")
    return lax.ppermute(value, "seq", [(i, i ^ (2 * step)) for i in range(size)])


def gather_z(piece):
    return [piece] + [swap_z(piece, k) for k in range(1, lax.axis_size("seq") // 2)]


def gather_bit(value, bit, axis, absolute=False):
    got = swap(value, bit)
    if absolute:
        upper = mine(bit) == 1
        return jnp.stack([jnp.where(upper, got, value), jnp.where(upper, value, got)], axis=axis)
    return jnp.stack([value, got], axis=axis)


def split_bit(value, bit, axis):
    return lax.index_in_dim(value, 0, axis, keepdims=False), lax.index_in_dim(value, 1, axis, keepdims=False).astype(low)


def bit_names(axis, size):
    return [(axis, 1 << k) for k in range(size.bit_length() - 1)]


def moments(rotated, first, second):
    new_first = beta_first * first + (1.0 - beta_first) * rotated
    new_second = beta_second * second + (1.0 - beta_second) * rotated * rotated
    first_scale, second_scale = 1.0 / (1.0 - beta_first**STEP), 1.0 / (1.0 - beta_second**STEP)
    ratio = new_first * first_scale / (jnp.sqrt(new_second * second_scale) + adam_eps)
    return ratio, new_first, new_second


def adam_step(weight, grad, first, second):
    ratio, new_first, new_second = moments(grad, first, second)
    return (weight - vector_rate * ratio, new_first, new_second)


def attention_kernel(blocks, width, q_ref, do_ref, start_ref, cos_ref, sin_ref, kv_ref, context_ref, dq_ref, dkv_own_ref, dkv_ref):
    length = q_ref.shape[1]
    keys = blocks * length
    key_t = jnp.concatenate([kv_ref[k, :HEAD, :] for k in reversed(range(blocks))], axis=1)
    value_t = jnp.concatenate([kv_ref[k, HEAD:, :] for k in reversed(range(blocks))], axis=1)
    key = key_t.astype(f32).T.astype(low)
    value = value_t.astype(f32).T.astype(low)
    key_pos = lax.broadcasted_iota(jnp.int32, (keys, length), 0) - (blocks - 1) * length
    query_pos = lax.broadcasted_iota(jnp.int32, (keys, length), 1)
    allowed = (key_pos >= start_ref[0]) & (key_pos <= query_pos)
    bias = jnp.where(allowed, 0.0, masked_score)
    cosine, sine = cos_ref[...], sin_ref[...]
    d_key = jnp.zeros((keys, HEAD), f32)
    d_value = jnp.zeros((keys, HEAD), f32)
    last = (((1,), (1,)), ((), ()))
    for first in range(0, HEADS, width):
        heads = range(first, first + width)
        query = jnp.concatenate([q_ref[h * HEAD : (h + 1) * HEAD, :] for h in heads], axis=1)
        d_out = jnp.concatenate([do_ref[h * HEAD : (h + 1) * HEAD, :] for h in heads], axis=1)
        scores = jnp.dot(key, query, preferred_element_type=f32)
        scores = scores + jnp.concatenate([bias] * width, axis=1)
        weights = jnp.exp(scores - jnp.max(scores, axis=0, keepdims=True))
        probs = weights * (1.0 / jnp.sum(weights, axis=0, keepdims=True))
        probs_low = probs.astype(low)
        context_t = jnp.dot(value_t, probs_low, preferred_element_type=f32)
        d_probs = jnp.dot(value, d_out, preferred_element_type=f32)
        inner = jnp.sum(probs * d_probs, axis=0, keepdims=True)
        d_scores = (probs * (d_probs - inner)).astype(low)
        d_query = jnp.dot(key_t, d_scores, preferred_element_type=f32) * HEAD ** (-0.5)
        d_value = d_value + lax.dot_general(probs_low, d_out, last, preferred_element_type=f32)
        d_key = d_key + lax.dot_general(d_scores, query, last, preferred_element_type=f32)
        for k, h in enumerate(heads):
            lanes = slice(k * length, (k + 1) * length)
            part = d_query[:, lanes]
            a, b = part[: ROT // 2], part[ROT // 2 : ROT]
            turned = jnp.concatenate([a * cosine + b * sine, b * cosine - a * sine, part[ROT:]], axis=0)
            dq_ref[h * HEAD : (h + 1) * HEAD, :] = turned.astype(low)
        for k in range(0, width, 2):
            h = first + k
            two = jnp.concatenate(
                [context_t[:, k * length : (k + 1) * length], context_t[:, (k + 1) * length : (k + 2) * length]], axis=0
            )
            context_ref[:, h * HEAD : (h + 2) * HEAD] = two.T.astype(low)
    d_kv = jnp.concatenate([d_key, d_value], axis=1).T
    for k in range(blocks):
        part = d_kv[:, (blocks - 1 - k) * length : (blocks - k) * length]
        if k == 0:
            dkv_own_ref[...] = part
        else:
            dkv_ref[k - 1] = part.astype(low)


def attention(q_t, do_t, start, cosine, sine, kv):
    rows, _, length = start.shape
    blocks = kv.shape[0]
    tokens = q_t.shape[1]
    by_row = lambda height: pl.BlockSpec((height, length), lambda r: (0, r))
    return pl.pallas_call(
        functools.partial(attention_kernel, blocks, HEADS),
        grid=(rows,),
        in_specs=[by_row(D), by_row(D), pl.BlockSpec((1, 1, length), lambda r: (r, 0, 0)), by_row(ROT // 2), by_row(ROT // 2)]
        + [pl.BlockSpec((blocks, 2 * HEAD, length), lambda r: (0, 0, r))],
        out_specs=[
            pl.BlockSpec((length, D), lambda r: (r, 0)),
            by_row(D),
            by_row(2 * HEAD),
            pl.BlockSpec((blocks - 1, 2 * HEAD, length), lambda r: (0, 0, r)),
        ],
        out_shape=[
            jax.ShapeDtypeStruct((tokens, D), low),
            jax.ShapeDtypeStruct((D, tokens), low),
            jax.ShapeDtypeStruct((2 * HEAD, tokens), f32),
            jax.ShapeDtypeStruct((blocks - 1, 2 * HEAD, tokens), low),
        ],
        compiler_params=pltpu.CompilerParams(vmem_limit_bytes=VMEM_LIMIT),
        cost_estimate=pl.CostEstimate(
            flops=4 * 7 * tokens * HEADS * blocks * length * HEAD * 2, bytes_accessed=8 << 20, transcendentals=0
        ),
        name="attention",
    )(q_t, do_t, start, cosine, sine, kv)


def gathered_parts(plane, refs, offset, rows):
    half = plane // 2
    out = []
    for end, ref in enumerate(refs):
        for j in range(half):
            out.append((0, end * half + j, ref.at[0, j, :, pl.ds(offset, rows)]))
            out.append((1, 2 * j + end, ref.at[1, j, :, pl.ds(offset, rows)]))
    return out


def feed_kernel(n_ref, dy_ref, first_far, last_far, first_near, last_near, bias_far_ref, bias_near_ref, *refs):
    far_refs, near_refs = (first_far, last_far), (first_near, last_near)
    before = refs[: len(refs) - 11]
    out_ref, dn_ref, far_grad_ref, near_grad_ref, bias_far_grad_ref, bias_near_grad_ref = refs[-11:-5]
    weights, far_sum, near_sum, held, sems = refs[-5:]
    plane = weights.shape[2]
    last = (((1,), (1,)), ((), ()))
    first = (((0,), (0,)), ((), ()))
    loads = [
        [
            pltpu.make_async_copy(source, weights.at[side, kind, k], sems.at[side, 2 * k + kind])
            for kind, k, source in gathered_parts(plane, refs_of, 0, weights.shape[4])
        ]
        for side, refs_of in enumerate((far_refs, near_refs))
    ]
    fetches = [pltpu.make_async_copy(ref, held.at[k], sems.at[2, k]) for k, ref in enumerate(before)]
    for copy in loads[0] + loads[1] + fetches:
        copy.start()
    normed, d_out = n_ref[...], dy_ref[...]
    units = far_sum.shape[1]
    out, d_normed = 0.0, 0.0
    stores = []
    for side, (bias_ref, bias_grad_ref, buffer, grad_ref) in enumerate(
        (
            (bias_far_ref, bias_far_grad_ref, far_sum, far_grad_ref),
            (bias_near_ref, bias_near_grad_ref, near_sum, near_grad_ref),
        )
    ):
        for copy in loads[side]:
            copy.wait()
        up, down = weights[side, 0].reshape(units, D), weights[side, 1].reshape(units, D)
        hidden = lax.dot_general(normed, up, last, preferred_element_type=f32) + bias_ref[...]
        share = 0.5 * (1.0 + lax.erf(hidden * (0.5**0.5)))
        slope = share + hidden * (jnp.exp(-0.5 * hidden * hidden) * (0.5 / 3.141592653589793) ** 0.5)
        active = (hidden * share).astype(low)
        d_active = lax.dot_general(d_out, down, last, preferred_element_type=f32)
        d_hidden = (d_active * slope).astype(low)
        for k, part in enumerate(
            (
                lax.dot_general(d_hidden, normed, first, preferred_element_type=f32),
                lax.dot_general(active, d_out, first, preferred_element_type=f32),
            )
        ):
            buffer[k] = part.astype(buffer.dtype)
            copy = pltpu.make_async_copy(buffer.at[k], grad_ref.at[k], sems.at[3, 2 * side + k])
            copy.start()
            stores.append(copy)
        bias_grad_ref[...] = jnp.sum(d_hidden.astype(f32), axis=0, keepdims=True)
        out = out + jnp.dot(active, down, preferred_element_type=f32)
        d_normed = d_normed + jnp.dot(d_hidden, up, preferred_element_type=f32)
    for copy in fetches:
        copy.wait()
    out_ref[...] = held[0] + out if before else out
    dn_ref[...] = held[1] + d_normed if before else d_normed
    for copy in stores:
        copy.wait()


def feed(normed, d_out, far, near, bias_far, bias_near, rows, before):
    tokens = normed.shape[0]
    plane, depth = 2 * far[0].shape[1], far[0].shape[2]
    units = plane * depth * rows
    before = before or []
    vmem, hbm = pl.BlockSpec(memory_space=pltpu.VMEM), pl.BlockSpec(memory_space=pl.ANY)
    return pl.pallas_call(
        feed_kernel,
        in_specs=[vmem, vmem, hbm, hbm, hbm, hbm, vmem, vmem] + [hbm] * len(before),
        out_specs=[vmem, vmem, hbm, hbm, vmem, vmem],
        out_shape=[
            jax.ShapeDtypeStruct((tokens, D), f32),
            jax.ShapeDtypeStruct((tokens, D), f32),
            jax.ShapeDtypeStruct((2, units, D), low),
            jax.ShapeDtypeStruct((2, units, D), f32),
            jax.ShapeDtypeStruct((1, units), f32),
            jax.ShapeDtypeStruct((1, units), f32),
        ],
        scratch_shapes=[
            pltpu.VMEM((2, 2, plane, depth, rows, D), low),
            pltpu.VMEM((2, units, D), low),
            pltpu.VMEM((2, units, D), f32),
            pltpu.VMEM((2, tokens, D), f32),
            pltpu.SemaphoreType.DMA((4, 2 * plane)),
        ],
        compiler_params=pltpu.CompilerParams(vmem_limit_bytes=FEED_VMEM),
        cost_estimate=pl.CostEstimate(flops=4 * 24 * tokens * units * D, bytes_accessed=8 << 20, transcendentals=0),
        name="feed",
    )(normed, d_out, *far, *near, bias_far, bias_near, *before)


def head_kernel(
    vec_len, offset, out_rows, device_ref, x_ref, first_near, last_near, first_far, last_far, cos_ref, sin_ref, n_one_ref,
    n_two_ref, q_ref, kv_ref, w_ref, gain_ref, bias_ref, *refs
):
    *bias_refs, out_ref, flat, units, held, pieces_of, outs_of, sems = refs if out_rows else (*refs[:-6], None, *refs[-6:])
    _, _, plane, depth, size, _ = held.shape
    copies = [
        pltpu.make_async_copy(source, held.at[side, kind, k], sems.at[side, 2 * k + kind])
        for side, refs_of in enumerate(((first_near, last_near), (first_far, last_far)))
        for kind, k, source in gathered_parts(plane, refs_of, offset, size)
    ]
    for copy in copies:
        copy.start()
    x = x_ref[...].astype(f32)
    center = x - jnp.mean(x, axis=-1, keepdims=True)
    xhat = center * lax.rsqrt(jnp.mean(center * center, axis=-1, keepdims=True) + layer_eps)
    for copy in copies:
        copy.wait()
    for side in range(2):
        for k in range(plane):
            for z in range(depth):
                number = device_ref[(side * plane + k) * depth + z]
                pieces_of[number] = held[side, 0, k, z].astype(f32)
                if out_rows:
                    outs_of[number] = held[side, 1, k, z][:out_rows].astype(f32)
    if out_rows:
        out_ref[...] = outs_of[...].reshape(out_ref.shape).astype(low)
    shards_of = (flat.shape[1]) // vec_len
    rows = (D + 2 * HEAD) // shards_of
    whole = pieces_of[...].reshape(shards_of, -1, D)
    for s in range(shards_of):
        left, row = vec_len, rows
        while left > 0:
            size = min(left, D)
            begin = s * vec_len + (row - rows) * D
            flat[:, begin : begin + size] = whole[s, row : row + 1, :size]
            left -= size
            row += 1
    vector = lambda begin, size: flat[:, begin : begin + size]
    gain_one, shift_one, gain_two, shift_two = [vector(k * D, D) for k in range(4)]
    gain_ref[0:1] = gain_one
    gain_ref[1:2] = gain_two
    qkv_bias = vector(4 * D, D + 2 * HEAD)
    start = 4 * D + D + 2 * HEAD
    bias_ref[...] = vector(start, D) + vector(start + D + FF, D)
    count, size_of = units.shape
    for k in range(count):
        units[k : k + 1, :] = vector(start + D + k * size_of, size_of)
    groups = len(bias_refs) // 2
    for k, ref in enumerate(bias_refs):
        side, g = k // groups, k % groups
        width = size_of // groups
        for i in range(count // 2):
            row = units[pl.ds(device_ref[side * (count // 2) + i], 1), :]
            ref[:, i * width : (i + 1) * width] = row[:, g * width : (g + 1) * width]
    n_one = (xhat * gain_one + shift_one).astype(low)
    n_one_ref[...] = n_one
    n_two_ref[...] = (xhat * gain_two + shift_two).astype(low)
    weight = whole[:, :rows].reshape(shards_of * rows, D).astype(low)
    w_ref[...] = weight
    column = jnp.broadcast_to(qkv_bias, (8, qkv_bias.shape[1])).T[:, 0:1]
    projected = lax.dot_general(weight, n_one, (((1,), (1,)), ((), ())), preferred_element_type=f32) + column
    cosine, sine = cos_ref[...], sin_ref[...]
    half = ROT // 2

    def turned(first):
        a, b = projected[first : first + half], projected[first + half : first + ROT]
        rest = projected[first + ROT : first + HEAD]
        return jnp.concatenate([a * cosine - b * sine, b * cosine + a * sine, rest], axis=0).astype(low)

    for h in range(HEADS):
        q_ref[h * HEAD : (h + 1) * HEAD, :] = turned(h * HEAD) * jnp.asarray(HEAD ** (-0.5), low)
    kv_ref[:HEAD, :] = turned(D)
    kv_ref[HEAD:, :] = projected[D + HEAD :].astype(low)


def head(device, x, near, far, offset, size, out_rows, cosine, sine, groups, vec_len, shards_of):
    tokens = x.shape[0]
    count = device.shape[0]
    plane, depth = 2 * near[0].shape[1], near[0].shape[2]
    vmem, hbm = pl.BlockSpec(memory_space=pltpu.VMEM), pl.BlockSpec(memory_space=pl.ANY)
    return pl.pallas_call(
        functools.partial(head_kernel, vec_len, offset, out_rows),
        in_specs=[pl.BlockSpec(memory_space=pltpu.SMEM), vmem, hbm, hbm, hbm, hbm, vmem, vmem],
        out_shape=[
            jax.ShapeDtypeStruct((tokens, D), low),
            jax.ShapeDtypeStruct((tokens, D), low),
            jax.ShapeDtypeStruct((D, tokens), low),
            jax.ShapeDtypeStruct((2 * HEAD, tokens), low),
            jax.ShapeDtypeStruct((D + 2 * HEAD, D), low),
            jax.ShapeDtypeStruct((2, D), f32),
            jax.ShapeDtypeStruct((1, D), f32),
        ]
        + [jax.ShapeDtypeStruct((1, FF // 2 // groups), f32)] * (2 * groups)
        + [jax.ShapeDtypeStruct((D, D), low)] * (out_rows > 0),
        scratch_shapes=[
            pltpu.VMEM((1, shards_of * vec_len), f32),
            pltpu.VMEM((count, FF // count), f32),
            pltpu.VMEM((2, 2, plane, depth, size, D), low),
            pltpu.VMEM((count, size, D), f32),
            pltpu.VMEM((count, max(out_rows, 8), D), f32),
            pltpu.SemaphoreType.DMA((2, 2 * plane)),
        ],
        compiler_params=pltpu.CompilerParams(vmem_limit_bytes=FEED_VMEM),
        cost_estimate=pl.CostEstimate(flops=4 * 2 * tokens * 896 * D, bytes_accessed=8 << 20, transcendentals=0),
        name="head",
    )(device, x, *near, *far, cosine, sine)


def tail_kernel(
    shards_of, entry_ref, x_ref, dy_ref, dq_ref, dkv_ref, cos_ref, sin_ref, w_ref, n_ref, context_ref, d_two_ref, gain_ref, *refs
):
    bias_refs, (in_grad_ref, qkv_ref, out_ref, flat, units) = refs[:-5], refs[-5:]
    d_kv = dkv_ref[...]
    a, b = d_kv[: ROT // 2], d_kv[ROT // 2 : ROT]
    cosine, sine = cos_ref[...], sin_ref[...]
    d_kv = jnp.concatenate([a * cosine + b * sine, b * cosine - a * sine, d_kv[ROT:]], axis=0).astype(low)
    d_proj = jnp.concatenate([dq_ref[...], d_kv], axis=0)
    first = (((0,), (0,)), ((), ()))
    qkv_grad = jnp.dot(d_proj, n_ref[...], preferred_element_type=f32)
    out_grad = lax.dot_general(dy_ref[...], context_ref[...], first, preferred_element_type=f32)
    d_one = lax.dot_general(d_proj, w_ref[...], first, preferred_element_type=f32)
    d_two = d_two_ref[...]
    x = x_ref[...].astype(f32)
    dy = dy_ref[...].astype(f32)
    center = x - jnp.mean(x, axis=-1, keepdims=True)
    inv_sigma = lax.rsqrt(jnp.mean(center * center, axis=-1, keepdims=True) + layer_eps)
    xhat = center * inv_sigma
    d_hat = d_one * gain_ref[0:1] + d_two * gain_ref[1:2]
    d_in = (
        d_hat - jnp.mean(d_hat, axis=-1, keepdims=True) - xhat * jnp.mean(d_hat * xhat, axis=-1, keepdims=True)
    ) * inv_sigma
    in_grad_ref[...] = (dy + d_in).astype(low)
    columns = lambda v: jnp.sum(v, axis=0, keepdims=True)
    dy_column = columns(dy)
    ones = jnp.ones((8, d_proj.shape[1]), low)
    proj_sum = lax.dot_general(ones, d_proj, (((1,), (1,)), ((), ())), preferred_element_type=f32)[0:1]
    pieces = [columns(d_one * xhat), columns(d_one), columns(d_two * xhat), columns(d_two)]
    pieces += [proj_sum, dy_column, None, dy_column]
    count, size = units.shape
    groups = len(bias_refs) // 2
    width = size // groups
    for k, ref in enumerate(bias_refs):
        side, g = k // groups, k % groups
        for i in range(count // 2):
            place = side * (count // 2) + i
            units[place : place + 1, g * width : (g + 1) * width] = ref[:, i * width : (i + 1) * width]
    offset = 0
    for piece in pieces:
        if piece is None:
            for k in range(count):
                flat[:, offset : offset + size] = units[pl.ds(entry_ref[k], 1), :]
                offset += size
        else:
            flat[:, offset : offset + piece.shape[1]] = piece
            offset += piece.shape[1]
    qkv_rows, vec_len = qkv_grad.shape[0] // shards_of, flat.shape[1] // shards_of
    to_shard = count // shards_of
    share = lambda k, total: [k // to_shard * total + min(-(-total // to_shard) * j, total) for j in (k % to_shard, k % to_shard + 1)]
    out_own = D // count
    vec_row = qkv_ref.shape[1] - 4
    for k in range(count):
        to = entry_ref[k]
        begin, end = share(k, qkv_rows)
        qkv_ref[to] = jnp.zeros(qkv_ref.shape[1:], f32)
        if end > begin:
            qkv_ref[to, : end - begin, :] = qkv_grad[begin:end]
        begin, end = share(k, vec_len)
        if end > begin:
            qkv_ref[to, vec_row : vec_row + 1, : end - begin] = flat[:, begin:end]
        out_ref[to] = jnp.zeros(out_ref.shape[1:], f32)
        out_ref[to, :out_own, :] = out_grad[k * out_own : (k + 1) * out_own]


def tail(entry, x, dy, dq_t, dkv, cosine, sine, weight, normed, context, d_two, gains, bias_grads, rows, shards_of, vec_len):
    tokens = x.shape[0]
    count = entry.shape[0]
    operands = (entry, x, dy, dq_t, dkv, cosine, sine, weight, normed, context, d_two, gains, *sum(bias_grads, []))
    return pl.pallas_call(
        functools.partial(tail_kernel, shards_of),
        in_specs=[pl.BlockSpec(memory_space=pltpu.SMEM)] + [pl.BlockSpec(memory_space=pltpu.VMEM)] * (len(operands) - 1),
        out_shape=[
            jax.ShapeDtypeStruct((tokens, D), low),
            jax.ShapeDtypeStruct((count, rows, D), f32),
            jax.ShapeDtypeStruct((count, rows, D), f32),
        ],
        scratch_shapes=[pltpu.VMEM((1, shards_of * vec_len), f32), pltpu.VMEM((count, FF // count), f32)],
        compiler_params=pltpu.CompilerParams(vmem_limit_bytes=VMEM_LIMIT),
        cost_estimate=pl.CostEstimate(flops=4 * 6 * tokens * 896 * D, bytes_accessed=8 << 20, transcendentals=0),
        name="tail",
    )(*operands)


def split_low(value):
    high = value.astype(low)
    return high, (value - high.astype(f32)).astype(low)


def update_step(across, grad, high, rest, w_ref, first_ref, second_ref, grad_ref, first_new_ref, second_new_ref, w_new_ref):
    rotated = jnp.dot(grad, high, preferred_element_type=f32) + jnp.dot(grad, rest, preferred_element_type=f32)
    grad = grad.astype(f32)
    if across:
        rotated, grad = rotated.T, grad.T
    grad_ref[...] = grad
    ratio, first_new, second_new = moments(rotated, first_ref[...], second_ref[...])
    first_new_ref[...] = first_new
    second_new_ref[...] = second_new
    r_high, r_rest = split_low(ratio)
    if across:
        product = lambda r, b: jnp.dot(b, r, preferred_element_type=f32)
    else:
        product = lambda r, b: lax.dot_general(r, b, (((1,), (1,)), ((), ())), preferred_element_type=f32)
    unrotated = product(r_high, high) + (product(r_high, rest) + product(r_rest, high))
    w_new_ref[...] = w_ref[...] - matrix_rate * unrotated


def update_kernel(across, number, grad_ref, bases_ref, *refs):
    *refs, basis, sem = refs
    copy = pltpu.make_async_copy(bases_ref.at[number], basis, sem)
    copy.start()
    copy.wait()
    high, rest = split_low(basis[...])
    update_step(across, grad_ref[...], high, rest, *refs)


def update(grad, bases, number, weight, first, second, across=False):
    vmem = pl.BlockSpec(memory_space=pltpu.VMEM)
    return pl.pallas_call(
        functools.partial(update_kernel, across, number),
        in_specs=[vmem, pl.BlockSpec(memory_space=pl.ANY), vmem, vmem, vmem],
        out_shape=[jax.ShapeDtypeStruct(weight.shape, f32)] * 4,
        scratch_shapes=[pltpu.VMEM((D, D), f32), pltpu.SemaphoreType.DMA(())],
        compiler_params=pltpu.CompilerParams(vmem_limit_bytes=UPDATE_VMEM),
        cost_estimate=pl.CostEstimate(flops=10 * grad.shape[0] * D * D, bytes_accessed=8 << 20, transcendentals=0),
        name="update",
    )(grad, bases, weight, first, second)


def shards(
    inputs,
    cotangent,
    doc_lengths,
    qkv_weight,
    out_weight,
    up_weight,
    down_weight,
    vectors,
    bases,
    qkv_first,
    out_first,
    up_first,
    down_first,
    vector_first,
    qkv_second,
    out_second,
    up_second,
    down_second,
    vector_second,
):
    seq_count, batch_count = lax.axis_size("seq"), lax.axis_size("batch")
    seq_index, batch_index = lax.axis_index("seq"), lax.axis_index("batch")
    row_count, shard_len = inputs.shape[:2]
    tokens = row_count * shard_len
    y_bit, *z_bits = bit_names("seq", seq_count)
    core_bit, *x_bits = bit_names("batch", batch_count)
    near = [core_bit] + x_bits[::-1] + [y_bit] + z_bits[::-1]
    depth = seq_count // 2
    plane = 2 ** (len(x_bits) + 1)
    x_low = inputs.reshape(tokens, D)
    dy = cotangent.reshape(tokens, D)

    first_pos = seq_index * shard_len
    query_pos = first_pos + jnp.arange(shard_len, dtype=jnp.int32)
    docs = doc_lengths.shape[1]
    earlier = jnp.arange(docs)[:, None] < jnp.arange(docs)[None, :]
    doc_starts = jnp.sum(jnp.where(earlier[None], doc_lengths[:, :, None], 0), axis=1)
    start = jnp.max(
        jnp.where(doc_starts[:, None, :] <= query_pos[None, :, None], doc_starts[:, None, :], 0), axis=-1
    )
    offsets = (query_pos[None, :] - start).reshape(tokens)
    inverse = 1.0 / rope_base ** (jnp.arange(0, ROT, 2).astype(f32) / ROT)
    angles = offsets.astype(f32)[None, :] * inverse[:, None]
    cosine, sine = jnp.cos(angles), jnp.sin(angles)
    start_here = (start - first_pos).astype(jnp.int32)[:, None, :]
    number = jnp.arange(seq_count * batch_count, dtype=jnp.int32)

    def bits_of(value, place_of):
        total = 0
        for k, (axis_name, step) in enumerate(near[::-1]):
            total = total + place_of(value, k, axis_name, step)
        return total

    differs = {"seq": (number // batch_count) ^ seq_index, "batch": (number % batch_count) ^ batch_index}
    entry = bits_of(number, lambda v, k, name, step: (differs[name] // step) % 2 << k).astype(jnp.int32)
    xor_of = lambda name: sum((number >> k) % 2 * step for k, (axis_name, step) in enumerate(near[::-1]) if axis_name == name)
    device = ((xor_of("seq") ^ seq_index) * batch_count + (xor_of("batch") ^ batch_index)).astype(jnp.int32)

    qkv_rows, out_rows, up_rows, vec_len = qkv_weight.shape[0], out_weight.shape[0], up_weight.shape[0], vectors.shape[0]
    vec_rows = -(-vec_len // D)
    used = qkv_rows + vec_rows
    head_rows = -(-used // (8 * batch_count)) * 8 * batch_count
    vec_pad = vec_rows * D - vec_len

    def own_part(rows):
        size = rows.shape[0] // batch_count
        return lax.dynamic_slice_in_dim(rows, batch_index * size, size, axis=0)

    head_shard = jnp.concatenate(
        [qkv_weight, jnp.pad(vectors, (0, vec_pad)).reshape(vec_rows, D), jnp.zeros((head_rows - used, D), f32)], axis=0
    ).astype(low)
    head_part_rows = head_rows // batch_count
    unit_rows = up_rows // batch_count // GROUPS
    out_own = out_rows // batch_count
    up_low, down_low = own_part(up_weight.astype(low)), own_part(down_weight.T.astype(low))
    outer = [
        own_part(head_shard),
        jnp.concatenate([own_part(out_weight.astype(low)), jnp.zeros((head_part_rows - out_own, D), low)], axis=0),
    ]
    parts_of = []
    for g in range(GROUPS):
        rows = slice(g * unit_rows, (g + 1) * unit_rows)
        pieces = [up_low[rows], outer[0], down_low[rows], outer[1]] if g == 0 else [up_low[rows], down_low[rows]]
        parts_of.append(jnp.concatenate(pieces, axis=0))

    def gather_first(parts):
        half = parts.shape[1] // 2
        up, down = parts[:, :half], parts[:, half:]
        for bit in x_bits[:-1]:
            down = gather_bit(down, bit, 0)
        return up, down, swap(up, y_bit), swap(down, x_bits[-1])

    def gather_second(up, down, up_got, down_got):
        up, down = jnp.stack([up, up_got]), jnp.stack([down, down_got])
        for bit in x_bits[:-1]:
            up = gather_bit(up, bit, 0)
        shape = (1, plane // 2, depth) + up.shape[-2:]
        return up, down, jnp.concatenate([up.reshape(shape), down.reshape(shape)], axis=0)

    def gather_last(up, down):
        return swap(up, x_bits[-1]), swap(down, y_bit)

    def joined(up, down):
        shape = (1, plane // 2, depth) + up.shape[-2:]
        return jnp.concatenate([up.reshape(shape), down.reshape(shape)], axis=0)

    z_zero = gather_z(parts_of[0])
    *z_zero, cosine, sine, start_here, entry, device, part_one = hold(
        *z_zero, cosine, sine, start_here, entry, device, parts_of[1]
    )
    up, down, up_got, down_got = gather_first(jnp.stack(z_zero))
    z_one = gather_z(part_one)
    up_got, down_got, *z_one = hold(up_got, down_got, *z_one)
    up, down, first_zero = gather_second(up, down, up_got, down_got)
    up_got, down_got = gather_last(up, down)
    first_far_zero = swap(first_zero, core_bit)
    up_got, down_got, first_far_zero = hold(up_got, down_got, first_far_zero)
    last_zero = joined(up_got, down_got)
    last_far_zero = swap(last_zero, core_bit)

    aligned = unit_rows % 16 == 0 and head_part_rows % 16 == 0
    trim = lambda values, begin, end: values if aligned else tuple(v[..., begin:end, :] for v in values)
    near_zero, far_zero = (first_zero, last_zero), (first_far_zero, last_far_zero)
    end = unit_rows + head_part_rows

    inside = out_own % 8 == 0
    normed_one, normed_two, q_t, kv_own, qkv_full, gains, out_bias, *bias_rows = head(
        device, x_low, trim(near_zero, unit_rows, end), trim(far_zero, unit_rows, end), unit_rows if aligned else 0,
        head_part_rows, out_own if inside else 0, cosine, sine, GROUPS, vec_len, seq_count,
    )
    if inside:
        out_full = bias_rows.pop()
    else:
        chosen = (entry[:, None] == number[None, :]).astype(low)
        sides = []
        for pair in (near_zero, far_zero):
            along = [v[1, :, :, unit_rows : unit_rows + out_own] for v in pair]
            sides.append(jnp.stack(along, axis=1).reshape(-1, out_own * D))
        out_full = jnp.dot(chosen, jnp.concatenate(sides, axis=0), preferred_element_type=f32).astype(low).reshape(D, D)
    bias_rows = [bias_rows[:GROUPS], bias_rows[GROUPS:]]
    reach = seq_count // 2

    def shifted(value, step, back=False):
        pairs = [(j, j + step) for j in range(seq_count - step)]
        return lax.ppermute(value, "seq", [(b, a) for a, b in pairs] if back else pairs)

    farthest, pair = shifted(kv_own, reach), shifted(kv_own[None], 1)
    up, down, up_got, down_got = gather_first(jnp.stack(z_one))
    farthest, pair, up_got, down_got, normed_two = hold(farthest, pair, up_got, down_got, normed_two)
    kv = jnp.concatenate([kv_own[None], pair], axis=0)
    while kv.shape[0] < reach:
        kv_got = shifted(kv, kv.shape[0])
        if 2 * kv.shape[0] < reach:
            kv = jnp.concatenate([kv, kv_got], axis=0)
        else:
            break
    up, down, first_one = gather_second(up, down, up_got, down_got)
    up_got, down_got = gather_last(up, down)
    first_far_one = swap(first_one, core_bit)

    last = (((1,), (1,)), ((), ()))
    bias_grads = [[], []]

    def feed_group(g, sums, normed, near, far, *beside):
        *sums, far_grad, near_grad, bias_far, bias_here = feed(
            normed, dy, trim(far, 0, unit_rows), trim(near, 0, unit_rows), bias_rows[1][g], bias_rows[0][g], unit_rows, sums
        )
        bias_grads[0].append(bias_here)
        bias_grads[1].append(bias_far)
        far_grad, *beside = hold(far_grad, *beside)
        shape = (2,) + (2,) * len(x_bits) + (2, depth, unit_rows, D)
        grad_sum = (near_grad + swap(far_grad, core_bit).astype(f32)).reshape(shape)
        return sums, grad_sum[0], grad_sum[1], *beside

    def sum_first(up, down):
        (up_kept, up_sent), (down_kept, down_sent) = split_bit(up, x_bits[-1], 0), split_bit(down, y_bit, len(x_bits))
        return up_kept, up_sent, down_kept, down_sent

    def sum_second(up_kept, up_sent, down_kept, down_sent):
        up = up_kept + swap(up_sent, x_bits[-1]).astype(f32)
        for bit in x_bits[-2::-1]:
            kept, sent = split_bit(up, bit, 0)
            up = kept + swap(sent, bit).astype(f32)
        down = down_kept + swap(down_sent, y_bit).astype(f32)
        (up_kept, up_sent), (down_kept, down_sent) = split_bit(up, y_bit, 0), split_bit(down, x_bits[-1], 0)
        return up_kept, up_sent, down_kept, down_sent

    def sum_third(up_kept, up_got, down_kept, down_got):
        up = up_kept + up_got.astype(f32)
        down = down_kept + down_got.astype(f32)
        for bit in x_bits[-2::-1]:
            kept, sent = split_bit(down, bit, 0)
            down = kept + swap(sent, bit).astype(f32)
        return jnp.concatenate([up, down], axis=1)

    def sum_z(value):
        got = [swap_z(value[k].astype(low), k) for k in range(1, depth)]
        total = value[0]
        for part in got:
            total = total + part.astype(f32)
        return total

    def spread(part):
        value = part.astype(low)
        for bit in x_bits:
            value = gather_bit(value, bit, 0, True)
        return gather_bit(value, core_bit, len(x_bits), True).reshape(batch_count, -1, D)

    sums, up_sum, down_sum, up_got, down_got, kv_got = feed_group(
        0, None, normed_two, near_zero, far_zero, up_got, down_got, kv_got
    )
    kv = jnp.concatenate([kv, kv_got, farthest[None]], axis=0)
    sum_zero = sum_first(up_sum, down_sum)
    *sum_zero, first_far_one, q_t = hold(*sum_zero, first_far_one, q_t)
    last_one = joined(up_got, down_got)
    last_far_one = swap(last_one, core_bit)

    do_t = lax.dot_general(out_full, dy, (((0,), (1,)), ((), ())), preferred_element_type=f32).astype(low)
    context, dq_t, dkv_own, dkv_sent = attention(q_t, do_t, start_here, cosine, sine, kv)
    sum_zero = sum_second(*sum_zero)
    last_far_one, dq_t, normed_late, *sum_zero = hold(last_far_one, dq_t, normed_two, *sum_zero)
    dkv_far = shifted(dkv_sent[reach - 1], reach, True)
    dkv = jnp.concatenate([dkv_own[None], dkv_sent[: reach - 1].astype(f32)], axis=0)
    middle = reach // 2
    got = shifted(dkv[middle:].astype(low), middle, True)
    up_got, down_got = swap(sum_zero[1], y_bit), swap(sum_zero[3], x_bits[-1])
    (mlp_out, d_normed_two), up_sum, down_sum, up_got, down_got, dkv_far, got = feed_group(
        1, sums, normed_late, (first_one, last_one), (first_far_one, last_far_one), up_got, down_got, dkv_far, got
    )
    sum_zero = sum_third(sum_zero[0], up_got, sum_zero[2], down_got)
    dkv = dkv[:middle] + got.astype(f32)
    while dkv.shape[0] > 1:
        middle = dkv.shape[0] // 2
        got = shifted(dkv[middle:].astype(low), middle, True)
        dkv = dkv[:middle] + got.astype(f32)
    dkv = dkv[0] + dkv_far.astype(f32)
    qkv_share, vec_share = -(-qkv_rows // batch_count), -(-vec_len // batch_count)
    input_grad, qkv_part, out_part = tail(
        entry, x_low, dy, dq_t, dkv, cosine, sine, qkv_full, normed_one, context, d_normed_two, gains, bias_grads,
        head_part_rows, seq_count, vec_len,
    )
    outer = jnp.stack([qkv_part, out_part]).reshape((2, 2) + (2,) * len(x_bits) + (2, depth, head_part_rows, D))
    outer = outer[:, 0] + swap(outer[:, 1].astype(low), core_bit).astype(f32)
    sum_one = sum_first(
        jnp.concatenate([up_sum, outer[0]], axis=-2), jnp.concatenate([down_sum, outer[1]], axis=-2)
    )
    feed_zero = sum_z(sum_zero)
    sum_one = sum_second(*sum_one)
    *sum_one, feed_zero = hold(*sum_one, feed_zero)
    grads_zero = spread(feed_zero)
    attn_out = lax.dot_general(context, out_full, last, preferred_element_type=f32)
    outputs = (x_low.astype(f32) + attn_out + mlp_out + out_bias).astype(low)
    sum_one = sum_third(sum_one[0], swap(sum_one[1], y_bit), sum_one[2], swap(sum_one[3], x_bits[-1]))
    sum_one, grads_zero, outputs = hold(sum_one, grads_zero, outputs)
    grads_one = spread(sum_z(sum_one))

    end = unit_rows + head_part_rows
    up_all = jnp.concatenate([grads_zero[:, :unit_rows], grads_one[:, :unit_rows]], axis=1).reshape(-1, D)
    down_all = jnp.concatenate([grads_zero[:, unit_rows:], grads_one[:, end : end + unit_rows]], axis=1).reshape(-1, D)
    qkv_all = grads_one[:, unit_rows : unit_rows + qkv_share].reshape(-1, D)[:qkv_rows]
    out_all = grads_one[:, end + unit_rows : end + unit_rows + out_own].reshape(-1, D)
    vector_grad = grads_one[:, end - 4, :vec_share].astype(f32).reshape(-1)[:vec_len]
    out_grad, *out_states = update(out_all, bases, 1, out_weight, out_first, out_second)
    qkv_grad, *qkv_states = update(qkv_all, bases, 0, qkv_weight, qkv_first, qkv_second)
    up_grad, *up_states = update(up_all, bases, 2, up_weight, up_first, up_second)
    down_grad, *down_states = update(down_all, bases, 3, down_weight, down_first, down_second, True)
    vector_new, *vector_states = adam_step(vectors, vector_grad, vector_first, vector_second)
    states = (qkv_states, out_states, up_states, down_states, (*vector_states, vector_new))
    return (
        outputs.reshape(inputs.shape),
        input_grad.reshape(inputs.shape),
        qkv_grad,
        out_grad,
        up_grad,
        down_grad,
        vector_grad,
        *(state[0] for state in states),
        *(state[1] for state in states),
        *(state[2] for state in states),
    )


def solution(mesh):
    tokens = P("batch", "seq", None)
    rows, columns, flat = P("seq", None), P(None, "seq"), P("seq")
    params = (rows, rows, rows, columns, flat)
    return jax.shard_map(
        shards,
        mesh=mesh,
        in_specs=(tokens, tokens, P("batch", None)) + params + (P(),) + params + params,
        out_specs=(tokens, tokens) + params * 4,
        check_vma=False,
    )
```

```python
import functools

import jax
import jax.numpy as jnp
from jax import lax
from jax.experimental import pallas as pl
from jax.experimental.pallas import tpu as pltpu
from jax.sharding import PartitionSpec as P

D = 768
HEADS = 12
HEAD = 64
ROT = 16
FF = 3072
STEP = 10

layer_eps = 1e-05
adam_eps = 1e-08
beta_first = 0.95
beta_second = 0.95
matrix_rate = 0.08
vector_rate = 0.3
rope_base = 10000.0
masked_score = -1e30
low = jnp.bfloat16
f32 = jnp.float32
VMEM_LIMIT = 56 * 1024 * 1024
GROUPS = 2
FEED_VMEM = 56 * 1024 * 1024
UPDATE_VMEM = 28 * 1024 * 1024


def swap(value, bit):
    axis, step = bit
    return lax.ppermute(value, axis, [(i, i ^ step) for i in range(lax.axis_size(axis))])


def mine(bit):
    axis, step = bit
    return lax.rem(lax.axis_index(axis) // step, 2)


def hold(*values):
    return lax.optimization_barrier(values)


def swap_z(value, step):
    size = lax.axis_size("seq")
    return lax.ppermute(value, "seq", [(i, i ^ (2 * step)) for i in range(size)])


def gather_z(piece):
    return [piece] + [swap_z(piece, k) for k in range(1, lax.axis_size("seq") // 2)]


def gather_bit(value, bit, axis, absolute=False):
    got = swap(value, bit)
    if absolute:
        upper = mine(bit) == 1
        return jnp.stack([jnp.where(upper, got, value), jnp.where(upper, value, got)], axis=axis)
    return jnp.stack([value, got], axis=axis)


def split_bit(value, bit, axis):
    return lax.index_in_dim(value, 0, axis, keepdims=False), lax.index_in_dim(value, 1, axis, keepdims=False).astype(low)


def bit_names(axis, size):
    return [(axis, 1 << k) for k in range(size.bit_length() - 1)]


def moments(rotated, first, second):
    new_first = beta_first * first + (1.0 - beta_first) * rotated
    new_second = beta_second * second + (1.0 - beta_second) * rotated * rotated
    first_scale, second_scale = 1.0 / (1.0 - beta_first**STEP), 1.0 / (1.0 - beta_second**STEP)
    ratio = new_first * first_scale / (jnp.sqrt(new_second * second_scale) + adam_eps)
    return ratio, new_first, new_second


def adam_step(weight, grad, first, second):
    ratio, new_first, new_second = moments(grad, first, second)
    return (weight - vector_rate * ratio, new_first, new_second)


def attention_kernel(blocks, width, q_ref, do_ref, start_ref, cos_ref, sin_ref, kv_ref, context_ref, dq_ref, dkv_own_ref, dkv_ref):
    length = q_ref.shape[1]
    keys = blocks * length
    key_t = jnp.concatenate([kv_ref[k, :HEAD, :] for k in reversed(range(blocks))], axis=1)
    value_t = jnp.concatenate([kv_ref[k, HEAD:, :] for k in reversed(range(blocks))], axis=1)
    key = key_t.astype(f32).T.astype(low)
    value = value_t.astype(f32).T.astype(low)
    key_pos = lax.broadcasted_iota(jnp.int32, (keys, length), 0) - (blocks - 1) * length
    query_pos = lax.broadcasted_iota(jnp.int32, (keys, length), 1)
    allowed = (key_pos >= start_ref[0]) & (key_pos <= query_pos)
    bias = jnp.where(allowed, 0.0, masked_score)
    cosine, sine = cos_ref[...], sin_ref[...]
    d_key = jnp.zeros((keys, HEAD), f32)
    d_value = jnp.zeros((keys, HEAD), f32)
    last = (((1,), (1,)), ((), ()))
    for first in range(0, HEADS, width):
        heads = range(first, first + width)
        query = jnp.concatenate([q_ref[h * HEAD : (h + 1) * HEAD, :] for h in heads], axis=1)
        d_out = jnp.concatenate([do_ref[h * HEAD : (h + 1) * HEAD, :] for h in heads], axis=1)
        scores = jnp.dot(key, query, preferred_element_type=f32)
        scores = scores + jnp.concatenate([bias] * width, axis=1)
        weights = jnp.exp(scores - jnp.max(scores, axis=0, keepdims=True))
        probs = weights * (1.0 / jnp.sum(weights, axis=0, keepdims=True))
        probs_low = probs.astype(low)
        context_t = jnp.dot(value_t, probs_low, preferred_element_type=f32)
        d_probs = jnp.dot(value, d_out, preferred_element_type=f32)
        inner = jnp.sum(probs * d_probs, axis=0, keepdims=True)
        d_scores = (probs * (d_probs - inner)).astype(low)
        d_query = jnp.dot(key_t, d_scores, preferred_element_type=f32) * HEAD ** (-0.5)
        d_value = d_value + lax.dot_general(probs_low, d_out, last, preferred_element_type=f32)
        d_key = d_key + lax.dot_general(d_scores, query, last, preferred_element_type=f32)
        for k, h in enumerate(heads):
            lanes = slice(k * length, (k + 1) * length)
            part = d_query[:, lanes]
            a, b = part[: ROT // 2], part[ROT // 2 : ROT]
            turned = jnp.concatenate([a * cosine + b * sine, b * cosine - a * sine, part[ROT:]], axis=0)
            dq_ref[h * HEAD : (h + 1) * HEAD, :] = turned.astype(low)
        for k in range(0, width, 2):
            h = first + k
            two = jnp.concatenate(
                [context_t[:, k * length : (k + 1) * length], context_t[:, (k + 1) * length : (k + 2) * length]], axis=0
            )
            context_ref[:, h * HEAD : (h + 2) * HEAD] = two.T.astype(low)
    d_kv = jnp.concatenate([d_key, d_value], axis=1).T
    for k in range(blocks):
        part = d_kv[:, (blocks - 1 - k) * length : (blocks - k) * length]
        if k == 0:
            dkv_own_ref[...] = part
        else:
            dkv_ref[k - 1] = part.astype(low)


def attention(q_t, do_t, start, cosine, sine, kv):
    rows, _, length = start.shape
    blocks = kv.shape[0]
    tokens = q_t.shape[1]
    by_row = lambda height: pl.BlockSpec((height, length), lambda r: (0, r))
    return pl.pallas_call(
        functools.partial(attention_kernel, blocks, HEADS),
        grid=(rows,),
        in_specs=[by_row(D), by_row(D), pl.BlockSpec((1, 1, length), lambda r: (r, 0, 0)), by_row(ROT // 2), by_row(ROT // 2)]
        + [pl.BlockSpec((blocks, 2 * HEAD, length), lambda r: (0, 0, r))],
        out_specs=[
            pl.BlockSpec((length, D), lambda r: (r, 0)),
            by_row(D),
            by_row(2 * HEAD),
            pl.BlockSpec((blocks - 1, 2 * HEAD, length), lambda r: (0, 0, r)),
        ],
        out_shape=[
            jax.ShapeDtypeStruct((tokens, D), low),
            jax.ShapeDtypeStruct((D, tokens), low),
            jax.ShapeDtypeStruct((2 * HEAD, tokens), f32),
            jax.ShapeDtypeStruct((blocks - 1, 2 * HEAD, tokens), low),
        ],
        compiler_params=pltpu.CompilerParams(vmem_limit_bytes=VMEM_LIMIT),
        cost_estimate=pl.CostEstimate(
            flops=4 * 7 * tokens * HEADS * blocks * length * HEAD * 2, bytes_accessed=8 << 20, transcendentals=0
        ),
        name="attention",
    )(q_t, do_t, start, cosine, sine, kv)


def gathered_parts(plane, refs, offset, rows):
    half = plane // 2
    out = []
    for end, ref in enumerate(refs):
        for j in range(half):
            out.append((0, end * half + j, ref.at[0, j, :, pl.ds(offset, rows)]))
            out.append((1, 2 * j + end, ref.at[1, j, :, pl.ds(offset, rows)]))
    return out


def feed_kernel(n_ref, dy_ref, first_far, last_far, first_near, last_near, bias_far_ref, bias_near_ref, *refs):
    far_refs, near_refs = (first_far, last_far), (first_near, last_near)
    before = refs[: len(refs) - 11]
    out_ref, dn_ref, far_grad_ref, near_grad_ref, bias_far_grad_ref, bias_near_grad_ref = refs[-11:-5]
    weights, far_sum, near_sum, held, sems = refs[-5:]
    plane = weights.shape[2]
    last = (((1,), (1,)), ((), ()))
    first = (((0,), (0,)), ((), ()))
    loads = [
        [
            pltpu.make_async_copy(source, weights.at[side, kind, k], sems.at[side, 2 * k + kind])
            for kind, k, source in gathered_parts(plane, refs_of, 0, weights.shape[4])
        ]
        for side, refs_of in enumerate((far_refs, near_refs))
    ]
    fetches = [pltpu.make_async_copy(ref, held.at[k], sems.at[2, k]) for k, ref in enumerate(before)]
    for copy in loads[0] + loads[1] + fetches:
        copy.start()
    normed, d_out = n_ref[...], dy_ref[...]
    units = far_sum.shape[1]
    out, d_normed = 0.0, 0.0
    stores = []
    for side, (bias_ref, bias_grad_ref, buffer, grad_ref) in enumerate(
        (
            (bias_far_ref, bias_far_grad_ref, far_sum, far_grad_ref),
            (bias_near_ref, bias_near_grad_ref, near_sum, near_grad_ref),
        )
    ):
        for copy in loads[side]:
            copy.wait()
        up, down = weights[side, 0].reshape(units, D), weights[side, 1].reshape(units, D)
        hidden = lax.dot_general(normed, up, last, preferred_element_type=f32) + bias_ref[...]
        share = 0.5 * (1.0 + lax.erf(hidden * (0.5**0.5)))
        slope = share + hidden * (jnp.exp(-0.5 * hidden * hidden) * (0.5 / 3.141592653589793) ** 0.5)
        active = (hidden * share).astype(low)
        d_active = lax.dot_general(d_out, down, last, preferred_element_type=f32)
        d_hidden = (d_active * slope).astype(low)
        for k, part in enumerate(
            (
                lax.dot_general(d_hidden, normed, first, preferred_element_type=f32),
                lax.dot_general(active, d_out, first, preferred_element_type=f32),
            )
        ):
            buffer[k] = part.astype(buffer.dtype)
            copy = pltpu.make_async_copy(buffer.at[k], grad_ref.at[k], sems.at[3, 2 * side + k])
            copy.start()
            stores.append(copy)
        bias_grad_ref[...] = jnp.sum(d_hidden.astype(f32), axis=0, keepdims=True)
        out = out + jnp.dot(active, down, preferred_element_type=f32)
        d_normed = d_normed + jnp.dot(d_hidden, up, preferred_element_type=f32)
    for copy in fetches:
        copy.wait()
    out_ref[...] = held[0] + out if before else out
    dn_ref[...] = held[1] + d_normed if before else d_normed
    for copy in stores:
        copy.wait()


def feed(normed, d_out, far, near, bias_far, bias_near, rows, before):
    tokens = normed.shape[0]
    plane, depth = 2 * far[0].shape[1], far[0].shape[2]
    units = plane * depth * rows
    before = before or []
    vmem, hbm = pl.BlockSpec(memory_space=pltpu.VMEM), pl.BlockSpec(memory_space=pl.ANY)
    return pl.pallas_call(
        feed_kernel,
        in_specs=[vmem, vmem, hbm, hbm, hbm, hbm, vmem, vmem] + [hbm] * len(before),
        out_specs=[vmem, vmem, hbm, hbm, vmem, vmem],
        out_shape=[
            jax.ShapeDtypeStruct((tokens, D), f32),
            jax.ShapeDtypeStruct((tokens, D), f32),
            jax.ShapeDtypeStruct((2, units, D), low),
            jax.ShapeDtypeStruct((2, units, D), f32),
            jax.ShapeDtypeStruct((1, units), f32),
            jax.ShapeDtypeStruct((1, units), f32),
        ],
        scratch_shapes=[
            pltpu.VMEM((2, 2, plane, depth, rows, D), low),
            pltpu.VMEM((2, units, D), low),
            pltpu.VMEM((2, units, D), f32),
            pltpu.VMEM((2, tokens, D), f32),
            pltpu.SemaphoreType.DMA((4, 2 * plane)),
        ],
        compiler_params=pltpu.CompilerParams(vmem_limit_bytes=FEED_VMEM),
        cost_estimate=pl.CostEstimate(flops=4 * 24 * tokens * units * D, bytes_accessed=8 << 20, transcendentals=0),
        name="feed",
    )(normed, d_out, *far, *near, bias_far, bias_near, *before)


def head_kernel(
    vec_len, offset, out_rows, device_ref, x_ref, first_near, last_near, first_far, last_far, cos_ref, sin_ref, n_one_ref,
    n_two_ref, q_ref, kv_ref, w_ref, gain_ref, bias_ref, *refs
):
    *bias_refs, out_ref, flat, units, held, pieces_of, outs_of, sems = refs if out_rows else (*refs[:-6], None, *refs[-6:])
    _, _, plane, depth, size, _ = held.shape
    copies = [
        pltpu.make_async_copy(source, held.at[side, kind, k], sems.at[side, 2 * k + kind])
        for side, refs_of in enumerate(((first_near, last_near), (first_far, last_far)))
        for kind, k, source in gathered_parts(plane, refs_of, offset, size)
    ]
    for copy in copies:
        copy.start()
    x = x_ref[...].astype(f32)
    center = x - jnp.mean(x, axis=-1, keepdims=True)
    xhat = center * lax.rsqrt(jnp.mean(center * center, axis=-1, keepdims=True) + layer_eps)
    for copy in copies:
        copy.wait()
    for side in range(2):
        for k in range(plane):
            for z in range(depth):
                number = device_ref[(side * plane + k) * depth + z]
                pieces_of[number] = held[side, 0, k, z].astype(f32)
                if out_rows:
                    outs_of[number] = held[side, 1, k, z][:out_rows].astype(f32)
    if out_rows:
        out_ref[...] = outs_of[...].reshape(out_ref.shape).astype(low)
    shards_of = (flat.shape[1]) // vec_len
    rows = (D + 2 * HEAD) // shards_of
    whole = pieces_of[...].reshape(shards_of, -1, D)
    for s in range(shards_of):
        left, row = vec_len, rows
        while left > 0:
            size = min(left, D)
            begin = s * vec_len + (row - rows) * D
            flat[:, begin : begin + size] = whole[s, row : row + 1, :size]
            left -= size
            row += 1
    vector = lambda begin, size: flat[:, begin : begin + size]
    gain_one, shift_one, gain_two, shift_two = [vector(k * D, D) for k in range(4)]
    gain_ref[0:1] = gain_one
    gain_ref[1:2] = gain_two
    qkv_bias = vector(4 * D, D + 2 * HEAD)
    start = 4 * D + D + 2 * HEAD
    bias_ref[...] = vector(start, D) + vector(start + D + FF, D)
    count, size_of = units.shape
    for k in range(count):
        units[k : k + 1, :] = vector(start + D + k * size_of, size_of)
    groups = len(bias_refs) // 2
    for k, ref in enumerate(bias_refs):
        side, g = k // groups, k % groups
        width = size_of // groups
        for i in range(count // 2):
            row = units[pl.ds(device_ref[side * (count // 2) + i], 1), :]
            ref[:, i * width : (i + 1) * width] = row[:, g * width : (g + 1) * width]
    n_one = (xhat * gain_one + shift_one).astype(low)
    n_one_ref[...] = n_one
    n_two_ref[...] = (xhat * gain_two + shift_two).astype(low)
    weight = whole[:, :rows].reshape(shards_of * rows, D).astype(low)
    w_ref[...] = weight
    column = jnp.broadcast_to(qkv_bias, (8, qkv_bias.shape[1])).T[:, 0:1]
    projected = lax.dot_general(weight, n_one, (((1,), (1,)), ((), ())), preferred_element_type=f32) + column
    cosine, sine = cos_ref[...], sin_ref[...]
    half = ROT // 2

    def turned(first):
        a, b = projected[first : first + half], projected[first + half : first + ROT]
        rest = projected[first + ROT : first + HEAD]
        return jnp.concatenate([a * cosine - b * sine, b * cosine + a * sine, rest], axis=0).astype(low)

    for h in range(HEADS):
        q_ref[h * HEAD : (h + 1) * HEAD, :] = turned(h * HEAD) * jnp.asarray(HEAD ** (-0.5), low)
    kv_ref[:HEAD, :] = turned(D)
    kv_ref[HEAD:, :] = projected[D + HEAD :].astype(low)


def head(device, x, near, far, offset, size, out_rows, cosine, sine, groups, vec_len, shards_of):
    tokens = x.shape[0]
    count = device.shape[0]
    plane, depth = 2 * near[0].shape[1], near[0].shape[2]
    vmem, hbm = pl.BlockSpec(memory_space=pltpu.VMEM), pl.BlockSpec(memory_space=pl.ANY)
    return pl.pallas_call(
        functools.partial(head_kernel, vec_len, offset, out_rows),
        in_specs=[pl.BlockSpec(memory_space=pltpu.SMEM), vmem, hbm, hbm, hbm, hbm, vmem, vmem],
        out_shape=[
            jax.ShapeDtypeStruct((tokens, D), low),
            jax.ShapeDtypeStruct((tokens, D), low),
            jax.ShapeDtypeStruct((D, tokens), low),
            jax.ShapeDtypeStruct((2 * HEAD, tokens), low),
            jax.ShapeDtypeStruct((D + 2 * HEAD, D), low),
            jax.ShapeDtypeStruct((2, D), f32),
            jax.ShapeDtypeStruct((1, D), f32),
        ]
        + [jax.ShapeDtypeStruct((1, FF // 2 // groups), f32)] * (2 * groups)
        + [jax.ShapeDtypeStruct((D, D), low)] * (out_rows > 0),
        scratch_shapes=[
            pltpu.VMEM((1, shards_of * vec_len), f32),
            pltpu.VMEM((count, FF // count), f32),
            pltpu.VMEM((2, 2, plane, depth, size, D), low),
            pltpu.VMEM((count, size, D), f32),
            pltpu.VMEM((count, max(out_rows, 8), D), f32),
            pltpu.SemaphoreType.DMA((2, 2 * plane)),
        ],
        compiler_params=pltpu.CompilerParams(vmem_limit_bytes=FEED_VMEM),
        cost_estimate=pl.CostEstimate(flops=4 * 2 * tokens * 896 * D, bytes_accessed=8 << 20, transcendentals=0),
        name="head",
    )(device, x, *near, *far, cosine, sine)


def tail_kernel(
    shards_of, entry_ref, x_ref, dy_ref, dq_ref, dkv_ref, cos_ref, sin_ref, w_ref, n_ref, context_ref, d_two_ref, gain_ref, *refs
):
    bias_refs, (in_grad_ref, qkv_ref, out_ref, flat, units) = refs[:-5], refs[-5:]
    d_kv = dkv_ref[...]
    a, b = d_kv[: ROT // 2], d_kv[ROT // 2 : ROT]
    cosine, sine = cos_ref[...], sin_ref[...]
    d_kv = jnp.concatenate([a * cosine + b * sine, b * cosine - a * sine, d_kv[ROT:]], axis=0).astype(low)
    d_proj = jnp.concatenate([dq_ref[...], d_kv], axis=0)
    first = (((0,), (0,)), ((), ()))
    qkv_grad = jnp.dot(d_proj, n_ref[...], preferred_element_type=f32)
    out_grad = lax.dot_general(dy_ref[...], context_ref[...], first, preferred_element_type=f32)
    d_one = lax.dot_general(d_proj, w_ref[...], first, preferred_element_type=f32)
    d_two = d_two_ref[...]
    x = x_ref[...].astype(f32)
    dy = dy_ref[...].astype(f32)
    center = x - jnp.mean(x, axis=-1, keepdims=True)
    inv_sigma = lax.rsqrt(jnp.mean(center * center, axis=-1, keepdims=True) + layer_eps)
    xhat = center * inv_sigma
    d_hat = d_one * gain_ref[0:1] + d_two * gain_ref[1:2]
    d_in = (
        d_hat - jnp.mean(d_hat, axis=-1, keepdims=True) - xhat * jnp.mean(d_hat * xhat, axis=-1, keepdims=True)
    ) * inv_sigma
    in_grad_ref[...] = (dy + d_in).astype(low)
    columns = lambda v: jnp.sum(v, axis=0, keepdims=True)
    dy_column = columns(dy)
    ones = jnp.ones((8, d_proj.shape[1]), low)
    proj_sum = lax.dot_general(ones, d_proj, (((1,), (1,)), ((), ())), preferred_element_type=f32)[0:1]
    pieces = [columns(d_one * xhat), columns(d_one), columns(d_two * xhat), columns(d_two)]
    pieces += [proj_sum, dy_column, None, dy_column]
    count, size = units.shape
    groups = len(bias_refs) // 2
    width = size // groups
    for k, ref in enumerate(bias_refs):
        side, g = k // groups, k % groups
        for i in range(count // 2):
            place = side * (count // 2) + i
            units[place : place + 1, g * width : (g + 1) * width] = ref[:, i * width : (i + 1) * width]
    offset = 0
    for piece in pieces:
        if piece is None:
            for k in range(count):
                flat[:, offset : offset + size] = units[pl.ds(entry_ref[k], 1), :]
                offset += size
        else:
            flat[:, offset : offset + piece.shape[1]] = piece
            offset += piece.shape[1]
    qkv_rows, vec_len = qkv_grad.shape[0] // shards_of, flat.shape[1] // shards_of
    to_shard = count // shards_of
    share = lambda k, total: [k // to_shard * total + min(-(-total // to_shard) * j, total) for j in (k % to_shard, k % to_shard + 1)]
    out_own = D // count
    vec_row = qkv_ref.shape[1] - 4
    for k in range(count):
        to = entry_ref[k]
        begin, end = share(k, qkv_rows)
        qkv_ref[to] = jnp.zeros(qkv_ref.shape[1:], f32)
        if end > begin:
            qkv_ref[to, : end - begin, :] = qkv_grad[begin:end]
        begin, end = share(k, vec_len)
        if end > begin:
            qkv_ref[to, vec_row : vec_row + 1, : end - begin] = flat[:, begin:end]
        out_ref[to] = jnp.zeros(out_ref.shape[1:], f32)
        out_ref[to, :out_own, :] = out_grad[k * out_own : (k + 1) * out_own]


def tail(entry, x, dy, dq_t, dkv, cosine, sine, weight, normed, context, d_two, gains, bias_grads, rows, shards_of, vec_len):
    tokens = x.shape[0]
    count = entry.shape[0]
    operands = (entry, x, dy, dq_t, dkv, cosine, sine, weight, normed, context, d_two, gains, *sum(bias_grads, []))
    return pl.pallas_call(
        functools.partial(tail_kernel, shards_of),
        in_specs=[pl.BlockSpec(memory_space=pltpu.SMEM)] + [pl.BlockSpec(memory_space=pltpu.VMEM)] * (len(operands) - 1),
        out_shape=[
            jax.ShapeDtypeStruct((tokens, D), low),
            jax.ShapeDtypeStruct((count, rows, D), f32),
            jax.ShapeDtypeStruct((count, rows, D), f32),
        ],
        scratch_shapes=[pltpu.VMEM((1, shards_of * vec_len), f32), pltpu.VMEM((count, FF // count), f32)],
        compiler_params=pltpu.CompilerParams(vmem_limit_bytes=VMEM_LIMIT),
        cost_estimate=pl.CostEstimate(flops=4 * 6 * tokens * 896 * D, bytes_accessed=8 << 20, transcendentals=0),
        name="tail",
    )(*operands)


def split_low(value):
    high = value.astype(low)
    return high, (value - high.astype(f32)).astype(low)


def update_step(across, grad, high, rest, w_ref, first_ref, second_ref, grad_ref, first_new_ref, second_new_ref, w_new_ref):
    rotated = jnp.dot(grad, high, preferred_element_type=f32) + jnp.dot(grad, rest, preferred_element_type=f32)
    grad = grad.astype(f32)
    if across:
        rotated, grad = rotated.T, grad.T
    grad_ref[...] = grad
    ratio, first_new, second_new = moments(rotated, first_ref[...], second_ref[...])
    first_new_ref[...] = first_new
    second_new_ref[...] = second_new
    r_high, r_rest = split_low(ratio)
    if across:
        product = lambda r, b: jnp.dot(b, r, preferred_element_type=f32)
    else:
        product = lambda r, b: lax.dot_general(r, b, (((1,), (1,)), ((), ())), preferred_element_type=f32)
    unrotated = product(r_high, high) + (product(r_high, rest) + product(r_rest, high))
    w_new_ref[...] = w_ref[...] - matrix_rate * unrotated


def update_kernel(across, grad_ref, high_ref, rest_ref, *refs):
    update_step(across, grad_ref[...], high_ref[...], rest_ref[...], *refs)


def update(grad, basis, weight, first, second, across=False):
    return pl.pallas_call(
        functools.partial(update_kernel, across),
        out_shape=[jax.ShapeDtypeStruct(weight.shape, f32)] * 4,
        compiler_params=pltpu.CompilerParams(vmem_limit_bytes=UPDATE_VMEM),
        cost_estimate=pl.CostEstimate(flops=10 * grad.shape[0] * D * D, bytes_accessed=8 << 20, transcendentals=0),
        name="update",
    )(grad, *basis, weight, first, second)


def shards(
    inputs,
    cotangent,
    doc_lengths,
    qkv_weight,
    out_weight,
    up_weight,
    down_weight,
    vectors,
    bases,
    qkv_first,
    out_first,
    up_first,
    down_first,
    vector_first,
    qkv_second,
    out_second,
    up_second,
    down_second,
    vector_second,
):
    seq_count, batch_count = lax.axis_size("seq"), lax.axis_size("batch")
    seq_index, batch_index = lax.axis_index("seq"), lax.axis_index("batch")
    row_count, shard_len = inputs.shape[:2]
    tokens = row_count * shard_len
    y_bit, *z_bits = bit_names("seq", seq_count)
    core_bit, *x_bits = bit_names("batch", batch_count)
    near = [core_bit] + x_bits[::-1] + [y_bit] + z_bits[::-1]
    depth = seq_count // 2
    plane = 2 ** (len(x_bits) + 1)
    x_low = inputs.reshape(tokens, D)
    dy = cotangent.reshape(tokens, D)

    first_pos = seq_index * shard_len
    query_pos = first_pos + jnp.arange(shard_len, dtype=jnp.int32)
    docs = doc_lengths.shape[1]
    earlier = jnp.arange(docs)[:, None] < jnp.arange(docs)[None, :]
    doc_starts = jnp.sum(jnp.where(earlier[None], doc_lengths[:, :, None], 0), axis=1)
    start = jnp.max(
        jnp.where(doc_starts[:, None, :] <= query_pos[None, :, None], doc_starts[:, None, :], 0), axis=-1
    )
    offsets = (query_pos[None, :] - start).reshape(tokens)
    inverse = 1.0 / rope_base ** (jnp.arange(0, ROT, 2).astype(f32) / ROT)
    angles = offsets.astype(f32)[None, :] * inverse[:, None]
    cosine, sine = jnp.cos(angles), jnp.sin(angles)
    start_here = (start - first_pos).astype(jnp.int32)[:, None, :]
    number = jnp.arange(seq_count * batch_count, dtype=jnp.int32)

    def bits_of(value, place_of):
        total = 0
        for k, (axis_name, step) in enumerate(near[::-1]):
            total = total + place_of(value, k, axis_name, step)
        return total

    differs = {"seq": (number // batch_count) ^ seq_index, "batch": (number % batch_count) ^ batch_index}
    entry = bits_of(number, lambda v, k, name, step: (differs[name] // step) % 2 << k).astype(jnp.int32)
    xor_of = lambda name: sum((number >> k) % 2 * step for k, (axis_name, step) in enumerate(near[::-1]) if axis_name == name)
    device = ((xor_of("seq") ^ seq_index) * batch_count + (xor_of("batch") ^ batch_index)).astype(jnp.int32)

    qkv_rows, out_rows, up_rows, vec_len = qkv_weight.shape[0], out_weight.shape[0], up_weight.shape[0], vectors.shape[0]
    vec_rows = -(-vec_len // D)
    used = qkv_rows + vec_rows
    head_rows = -(-used // (8 * batch_count)) * 8 * batch_count
    vec_pad = vec_rows * D - vec_len

    def own_part(rows):
        size = rows.shape[0] // batch_count
        return lax.dynamic_slice_in_dim(rows, batch_index * size, size, axis=0)

    head_shard = jnp.concatenate(
        [qkv_weight, jnp.pad(vectors, (0, vec_pad)).reshape(vec_rows, D), jnp.zeros((head_rows - used, D), f32)], axis=0
    ).astype(low)
    head_part_rows = head_rows // batch_count
    unit_rows = up_rows // batch_count // GROUPS
    out_own = out_rows // batch_count
    up_low, down_low = own_part(up_weight.astype(low)), own_part(down_weight.T.astype(low))
    outer = [
        own_part(head_shard),
        jnp.concatenate([own_part(out_weight.astype(low)), jnp.zeros((head_part_rows - out_own, D), low)], axis=0),
    ]
    parts_of = []
    for g in range(GROUPS):
        rows = slice(g * unit_rows, (g + 1) * unit_rows)
        pieces = [up_low[rows], outer[0], down_low[rows], outer[1]] if g == 0 else [up_low[rows], down_low[rows]]
        parts_of.append(jnp.concatenate(pieces, axis=0))

    def gather_first(parts):
        half = parts.shape[1] // 2
        up, down = parts[:, :half], parts[:, half:]
        for bit in x_bits[:-1]:
            down = gather_bit(down, bit, 0)
        return up, down, swap(up, y_bit), swap(down, x_bits[-1])

    def gather_second(up, down, up_got, down_got):
        up, down = jnp.stack([up, up_got]), jnp.stack([down, down_got])
        for bit in x_bits[:-1]:
            up = gather_bit(up, bit, 0)
        shape = (1, plane // 2, depth) + up.shape[-2:]
        return up, down, jnp.concatenate([up.reshape(shape), down.reshape(shape)], axis=0)

    def gather_last(up, down):
        return swap(up, x_bits[-1]), swap(down, y_bit)

    def joined(up, down):
        shape = (1, plane // 2, depth) + up.shape[-2:]
        return jnp.concatenate([up.reshape(shape), down.reshape(shape)], axis=0)

    z_zero = gather_z(parts_of[0])
    *z_zero, cosine, sine, start_here, entry, device, part_one = hold(
        *z_zero, cosine, sine, start_here, entry, device, parts_of[1]
    )
    up, down, up_got, down_got = gather_first(jnp.stack(z_zero))
    z_one = gather_z(part_one)
    up_got, down_got, z_one[1] = hold(up_got, down_got, z_one[1])
    up, down, first_zero = gather_second(up, down, up_got, down_got)
    up_got, down_got = gather_last(up, down)
    first_far_zero = swap(first_zero, core_bit)
    late_bases, up, down = hold(bases, up, down)
    split_bases = [part for k in range(4) for part in split_low(late_bases[k])]
    up_got, down_got, first_far_zero, *rest = hold(up_got, down_got, first_far_zero, *z_one[2:], *split_bases)
    z_one[2:], split_bases = rest[: len(z_one) - 2], rest[len(z_one) - 2 :]
    split_bases = [split_bases[2 * k : 2 * k + 2] for k in range(4)]
    last_zero = joined(up_got, down_got)
    last_far_zero = swap(last_zero, core_bit)

    aligned = unit_rows % 16 == 0 and head_part_rows % 16 == 0
    trim = lambda values, begin, end: values if aligned else tuple(v[..., begin:end, :] for v in values)
    near_zero, far_zero = (first_zero, last_zero), (first_far_zero, last_far_zero)
    end = unit_rows + head_part_rows

    inside = out_own % 8 == 0
    normed_one, normed_two, q_t, kv_own, qkv_full, gains, out_bias, *bias_rows = head(
        device, x_low, trim(near_zero, unit_rows, end), trim(far_zero, unit_rows, end), unit_rows if aligned else 0,
        head_part_rows, out_own if inside else 0, cosine, sine, GROUPS, vec_len, seq_count,
    )
    if inside:
        out_full = bias_rows.pop()
    else:
        chosen = (entry[:, None] == number[None, :]).astype(low)
        sides = []
        for pair in (near_zero, far_zero):
            along = [v[1, :, :, unit_rows : unit_rows + out_own] for v in pair]
            sides.append(jnp.stack(along, axis=1).reshape(-1, out_own * D))
        out_full = jnp.dot(chosen, jnp.concatenate(sides, axis=0), preferred_element_type=f32).astype(low).reshape(D, D)
    bias_rows = [bias_rows[:GROUPS], bias_rows[GROUPS:]]
    reach = seq_count // 2

    def shifted(value, step, back=False):
        pairs = [(j, j + step) for j in range(seq_count - step)]
        return lax.ppermute(value, "seq", [(b, a) for a, b in pairs] if back else pairs)

    farthest, pair = shifted(kv_own, reach), shifted(kv_own[None], 1)
    up, down, up_got, down_got = gather_first(jnp.stack(z_one))
    up_got, down_got, normed_two = hold(up_got, down_got, normed_two)
    up, down, first_one = gather_second(up, down, up_got, down_got)
    up_got, down_got = gather_last(up, down)
    first_far_one = swap(first_one, core_bit)

    last = (((1,), (1,)), ((), ()))
    bias_grads = [[], []]

    def feed_group(g, sums, normed, near, far, *beside):
        *sums, far_grad, near_grad, bias_far, bias_here = feed(
            normed, dy, trim(far, 0, unit_rows), trim(near, 0, unit_rows), bias_rows[1][g], bias_rows[0][g], unit_rows, sums
        )
        bias_grads[0].append(bias_here)
        bias_grads[1].append(bias_far)
        far_grad, *beside = hold(far_grad, *beside)
        shape = (2,) + (2,) * len(x_bits) + (2, depth, unit_rows, D)
        grad_sum = (near_grad + swap(far_grad, core_bit).astype(f32)).reshape(shape)
        return sums, grad_sum[0], grad_sum[1], *beside

    def sum_first(up, down):
        (up_kept, up_sent), (down_kept, down_sent) = split_bit(up, x_bits[-1], 0), split_bit(down, y_bit, len(x_bits))
        return up_kept, up_sent, down_kept, down_sent

    def sum_second(up_kept, up_sent, down_kept, down_sent):
        up = up_kept + swap(up_sent, x_bits[-1]).astype(f32)
        for bit in x_bits[-2::-1]:
            kept, sent = split_bit(up, bit, 0)
            up = kept + swap(sent, bit).astype(f32)
        down = down_kept + swap(down_sent, y_bit).astype(f32)
        (up_kept, up_sent), (down_kept, down_sent) = split_bit(up, y_bit, 0), split_bit(down, x_bits[-1], 0)
        return up_kept, up_sent, down_kept, down_sent

    def sum_third(up_kept, up_got, down_kept, down_got):
        up = up_kept + up_got.astype(f32)
        down = down_kept + down_got.astype(f32)
        for bit in x_bits[-2::-1]:
            kept, sent = split_bit(down, bit, 0)
            down = kept + swap(sent, bit).astype(f32)
        return jnp.concatenate([up, down], axis=1)

    def sum_z(value):
        got = [swap_z(value[k].astype(low), k) for k in range(1, depth)]
        total = value[0]
        for part in got:
            total = total + part.astype(f32)
        return total

    def spread(part):
        value = part.astype(low)
        for bit in x_bits:
            value = gather_bit(value, bit, 0, True)
        return gather_bit(value, core_bit, len(x_bits), True).reshape(batch_count, -1, D)

    sums, up_sum, down_sum, up_got, down_got, farthest, pair = feed_group(
        0, None, normed_two, near_zero, far_zero, up_got, down_got, farthest, pair
    )
    kv = jnp.concatenate([kv_own[None], pair], axis=0)
    while kv.shape[0] < reach:
        kv = jnp.concatenate([kv, shifted(kv, kv.shape[0])], axis=0)
    kv = jnp.concatenate([kv, farthest[None]], axis=0)
    sum_zero = sum_first(up_sum, down_sum)
    *sum_zero, first_far_one, q_t = hold(*sum_zero, first_far_one, q_t)
    last_one = joined(up_got, down_got)
    last_far_one = swap(last_one, core_bit)

    do_t = lax.dot_general(out_full, dy, (((0,), (1,)), ((), ())), preferred_element_type=f32).astype(low)
    context, dq_t, dkv_own, dkv_sent = attention(q_t, do_t, start_here, cosine, sine, kv)
    sum_zero = sum_second(*sum_zero)
    last_far_one, dq_t, normed_late, *sum_zero = hold(last_far_one, dq_t, normed_two, *sum_zero)
    dkv_far = shifted(dkv_sent[reach - 1], reach, True)
    dkv = jnp.concatenate([dkv_own[None], dkv_sent[: reach - 1].astype(f32)], axis=0)
    middle = reach // 2
    got = shifted(dkv[middle:].astype(low), middle, True)
    up_got, down_got = swap(sum_zero[1], y_bit), swap(sum_zero[3], x_bits[-1])
    (mlp_out, d_normed_two), up_sum, down_sum, up_got, down_got, dkv_far, got = feed_group(
        1, sums, normed_late, (first_one, last_one), (first_far_one, last_far_one), up_got, down_got, dkv_far, got
    )
    sum_zero = sum_third(sum_zero[0], up_got, sum_zero[2], down_got)
    dkv = dkv[:middle] + got.astype(f32)
    while dkv.shape[0] > 1:
        middle = dkv.shape[0] // 2
        got = shifted(dkv[middle:].astype(low), middle, True)
        dkv = dkv[:middle] + got.astype(f32)
    dkv = dkv[0] + dkv_far.astype(f32)
    qkv_share, vec_share = -(-qkv_rows // batch_count), -(-vec_len // batch_count)
    input_grad, qkv_part, out_part = tail(
        entry, x_low, dy, dq_t, dkv, cosine, sine, qkv_full, normed_one, context, d_normed_two, gains, bias_grads,
        head_part_rows, seq_count, vec_len,
    )
    z_got = [swap_z(sum_zero[k].astype(low), k) for k in range(1, depth)]
    qkv_part, *z_got = hold(qkv_part, *z_got)
    feed_zero = sum_zero[0] + sum(part.astype(f32) for part in z_got)
    outer = jnp.stack([qkv_part, out_part]).reshape((2, 2) + (2,) * len(x_bits) + (2, depth, head_part_rows, D))
    outer = outer[:, 0] + swap(outer[:, 1].astype(low), core_bit).astype(f32)
    sum_one = sum_first(
        jnp.concatenate([up_sum, outer[0]], axis=-2), jnp.concatenate([down_sum, outer[1]], axis=-2)
    )
    grads_zero = spread(feed_zero)
    sum_one = sum_second(*sum_one)
    *sum_one, grads_zero = hold(*sum_one, grads_zero)
    attn_out = lax.dot_general(context, out_full, last, preferred_element_type=f32)
    outputs = (x_low.astype(f32) + attn_out + mlp_out + out_bias).astype(low)
    sum_one = sum_third(sum_one[0], swap(sum_one[1], y_bit), sum_one[2], swap(sum_one[3], x_bits[-1]))
    sum_one, outputs = hold(sum_one, outputs)
    grads_one = spread(sum_z(sum_one))

    end = unit_rows + head_part_rows
    up_all = jnp.concatenate([grads_zero[:, :unit_rows], grads_one[:, :unit_rows]], axis=1).reshape(-1, D)
    down_all = jnp.concatenate([grads_zero[:, unit_rows:], grads_one[:, end : end + unit_rows]], axis=1).reshape(-1, D)
    qkv_all = grads_one[:, unit_rows : unit_rows + qkv_share].reshape(-1, D)[:qkv_rows]
    out_all = grads_one[:, end + unit_rows : end + unit_rows + out_own].reshape(-1, D)
    vector_grad = grads_one[:, end - 4, :vec_share].astype(f32).reshape(-1)[:vec_len]
    out_grad, *out_states = update(out_all, split_bases[1], out_weight, out_first, out_second)
    qkv_grad, *qkv_states = update(qkv_all, split_bases[0], qkv_weight, qkv_first, qkv_second)
    up_grad, *up_states = update(up_all, split_bases[2], up_weight, up_first, up_second)
    down_grad, *down_states = update(down_all, split_bases[3], down_weight, down_first, down_second, True)
    vector_new, *vector_states = adam_step(vectors, vector_grad, vector_first, vector_second)
    states = (qkv_states, out_states, up_states, down_states, (*vector_states, vector_new))
    return (
        outputs.reshape(inputs.shape),
        input_grad.reshape(inputs.shape),
        qkv_grad,
        out_grad,
        up_grad,
        down_grad,
        vector_grad,
        *(state[0] for state in states),
        *(state[1] for state in states),
        *(state[2] for state in states),
    )


def solution(mesh):
    tokens = P("batch", "seq", None)
    rows, columns, flat = P("seq", None), P(None, "seq"), P("seq")
    params = (rows, rows, rows, columns, flat)
    return jax.shard_map(
        shards,
        mesh=mesh,
        in_specs=(tokens, tokens, P("batch", None)) + params + (P(),) + params + params,
        out_specs=(tokens, tokens) + params * 4,
        check_vma=False,
    )
```

```python
import functools

import jax
import jax.numpy as jnp
from jax import lax
from jax.experimental import pallas as pl
from jax.experimental.pallas import tpu as pltpu
from jax.sharding import PartitionSpec as P

D = 768
HEADS = 12
HEAD = 64
ROT = 16
FF = 3072
STEP = 10

layer_eps = 1e-05
adam_eps = 1e-08
beta_first = 0.95
beta_second = 0.95
matrix_rate = 0.08
vector_rate = 0.3
rope_base = 10000.0
masked_score = -1e30
low = jnp.bfloat16
f32 = jnp.float32
VMEM_LIMIT = 56 * 1024 * 1024
GROUPS = 2
FEED_VMEM = 56 * 1024 * 1024
UPDATE_VMEM = 28 * 1024 * 1024


def swap(value, bit):
    axis, step = bit
    return lax.ppermute(value, axis, [(i, i ^ step) for i in range(lax.axis_size(axis))])


def mine(bit):
    axis, step = bit
    return lax.rem(lax.axis_index(axis) // step, 2)


def hold(*values):
    return lax.optimization_barrier(values)


def swap_z(value, step):
    size = lax.axis_size("seq")
    return lax.ppermute(value, "seq", [(i, i ^ (2 * step)) for i in range(size)])


def gather_z(piece):
    return [piece] + [swap_z(piece, k) for k in range(1, lax.axis_size("seq") // 2)]


def gather_bit(value, bit, axis, absolute=False):
    got = swap(value, bit)
    if absolute:
        upper = mine(bit) == 1
        return jnp.stack([jnp.where(upper, got, value), jnp.where(upper, value, got)], axis=axis)
    return jnp.stack([value, got], axis=axis)


def split_bit(value, bit, axis):
    return lax.index_in_dim(value, 0, axis, keepdims=False), lax.index_in_dim(value, 1, axis, keepdims=False).astype(low)


def bit_names(axis, size):
    return [(axis, 1 << k) for k in range(size.bit_length() - 1)]


def moments(rotated, first, second):
    new_first = beta_first * first + (1.0 - beta_first) * rotated
    new_second = beta_second * second + (1.0 - beta_second) * rotated * rotated
    first_scale, second_scale = 1.0 / (1.0 - beta_first**STEP), 1.0 / (1.0 - beta_second**STEP)
    ratio = new_first * first_scale / (jnp.sqrt(new_second * second_scale) + adam_eps)
    return ratio, new_first, new_second


def adam_step(weight, grad, first, second):
    ratio, new_first, new_second = moments(grad, first, second)
    return (weight - vector_rate * ratio, new_first, new_second)


def attention_kernel(blocks, width, q_ref, do_ref, start_ref, cos_ref, sin_ref, kv_ref, context_ref, dq_ref, dkv_own_ref, dkv_ref):
    length = q_ref.shape[1]
    keys = blocks * length
    key_t = jnp.concatenate([kv_ref[k, :HEAD, :] for k in reversed(range(blocks))], axis=1)
    value_t = jnp.concatenate([kv_ref[k, HEAD:, :] for k in reversed(range(blocks))], axis=1)
    key = key_t.astype(f32).T.astype(low)
    value = value_t.astype(f32).T.astype(low)
    key_pos = lax.broadcasted_iota(jnp.int32, (keys, length), 0) - (blocks - 1) * length
    query_pos = lax.broadcasted_iota(jnp.int32, (keys, length), 1)
    allowed = (key_pos >= start_ref[0]) & (key_pos <= query_pos)
    bias = jnp.where(allowed, 0.0, masked_score)
    cosine, sine = cos_ref[...], sin_ref[...]
    d_key = jnp.zeros((keys, HEAD), f32)
    d_value = jnp.zeros((keys, HEAD), f32)
    last = (((1,), (1,)), ((), ()))
    for first in range(0, HEADS, width):
        heads = range(first, first + width)
        query = jnp.concatenate([q_ref[h * HEAD : (h + 1) * HEAD, :] for h in heads], axis=1)
        d_out = jnp.concatenate([do_ref[h * HEAD : (h + 1) * HEAD, :] for h in heads], axis=1)
        scores = jnp.dot(key, query, preferred_element_type=f32)
        scores = scores + jnp.concatenate([bias] * width, axis=1)
        weights = jnp.exp(scores - jnp.max(scores, axis=0, keepdims=True))
        probs = weights * (1.0 / jnp.sum(weights, axis=0, keepdims=True))
        probs_low = probs.astype(low)
        context_t = jnp.dot(value_t, probs_low, preferred_element_type=f32)
        d_probs = jnp.dot(value, d_out, preferred_element_type=f32)
        inner = jnp.sum(probs * d_probs, axis=0, keepdims=True)
        d_scores = (probs * (d_probs - inner)).astype(low)
        d_query = jnp.dot(key_t, d_scores, preferred_element_type=f32) * HEAD ** (-0.5)
        d_value = d_value + lax.dot_general(probs_low, d_out, last, preferred_element_type=f32)
        d_key = d_key + lax.dot_general(d_scores, query, last, preferred_element_type=f32)
        for k, h in enumerate(heads):
            lanes = slice(k * length, (k + 1) * length)
            part = d_query[:, lanes]
            a, b = part[: ROT // 2], part[ROT // 2 : ROT]
            turned = jnp.concatenate([a * cosine + b * sine, b * cosine - a * sine, part[ROT:]], axis=0)
            dq_ref[h * HEAD : (h + 1) * HEAD, :] = turned.astype(low)
        for k in range(0, width, 2):
            h = first + k
            two = jnp.concatenate(
                [context_t[:, k * length : (k + 1) * length], context_t[:, (k + 1) * length : (k + 2) * length]], axis=0
            )
            context_ref[:, h * HEAD : (h + 2) * HEAD] = two.T.astype(low)
    d_kv = jnp.concatenate([d_key, d_value], axis=1).T
    for k in range(blocks):
        part = d_kv[:, (blocks - 1 - k) * length : (blocks - k) * length]
        if k == 0:
            dkv_own_ref[...] = part
        else:
            dkv_ref[k - 1] = part.astype(low)


def attention(q_t, do_t, start, cosine, sine, kv):
    rows, _, length = start.shape
    blocks = kv.shape[0]
    tokens = q_t.shape[1]
    by_row = lambda height: pl.BlockSpec((height, length), lambda r: (0, r))
    return pl.pallas_call(
        functools.partial(attention_kernel, blocks, HEADS),
        grid=(rows,),
        in_specs=[by_row(D), by_row(D), pl.BlockSpec((1, 1, length), lambda r: (r, 0, 0)), by_row(ROT // 2), by_row(ROT // 2)]
        + [pl.BlockSpec((blocks, 2 * HEAD, length), lambda r: (0, 0, r))],
        out_specs=[
            pl.BlockSpec((length, D), lambda r: (r, 0)),
            by_row(D),
            by_row(2 * HEAD),
            pl.BlockSpec((blocks - 1, 2 * HEAD, length), lambda r: (0, 0, r)),
        ],
        out_shape=[
            jax.ShapeDtypeStruct((tokens, D), low),
            jax.ShapeDtypeStruct((D, tokens), low),
            jax.ShapeDtypeStruct((2 * HEAD, tokens), f32),
            jax.ShapeDtypeStruct((blocks - 1, 2 * HEAD, tokens), low),
        ],
        compiler_params=pltpu.CompilerParams(vmem_limit_bytes=VMEM_LIMIT),
        cost_estimate=pl.CostEstimate(
            flops=4 * 7 * tokens * HEADS * blocks * length * HEAD * 2, bytes_accessed=8 << 20, transcendentals=0
        ),
        name="attention",
    )(q_t, do_t, start, cosine, sine, kv)


def gathered_parts(plane, refs, offset, rows):
    half = plane // 2
    out = []
    for end, ref in enumerate(refs):
        for j in range(half):
            out.append((0, end * half + j, ref.at[0, j, :, pl.ds(offset, rows)]))
            out.append((1, 2 * j + end, ref.at[1, j, :, pl.ds(offset, rows)]))
    return out


def feed_kernel(n_ref, dy_ref, first_far, last_far, first_near, last_near, bias_far_ref, bias_near_ref, *refs):
    far_refs, near_refs = (first_far, last_far), (first_near, last_near)
    before = refs[: len(refs) - 11]
    out_ref, dn_ref, far_grad_ref, near_grad_ref, bias_far_grad_ref, bias_near_grad_ref = refs[-11:-5]
    weights, far_sum, near_sum, held, sems = refs[-5:]
    plane = weights.shape[2]
    last = (((1,), (1,)), ((), ()))
    first = (((0,), (0,)), ((), ()))
    loads = [
        [
            pltpu.make_async_copy(source, weights.at[side, kind, k], sems.at[side, 2 * k + kind])
            for kind, k, source in gathered_parts(plane, refs_of, 0, weights.shape[4])
        ]
        for side, refs_of in enumerate((far_refs, near_refs))
    ]
    fetches = [pltpu.make_async_copy(ref, held.at[k], sems.at[2, k]) for k, ref in enumerate(before)]
    for copy in loads[0] + loads[1] + fetches:
        copy.start()
    normed, d_out = n_ref[...], dy_ref[...]
    units = far_sum.shape[1]
    out, d_normed = 0.0, 0.0
    stores = []
    for side, (bias_ref, bias_grad_ref, buffer, grad_ref) in enumerate(
        (
            (bias_far_ref, bias_far_grad_ref, far_sum, far_grad_ref),
            (bias_near_ref, bias_near_grad_ref, near_sum, near_grad_ref),
        )
    ):
        for copy in loads[side]:
            copy.wait()
        up, down = weights[side, 0].reshape(units, D), weights[side, 1].reshape(units, D)
        hidden = lax.dot_general(normed, up, last, preferred_element_type=f32) + bias_ref[...]
        share = 0.5 * (1.0 + lax.erf(hidden * (0.5**0.5)))
        slope = share + hidden * (jnp.exp(-0.5 * hidden * hidden) * (0.5 / 3.141592653589793) ** 0.5)
        active = (hidden * share).astype(low)
        d_active = lax.dot_general(d_out, down, last, preferred_element_type=f32)
        d_hidden = (d_active * slope).astype(low)
        for k, part in enumerate(
            (
                lax.dot_general(d_hidden, normed, first, preferred_element_type=f32),
                lax.dot_general(active, d_out, first, preferred_element_type=f32),
            )
        ):
            buffer[k] = part.astype(buffer.dtype)
            copy = pltpu.make_async_copy(buffer.at[k], grad_ref.at[k], sems.at[3, 2 * side + k])
            copy.start()
            stores.append(copy)
        bias_grad_ref[...] = jnp.sum(d_hidden.astype(f32), axis=0, keepdims=True)
        out = out + jnp.dot(active, down, preferred_element_type=f32)
        d_normed = d_normed + jnp.dot(d_hidden, up, preferred_element_type=f32)
    for copy in fetches:
        copy.wait()
    out_ref[...] = held[0] + out if before else out
    dn_ref[...] = held[1] + d_normed if before else d_normed
    for copy in stores:
        copy.wait()


def feed(normed, d_out, far, near, bias_far, bias_near, rows, before):
    tokens = normed.shape[0]
    plane, depth = 2 * far[0].shape[1], far[0].shape[2]
    units = plane * depth * rows
    before = before or []
    vmem, hbm = pl.BlockSpec(memory_space=pltpu.VMEM), pl.BlockSpec(memory_space=pl.ANY)
    return pl.pallas_call(
        feed_kernel,
        in_specs=[vmem, vmem, hbm, hbm, hbm, hbm, vmem, vmem] + [hbm] * len(before),
        out_specs=[vmem, vmem, hbm, hbm, vmem, vmem],
        out_shape=[
            jax.ShapeDtypeStruct((tokens, D), f32),
            jax.ShapeDtypeStruct((tokens, D), f32),
            jax.ShapeDtypeStruct((2, units, D), low),
            jax.ShapeDtypeStruct((2, units, D), f32),
            jax.ShapeDtypeStruct((1, units), f32),
            jax.ShapeDtypeStruct((1, units), f32),
        ],
        scratch_shapes=[
            pltpu.VMEM((2, 2, plane, depth, rows, D), low),
            pltpu.VMEM((2, units, D), low),
            pltpu.VMEM((2, units, D), f32),
            pltpu.VMEM((2, tokens, D), f32),
            pltpu.SemaphoreType.DMA((4, 2 * plane)),
        ],
        compiler_params=pltpu.CompilerParams(vmem_limit_bytes=FEED_VMEM),
        cost_estimate=pl.CostEstimate(flops=4 * 24 * tokens * units * D, bytes_accessed=8 << 20, transcendentals=0),
        name="feed",
    )(normed, d_out, *far, *near, bias_far, bias_near, *before)


def head_kernel(
    vec_len, offset, out_rows, device_ref, x_ref, first_near, last_near, first_far, last_far, cos_ref, sin_ref, n_one_ref,
    n_two_ref, q_ref, kv_ref, w_ref, gain_ref, bias_ref, *refs
):
    *bias_refs, out_ref, flat, units, held, pieces_of, outs_of, sems = refs if out_rows else (*refs[:-6], None, *refs[-6:])
    _, _, plane, depth, size, _ = held.shape
    copies = [
        pltpu.make_async_copy(source, held.at[side, kind, k], sems.at[side, 2 * k + kind])
        for side, refs_of in enumerate(((first_near, last_near), (first_far, last_far)))
        for kind, k, source in gathered_parts(plane, refs_of, offset, size)
    ]
    for copy in copies:
        copy.start()
    x = x_ref[...].astype(f32)
    center = x - jnp.mean(x, axis=-1, keepdims=True)
    xhat = center * lax.rsqrt(jnp.mean(center * center, axis=-1, keepdims=True) + layer_eps)
    for copy in copies:
        copy.wait()
    for side in range(2):
        for k in range(plane):
            for z in range(depth):
                number = device_ref[(side * plane + k) * depth + z]
                pieces_of[number] = held[side, 0, k, z].astype(f32)
                if out_rows:
                    outs_of[number] = held[side, 1, k, z][:out_rows].astype(f32)
    if out_rows:
        out_ref[...] = outs_of[...].reshape(out_ref.shape).astype(low)
    shards_of = (flat.shape[1]) // vec_len
    rows = (D + 2 * HEAD) // shards_of
    whole = pieces_of[...].reshape(shards_of, -1, D)
    for s in range(shards_of):
        left, row = vec_len, rows
        while left > 0:
            size = min(left, D)
            begin = s * vec_len + (row - rows) * D
            flat[:, begin : begin + size] = whole[s, row : row + 1, :size]
            left -= size
            row += 1
    vector = lambda begin, size: flat[:, begin : begin + size]
    gain_one, shift_one, gain_two, shift_two = [vector(k * D, D) for k in range(4)]
    gain_ref[0:1] = gain_one
    gain_ref[1:2] = gain_two
    qkv_bias = vector(4 * D, D + 2 * HEAD)
    start = 4 * D + D + 2 * HEAD
    bias_ref[...] = vector(start, D) + vector(start + D + FF, D)
    count, size_of = units.shape
    for k in range(count):
        units[k : k + 1, :] = vector(start + D + k * size_of, size_of)
    groups = len(bias_refs) // 2
    for k, ref in enumerate(bias_refs):
        side, g = k // groups, k % groups
        width = size_of // groups
        for i in range(count // 2):
            row = units[pl.ds(device_ref[side * (count // 2) + i], 1), :]
            ref[:, i * width : (i + 1) * width] = row[:, g * width : (g + 1) * width]
    n_one = (xhat * gain_one + shift_one).astype(low)
    n_one_ref[...] = n_one
    n_two_ref[...] = (xhat * gain_two + shift_two).astype(low)
    weight = whole[:, :rows].reshape(shards_of * rows, D).astype(low)
    w_ref[...] = weight
    column = jnp.broadcast_to(qkv_bias, (8, qkv_bias.shape[1])).T[:, 0:1]
    projected = lax.dot_general(weight, n_one, (((1,), (1,)), ((), ())), preferred_element_type=f32) + column
    cosine, sine = cos_ref[...], sin_ref[...]
    half = ROT // 2

    def turned(first):
        a, b = projected[first : first + half], projected[first + half : first + ROT]
        rest = projected[first + ROT : first + HEAD]
        return jnp.concatenate([a * cosine - b * sine, b * cosine + a * sine, rest], axis=0).astype(low)

    for h in range(HEADS):
        q_ref[h * HEAD : (h + 1) * HEAD, :] = turned(h * HEAD) * jnp.asarray(HEAD ** (-0.5), low)
    kv_ref[:HEAD, :] = turned(D)
    kv_ref[HEAD:, :] = projected[D + HEAD :].astype(low)


def head(device, x, near, far, offset, size, out_rows, cosine, sine, groups, vec_len, shards_of):
    tokens = x.shape[0]
    count = device.shape[0]
    plane, depth = 2 * near[0].shape[1], near[0].shape[2]
    vmem, hbm = pl.BlockSpec(memory_space=pltpu.VMEM), pl.BlockSpec(memory_space=pl.ANY)
    return pl.pallas_call(
        functools.partial(head_kernel, vec_len, offset, out_rows),
        in_specs=[pl.BlockSpec(memory_space=pltpu.SMEM), vmem, hbm, hbm, hbm, hbm, vmem, vmem],
        out_shape=[
            jax.ShapeDtypeStruct((tokens, D), low),
            jax.ShapeDtypeStruct((tokens, D), low),
            jax.ShapeDtypeStruct((D, tokens), low),
            jax.ShapeDtypeStruct((2 * HEAD, tokens), low),
            jax.ShapeDtypeStruct((D + 2 * HEAD, D), low),
            jax.ShapeDtypeStruct((2, D), f32),
            jax.ShapeDtypeStruct((1, D), f32),
        ]
        + [jax.ShapeDtypeStruct((1, FF // 2 // groups), f32)] * (2 * groups)
        + [jax.ShapeDtypeStruct((D, D), low)] * (out_rows > 0),
        scratch_shapes=[
            pltpu.VMEM((1, shards_of * vec_len), f32),
            pltpu.VMEM((count, FF // count), f32),
            pltpu.VMEM((2, 2, plane, depth, size, D), low),
            pltpu.VMEM((count, size, D), f32),
            pltpu.VMEM((count, max(out_rows, 8), D), f32),
            pltpu.SemaphoreType.DMA((2, 2 * plane)),
        ],
        compiler_params=pltpu.CompilerParams(vmem_limit_bytes=FEED_VMEM),
        cost_estimate=pl.CostEstimate(flops=4 * 2 * tokens * 896 * D, bytes_accessed=8 << 20, transcendentals=0),
        name="head",
    )(device, x, *near, *far, cosine, sine)


def tail_kernel(
    shards_of, entry_ref, x_ref, dy_ref, dq_ref, dkv_ref, cos_ref, sin_ref, w_ref, n_ref, context_ref, d_two_ref, gain_ref, *refs
):
    bias_refs, (in_grad_ref, qkv_ref, out_ref, flat, units) = refs[:-5], refs[-5:]
    d_kv = dkv_ref[...]
    a, b = d_kv[: ROT // 2], d_kv[ROT // 2 : ROT]
    cosine, sine = cos_ref[...], sin_ref[...]
    d_kv = jnp.concatenate([a * cosine + b * sine, b * cosine - a * sine, d_kv[ROT:]], axis=0).astype(low)
    d_proj = jnp.concatenate([dq_ref[...], d_kv], axis=0)
    first = (((0,), (0,)), ((), ()))
    qkv_grad = jnp.dot(d_proj, n_ref[...], preferred_element_type=f32)
    out_grad = lax.dot_general(dy_ref[...], context_ref[...], first, preferred_element_type=f32)
    d_one = lax.dot_general(d_proj, w_ref[...], first, preferred_element_type=f32)
    d_two = d_two_ref[...]
    x = x_ref[...].astype(f32)
    dy = dy_ref[...].astype(f32)
    center = x - jnp.mean(x, axis=-1, keepdims=True)
    inv_sigma = lax.rsqrt(jnp.mean(center * center, axis=-1, keepdims=True) + layer_eps)
    xhat = center * inv_sigma
    d_hat = d_one * gain_ref[0:1] + d_two * gain_ref[1:2]
    d_in = (
        d_hat - jnp.mean(d_hat, axis=-1, keepdims=True) - xhat * jnp.mean(d_hat * xhat, axis=-1, keepdims=True)
    ) * inv_sigma
    in_grad_ref[...] = (dy + d_in).astype(low)
    columns = lambda v: jnp.sum(v, axis=0, keepdims=True)
    dy_column = columns(dy)
    ones = jnp.ones((8, d_proj.shape[1]), low)
    proj_sum = lax.dot_general(ones, d_proj, (((1,), (1,)), ((), ())), preferred_element_type=f32)[0:1]
    pieces = [columns(d_one * xhat), columns(d_one), columns(d_two * xhat), columns(d_two)]
    pieces += [proj_sum, dy_column, None, dy_column]
    count, size = units.shape
    groups = len(bias_refs) // 2
    width = size // groups
    for k, ref in enumerate(bias_refs):
        side, g = k // groups, k % groups
        for i in range(count // 2):
            place = side * (count // 2) + i
            units[place : place + 1, g * width : (g + 1) * width] = ref[:, i * width : (i + 1) * width]
    offset = 0
    for piece in pieces:
        if piece is None:
            for k in range(count):
                flat[:, offset : offset + size] = units[pl.ds(entry_ref[k], 1), :]
                offset += size
        else:
            flat[:, offset : offset + piece.shape[1]] = piece
            offset += piece.shape[1]
    qkv_rows, vec_len = qkv_grad.shape[0] // shards_of, flat.shape[1] // shards_of
    to_shard = count // shards_of
    share = lambda k, total: [k // to_shard * total + min(-(-total // to_shard) * j, total) for j in (k % to_shard, k % to_shard + 1)]
    out_own = D // count
    vec_row = qkv_ref.shape[1] - 4
    for k in range(count):
        to = entry_ref[k]
        begin, end = share(k, qkv_rows)
        qkv_ref[to] = jnp.zeros(qkv_ref.shape[1:], f32)
        if end > begin:
            qkv_ref[to, : end - begin, :] = qkv_grad[begin:end]
        begin, end = share(k, vec_len)
        if end > begin:
            qkv_ref[to, vec_row : vec_row + 1, : end - begin] = flat[:, begin:end]
        out_ref[to] = jnp.zeros(out_ref.shape[1:], f32)
        out_ref[to, :out_own, :] = out_grad[k * out_own : (k + 1) * out_own]


def tail(entry, x, dy, dq_t, dkv, cosine, sine, weight, normed, context, d_two, gains, bias_grads, rows, shards_of, vec_len):
    tokens = x.shape[0]
    count = entry.shape[0]
    operands = (entry, x, dy, dq_t, dkv, cosine, sine, weight, normed, context, d_two, gains, *sum(bias_grads, []))
    return pl.pallas_call(
        functools.partial(tail_kernel, shards_of),
        in_specs=[pl.BlockSpec(memory_space=pltpu.SMEM)] + [pl.BlockSpec(memory_space=pltpu.VMEM)] * (len(operands) - 1),
        out_shape=[
            jax.ShapeDtypeStruct((tokens, D), low),
            jax.ShapeDtypeStruct((count, rows, D), f32),
            jax.ShapeDtypeStruct((count, rows, D), f32),
        ],
        scratch_shapes=[pltpu.VMEM((1, shards_of * vec_len), f32), pltpu.VMEM((count, FF // count), f32)],
        compiler_params=pltpu.CompilerParams(vmem_limit_bytes=VMEM_LIMIT),
        cost_estimate=pl.CostEstimate(flops=4 * 6 * tokens * 896 * D, bytes_accessed=8 << 20, transcendentals=0),
        name="tail",
    )(*operands)


def split_low(value):
    high = value.astype(low)
    return high, (value - high.astype(f32)).astype(low)


def update_step(across, grad, high, rest, w_ref, first_ref, second_ref, grad_ref, first_new_ref, second_new_ref, w_new_ref):
    rotated = jnp.dot(grad, high, preferred_element_type=f32) + jnp.dot(grad, rest, preferred_element_type=f32)
    grad = grad.astype(f32)
    if across:
        rotated, grad = rotated.T, grad.T
    grad_ref[...] = grad
    ratio, first_new, second_new = moments(rotated, first_ref[...], second_ref[...])
    first_new_ref[...] = first_new
    second_new_ref[...] = second_new
    r_high, r_rest = split_low(ratio)
    if across:
        product = lambda r, b: jnp.dot(b, r, preferred_element_type=f32)
    else:
        product = lambda r, b: lax.dot_general(r, b, (((1,), (1,)), ((), ())), preferred_element_type=f32)
    unrotated = product(r_high, high) + (product(r_high, rest) + product(r_rest, high))
    w_new_ref[...] = w_ref[...] - matrix_rate * unrotated


def update_kernel(across, grad_ref, high_ref, rest_ref, *refs):
    update_step(across, grad_ref[...], high_ref[...], rest_ref[...], *refs)


def update(grad, basis, weight, first, second, across=False):
    return pl.pallas_call(
        functools.partial(update_kernel, across),
        out_shape=[jax.ShapeDtypeStruct(weight.shape, f32)] * 4,
        compiler_params=pltpu.CompilerParams(vmem_limit_bytes=UPDATE_VMEM),
        cost_estimate=pl.CostEstimate(flops=10 * grad.shape[0] * D * D, bytes_accessed=8 << 20, transcendentals=0),
        name="update",
    )(grad, *basis, weight, first, second)


def shards(
    inputs,
    cotangent,
    doc_lengths,
    qkv_weight,
    out_weight,
    up_weight,
    down_weight,
    vectors,
    bases,
    qkv_first,
    out_first,
    up_first,
    down_first,
    vector_first,
    qkv_second,
    out_second,
    up_second,
    down_second,
    vector_second,
):
    seq_count, batch_count = lax.axis_size("seq"), lax.axis_size("batch")
    seq_index, batch_index = lax.axis_index("seq"), lax.axis_index("batch")
    row_count, shard_len = inputs.shape[:2]
    tokens = row_count * shard_len
    y_bit, *z_bits = bit_names("seq", seq_count)
    core_bit, *x_bits = bit_names("batch", batch_count)
    near = [core_bit] + x_bits[::-1] + [y_bit] + z_bits[::-1]
    depth = seq_count // 2
    plane = 2 ** (len(x_bits) + 1)
    x_low = inputs.reshape(tokens, D)
    dy = cotangent.reshape(tokens, D)

    first_pos = seq_index * shard_len
    query_pos = first_pos + jnp.arange(shard_len, dtype=jnp.int32)
    docs = doc_lengths.shape[1]
    earlier = jnp.arange(docs)[:, None] < jnp.arange(docs)[None, :]
    doc_starts = jnp.sum(jnp.where(earlier[None], doc_lengths[:, :, None], 0), axis=1)
    start = jnp.max(
        jnp.where(doc_starts[:, None, :] <= query_pos[None, :, None], doc_starts[:, None, :], 0), axis=-1
    )
    offsets = (query_pos[None, :] - start).reshape(tokens)
    inverse = 1.0 / rope_base ** (jnp.arange(0, ROT, 2).astype(f32) / ROT)
    angles = offsets.astype(f32)[None, :] * inverse[:, None]
    cosine, sine = jnp.cos(angles), jnp.sin(angles)
    start_here = (start - first_pos).astype(jnp.int32)[:, None, :]
    number = jnp.arange(seq_count * batch_count, dtype=jnp.int32)

    def bits_of(value, place_of):
        total = 0
        for k, (axis_name, step) in enumerate(near[::-1]):
            total = total + place_of(value, k, axis_name, step)
        return total

    differs = {"seq": (number // batch_count) ^ seq_index, "batch": (number % batch_count) ^ batch_index}
    entry = bits_of(number, lambda v, k, name, step: (differs[name] // step) % 2 << k).astype(jnp.int32)
    xor_of = lambda name: sum((number >> k) % 2 * step for k, (axis_name, step) in enumerate(near[::-1]) if axis_name == name)
    device = ((xor_of("seq") ^ seq_index) * batch_count + (xor_of("batch") ^ batch_index)).astype(jnp.int32)

    qkv_rows, out_rows, up_rows, vec_len = qkv_weight.shape[0], out_weight.shape[0], up_weight.shape[0], vectors.shape[0]
    vec_rows = -(-vec_len // D)
    used = qkv_rows + vec_rows
    head_rows = -(-used // (8 * batch_count)) * 8 * batch_count
    vec_pad = vec_rows * D - vec_len

    def own_part(rows):
        size = rows.shape[0] // batch_count
        return lax.dynamic_slice_in_dim(rows, batch_index * size, size, axis=0)

    head_shard = jnp.concatenate(
        [qkv_weight, jnp.pad(vectors, (0, vec_pad)).reshape(vec_rows, D), jnp.zeros((head_rows - used, D), f32)], axis=0
    ).astype(low)
    head_part_rows = head_rows // batch_count
    unit_rows = up_rows // batch_count // GROUPS
    out_own = out_rows // batch_count
    up_low, down_low = own_part(up_weight.astype(low)), own_part(down_weight.T.astype(low))
    outer = [
        own_part(head_shard),
        jnp.concatenate([own_part(out_weight.astype(low)), jnp.zeros((head_part_rows - out_own, D), low)], axis=0),
    ]
    parts_of = []
    for g in range(GROUPS):
        rows = slice(g * unit_rows, (g + 1) * unit_rows)
        pieces = [up_low[rows], outer[0], down_low[rows], outer[1]] if g == 0 else [up_low[rows], down_low[rows]]
        parts_of.append(jnp.concatenate(pieces, axis=0))

    def gather_first(parts):
        half = parts.shape[1] // 2
        up, down = parts[:, :half], parts[:, half:]
        for bit in x_bits[:-1]:
            down = gather_bit(down, bit, 0)
        return up, down, swap(up, y_bit), swap(down, x_bits[-1])

    def gather_second(up, down, up_got, down_got):
        up, down = jnp.stack([up, up_got]), jnp.stack([down, down_got])
        for bit in x_bits[:-1]:
            up = gather_bit(up, bit, 0)
        shape = (1, plane // 2, depth) + up.shape[-2:]
        return up, down, jnp.concatenate([up.reshape(shape), down.reshape(shape)], axis=0)

    def gather_last(up, down):
        return swap(up, x_bits[-1]), swap(down, y_bit)

    def joined(up, down):
        shape = (1, plane // 2, depth) + up.shape[-2:]
        return jnp.concatenate([up.reshape(shape), down.reshape(shape)], axis=0)

    z_zero = gather_z(parts_of[0])
    *z_zero, cosine, sine, start_here, entry, device, part_one = hold(
        *z_zero, cosine, sine, start_here, entry, device, parts_of[1]
    )
    up, down, up_got, down_got = gather_first(jnp.stack(z_zero))
    z_one = gather_z(part_one)
    up_got, down_got, z_one[1] = hold(up_got, down_got, z_one[1])
    up, down, first_zero = gather_second(up, down, up_got, down_got)
    up_got, down_got = gather_last(up, down)
    first_far_zero = swap(first_zero, core_bit)
    late_bases, up, down = hold(bases, up, down)
    split_bases = [part for k in range(4) for part in split_low(late_bases[k])]
    up_got, down_got, first_far_zero, *rest = hold(up_got, down_got, first_far_zero, *z_one[2:], *split_bases)
    z_one[2:], split_bases = rest[: len(z_one) - 2], rest[len(z_one) - 2 :]
    split_bases = [split_bases[2 * k : 2 * k + 2] for k in range(4)]
    last_zero = joined(up_got, down_got)
    last_far_zero = swap(last_zero, core_bit)

    aligned = unit_rows % 16 == 0 and head_part_rows % 16 == 0
    trim = lambda values, begin, end: values if aligned else tuple(v[..., begin:end, :] for v in values)
    near_zero, far_zero = (first_zero, last_zero), (first_far_zero, last_far_zero)
    end = unit_rows + head_part_rows

    inside = out_own % 8 == 0
    normed_one, normed_two, q_t, kv_own, qkv_full, gains, out_bias, *bias_rows = head(
        device, x_low, trim(near_zero, unit_rows, end), trim(far_zero, unit_rows, end), unit_rows if aligned else 0,
        head_part_rows, out_own if inside else 0, cosine, sine, GROUPS, vec_len, seq_count,
    )
    if inside:
        out_full = bias_rows.pop()
    else:
        chosen = (entry[:, None] == number[None, :]).astype(low)
        sides = []
        for pair in (near_zero, far_zero):
            along = [v[1, :, :, unit_rows : unit_rows + out_own] for v in pair]
            sides.append(jnp.stack(along, axis=1).reshape(-1, out_own * D))
        out_full = jnp.dot(chosen, jnp.concatenate(sides, axis=0), preferred_element_type=f32).astype(low).reshape(D, D)
    bias_rows = [bias_rows[:GROUPS], bias_rows[GROUPS:]]
    reach = seq_count // 2

    def shifted(value, step, back=False):
        pairs = [(j, j + step) for j in range(seq_count - step)]
        return lax.ppermute(value, "seq", [(b, a) for a, b in pairs] if back else pairs)

    farthest, pair = shifted(kv_own, reach), shifted(kv_own[None], 1)
    up, down, up_got, down_got = gather_first(jnp.stack(z_one))
    up_got, down_got, normed_two = hold(up_got, down_got, normed_two)
    up, down, first_one = gather_second(up, down, up_got, down_got)
    up_got, down_got = gather_last(up, down)
    first_far_one = swap(first_one, core_bit)

    last = (((1,), (1,)), ((), ()))
    bias_grads = [[], []]

    def feed_group(g, sums, normed, near, far, *beside):
        *sums, far_grad, near_grad, bias_far, bias_here = feed(
            normed, dy, trim(far, 0, unit_rows), trim(near, 0, unit_rows), bias_rows[1][g], bias_rows[0][g], unit_rows, sums
        )
        bias_grads[0].append(bias_here)
        bias_grads[1].append(bias_far)
        far_grad, *beside = hold(far_grad, *beside)
        shape = (2,) + (2,) * len(x_bits) + (2, depth, unit_rows, D)
        grad_sum = (near_grad + swap(far_grad, core_bit).astype(f32)).reshape(shape)
        return sums, grad_sum[0], grad_sum[1], *beside

    def sum_first(up, down):
        (up_kept, up_sent), (down_kept, down_sent) = split_bit(up, x_bits[-1], 0), split_bit(down, y_bit, len(x_bits))
        return up_kept, up_sent, down_kept, down_sent

    def send_first(sums):
        return swap(sums[1], x_bits[-1]), swap(sums[3], y_bit)

    def sum_second(sums, up_got, down_got):
        up = sums[0] + up_got.astype(f32)
        for bit in x_bits[-2::-1]:
            kept, sent = split_bit(up, bit, 0)
            up = kept + swap(sent, bit).astype(f32)
        down = sums[2] + down_got.astype(f32)
        (up_kept, up_sent), (down_kept, down_sent) = split_bit(up, y_bit, 0), split_bit(down, x_bits[-1], 0)
        return up_kept, up_sent, down_kept, down_sent

    def send_second(sums):
        return swap(sums[1], y_bit), swap(sums[3], x_bits[-1])

    def sum_third(up_kept, up_got, down_kept, down_got):
        up = up_kept + up_got.astype(f32)
        down = down_kept + down_got.astype(f32)
        for bit in x_bits[-2::-1]:
            kept, sent = split_bit(down, bit, 0)
            down = kept + swap(sent, bit).astype(f32)
        return jnp.concatenate([up, down], axis=1)

    def sum_z(value):
        got = [swap_z(value[k].astype(low), k) for k in range(1, depth)]
        total = value[0]
        for part in got:
            total = total + part.astype(f32)
        return total

    def spread(part):
        value = part.astype(low)
        for bit in x_bits:
            value = gather_bit(value, bit, 0, True)
        return gather_bit(value, core_bit, len(x_bits), True).reshape(batch_count, -1, D)

    sums, up_sum, down_sum, up_got, down_got, farthest, pair = feed_group(
        0, None, normed_two, near_zero, far_zero, up_got, down_got, farthest, pair
    )
    kv = jnp.concatenate([kv_own[None], pair], axis=0)
    while kv.shape[0] < reach:
        kv = jnp.concatenate([kv, shifted(kv, kv.shape[0])], axis=0)
    kv = jnp.concatenate([kv, farthest[None]], axis=0)
    sum_zero = sum_first(up_sum, down_sum)
    *sum_zero, first_far_one, q_t = hold(*sum_zero, first_far_one, q_t)
    last_one = joined(up_got, down_got)
    last_far_one = swap(last_one, core_bit)

    do_t = lax.dot_general(out_full, dy, (((0,), (1,)), ((), ())), preferred_element_type=f32).astype(low)
    context, dq_t, dkv_own, dkv_sent = attention(q_t, do_t, start_here, cosine, sine, kv)
    sum_zero = sum_second(sum_zero, *send_first(sum_zero))
    last_far_one, dq_t, normed_late, *sum_zero = hold(last_far_one, dq_t, normed_two, *sum_zero)
    dkv_far = shifted(dkv_sent[reach - 1], reach, True)
    dkv = jnp.concatenate([dkv_own[None], dkv_sent[: reach - 1].astype(f32)], axis=0)
    middle = reach // 2
    got = shifted(dkv[middle:].astype(low), middle, True)
    up_got, down_got = send_second(sum_zero)
    (mlp_out, d_normed_two), up_sum, down_sum, up_got, down_got, dkv_far, got = feed_group(
        1, sums, normed_late, (first_one, last_one), (first_far_one, last_far_one), up_got, down_got, dkv_far, got
    )
    sum_zero = sum_third(sum_zero[0], up_got, sum_zero[2], down_got)
    dkv = dkv[:middle] + got.astype(f32)
    while dkv.shape[0] > 1:
        middle = dkv.shape[0] // 2
        got = shifted(dkv[middle:].astype(low), middle, True)
        dkv = dkv[:middle] + got.astype(f32)
    dkv = dkv[0] + dkv_far.astype(f32)
    qkv_share, vec_share = -(-qkv_rows // batch_count), -(-vec_len // batch_count)
    sum_one = sum_first(up_sum, down_sum)
    dkv, *sum_one = hold(dkv, *sum_one)
    up_got, down_got = send_first(sum_one)
    input_grad, qkv_part, out_part = tail(
        entry, x_low, dy, dq_t, dkv, cosine, sine, qkv_full, normed_one, context, d_normed_two, gains, bias_grads,
        head_part_rows, seq_count, vec_len,
    )
    qkv_part, up_got, down_got = hold(qkv_part, up_got, down_got)
    outer = jnp.stack([qkv_part, out_part]).reshape((2, 2) + (2,) * len(x_bits) + (2, depth, head_part_rows, D))
    got = swap(outer[:, 1].astype(low), core_bit)
    sum_one = sum_second(sum_one, up_got, down_got)
    outer = outer[:, 0] + got.astype(f32)
    sum_outer = sum_first(outer[0], outer[1])
    one_got, outer_got = send_second(sum_one), send_first(sum_outer)
    z_got = [swap_z(sum_zero[k].astype(low), k) for k in range(1, depth)]
    *outer_got, z_first = hold(*outer_got, z_got[0])
    *one_got, z_got[0] = hold(*one_got, z_first)
    *z_got, one_got[0] = hold(*z_got, one_got[0])
    feed_zero = sum_zero[0] + sum(part.astype(f32) for part in z_got)
    grads_zero = spread(feed_zero)
    attn_out = lax.dot_general(context, out_full, last, preferred_element_type=f32)
    outputs = (x_low.astype(f32) + attn_out + mlp_out + out_bias).astype(low)
    sum_outer = sum_second(sum_outer, *outer_got)
    outer_got = send_second(sum_outer)
    sum_one = sum_third(sum_one[0], one_got[0], sum_one[2], one_got[1])
    sum_outer = sum_third(sum_outer[0], outer_got[0], sum_outer[2], outer_got[1])
    both, outputs, grads_zero = hold(jnp.concatenate([sum_one, sum_outer], axis=1), outputs, grads_zero)
    grads_one = spread(sum_z(both))

    begin, end = 2 * unit_rows, 2 * unit_rows + head_part_rows
    up_all = jnp.concatenate([grads_zero[:, :unit_rows], grads_one[:, :unit_rows]], axis=1).reshape(-1, D)
    down_all = jnp.concatenate([grads_zero[:, unit_rows:], grads_one[:, unit_rows:begin]], axis=1).reshape(-1, D)
    qkv_all = grads_one[:, begin : begin + qkv_share].reshape(-1, D)[:qkv_rows]
    out_all = grads_one[:, end : end + out_own].reshape(-1, D)
    vector_grad = grads_one[:, end - 4, :vec_share].astype(f32).reshape(-1)[:vec_len]
    out_grad, *out_states = update(out_all, split_bases[1], out_weight, out_first, out_second)
    qkv_grad, *qkv_states = update(qkv_all, split_bases[0], qkv_weight, qkv_first, qkv_second)
    up_grad, *up_states = update(up_all, split_bases[2], up_weight, up_first, up_second)
    down_grad, *down_states = update(down_all, split_bases[3], down_weight, down_first, down_second, True)
    vector_new, *vector_states = adam_step(vectors, vector_grad, vector_first, vector_second)
    states = (qkv_states, out_states, up_states, down_states, (*vector_states, vector_new))
    return (
        outputs.reshape(inputs.shape),
        input_grad.reshape(inputs.shape),
        qkv_grad,
        out_grad,
        up_grad,
        down_grad,
        vector_grad,
        *(state[0] for state in states),
        *(state[1] for state in states),
        *(state[2] for state in states),
    )


def solution(mesh):
    tokens = P("batch", "seq", None)
    rows, columns, flat = P("seq", None), P(None, "seq"), P("seq")
    params = (rows, rows, rows, columns, flat)
    return jax.shard_map(
        shards,
        mesh=mesh,
        in_specs=(tokens, tokens, P("batch", None)) + params + (P(),) + params + params,
        out_specs=(tokens, tokens) + params * 4,
        check_vma=False,
    )
```

```python
import functools

import jax
import jax.numpy as jnp
from jax import lax
from jax.experimental import pallas as pl
from jax.experimental.pallas import tpu as pltpu
from jax.sharding import PartitionSpec as P

D = 768
HEADS = 12
HEAD = 64
ROT = 16
FF = 3072
STEP = 10

layer_eps = 1e-05
adam_eps = 1e-08
beta_first = 0.95
beta_second = 0.95
matrix_rate = 0.08
vector_rate = 0.3
rope_base = 10000.0
masked_score = -1e30
low = jnp.bfloat16
f32 = jnp.float32
VMEM_LIMIT = 56 * 1024 * 1024
GROUPS = 2
FEED_VMEM = 56 * 1024 * 1024
UPDATE_VMEM = 28 * 1024 * 1024


def swap(value, bit):
    axis, step = bit
    return lax.ppermute(value, axis, [(i, i ^ step) for i in range(lax.axis_size(axis))])


def mine(bit):
    axis, step = bit
    return lax.rem(lax.axis_index(axis) // step, 2)


def hold(*values):
    return lax.optimization_barrier(values)


def hold_lists(*lists):
    flat = iter(hold(*(value for values in lists for value in values)))
    return [[next(flat) for _ in values] for values in lists]


def swap_z(value, step):
    size = lax.axis_size("seq")
    return lax.ppermute(value, "seq", [(i, i ^ (2 * step)) for i in range(size)])


def gather_z(piece):
    return [piece] + [swap_z(piece, k) for k in range(1, lax.axis_size("seq") // 2)]


def gather_bit(value, bit, axis, absolute=False):
    got = swap(value, bit)
    if absolute:
        upper = mine(bit) == 1
        return jnp.stack([jnp.where(upper, got, value), jnp.where(upper, value, got)], axis=axis)
    return jnp.stack([value, got], axis=axis)


def split_bit(value, bit, axis):
    return lax.index_in_dim(value, 0, axis, keepdims=False), lax.index_in_dim(value, 1, axis, keepdims=False).astype(low)


def bit_names(axis, size):
    return [(axis, 1 << k) for k in range(size.bit_length() - 1)]


def moments(rotated, first, second):
    new_first = beta_first * first + (1.0 - beta_first) * rotated
    new_second = beta_second * second + (1.0 - beta_second) * rotated * rotated
    first_scale, second_scale = 1.0 / (1.0 - beta_first**STEP), 1.0 / (1.0 - beta_second**STEP)
    ratio = new_first * first_scale / (jnp.sqrt(new_second * second_scale) + adam_eps)
    return ratio, new_first, new_second


def adam_step(weight, grad, first, second):
    ratio, new_first, new_second = moments(grad, first, second)
    return (weight - vector_rate * ratio, new_first, new_second)


def attention_kernel(blocks, width, q_ref, do_ref, start_ref, cos_ref, sin_ref, kv_ref, context_ref, dq_ref, dkv_own_ref, dkv_ref):
    length = q_ref.shape[1]
    keys = blocks * length
    key_t = jnp.concatenate([kv_ref[k, :HEAD, :] for k in reversed(range(blocks))], axis=1)
    value_t = jnp.concatenate([kv_ref[k, HEAD:, :] for k in reversed(range(blocks))], axis=1)
    key = key_t.astype(f32).T.astype(low)
    value = value_t.astype(f32).T.astype(low)
    key_pos = lax.broadcasted_iota(jnp.int32, (keys, length), 0) - (blocks - 1) * length
    query_pos = lax.broadcasted_iota(jnp.int32, (keys, length), 1)
    allowed = (key_pos >= start_ref[0]) & (key_pos <= query_pos)
    bias = jnp.where(allowed, 0.0, masked_score)
    cosine, sine = cos_ref[...], sin_ref[...]
    d_key = jnp.zeros((keys, HEAD), f32)
    d_value = jnp.zeros((keys, HEAD), f32)
    last = (((1,), (1,)), ((), ()))
    for first in range(0, HEADS, width):
        heads = range(first, first + width)
        query = jnp.concatenate([q_ref[h * HEAD : (h + 1) * HEAD, :] for h in heads], axis=1)
        d_out = jnp.concatenate([do_ref[h * HEAD : (h + 1) * HEAD, :] for h in heads], axis=1)
        scores = jnp.dot(key, query, preferred_element_type=f32)
        scores = scores + jnp.concatenate([bias] * width, axis=1)
        weights = jnp.exp(scores - jnp.max(scores, axis=0, keepdims=True))
        probs = weights * (1.0 / jnp.sum(weights, axis=0, keepdims=True))
        probs_low = probs.astype(low)
        context_t = jnp.dot(value_t, probs_low, preferred_element_type=f32)
        d_probs = jnp.dot(value, d_out, preferred_element_type=f32)
        inner = jnp.sum(probs * d_probs, axis=0, keepdims=True)
        d_scores = (probs * (d_probs - inner)).astype(low)
        d_query = jnp.dot(key_t, d_scores, preferred_element_type=f32) * HEAD ** (-0.5)
        d_value = d_value + lax.dot_general(probs_low, d_out, last, preferred_element_type=f32)
        d_key = d_key + lax.dot_general(d_scores, query, last, preferred_element_type=f32)
        for k, h in enumerate(heads):
            lanes = slice(k * length, (k + 1) * length)
            part = d_query[:, lanes]
            a, b = part[: ROT // 2], part[ROT // 2 : ROT]
            turned = jnp.concatenate([a * cosine + b * sine, b * cosine - a * sine, part[ROT:]], axis=0)
            dq_ref[h * HEAD : (h + 1) * HEAD, :] = turned.astype(low)
        for k in range(0, width, 2):
            h = first + k
            two = jnp.concatenate(
                [context_t[:, k * length : (k + 1) * length], context_t[:, (k + 1) * length : (k + 2) * length]], axis=0
            )
            context_ref[:, h * HEAD : (h + 2) * HEAD] = two.T.astype(low)
    d_kv = jnp.concatenate([d_key, d_value], axis=1).T
    for k in range(blocks):
        part = d_kv[:, (blocks - 1 - k) * length : (blocks - k) * length]
        if k == 0:
            dkv_own_ref[...] = part
        else:
            dkv_ref[k - 1] = part.astype(low)


def attention(q_t, do_t, start, cosine, sine, kv):
    rows, _, length = start.shape
    blocks = kv.shape[0]
    tokens = q_t.shape[1]
    by_row = lambda height: pl.BlockSpec((height, length), lambda r: (0, r))
    return pl.pallas_call(
        functools.partial(attention_kernel, blocks, HEADS),
        grid=(rows,),
        in_specs=[by_row(D), by_row(D), pl.BlockSpec((1, 1, length), lambda r: (r, 0, 0)), by_row(ROT // 2), by_row(ROT // 2)]
        + [pl.BlockSpec((blocks, 2 * HEAD, length), lambda r: (0, 0, r))],
        out_specs=[
            pl.BlockSpec((length, D), lambda r: (r, 0)),
            by_row(D),
            by_row(2 * HEAD),
            pl.BlockSpec((blocks - 1, 2 * HEAD, length), lambda r: (0, 0, r)),
        ],
        out_shape=[
            jax.ShapeDtypeStruct((tokens, D), low),
            jax.ShapeDtypeStruct((D, tokens), low),
            jax.ShapeDtypeStruct((2 * HEAD, tokens), f32),
            jax.ShapeDtypeStruct((blocks - 1, 2 * HEAD, tokens), low),
        ],
        compiler_params=pltpu.CompilerParams(vmem_limit_bytes=VMEM_LIMIT),
        cost_estimate=pl.CostEstimate(
            flops=4 * 7 * tokens * HEADS * blocks * length * HEAD * 2, bytes_accessed=8 << 20, transcendentals=0
        ),
        name="attention",
    )(q_t, do_t, start, cosine, sine, kv)


def gathered_parts(plane, refs, offset, rows):
    half = plane // 2
    out = []
    for end, ref in enumerate(refs):
        for j in range(half):
            out.append((0, end * half + j, ref.at[0, j, :, pl.ds(offset, rows)]))
            out.append((1, 2 * j + end, ref.at[1, j, :, pl.ds(offset, rows)]))
    return out


def feed_kernel(n_ref, dy_ref, first_far, last_far, first_near, last_near, bias_far_ref, bias_near_ref, *refs):
    far_refs, near_refs = (first_far, last_far), (first_near, last_near)
    before = refs[: len(refs) - 11]
    out_ref, dn_ref, far_grad_ref, near_grad_ref, bias_far_grad_ref, bias_near_grad_ref = refs[-11:-5]
    weights, far_sum, near_sum, held, sems = refs[-5:]
    plane = weights.shape[2]
    last = (((1,), (1,)), ((), ()))
    first = (((0,), (0,)), ((), ()))
    loads = [
        [
            pltpu.make_async_copy(source, weights.at[side, kind, k], sems.at[side, 2 * k + kind])
            for kind, k, source in gathered_parts(plane, refs_of, 0, weights.shape[4])
        ]
        for side, refs_of in enumerate((far_refs, near_refs))
    ]
    fetches = [pltpu.make_async_copy(ref, held.at[k], sems.at[2, k]) for k, ref in enumerate(before)]
    for copy in loads[0] + loads[1] + fetches:
        copy.start()
    normed, d_out = n_ref[...], dy_ref[...]
    units = far_sum.shape[1]
    out, d_normed = 0.0, 0.0
    stores = []
    for side, (bias_ref, bias_grad_ref, buffer, grad_ref) in enumerate(
        (
            (bias_far_ref, bias_far_grad_ref, far_sum, far_grad_ref),
            (bias_near_ref, bias_near_grad_ref, near_sum, near_grad_ref),
        )
    ):
        for copy in loads[side]:
            copy.wait()
        up, down = weights[side, 0].reshape(units, D), weights[side, 1].reshape(units, D)
        hidden = lax.dot_general(normed, up, last, preferred_element_type=f32) + bias_ref[...]
        share = 0.5 * (1.0 + lax.erf(hidden * (0.5**0.5)))
        slope = share + hidden * (jnp.exp(-0.5 * hidden * hidden) * (0.5 / 3.141592653589793) ** 0.5)
        active = (hidden * share).astype(low)
        d_active = lax.dot_general(d_out, down, last, preferred_element_type=f32)
        d_hidden = (d_active * slope).astype(low)
        for k, part in enumerate(
            (
                lax.dot_general(d_hidden, normed, first, preferred_element_type=f32),
                lax.dot_general(active, d_out, first, preferred_element_type=f32),
            )
        ):
            buffer[k] = part.astype(buffer.dtype)
            copy = pltpu.make_async_copy(buffer.at[k], grad_ref.at[k], sems.at[3, 2 * side + k])
            copy.start()
            stores.append(copy)
        bias_grad_ref[...] = jnp.sum(d_hidden.astype(f32), axis=0, keepdims=True)
        out = out + jnp.dot(active, down, preferred_element_type=f32)
        d_normed = d_normed + jnp.dot(d_hidden, up, preferred_element_type=f32)
    for copy in fetches:
        copy.wait()
    out_ref[...] = held[0] + out if before else out
    dn_ref[...] = held[1] + d_normed if before else d_normed
    for copy in stores:
        copy.wait()


def feed(normed, d_out, far, near, bias_far, bias_near, rows, before):
    tokens = normed.shape[0]
    plane, depth = 2 * far[0].shape[1], far[0].shape[2]
    units = plane * depth * rows
    before = before or []
    vmem, hbm = pl.BlockSpec(memory_space=pltpu.VMEM), pl.BlockSpec(memory_space=pl.ANY)
    return pl.pallas_call(
        feed_kernel,
        in_specs=[vmem, vmem, hbm, hbm, hbm, hbm, vmem, vmem] + [hbm] * len(before),
        out_specs=[vmem, vmem, hbm, hbm, vmem, vmem],
        out_shape=[
            jax.ShapeDtypeStruct((tokens, D), f32),
            jax.ShapeDtypeStruct((tokens, D), f32),
            jax.ShapeDtypeStruct((2, units, D), low),
            jax.ShapeDtypeStruct((2, units, D), f32),
            jax.ShapeDtypeStruct((1, units), f32),
            jax.ShapeDtypeStruct((1, units), f32),
        ],
        scratch_shapes=[
            pltpu.VMEM((2, 2, plane, depth, rows, D), low),
            pltpu.VMEM((2, units, D), low),
            pltpu.VMEM((2, units, D), f32),
            pltpu.VMEM((2, tokens, D), f32),
            pltpu.SemaphoreType.DMA((4, 2 * plane)),
        ],
        compiler_params=pltpu.CompilerParams(vmem_limit_bytes=FEED_VMEM),
        cost_estimate=pl.CostEstimate(flops=4 * 24 * tokens * units * D, bytes_accessed=8 << 20, transcendentals=0),
        name="feed",
    )(normed, d_out, *far, *near, bias_far, bias_near, *before)


def head_kernel(
    vec_len, offset, out_rows, device_ref, x_ref, first_near, last_near, first_far, last_far, cos_ref, sin_ref, n_one_ref,
    n_two_ref, q_ref, kv_ref, w_ref, gain_ref, bias_ref, *refs
):
    *bias_refs, out_ref, flat, units, held, pieces_of, outs_of, sems = refs if out_rows else (*refs[:-6], None, *refs[-6:])
    _, _, plane, depth, size, _ = held.shape
    copies = [
        pltpu.make_async_copy(source, held.at[side, kind, k], sems.at[side, 2 * k + kind])
        for side, refs_of in enumerate(((first_near, last_near), (first_far, last_far)))
        for kind, k, source in gathered_parts(plane, refs_of, offset, size)
    ]
    for copy in copies:
        copy.start()
    x = x_ref[...].astype(f32)
    center = x - jnp.mean(x, axis=-1, keepdims=True)
    xhat = center * lax.rsqrt(jnp.mean(center * center, axis=-1, keepdims=True) + layer_eps)
    for copy in copies:
        copy.wait()
    for side in range(2):
        for k in range(plane):
            for z in range(depth):
                number = device_ref[(side * plane + k) * depth + z]
                pieces_of[number] = held[side, 0, k, z].astype(f32)
                if out_rows:
                    outs_of[number] = held[side, 1, k, z][:out_rows].astype(f32)
    if out_rows:
        out_ref[...] = outs_of[...].reshape(out_ref.shape).astype(low)
    shards_of = (flat.shape[1]) // vec_len
    rows = (D + 2 * HEAD) // shards_of
    whole = pieces_of[...].reshape(shards_of, -1, D)
    for s in range(shards_of):
        left, row = vec_len, rows
        while left > 0:
            size = min(left, D)
            begin = s * vec_len + (row - rows) * D
            flat[:, begin : begin + size] = whole[s, row : row + 1, :size]
            left -= size
            row += 1
    vector = lambda begin, size: flat[:, begin : begin + size]
    gain_one, shift_one, gain_two, shift_two = [vector(k * D, D) for k in range(4)]
    gain_ref[0:1] = gain_one
    gain_ref[1:2] = gain_two
    qkv_bias = vector(4 * D, D + 2 * HEAD)
    start = 4 * D + D + 2 * HEAD
    bias_ref[...] = vector(start, D) + vector(start + D + FF, D)
    count, size_of = units.shape
    for k in range(count):
        units[k : k + 1, :] = vector(start + D + k * size_of, size_of)
    groups = len(bias_refs) // 2
    for k, ref in enumerate(bias_refs):
        side, g = k // groups, k % groups
        width = size_of // groups
        for i in range(count // 2):
            row = units[pl.ds(device_ref[side * (count // 2) + i], 1), :]
            ref[:, i * width : (i + 1) * width] = row[:, g * width : (g + 1) * width]
    n_one = (xhat * gain_one + shift_one).astype(low)
    n_one_ref[...] = n_one
    n_two_ref[...] = (xhat * gain_two + shift_two).astype(low)
    weight = whole[:, :rows].reshape(shards_of * rows, D).astype(low)
    w_ref[...] = weight
    column = jnp.broadcast_to(qkv_bias, (8, qkv_bias.shape[1])).T[:, 0:1]
    projected = lax.dot_general(weight, n_one, (((1,), (1,)), ((), ())), preferred_element_type=f32) + column
    cosine, sine = cos_ref[...], sin_ref[...]
    half = ROT // 2

    def turned(first):
        a, b = projected[first : first + half], projected[first + half : first + ROT]
        rest = projected[first + ROT : first + HEAD]
        return jnp.concatenate([a * cosine - b * sine, b * cosine + a * sine, rest], axis=0).astype(low)

    for h in range(HEADS):
        q_ref[h * HEAD : (h + 1) * HEAD, :] = turned(h * HEAD) * jnp.asarray(HEAD ** (-0.5), low)
    kv_ref[:HEAD, :] = turned(D)
    kv_ref[HEAD:, :] = projected[D + HEAD :].astype(low)


def head(device, x, near, far, offset, size, out_rows, cosine, sine, groups, vec_len, shards_of):
    tokens = x.shape[0]
    count = device.shape[0]
    plane, depth = 2 * near[0].shape[1], near[0].shape[2]
    vmem, hbm = pl.BlockSpec(memory_space=pltpu.VMEM), pl.BlockSpec(memory_space=pl.ANY)
    return pl.pallas_call(
        functools.partial(head_kernel, vec_len, offset, out_rows),
        in_specs=[pl.BlockSpec(memory_space=pltpu.SMEM), vmem, hbm, hbm, hbm, hbm, vmem, vmem],
        out_shape=[
            jax.ShapeDtypeStruct((tokens, D), low),
            jax.ShapeDtypeStruct((tokens, D), low),
            jax.ShapeDtypeStruct((D, tokens), low),
            jax.ShapeDtypeStruct((2 * HEAD, tokens), low),
            jax.ShapeDtypeStruct((D + 2 * HEAD, D), low),
            jax.ShapeDtypeStruct((2, D), f32),
            jax.ShapeDtypeStruct((1, D), f32),
        ]
        + [jax.ShapeDtypeStruct((1, FF // 2 // groups), f32)] * (2 * groups)
        + [jax.ShapeDtypeStruct((D, D), low)] * (out_rows > 0),
        scratch_shapes=[
            pltpu.VMEM((1, shards_of * vec_len), f32),
            pltpu.VMEM((count, FF // count), f32),
            pltpu.VMEM((2, 2, plane, depth, size, D), low),
            pltpu.VMEM((count, size, D), f32),
            pltpu.VMEM((count, max(out_rows, 8), D), f32),
            pltpu.SemaphoreType.DMA((2, 2 * plane)),
        ],
        compiler_params=pltpu.CompilerParams(vmem_limit_bytes=FEED_VMEM),
        cost_estimate=pl.CostEstimate(flops=4 * 2 * tokens * 896 * D, bytes_accessed=8 << 20, transcendentals=0),
        name="head",
    )(device, x, *near, *far, cosine, sine)


def tail_kernel(
    shards_of, entry_ref, x_ref, dy_ref, dq_ref, dkv_ref, cos_ref, sin_ref, w_ref, n_ref, context_ref, d_two_ref, gain_ref, *refs
):
    bias_refs, (in_grad_ref, qkv_ref, out_ref, flat, units) = refs[:-5], refs[-5:]
    d_kv = dkv_ref[...]
    a, b = d_kv[: ROT // 2], d_kv[ROT // 2 : ROT]
    cosine, sine = cos_ref[...], sin_ref[...]
    d_kv = jnp.concatenate([a * cosine + b * sine, b * cosine - a * sine, d_kv[ROT:]], axis=0).astype(low)
    d_proj = jnp.concatenate([dq_ref[...], d_kv], axis=0)
    first = (((0,), (0,)), ((), ()))
    qkv_grad = jnp.dot(d_proj, n_ref[...], preferred_element_type=f32)
    out_grad = lax.dot_general(dy_ref[...], context_ref[...], first, preferred_element_type=f32)
    d_one = lax.dot_general(d_proj, w_ref[...], first, preferred_element_type=f32)
    d_two = d_two_ref[...]
    x = x_ref[...].astype(f32)
    dy = dy_ref[...].astype(f32)
    center = x - jnp.mean(x, axis=-1, keepdims=True)
    inv_sigma = lax.rsqrt(jnp.mean(center * center, axis=-1, keepdims=True) + layer_eps)
    xhat = center * inv_sigma
    d_hat = d_one * gain_ref[0:1] + d_two * gain_ref[1:2]
    d_in = (
        d_hat - jnp.mean(d_hat, axis=-1, keepdims=True) - xhat * jnp.mean(d_hat * xhat, axis=-1, keepdims=True)
    ) * inv_sigma
    in_grad_ref[...] = (dy + d_in).astype(low)
    columns = lambda v: jnp.sum(v, axis=0, keepdims=True)
    dy_column = columns(dy)
    ones = jnp.ones((8, d_proj.shape[1]), low)
    proj_sum = lax.dot_general(ones, d_proj, (((1,), (1,)), ((), ())), preferred_element_type=f32)[0:1]
    pieces = [columns(d_one * xhat), columns(d_one), columns(d_two * xhat), columns(d_two)]
    pieces += [proj_sum, dy_column, None, dy_column]
    count, size = units.shape
    groups = len(bias_refs) // 2
    width = size // groups
    for k, ref in enumerate(bias_refs):
        side, g = k // groups, k % groups
        for i in range(count // 2):
            place = side * (count // 2) + i
            units[place : place + 1, g * width : (g + 1) * width] = ref[:, i * width : (i + 1) * width]
    offset = 0
    for piece in pieces:
        if piece is None:
            for k in range(count):
                flat[:, offset : offset + size] = units[pl.ds(entry_ref[k], 1), :]
                offset += size
        else:
            flat[:, offset : offset + piece.shape[1]] = piece
            offset += piece.shape[1]
    qkv_rows, vec_len = qkv_grad.shape[0] // shards_of, flat.shape[1] // shards_of
    to_shard = count // shards_of
    share = lambda k, total: [k // to_shard * total + min(-(-total // to_shard) * j, total) for j in (k % to_shard, k % to_shard + 1)]
    out_own = D // count
    vec_row = qkv_ref.shape[1] - 4
    for k in range(count):
        to = entry_ref[k]
        begin, end = share(k, qkv_rows)
        qkv_ref[to] = jnp.zeros(qkv_ref.shape[1:], f32)
        if end > begin:
            qkv_ref[to, : end - begin, :] = qkv_grad[begin:end]
        begin, end = share(k, vec_len)
        if end > begin:
            qkv_ref[to, vec_row : vec_row + 1, : end - begin] = flat[:, begin:end]
        out_ref[to] = jnp.zeros(out_ref.shape[1:], f32)
        out_ref[to, :out_own, :] = out_grad[k * out_own : (k + 1) * out_own]


def tail(entry, x, dy, dq_t, dkv, cosine, sine, weight, normed, context, d_two, gains, bias_grads, rows, shards_of, vec_len):
    tokens = x.shape[0]
    count = entry.shape[0]
    operands = (entry, x, dy, dq_t, dkv, cosine, sine, weight, normed, context, d_two, gains, *sum(bias_grads, []))
    return pl.pallas_call(
        functools.partial(tail_kernel, shards_of),
        in_specs=[pl.BlockSpec(memory_space=pltpu.SMEM)] + [pl.BlockSpec(memory_space=pltpu.VMEM)] * (len(operands) - 1),
        out_shape=[
            jax.ShapeDtypeStruct((tokens, D), low),
            jax.ShapeDtypeStruct((count, rows, D), f32),
            jax.ShapeDtypeStruct((count, rows, D), f32),
        ],
        scratch_shapes=[pltpu.VMEM((1, shards_of * vec_len), f32), pltpu.VMEM((count, FF // count), f32)],
        compiler_params=pltpu.CompilerParams(vmem_limit_bytes=VMEM_LIMIT),
        cost_estimate=pl.CostEstimate(flops=4 * 6 * tokens * 896 * D, bytes_accessed=8 << 20, transcendentals=0),
        name="tail",
    )(*operands)


def split_low(value):
    high = value.astype(low)
    return high, (value - high.astype(f32)).astype(low)


def update_step(across, grad, high, rest, w_ref, first_ref, second_ref, grad_ref, first_new_ref, second_new_ref, w_new_ref):
    rotated = jnp.dot(grad, high, preferred_element_type=f32) + jnp.dot(grad, rest, preferred_element_type=f32)
    grad = grad.astype(f32)
    if across:
        rotated, grad = rotated.T, grad.T
    grad_ref[...] = grad
    ratio, first_new, second_new = moments(rotated, first_ref[...], second_ref[...])
    first_new_ref[...] = first_new
    second_new_ref[...] = second_new
    r_high, r_rest = split_low(ratio)
    if across:
        product = lambda r, b: jnp.dot(b, r, preferred_element_type=f32)
    else:
        product = lambda r, b: lax.dot_general(r, b, (((1,), (1,)), ((), ())), preferred_element_type=f32)
    unrotated = product(r_high, high) + (product(r_high, rest) + product(r_rest, high))
    w_new_ref[...] = w_ref[...] - matrix_rate * unrotated


def update_kernel(across, grad_ref, high_ref, rest_ref, *refs):
    update_step(across, grad_ref[...], high_ref[...], rest_ref[...], *refs)


def update(grad, basis, weight, first, second, across=False):
    return pl.pallas_call(
        functools.partial(update_kernel, across),
        out_shape=[jax.ShapeDtypeStruct(weight.shape, f32)] * 4,
        compiler_params=pltpu.CompilerParams(vmem_limit_bytes=UPDATE_VMEM),
        cost_estimate=pl.CostEstimate(flops=10 * grad.shape[0] * D * D, bytes_accessed=8 << 20, transcendentals=0),
        name="update",
    )(grad, *basis, weight, first, second)


def shards(
    inputs,
    cotangent,
    doc_lengths,
    qkv_weight,
    out_weight,
    up_weight,
    down_weight,
    vectors,
    bases,
    qkv_first,
    out_first,
    up_first,
    down_first,
    vector_first,
    qkv_second,
    out_second,
    up_second,
    down_second,
    vector_second,
):
    seq_count, batch_count = lax.axis_size("seq"), lax.axis_size("batch")
    seq_index, batch_index = lax.axis_index("seq"), lax.axis_index("batch")
    row_count, shard_len = inputs.shape[:2]
    tokens = row_count * shard_len
    y_bit, *z_bits = bit_names("seq", seq_count)
    core_bit, *x_bits = bit_names("batch", batch_count)
    near = [core_bit] + x_bits[::-1] + [y_bit] + z_bits[::-1]
    depth = seq_count // 2
    plane = 2 ** (len(x_bits) + 1)
    x_low = inputs.reshape(tokens, D)
    dy = cotangent.reshape(tokens, D)

    first_pos = seq_index * shard_len
    query_pos = first_pos + jnp.arange(shard_len, dtype=jnp.int32)
    docs = doc_lengths.shape[1]
    earlier = jnp.arange(docs)[:, None] < jnp.arange(docs)[None, :]
    doc_starts = jnp.sum(jnp.where(earlier[None], doc_lengths[:, :, None], 0), axis=1)
    start = jnp.max(
        jnp.where(doc_starts[:, None, :] <= query_pos[None, :, None], doc_starts[:, None, :], 0), axis=-1
    )
    offsets = (query_pos[None, :] - start).reshape(tokens)
    inverse = 1.0 / rope_base ** (jnp.arange(0, ROT, 2).astype(f32) / ROT)
    angles = offsets.astype(f32)[None, :] * inverse[:, None]
    cosine, sine = jnp.cos(angles), jnp.sin(angles)
    start_here = (start - first_pos).astype(jnp.int32)[:, None, :]
    number = jnp.arange(seq_count * batch_count, dtype=jnp.int32)

    def bits_of(value, place_of):
        total = 0
        for k, (axis_name, step) in enumerate(near[::-1]):
            total = total + place_of(value, k, axis_name, step)
        return total

    differs = {"seq": (number // batch_count) ^ seq_index, "batch": (number % batch_count) ^ batch_index}
    entry = bits_of(number, lambda v, k, name, step: (differs[name] // step) % 2 << k).astype(jnp.int32)
    xor_of = lambda name: sum((number >> k) % 2 * step for k, (axis_name, step) in enumerate(near[::-1]) if axis_name == name)
    device = ((xor_of("seq") ^ seq_index) * batch_count + (xor_of("batch") ^ batch_index)).astype(jnp.int32)

    qkv_rows, out_rows, up_rows, vec_len = qkv_weight.shape[0], out_weight.shape[0], up_weight.shape[0], vectors.shape[0]
    vec_rows = -(-vec_len // D)
    used = qkv_rows + vec_rows
    head_rows = -(-used // (8 * batch_count)) * 8 * batch_count
    vec_pad = vec_rows * D - vec_len

    def own_part(rows):
        size = rows.shape[0] // batch_count
        return lax.dynamic_slice_in_dim(rows, batch_index * size, size, axis=0)

    head_shard = jnp.concatenate(
        [qkv_weight, jnp.pad(vectors, (0, vec_pad)).reshape(vec_rows, D), jnp.zeros((head_rows - used, D), f32)], axis=0
    ).astype(low)
    head_part_rows = head_rows // batch_count
    unit_rows = up_rows // batch_count // GROUPS
    out_own = out_rows // batch_count
    up_low, down_low = own_part(up_weight.astype(low)), own_part(down_weight.T.astype(low))
    outer = [
        own_part(head_shard),
        jnp.concatenate([own_part(out_weight.astype(low)), jnp.zeros((head_part_rows - out_own, D), low)], axis=0),
    ]
    parts_of = []
    for g in range(GROUPS):
        rows = slice(g * unit_rows, (g + 1) * unit_rows)
        pieces = [up_low[rows], outer[0], down_low[rows], outer[1]] if g == 0 else [up_low[rows], down_low[rows]]
        parts_of.append(jnp.concatenate(pieces, axis=0))

    def gather_first(parts):
        half = parts.shape[1] // 2
        up, down = parts[:, :half], parts[:, half:]
        for bit in x_bits[:-1]:
            down = gather_bit(down, bit, 0)
        return up, down, swap(up, y_bit), swap(down, x_bits[-1])

    def gather_second(up, down, up_got, down_got):
        up, down = jnp.stack([up, up_got]), jnp.stack([down, down_got])
        for bit in x_bits[:-1]:
            up = gather_bit(up, bit, 0)
        shape = (1, plane // 2, depth) + up.shape[-2:]
        return up, down, jnp.concatenate([up.reshape(shape), down.reshape(shape)], axis=0)

    def gather_last(up, down):
        return swap(up, x_bits[-1]), swap(down, y_bit)

    def joined(up, down):
        shape = (1, plane // 2, depth) + up.shape[-2:]
        return jnp.concatenate([up.reshape(shape), down.reshape(shape)], axis=0)

    z_zero = gather_z(parts_of[0])
    *z_zero, cosine, sine, start_here, entry, device, part_one = hold(
        *z_zero, cosine, sine, start_here, entry, device, parts_of[1]
    )
    up, down, up_got, down_got = gather_first(jnp.stack(z_zero))
    z_one = gather_z(part_one)
    up_got, down_got, z_one[1] = hold(up_got, down_got, z_one[1])
    up, down, first_zero = gather_second(up, down, up_got, down_got)
    up_got, down_got = gather_last(up, down)
    first_far_zero = swap(first_zero, core_bit)
    late_bases, up, down = hold(bases, up, down)
    split_bases = [part for k in range(4) for part in split_low(late_bases[k])]
    up_got, down_got, first_far_zero, *rest = hold(up_got, down_got, first_far_zero, *z_one[2:], *split_bases)
    z_one[2:], split_bases = rest[: len(z_one) - 2], rest[len(z_one) - 2 :]
    split_bases = [split_bases[2 * k : 2 * k + 2] for k in range(4)]
    last_zero = joined(up_got, down_got)
    last_far_zero = swap(last_zero, core_bit)

    aligned = unit_rows % 16 == 0 and head_part_rows % 16 == 0
    trim = lambda values, begin, end: values if aligned else tuple(v[..., begin:end, :] for v in values)
    near_zero, far_zero = (first_zero, last_zero), (first_far_zero, last_far_zero)
    end = unit_rows + head_part_rows

    inside = out_own % 8 == 0
    normed_one, normed_two, q_t, kv_own, qkv_full, gains, out_bias, *bias_rows = head(
        device, x_low, trim(near_zero, unit_rows, end), trim(far_zero, unit_rows, end), unit_rows if aligned else 0,
        head_part_rows, out_own if inside else 0, cosine, sine, GROUPS, vec_len, seq_count,
    )
    if inside:
        out_full = bias_rows.pop()
    else:
        chosen = (entry[:, None] == number[None, :]).astype(low)
        sides = []
        for pair in (near_zero, far_zero):
            along = [v[1, :, :, unit_rows : unit_rows + out_own] for v in pair]
            sides.append(jnp.stack(along, axis=1).reshape(-1, out_own * D))
        out_full = jnp.dot(chosen, jnp.concatenate(sides, axis=0), preferred_element_type=f32).astype(low).reshape(D, D)
    bias_rows = [bias_rows[:GROUPS], bias_rows[GROUPS:]]
    reach = seq_count // 2

    def shifted(value, step, back=False):
        pairs = [(j, j + step) for j in range(seq_count - step)]
        return lax.ppermute(value, "seq", [(b, a) for a, b in pairs] if back else pairs)

    farthest, pair = shifted(kv_own, reach), shifted(kv_own[None], 1)
    up, down, up_got, down_got = gather_first(jnp.stack(z_one))
    up_got, down_got, normed_two = hold(up_got, down_got, normed_two)
    up, down, first_one = gather_second(up, down, up_got, down_got)
    up_got, down_got = gather_last(up, down)
    first_far_one = swap(first_one, core_bit)

    last = (((1,), (1,)), ((), ()))
    bias_grads = [[], []]

    def feed_group(g, sums, normed, near, far, *beside):
        *sums, far_grad, near_grad, bias_far, bias_here = feed(
            normed, dy, trim(far, 0, unit_rows), trim(near, 0, unit_rows), bias_rows[1][g], bias_rows[0][g], unit_rows, sums
        )
        bias_grads[0].append(bias_here)
        bias_grads[1].append(bias_far)
        far_grad, *beside = hold(far_grad, *beside)
        shape = (2,) + (2,) * len(x_bits) + (2, depth, unit_rows, D)
        grad_sum = (near_grad + swap(far_grad, core_bit).astype(f32)).reshape(shape)
        return sums, grad_sum[0], grad_sum[1], *beside

    def sum_first(up, down):
        (up_kept, up_sent), (down_kept, down_sent) = split_bit(up, x_bits[-1], 0), split_bit(down, y_bit, len(x_bits))
        return up_kept, up_sent, down_kept, down_sent

    def send_first(sums):
        return swap(sums[1], x_bits[-1]), swap(sums[3], y_bit)

    def sum_second(sums, up_got, down_got):
        up = sums[0] + up_got.astype(f32)
        for bit in x_bits[-2::-1]:
            kept, sent = split_bit(up, bit, 0)
            up = kept + swap(sent, bit).astype(f32)
        down = sums[2] + down_got.astype(f32)
        (up_kept, up_sent), (down_kept, down_sent) = split_bit(up, y_bit, 0), split_bit(down, x_bits[-1], 0)
        return up_kept, up_sent, down_kept, down_sent

    def send_second(sums):
        return swap(sums[1], y_bit), swap(sums[3], x_bits[-1])

    def sum_third(up_kept, up_got, down_kept, down_got):
        up = up_kept + up_got.astype(f32)
        down = down_kept + down_got.astype(f32)
        for bit in x_bits[-2::-1]:
            kept, sent = split_bit(down, bit, 0)
            down = kept + swap(sent, bit).astype(f32)
        return jnp.concatenate([up, down], axis=1)

    def send_z(value):
        return [swap_z(value[k].astype(low), k) for k in range(1, depth)]

    def sum_z(value, got):
        return value[0] + sum(part.astype(f32) for part in got)

    def spread(part):
        value = part.astype(low)
        for bit in x_bits:
            value = gather_bit(value, bit, 0, True)
        return gather_bit(value, core_bit, len(x_bits), True).reshape(batch_count, -1, D)

    sums, up_sum, down_sum, up_got, down_got, farthest, pair = feed_group(
        0, None, normed_two, near_zero, far_zero, up_got, down_got, farthest, pair
    )
    kv = jnp.concatenate([kv_own[None], pair], axis=0)
    while kv.shape[0] < reach:
        kv = jnp.concatenate([kv, shifted(kv, kv.shape[0])], axis=0)
    kv = jnp.concatenate([kv, farthest[None]], axis=0)
    sum_zero = sum_first(up_sum, down_sum)
    *sum_zero, first_far_one, q_t = hold(*sum_zero, first_far_one, q_t)
    last_one = joined(up_got, down_got)
    last_far_one = swap(last_one, core_bit)

    do_t = lax.dot_general(out_full, dy, (((0,), (1,)), ((), ())), preferred_element_type=f32).astype(low)
    context, dq_t, dkv_own, dkv_sent = attention(q_t, do_t, start_here, cosine, sine, kv)
    sum_zero = sum_second(sum_zero, *send_first(sum_zero))
    last_far_one, dq_t, normed_late, *sum_zero = hold(last_far_one, dq_t, normed_two, *sum_zero)
    dkv_far = shifted(dkv_sent[reach - 1], reach, True)
    dkv = jnp.concatenate([dkv_own[None], dkv_sent[: reach - 1].astype(f32)], axis=0)
    middle = reach // 2
    got = shifted(dkv[middle:].astype(low), middle, True)
    up_got, down_got = send_second(sum_zero)
    (mlp_out, d_normed_two), up_sum, down_sum, up_got, down_got, dkv_far, got = feed_group(
        1, sums, normed_late, (first_one, last_one), (first_far_one, last_far_one), up_got, down_got, dkv_far, got
    )
    sum_zero = sum_third(sum_zero[0], up_got, sum_zero[2], down_got)
    dkv = dkv[:middle] + got.astype(f32)
    while dkv.shape[0] > 1:
        middle = dkv.shape[0] // 2
        got = shifted(dkv[middle:].astype(low), middle, True)
        dkv = dkv[:middle] + got.astype(f32)
    dkv = dkv[0] + dkv_far.astype(f32)
    qkv_share, vec_share = -(-qkv_rows // batch_count), -(-vec_len // batch_count)
    sum_one = sum_first(up_sum, down_sum)
    dkv, *sum_one = hold(dkv, *sum_one)
    up_got, down_got = send_first(sum_one)
    z_got = send_z(sum_zero)
    input_grad, qkv_part, out_part = tail(
        entry, x_low, dy, dq_t, dkv, cosine, sine, qkv_full, normed_one, context, d_normed_two, gains, bias_grads,
        head_part_rows, seq_count, vec_len,
    )
    qkv_part, up_got, down_got, *z_got = hold(qkv_part, up_got, down_got, *z_got)
    sum_one = sum_second(sum_one, up_got, down_got)
    one_got = send_second(sum_one)
    outer = jnp.stack([qkv_part, out_part]).reshape((2, 2) + (2,) * len(x_bits) + (2, depth, head_part_rows, D))
    got = swap(outer[:, 1].astype(low), core_bit)
    got, *one_got = hold(got, *one_got)
    outer = outer[:, 0] + got.astype(f32)
    sum_outer = sum_first(outer[0], outer[1])
    outer_got = send_first(sum_outer)
    sum_one = sum_third(sum_one[0], one_got[0], sum_one[2], one_got[1])
    one_got = send_z(sum_one)
    grads_zero = spread(sum_z(sum_zero, z_got))
    attn_out = lax.dot_general(context, out_full, last, preferred_element_type=f32)
    outputs = (x_low.astype(f32) + attn_out + mlp_out + out_bias).astype(low)
    sum_outer = sum_second(sum_outer, *outer_got)
    outer_got = send_second(sum_outer)
    outer_got, one_got, (outputs, grads_zero) = hold_lists(outer_got, one_got, [outputs, grads_zero])
    sum_outer = sum_third(sum_outer[0], outer_got[0], sum_outer[2], outer_got[1])
    outer_got = send_z(sum_outer)
    grads_one = spread(sum_z(sum_one, one_got))
    up_all = jnp.concatenate([grads_zero[:, :unit_rows], grads_one[:, :unit_rows]], axis=1).reshape(-1, D)
    down_all = jnp.concatenate([grads_zero[:, unit_rows:], grads_one[:, unit_rows:]], axis=1).reshape(-1, D)
    up_out = update(up_all, split_bases[2], up_weight, up_first, up_second)
    up_out, outer_got = hold_lists(up_out, outer_got)
    grads_outer = spread(sum_z(sum_outer, outer_got))
    down_out = update(down_all, split_bases[3], down_weight, down_first, down_second, True)
    down_out, grads_outer = hold_lists(down_out, [grads_outer])
    grads_outer = grads_outer[0]
    (up_grad, *up_states), (down_grad, *down_states) = up_out, down_out
    qkv_all = grads_outer[:, :qkv_share].reshape(-1, D)[:qkv_rows]
    out_all = grads_outer[:, head_part_rows : head_part_rows + out_own].reshape(-1, D)
    vector_grad = grads_outer[:, head_part_rows - 4, :vec_share].astype(f32).reshape(-1)[:vec_len]
    out_grad, *out_states = update(out_all, split_bases[1], out_weight, out_first, out_second)
    qkv_grad, *qkv_states = update(qkv_all, split_bases[0], qkv_weight, qkv_first, qkv_second)
    vector_new, *vector_states = adam_step(vectors, vector_grad, vector_first, vector_second)
    states = (qkv_states, out_states, up_states, down_states, (*vector_states, vector_new))
    return (
        outputs.reshape(inputs.shape),
        input_grad.reshape(inputs.shape),
        qkv_grad,
        out_grad,
        up_grad,
        down_grad,
        vector_grad,
        *(state[0] for state in states),
        *(state[1] for state in states),
        *(state[2] for state in states),
    )


def solution(mesh):
    tokens = P("batch", "seq", None)
    rows, columns, flat = P("seq", None), P(None, "seq"), P("seq")
    params = (rows, rows, rows, columns, flat)
    return jax.shard_map(
        shards,
        mesh=mesh,
        in_specs=(tokens, tokens, P("batch", None)) + params + (P(),) + params + params,
        out_specs=(tokens, tokens) + params * 4,
        check_vma=False,
    )
```

```python
import functools

import jax
import jax.numpy as jnp
from jax import lax
from jax.experimental import pallas as pl
from jax.experimental.pallas import tpu as pltpu
from jax.sharding import PartitionSpec as P

D = 768
HEADS = 12
HEAD = 64
ROT = 16
FF = 3072
STEP = 10

layer_eps = 1e-05
adam_eps = 1e-08
beta_first = 0.95
beta_second = 0.95
matrix_rate = 0.08
vector_rate = 0.3
rope_base = 10000.0
masked_score = -1e30
low = jnp.bfloat16
f32 = jnp.float32
VMEM_LIMIT = 56 * 1024 * 1024
GROUPS = 2
FEED_VMEM = 56 * 1024 * 1024
UPDATE_VMEM = 28 * 1024 * 1024


def swap(value, bit):
    axis, step = bit
    return lax.ppermute(value, axis, [(i, i ^ step) for i in range(lax.axis_size(axis))])


def mine(bit):
    axis, step = bit
    return lax.rem(lax.axis_index(axis) // step, 2)


def hold(*values):
    return lax.optimization_barrier(values)


def hold_lists(*lists):
    flat = iter(hold(*(value for values in lists for value in values)))
    return [[next(flat) for _ in values] for values in lists]


def swap_z(value, step):
    size = lax.axis_size("seq")
    return lax.ppermute(value, "seq", [(i, i ^ (2 * step)) for i in range(size)])


def gather_z(piece):
    return [piece] + [swap_z(piece, k) for k in range(1, lax.axis_size("seq") // 2)]


def gather_bit(value, bit, axis, absolute=False):
    got = swap(value, bit)
    if absolute:
        upper = mine(bit) == 1
        return jnp.stack([jnp.where(upper, got, value), jnp.where(upper, value, got)], axis=axis)
    return jnp.stack([value, got], axis=axis)


def split_bit(value, bit, axis):
    return lax.index_in_dim(value, 0, axis, keepdims=False), lax.index_in_dim(value, 1, axis, keepdims=False).astype(low)


def bit_names(axis, size):
    return [(axis, 1 << k) for k in range(size.bit_length() - 1)]


def moments(rotated, first, second):
    new_first = beta_first * first + (1.0 - beta_first) * rotated
    new_second = beta_second * second + (1.0 - beta_second) * rotated * rotated
    first_scale, second_scale = 1.0 / (1.0 - beta_first**STEP), 1.0 / (1.0 - beta_second**STEP)
    ratio = new_first * first_scale / (jnp.sqrt(new_second * second_scale) + adam_eps)
    return ratio, new_first, new_second


def adam_step(weight, grad, first, second):
    ratio, new_first, new_second = moments(grad, first, second)
    return (weight - vector_rate * ratio, new_first, new_second)


def attention_kernel(blocks, width, q_ref, do_ref, start_ref, cos_ref, sin_ref, kv_ref, context_ref, dq_ref, dkv_own_ref, dkv_ref):
    length = q_ref.shape[1]
    keys = blocks * length
    key_t = jnp.concatenate([kv_ref[k, :HEAD, :] for k in reversed(range(blocks))], axis=1)
    value_t = jnp.concatenate([kv_ref[k, HEAD:, :] for k in reversed(range(blocks))], axis=1)
    key = key_t.astype(f32).T.astype(low)
    value = value_t.astype(f32).T.astype(low)
    key_pos = lax.broadcasted_iota(jnp.int32, (keys, length), 0) - (blocks - 1) * length
    query_pos = lax.broadcasted_iota(jnp.int32, (keys, length), 1)
    allowed = (key_pos >= start_ref[0]) & (key_pos <= query_pos)
    bias = jnp.where(allowed, 0.0, masked_score)
    cosine, sine = cos_ref[...], sin_ref[...]
    d_key = jnp.zeros((keys, HEAD), f32)
    d_value = jnp.zeros((keys, HEAD), f32)
    last = (((1,), (1,)), ((), ()))
    for first in range(0, HEADS, width):
        heads = range(first, first + width)
        query = jnp.concatenate([q_ref[h * HEAD : (h + 1) * HEAD, :] for h in heads], axis=1)
        d_out = jnp.concatenate([do_ref[h * HEAD : (h + 1) * HEAD, :] for h in heads], axis=1)
        scores = jnp.dot(key, query, preferred_element_type=f32)
        scores = scores + jnp.concatenate([bias] * width, axis=1)
        weights = jnp.exp(scores - jnp.max(scores, axis=0, keepdims=True))
        probs = weights * (1.0 / jnp.sum(weights, axis=0, keepdims=True))
        probs_low = probs.astype(low)
        context_t = jnp.dot(value_t, probs_low, preferred_element_type=f32)
        d_probs = jnp.dot(value, d_out, preferred_element_type=f32)
        inner = jnp.sum(probs * d_probs, axis=0, keepdims=True)
        d_scores = (probs * (d_probs - inner)).astype(low)
        d_query = jnp.dot(key_t, d_scores, preferred_element_type=f32) * HEAD ** (-0.5)
        d_value = d_value + lax.dot_general(probs_low, d_out, last, preferred_element_type=f32)
        d_key = d_key + lax.dot_general(d_scores, query, last, preferred_element_type=f32)
        for k, h in enumerate(heads):
            lanes = slice(k * length, (k + 1) * length)
            part = d_query[:, lanes]
            a, b = part[: ROT // 2], part[ROT // 2 : ROT]
            turned = jnp.concatenate([a * cosine + b * sine, b * cosine - a * sine, part[ROT:]], axis=0)
            dq_ref[h * HEAD : (h + 1) * HEAD, :] = turned.astype(low)
        for k in range(0, width, 2):
            h = first + k
            two = jnp.concatenate(
                [context_t[:, k * length : (k + 1) * length], context_t[:, (k + 1) * length : (k + 2) * length]], axis=0
            )
            context_ref[:, h * HEAD : (h + 2) * HEAD] = two.T.astype(low)
    d_kv = jnp.concatenate([d_key, d_value], axis=1).T
    for k in range(blocks):
        part = d_kv[:, (blocks - 1 - k) * length : (blocks - k) * length]
        if k == 0:
            dkv_own_ref[...] = part
        else:
            dkv_ref[k - 1] = part.astype(low)


def attention(q_t, do_t, start, cosine, sine, kv):
    rows, _, length = start.shape
    blocks = kv.shape[0]
    tokens = q_t.shape[1]
    by_row = lambda height: pl.BlockSpec((height, length), lambda r: (0, r))
    return pl.pallas_call(
        functools.partial(attention_kernel, blocks, HEADS),
        grid=(rows,),
        in_specs=[by_row(D), by_row(D), pl.BlockSpec((1, 1, length), lambda r: (r, 0, 0)), by_row(ROT // 2), by_row(ROT // 2)]
        + [pl.BlockSpec((blocks, 2 * HEAD, length), lambda r: (0, 0, r))],
        out_specs=[
            pl.BlockSpec((length, D), lambda r: (r, 0)),
            by_row(D),
            by_row(2 * HEAD),
            pl.BlockSpec((blocks - 1, 2 * HEAD, length), lambda r: (0, 0, r)),
        ],
        out_shape=[
            jax.ShapeDtypeStruct((tokens, D), low),
            jax.ShapeDtypeStruct((D, tokens), low),
            jax.ShapeDtypeStruct((2 * HEAD, tokens), f32),
            jax.ShapeDtypeStruct((blocks - 1, 2 * HEAD, tokens), low),
        ],
        compiler_params=pltpu.CompilerParams(vmem_limit_bytes=VMEM_LIMIT),
        cost_estimate=pl.CostEstimate(
            flops=4 * 7 * tokens * HEADS * blocks * length * HEAD * 2, bytes_accessed=8 << 20, transcendentals=0
        ),
        name="attention",
    )(q_t, do_t, start, cosine, sine, kv)


def gathered_parts(plane, refs, offset, rows):
    half = plane // 2
    out = []
    for end, ref in enumerate(refs):
        for j in range(half):
            out.append((0, end * half + j, ref.at[0, j, :, pl.ds(offset, rows)]))
            out.append((1, 2 * j + end, ref.at[1, j, :, pl.ds(offset, rows)]))
    return out


def feed_kernel(n_ref, dy_ref, first_far, last_far, first_near, last_near, bias_far_ref, bias_near_ref, *refs):
    far_refs, near_refs = (first_far, last_far), (first_near, last_near)
    before = refs[: len(refs) - 11]
    out_ref, dn_ref, far_grad_ref, near_grad_ref, bias_far_grad_ref, bias_near_grad_ref = refs[-11:-5]
    weights, far_sum, near_sum, held, sems = refs[-5:]
    plane = weights.shape[2]
    last = (((1,), (1,)), ((), ()))
    first = (((0,), (0,)), ((), ()))
    loads = [
        [
            pltpu.make_async_copy(source, weights.at[side, kind, k], sems.at[side, 2 * k + kind])
            for kind, k, source in gathered_parts(plane, refs_of, 0, weights.shape[4])
        ]
        for side, refs_of in enumerate((far_refs, near_refs))
    ]
    fetches = [pltpu.make_async_copy(ref, held.at[k], sems.at[2, k]) for k, ref in enumerate(before)]
    for copy in loads[0] + loads[1] + fetches:
        copy.start()
    normed, d_out = n_ref[...], dy_ref[...]
    units = far_sum.shape[1]
    out, d_normed = 0.0, 0.0
    stores = []
    for side, (bias_ref, bias_grad_ref, buffer, grad_ref) in enumerate(
        (
            (bias_far_ref, bias_far_grad_ref, far_sum, far_grad_ref),
            (bias_near_ref, bias_near_grad_ref, near_sum, near_grad_ref),
        )
    ):
        for copy in loads[side]:
            copy.wait()
        up, down = weights[side, 0].reshape(units, D), weights[side, 1].reshape(units, D)
        hidden = lax.dot_general(normed, up, last, preferred_element_type=f32) + bias_ref[...]
        share = 0.5 * (1.0 + lax.erf(hidden * (0.5**0.5)))
        slope = share + hidden * (jnp.exp(-0.5 * hidden * hidden) * (0.5 / 3.141592653589793) ** 0.5)
        active = (hidden * share).astype(low)
        d_active = lax.dot_general(d_out, down, last, preferred_element_type=f32)
        d_hidden = (d_active * slope).astype(low)
        for k, part in enumerate(
            (
                lax.dot_general(d_hidden, normed, first, preferred_element_type=f32),
                lax.dot_general(active, d_out, first, preferred_element_type=f32),
            )
        ):
            buffer[k] = part.astype(buffer.dtype)
            copy = pltpu.make_async_copy(buffer.at[k], grad_ref.at[k], sems.at[3, 2 * side + k])
            copy.start()
            stores.append(copy)
        bias_grad_ref[...] = jnp.sum(d_hidden.astype(f32), axis=0, keepdims=True)
        out = out + jnp.dot(active, down, preferred_element_type=f32)
        d_normed = d_normed + jnp.dot(d_hidden, up, preferred_element_type=f32)
    for copy in fetches:
        copy.wait()
    out_ref[...] = held[0] + out if before else out
    dn_ref[...] = held[1] + d_normed if before else d_normed
    for copy in stores:
        copy.wait()


def feed(normed, d_out, far, near, bias_far, bias_near, rows, before):
    tokens = normed.shape[0]
    plane, depth = 2 * far[0].shape[1], far[0].shape[2]
    units = plane * depth * rows
    before = before or []
    vmem, hbm = pl.BlockSpec(memory_space=pltpu.VMEM), pl.BlockSpec(memory_space=pl.ANY)
    return pl.pallas_call(
        feed_kernel,
        in_specs=[vmem, vmem, hbm, hbm, hbm, hbm, vmem, vmem] + [hbm] * len(before),
        out_specs=[vmem, vmem, hbm, hbm, vmem, vmem],
        out_shape=[
            jax.ShapeDtypeStruct((tokens, D), f32),
            jax.ShapeDtypeStruct((tokens, D), f32),
            jax.ShapeDtypeStruct((2, units, D), low),
            jax.ShapeDtypeStruct((2, units, D), f32),
            jax.ShapeDtypeStruct((1, units), f32),
            jax.ShapeDtypeStruct((1, units), f32),
        ],
        scratch_shapes=[
            pltpu.VMEM((2, 2, plane, depth, rows, D), low),
            pltpu.VMEM((2, units, D), low),
            pltpu.VMEM((2, units, D), f32),
            pltpu.VMEM((2, tokens, D), f32),
            pltpu.SemaphoreType.DMA((4, 2 * plane)),
        ],
        compiler_params=pltpu.CompilerParams(vmem_limit_bytes=FEED_VMEM),
        cost_estimate=pl.CostEstimate(flops=4 * 24 * tokens * units * D, bytes_accessed=8 << 20, transcendentals=0),
        name="feed",
    )(normed, d_out, *far, *near, bias_far, bias_near, *before)


def head_kernel(
    vec_len, offset, out_rows, device_ref, x_ref, first_near, last_near, first_far, last_far, cos_ref, sin_ref, n_one_ref,
    n_two_ref, q_ref, kv_ref, w_ref, gain_ref, bias_ref, *refs
):
    *bias_refs, out_ref, flat, units, held, pieces_of, outs_of, sems = refs if out_rows else (*refs[:-6], None, *refs[-6:])
    _, _, plane, depth, size, _ = held.shape
    copies = [
        pltpu.make_async_copy(source, held.at[side, kind, k], sems.at[side, 2 * k + kind])
        for side, refs_of in enumerate(((first_near, last_near), (first_far, last_far)))
        for kind, k, source in gathered_parts(plane, refs_of, offset, size)
    ]
    for copy in copies:
        copy.start()
    x = x_ref[...].astype(f32)
    center = x - jnp.mean(x, axis=-1, keepdims=True)
    xhat = center * lax.rsqrt(jnp.mean(center * center, axis=-1, keepdims=True) + layer_eps)
    for copy in copies:
        copy.wait()
    for side in range(2):
        for k in range(plane):
            for z in range(depth):
                number = device_ref[(side * plane + k) * depth + z]
                pieces_of[number] = held[side, 0, k, z].astype(f32)
                if out_rows:
                    outs_of[number] = held[side, 1, k, z][:out_rows].astype(f32)
    if out_rows:
        out_ref[...] = outs_of[...].reshape(out_ref.shape).astype(low)
    shards_of = (flat.shape[1]) // vec_len
    rows = (D + 2 * HEAD) // shards_of
    whole = pieces_of[...].reshape(shards_of, -1, D)
    for s in range(shards_of):
        left, row = vec_len, rows
        while left > 0:
            size = min(left, D)
            begin = s * vec_len + (row - rows) * D
            flat[:, begin : begin + size] = whole[s, row : row + 1, :size]
            left -= size
            row += 1
    vector = lambda begin, size: flat[:, begin : begin + size]
    gain_one, shift_one, gain_two, shift_two = [vector(k * D, D) for k in range(4)]
    gain_ref[0:1] = gain_one
    gain_ref[1:2] = gain_two
    qkv_bias = vector(4 * D, D + 2 * HEAD)
    start = 4 * D + D + 2 * HEAD
    bias_ref[...] = vector(start, D) + vector(start + D + FF, D)
    count, size_of = units.shape
    for k in range(count):
        units[k : k + 1, :] = vector(start + D + k * size_of, size_of)
    groups = len(bias_refs) // 2
    for k, ref in enumerate(bias_refs):
        side, g = k // groups, k % groups
        width = size_of // groups
        for i in range(count // 2):
            row = units[pl.ds(device_ref[side * (count // 2) + i], 1), :]
            ref[:, i * width : (i + 1) * width] = row[:, g * width : (g + 1) * width]
    n_one = (xhat * gain_one + shift_one).astype(low)
    n_one_ref[...] = n_one
    n_two_ref[...] = (xhat * gain_two + shift_two).astype(low)
    weight = whole[:, :rows].reshape(shards_of * rows, D).astype(low)
    w_ref[...] = weight
    column = jnp.broadcast_to(qkv_bias, (8, qkv_bias.shape[1])).T[:, 0:1]
    projected = lax.dot_general(weight, n_one, (((1,), (1,)), ((), ())), preferred_element_type=f32) + column
    cosine, sine = cos_ref[...], sin_ref[...]
    half = ROT // 2

    def turned(first):
        a, b = projected[first : first + half], projected[first + half : first + ROT]
        rest = projected[first + ROT : first + HEAD]
        return jnp.concatenate([a * cosine - b * sine, b * cosine + a * sine, rest], axis=0).astype(low)

    for h in range(HEADS):
        q_ref[h * HEAD : (h + 1) * HEAD, :] = turned(h * HEAD) * jnp.asarray(HEAD ** (-0.5), low)
    kv_ref[:HEAD, :] = turned(D)
    kv_ref[HEAD:, :] = projected[D + HEAD :].astype(low)


def head(device, x, near, far, offset, size, out_rows, cosine, sine, groups, vec_len, shards_of):
    tokens = x.shape[0]
    count = device.shape[0]
    plane, depth = 2 * near[0].shape[1], near[0].shape[2]
    vmem, hbm = pl.BlockSpec(memory_space=pltpu.VMEM), pl.BlockSpec(memory_space=pl.ANY)
    return pl.pallas_call(
        functools.partial(head_kernel, vec_len, offset, out_rows),
        in_specs=[pl.BlockSpec(memory_space=pltpu.SMEM), vmem, hbm, hbm, hbm, hbm, vmem, vmem],
        out_shape=[
            jax.ShapeDtypeStruct((tokens, D), low),
            jax.ShapeDtypeStruct((tokens, D), low),
            jax.ShapeDtypeStruct((D, tokens), low),
            jax.ShapeDtypeStruct((2 * HEAD, tokens), low),
            jax.ShapeDtypeStruct((D + 2 * HEAD, D), low),
            jax.ShapeDtypeStruct((2, D), f32),
            jax.ShapeDtypeStruct((1, D), f32),
        ]
        + [jax.ShapeDtypeStruct((1, FF // 2 // groups), f32)] * (2 * groups)
        + [jax.ShapeDtypeStruct((D, D), low)] * (out_rows > 0),
        scratch_shapes=[
            pltpu.VMEM((1, shards_of * vec_len), f32),
            pltpu.VMEM((count, FF // count), f32),
            pltpu.VMEM((2, 2, plane, depth, size, D), low),
            pltpu.VMEM((count, size, D), f32),
            pltpu.VMEM((count, max(out_rows, 8), D), f32),
            pltpu.SemaphoreType.DMA((2, 2 * plane)),
        ],
        compiler_params=pltpu.CompilerParams(vmem_limit_bytes=FEED_VMEM),
        cost_estimate=pl.CostEstimate(flops=4 * 2 * tokens * 896 * D, bytes_accessed=8 << 20, transcendentals=0),
        name="head",
    )(device, x, *near, *far, cosine, sine)


def tail_kernel(
    shards_of, entry_ref, x_ref, dy_ref, dq_ref, dkv_ref, cos_ref, sin_ref, w_ref, n_ref, context_ref, d_two_ref, gain_ref, *refs
):
    bias_refs, (in_grad_ref, qkv_ref, out_ref, flat, units) = refs[:-5], refs[-5:]
    d_kv = dkv_ref[...]
    a, b = d_kv[: ROT // 2], d_kv[ROT // 2 : ROT]
    cosine, sine = cos_ref[...], sin_ref[...]
    d_kv = jnp.concatenate([a * cosine + b * sine, b * cosine - a * sine, d_kv[ROT:]], axis=0).astype(low)
    d_proj = jnp.concatenate([dq_ref[...], d_kv], axis=0)
    first = (((0,), (0,)), ((), ()))
    qkv_grad = jnp.dot(d_proj, n_ref[...], preferred_element_type=f32)
    out_grad = lax.dot_general(dy_ref[...], context_ref[...], first, preferred_element_type=f32)
    d_one = lax.dot_general(d_proj, w_ref[...], first, preferred_element_type=f32)
    d_two = d_two_ref[...]
    x = x_ref[...].astype(f32)
    dy = dy_ref[...].astype(f32)
    center = x - jnp.mean(x, axis=-1, keepdims=True)
    inv_sigma = lax.rsqrt(jnp.mean(center * center, axis=-1, keepdims=True) + layer_eps)
    xhat = center * inv_sigma
    d_hat = d_one * gain_ref[0:1] + d_two * gain_ref[1:2]
    d_in = (
        d_hat - jnp.mean(d_hat, axis=-1, keepdims=True) - xhat * jnp.mean(d_hat * xhat, axis=-1, keepdims=True)
    ) * inv_sigma
    in_grad_ref[...] = (dy + d_in).astype(low)
    columns = lambda v: jnp.sum(v, axis=0, keepdims=True)
    dy_column = columns(dy)
    ones = jnp.ones((8, d_proj.shape[1]), low)
    proj_sum = lax.dot_general(ones, d_proj, (((1,), (1,)), ((), ())), preferred_element_type=f32)[0:1]
    pieces = [columns(d_one * xhat), columns(d_one), columns(d_two * xhat), columns(d_two)]
    pieces += [proj_sum, dy_column, None, dy_column]
    count, size = units.shape
    groups = len(bias_refs) // 2
    width = size // groups
    for k, ref in enumerate(bias_refs):
        side, g = k // groups, k % groups
        for i in range(count // 2):
            place = side * (count // 2) + i
            units[place : place + 1, g * width : (g + 1) * width] = ref[:, i * width : (i + 1) * width]
    offset = 0
    for piece in pieces:
        if piece is None:
            for k in range(count):
                flat[:, offset : offset + size] = units[pl.ds(entry_ref[k], 1), :]
                offset += size
        else:
            flat[:, offset : offset + piece.shape[1]] = piece
            offset += piece.shape[1]
    qkv_rows, vec_len = qkv_grad.shape[0] // shards_of, flat.shape[1] // shards_of
    to_shard = count // shards_of
    share = lambda k, total: [k // to_shard * total + min(-(-total // to_shard) * j, total) for j in (k % to_shard, k % to_shard + 1)]
    out_own = D // count
    vec_row = qkv_ref.shape[1] - 4
    for k in range(count):
        to = entry_ref[k]
        begin, end = share(k, qkv_rows)
        qkv_ref[to] = jnp.zeros(qkv_ref.shape[1:], f32)
        if end > begin:
            qkv_ref[to, : end - begin, :] = qkv_grad[begin:end]
        begin, end = share(k, vec_len)
        if end > begin:
            qkv_ref[to, vec_row : vec_row + 1, : end - begin] = flat[:, begin:end]
        out_ref[to] = jnp.zeros(out_ref.shape[1:], f32)
        out_ref[to, :out_own, :] = out_grad[k * out_own : (k + 1) * out_own]


def tail(entry, x, dy, dq_t, dkv, cosine, sine, weight, normed, context, d_two, gains, bias_grads, rows, shards_of, vec_len):
    tokens = x.shape[0]
    count = entry.shape[0]
    operands = (entry, x, dy, dq_t, dkv, cosine, sine, weight, normed, context, d_two, gains, *sum(bias_grads, []))
    return pl.pallas_call(
        functools.partial(tail_kernel, shards_of),
        in_specs=[pl.BlockSpec(memory_space=pltpu.SMEM)] + [pl.BlockSpec(memory_space=pltpu.VMEM)] * (len(operands) - 1),
        out_shape=[
            jax.ShapeDtypeStruct((tokens, D), low),
            jax.ShapeDtypeStruct((count, rows, D), f32),
            jax.ShapeDtypeStruct((count, rows, D), f32),
        ],
        scratch_shapes=[pltpu.VMEM((1, shards_of * vec_len), f32), pltpu.VMEM((count, FF // count), f32)],
        compiler_params=pltpu.CompilerParams(vmem_limit_bytes=VMEM_LIMIT),
        cost_estimate=pl.CostEstimate(flops=4 * 6 * tokens * 896 * D, bytes_accessed=8 << 20, transcendentals=0),
        name="tail",
    )(*operands)


def split_low(value):
    high = value.astype(low)
    return high, (value - high.astype(f32)).astype(low)


def update_step(across, grad, high, rest, w_ref, first_ref, second_ref, grad_ref, first_new_ref, second_new_ref, w_new_ref):
    rotated = jnp.dot(grad, high, preferred_element_type=f32) + jnp.dot(grad, rest, preferred_element_type=f32)
    grad = grad.astype(f32)
    if across:
        rotated, grad = rotated.T, grad.T
    grad_ref[...] = grad
    ratio, first_new, second_new = moments(rotated, first_ref[...], second_ref[...])
    first_new_ref[...] = first_new
    second_new_ref[...] = second_new
    r_high, r_rest = split_low(ratio)
    if across:
        product = lambda r, b: jnp.dot(b, r, preferred_element_type=f32)
    else:
        product = lambda r, b: lax.dot_general(r, b, (((1,), (1,)), ((), ())), preferred_element_type=f32)
    unrotated = product(r_high, high) + (product(r_high, rest) + product(r_rest, high))
    w_new_ref[...] = w_ref[...] - matrix_rate * unrotated


def update_kernel(across, grad_ref, high_ref, rest_ref, *refs):
    update_step(across, grad_ref[...], high_ref[...], rest_ref[...], *refs)


def update(grad, basis, weight, first, second, across=False):
    return pl.pallas_call(
        functools.partial(update_kernel, across),
        out_shape=[jax.ShapeDtypeStruct(weight.shape, f32)] * 4,
        compiler_params=pltpu.CompilerParams(vmem_limit_bytes=UPDATE_VMEM),
        cost_estimate=pl.CostEstimate(flops=10 * grad.shape[0] * D * D, bytes_accessed=8 << 20, transcendentals=0),
        name="update",
    )(grad, *basis, weight, first, second)


def outer_update_kernel(share, own, offset, g_ref, *refs):
    qkv_in, out_in, qkv_out, out_out, (qkv_rows, out_rows) = refs[:5], refs[5:10], refs[10:14], refs[14:18], refs[18:]
    for q in range(g_ref.shape[0]):
        part = g_ref[q].astype(f32)
        count = min(share, qkv_rows.shape[0] - q * share)
        if count > 0:
            qkv_rows[q * share : q * share + count, :] = part[:count]
        out_rows[q * own : (q + 1) * own, :] = part[offset : offset + own]
    for rows, (high_ref, rest_ref, *state), outs in ((qkv_rows, qkv_in, qkv_out), (out_rows, out_in, out_out)):
        update_step(False, rows[...].astype(low), high_ref[...], rest_ref[...], *state, *outs)


def outer_update(grads, share, own, offset, qkv, out):
    operands = [value for basis, *state in (qkv, out) for value in (*basis, *state)]
    shapes = [qkv[1].shape] * 4 + [out[1].shape] * 4
    new = pl.pallas_call(
        functools.partial(outer_update_kernel, share, own, offset),
        out_shape=[jax.ShapeDtypeStruct(shape, f32) for shape in shapes],
        scratch_shapes=[pltpu.VMEM(qkv[1].shape, f32), pltpu.VMEM(out[1].shape, f32)],
        compiler_params=pltpu.CompilerParams(vmem_limit_bytes=UPDATE_VMEM),
        cost_estimate=pl.CostEstimate(flops=10 * 208 * D * D, bytes_accessed=8 << 20, transcendentals=0),
        name="outer_update",
    )(grads, *operands)
    return new[:4], new[4:]


def shards(
    inputs,
    cotangent,
    doc_lengths,
    qkv_weight,
    out_weight,
    up_weight,
    down_weight,
    vectors,
    bases,
    qkv_first,
    out_first,
    up_first,
    down_first,
    vector_first,
    qkv_second,
    out_second,
    up_second,
    down_second,
    vector_second,
):
    seq_count, batch_count = lax.axis_size("seq"), lax.axis_size("batch")
    seq_index, batch_index = lax.axis_index("seq"), lax.axis_index("batch")
    row_count, shard_len = inputs.shape[:2]
    tokens = row_count * shard_len
    y_bit, *z_bits = bit_names("seq", seq_count)
    core_bit, *x_bits = bit_names("batch", batch_count)
    near = [core_bit] + x_bits[::-1] + [y_bit] + z_bits[::-1]
    depth = seq_count // 2
    plane = 2 ** (len(x_bits) + 1)
    x_low = inputs.reshape(tokens, D)
    dy = cotangent.reshape(tokens, D)

    first_pos = seq_index * shard_len
    query_pos = first_pos + jnp.arange(shard_len, dtype=jnp.int32)
    docs = doc_lengths.shape[1]
    earlier = jnp.arange(docs)[:, None] < jnp.arange(docs)[None, :]
    doc_starts = jnp.sum(jnp.where(earlier[None], doc_lengths[:, :, None], 0), axis=1)
    start = jnp.max(
        jnp.where(doc_starts[:, None, :] <= query_pos[None, :, None], doc_starts[:, None, :], 0), axis=-1
    )
    offsets = (query_pos[None, :] - start).reshape(tokens)
    inverse = 1.0 / rope_base ** (jnp.arange(0, ROT, 2).astype(f32) / ROT)
    angles = offsets.astype(f32)[None, :] * inverse[:, None]
    cosine, sine = jnp.cos(angles), jnp.sin(angles)
    start_here = (start - first_pos).astype(jnp.int32)[:, None, :]
    number = jnp.arange(seq_count * batch_count, dtype=jnp.int32)

    def bits_of(value, place_of):
        total = 0
        for k, (axis_name, step) in enumerate(near[::-1]):
            total = total + place_of(value, k, axis_name, step)
        return total

    differs = {"seq": (number // batch_count) ^ seq_index, "batch": (number % batch_count) ^ batch_index}
    entry = bits_of(number, lambda v, k, name, step: (differs[name] // step) % 2 << k).astype(jnp.int32)
    xor_of = lambda name: sum((number >> k) % 2 * step for k, (axis_name, step) in enumerate(near[::-1]) if axis_name == name)
    device = ((xor_of("seq") ^ seq_index) * batch_count + (xor_of("batch") ^ batch_index)).astype(jnp.int32)

    qkv_rows, out_rows, up_rows, vec_len = qkv_weight.shape[0], out_weight.shape[0], up_weight.shape[0], vectors.shape[0]
    vec_rows = -(-vec_len // D)
    used = qkv_rows + vec_rows
    head_rows = -(-used // (8 * batch_count)) * 8 * batch_count
    vec_pad = vec_rows * D - vec_len

    def own_part(rows):
        size = rows.shape[0] // batch_count
        return lax.dynamic_slice_in_dim(rows, batch_index * size, size, axis=0)

    head_shard = jnp.concatenate(
        [qkv_weight, jnp.pad(vectors, (0, vec_pad)).reshape(vec_rows, D), jnp.zeros((head_rows - used, D), f32)], axis=0
    ).astype(low)
    head_part_rows = head_rows // batch_count
    unit_rows = up_rows // batch_count // GROUPS
    out_own = out_rows // batch_count
    up_low, down_low = own_part(up_weight.astype(low)), own_part(down_weight.T.astype(low))
    outer = [
        own_part(head_shard),
        jnp.concatenate([own_part(out_weight.astype(low)), jnp.zeros((head_part_rows - out_own, D), low)], axis=0),
    ]
    parts_of = []
    for g in range(GROUPS):
        rows = slice(g * unit_rows, (g + 1) * unit_rows)
        pieces = [up_low[rows], outer[0], down_low[rows], outer[1]] if g == 0 else [up_low[rows], down_low[rows]]
        parts_of.append(jnp.concatenate(pieces, axis=0))

    def gather_first(parts):
        half = parts.shape[1] // 2
        up, down = parts[:, :half], parts[:, half:]
        for bit in x_bits[:-1]:
            down = gather_bit(down, bit, 0)
        return up, down, swap(up, y_bit), swap(down, x_bits[-1])

    def gather_second(up, down, up_got, down_got):
        up, down = jnp.stack([up, up_got]), jnp.stack([down, down_got])
        for bit in x_bits[:-1]:
            up = gather_bit(up, bit, 0)
        shape = (1, plane // 2, depth) + up.shape[-2:]
        return up, down, jnp.concatenate([up.reshape(shape), down.reshape(shape)], axis=0)

    def gather_last(up, down):
        return swap(up, x_bits[-1]), swap(down, y_bit)

    def joined(up, down):
        shape = (1, plane // 2, depth) + up.shape[-2:]
        return jnp.concatenate([up.reshape(shape), down.reshape(shape)], axis=0)

    z_zero = gather_z(parts_of[0])
    *z_zero, cosine, sine, start_here, entry, device, part_one = hold(
        *z_zero, cosine, sine, start_here, entry, device, parts_of[1]
    )
    up, down, up_got, down_got = gather_first(jnp.stack(z_zero))
    z_one = gather_z(part_one)
    up_got, down_got, z_one[1] = hold(up_got, down_got, z_one[1])
    up, down, first_zero = gather_second(up, down, up_got, down_got)
    up_got, down_got = gather_last(up, down)
    first_far_zero = swap(first_zero, core_bit)
    late_bases, up, down = hold(bases, up, down)
    split_bases = [part for k in range(4) for part in split_low(late_bases[k])]
    up_got, down_got, first_far_zero, *rest = hold(up_got, down_got, first_far_zero, *z_one[2:], *split_bases)
    z_one[2:], split_bases = rest[: len(z_one) - 2], rest[len(z_one) - 2 :]
    split_bases = [split_bases[2 * k : 2 * k + 2] for k in range(4)]
    last_zero = joined(up_got, down_got)
    last_far_zero = swap(last_zero, core_bit)

    aligned = unit_rows % 16 == 0 and head_part_rows % 16 == 0
    trim = lambda values, begin, end: values if aligned else tuple(v[..., begin:end, :] for v in values)
    near_zero, far_zero = (first_zero, last_zero), (first_far_zero, last_far_zero)
    end = unit_rows + head_part_rows

    inside = out_own % 8 == 0
    normed_one, normed_two, q_t, kv_own, qkv_full, gains, out_bias, *bias_rows = head(
        device, x_low, trim(near_zero, unit_rows, end), trim(far_zero, unit_rows, end), unit_rows if aligned else 0,
        head_part_rows, out_own if inside else 0, cosine, sine, GROUPS, vec_len, seq_count,
    )
    if inside:
        out_full = bias_rows.pop()
    else:
        chosen = (entry[:, None] == number[None, :]).astype(low)
        sides = []
        for pair in (near_zero, far_zero):
            along = [v[1, :, :, unit_rows : unit_rows + out_own] for v in pair]
            sides.append(jnp.stack(along, axis=1).reshape(-1, out_own * D))
        out_full = jnp.dot(chosen, jnp.concatenate(sides, axis=0), preferred_element_type=f32).astype(low).reshape(D, D)
    bias_rows = [bias_rows[:GROUPS], bias_rows[GROUPS:]]
    reach = seq_count // 2

    def shifted(value, step, back=False):
        pairs = [(j, j + step) for j in range(seq_count - step)]
        return lax.ppermute(value, "seq", [(b, a) for a, b in pairs] if back else pairs)

    farthest, pair = shifted(kv_own, reach), shifted(kv_own[None], 1)
    up, down, up_got, down_got = gather_first(jnp.stack(z_one))
    up_got, down_got, normed_two = hold(up_got, down_got, normed_two)
    up, down, first_one = gather_second(up, down, up_got, down_got)
    up_got, down_got = gather_last(up, down)
    first_far_one = swap(first_one, core_bit)

    last = (((1,), (1,)), ((), ()))
    bias_grads = [[], []]

    def feed_group(g, sums, normed, near, far, *beside):
        *sums, far_grad, near_grad, bias_far, bias_here = feed(
            normed, dy, trim(far, 0, unit_rows), trim(near, 0, unit_rows), bias_rows[1][g], bias_rows[0][g], unit_rows, sums
        )
        bias_grads[0].append(bias_here)
        bias_grads[1].append(bias_far)
        far_grad, *beside = hold(far_grad, *beside)
        shape = (2,) + (2,) * len(x_bits) + (2, depth, unit_rows, D)
        grad_sum = (near_grad + swap(far_grad, core_bit).astype(f32)).reshape(shape)
        return sums, grad_sum[0], grad_sum[1], *beside

    def sum_first(up, down):
        (up_kept, up_sent), (down_kept, down_sent) = split_bit(up, x_bits[-1], 0), split_bit(down, y_bit, len(x_bits))
        return up_kept, up_sent, down_kept, down_sent

    def send_first(sums):
        return swap(sums[1], x_bits[-1]), swap(sums[3], y_bit)

    def sum_second(sums, up_got, down_got):
        up = sums[0] + up_got.astype(f32)
        for bit in x_bits[-2::-1]:
            kept, sent = split_bit(up, bit, 0)
            up = kept + swap(sent, bit).astype(f32)
        down = sums[2] + down_got.astype(f32)
        (up_kept, up_sent), (down_kept, down_sent) = split_bit(up, y_bit, 0), split_bit(down, x_bits[-1], 0)
        return up_kept, up_sent, down_kept, down_sent

    def send_second(sums):
        return swap(sums[1], y_bit), swap(sums[3], x_bits[-1])

    def sum_third(up_kept, up_got, down_kept, down_got):
        up = up_kept + up_got.astype(f32)
        down = down_kept + down_got.astype(f32)
        for bit in x_bits[-2::-1]:
            kept, sent = split_bit(down, bit, 0)
            down = kept + swap(sent, bit).astype(f32)
        return jnp.concatenate([up, down], axis=1)

    def send_z(value):
        return [swap_z(value[k].astype(low), k) for k in range(1, depth)]

    def sum_z(value, got):
        return value[0] + sum(part.astype(f32) for part in got)

    def spread(part):
        value = part.astype(low)
        for bit in x_bits:
            value = gather_bit(value, bit, 0, True)
        return gather_bit(value, core_bit, len(x_bits), True).reshape(batch_count, -1, D)

    sums, up_sum, down_sum, up_got, down_got, farthest, pair = feed_group(
        0, None, normed_two, near_zero, far_zero, up_got, down_got, farthest, pair
    )
    kv = jnp.concatenate([kv_own[None], pair], axis=0)
    while kv.shape[0] < reach:
        kv = jnp.concatenate([kv, shifted(kv, kv.shape[0])], axis=0)
    kv = jnp.concatenate([kv, farthest[None]], axis=0)
    sum_zero = sum_first(up_sum, down_sum)
    *sum_zero, first_far_one, q_t = hold(*sum_zero, first_far_one, q_t)
    last_one = joined(up_got, down_got)
    last_far_one = swap(last_one, core_bit)

    do_t = lax.dot_general(out_full, dy, (((0,), (1,)), ((), ())), preferred_element_type=f32).astype(low)
    context, dq_t, dkv_own, dkv_sent = attention(q_t, do_t, start_here, cosine, sine, kv)
    sum_zero = sum_second(sum_zero, *send_first(sum_zero))
    last_far_one, dq_t, normed_late, *sum_zero = hold(last_far_one, dq_t, normed_two, *sum_zero)
    dkv_far = shifted(dkv_sent[reach - 1], reach, True)
    dkv = [dkv_own] + [dkv_sent[i] for i in range(reach - 1)]
    middle = reach // 2
    got = shifted(dkv_sent[middle - 1 : reach - 1], middle, True)
    up_got, down_got = send_second(sum_zero)
    (mlp_out, d_normed_two), up_sum, down_sum, up_got, down_got, dkv_far, got = feed_group(
        1, sums, normed_late, (first_one, last_one), (first_far_one, last_far_one), up_got, down_got, dkv_far, got
    )
    sum_zero = sum_third(sum_zero[0], up_got, sum_zero[2], down_got)
    dkv = [dkv[i].astype(f32) + got[i].astype(f32) for i in range(middle)]
    while middle > 1:
        middle //= 2
        got = shifted(jnp.stack([part.astype(low) for part in dkv[middle : 2 * middle]]), middle, True)
        dkv = [dkv[i] + got[i].astype(f32) for i in range(middle)]
    dkv = dkv[0] + dkv_far.astype(f32)
    qkv_share, vec_share = -(-qkv_rows // batch_count), -(-vec_len // batch_count)
    sum_one = sum_first(up_sum, down_sum)
    dkv, *sum_one = hold(dkv, *sum_one)
    up_got, down_got = send_first(sum_one)
    z_got = send_z(sum_zero)
    input_grad, qkv_part, out_part = tail(
        entry, x_low, dy, dq_t, dkv, cosine, sine, qkv_full, normed_one, context, d_normed_two, gains, bias_grads,
        head_part_rows, seq_count, vec_len,
    )
    qkv_part, up_got, down_got, *z_got = hold(qkv_part, up_got, down_got, *z_got)
    sum_one = sum_second(sum_one, up_got, down_got)
    one_got = send_second(sum_one)
    outer = jnp.stack([qkv_part, out_part]).reshape((2, 2) + (2,) * len(x_bits) + (2, depth, head_part_rows, D))
    got = swap(outer[:, 1].astype(low), core_bit)
    got, mlp_late, context_late, *one_got = hold(got, mlp_out, context, *one_got)
    outer = outer[:, 0] + got.astype(f32)
    sum_outer = sum_first(outer[0], outer[1])
    outer_got = send_first(sum_outer)
    sum_one = sum_third(sum_one[0], one_got[0], sum_one[2], one_got[1])
    one_got = send_z(sum_one)
    feed_zero = sum_z(sum_zero, z_got)
    attn_out = lax.dot_general(context_late, out_full, last, preferred_element_type=f32)
    outputs = (x_low.astype(f32) + attn_out + mlp_late + out_bias).astype(low)
    sum_outer = sum_second(sum_outer, *outer_got)
    outer_got = send_second(sum_outer)
    outer_got, one_got, (outputs,) = hold_lists(outer_got, one_got, [outputs])
    sum_outer = sum_third(sum_outer[0], outer_got[0], sum_outer[2], outer_got[1])
    outer_got = send_z(sum_outer)
    grads_feed = spread(jnp.concatenate([feed_zero, sum_z(sum_one, one_got)], axis=0))
    grads_feed = grads_feed.reshape(batch_count, GROUPS, 2, unit_rows, D).transpose(2, 0, 1, 3, 4).reshape(2, -1, D)
    (up_all, down_all), outer_got = hold_lists([grads_feed[0], grads_feed[1]], outer_got)
    up_out = update(up_all, split_bases[2], up_weight, up_first, up_second)
    grads_outer = spread(sum_z(sum_outer, outer_got))
    down_out = update(down_all, split_bases[3], down_weight, down_first, down_second, True)
    down_out, grads_outer = hold_lists(down_out, [grads_outer])
    grads_outer = grads_outer[0]
    (up_grad, *up_states), (down_grad, *down_states) = up_out, down_out
    (qkv_grad, *qkv_states), (out_grad, *out_states) = outer_update(
        grads_outer, qkv_share, out_own, head_part_rows,
        (split_bases[0], qkv_weight, qkv_first, qkv_second), (split_bases[1], out_weight, out_first, out_second),
    )
    vector_grad = grads_outer[:, head_part_rows - 4, :vec_share].astype(f32).reshape(-1)[:vec_len]
    vector_new, *vector_states = adam_step(vectors, vector_grad, vector_first, vector_second)
    states = (qkv_states, out_states, up_states, down_states, (*vector_states, vector_new))
    return (
        outputs.reshape(inputs.shape),
        input_grad.reshape(inputs.shape),
        qkv_grad,
        out_grad,
        up_grad,
        down_grad,
        vector_grad,
        *(state[0] for state in states),
        *(state[1] for state in states),
        *(state[2] for state in states),
    )


def solution(mesh):
    tokens = P("batch", "seq", None)
    rows, columns, flat = P("seq", None), P(None, "seq"), P("seq")
    params = (rows, rows, rows, columns, flat)
    return jax.shard_map(
        shards,
        mesh=mesh,
        in_specs=(tokens, tokens, P("batch", None)) + params + (P(),) + params + params,
        out_specs=(tokens, tokens) + params * 4,
        check_vma=False,
    )
```

```python
import functools

import jax
import jax.numpy as jnp
from jax import lax
from jax.experimental import pallas as pl
from jax.experimental.pallas import tpu as pltpu
from jax.sharding import PartitionSpec as P

D = 768
HEADS = 12
HEAD = 64
ROT = 16
FF = 3072
STEP = 10

layer_eps = 1e-05
adam_eps = 1e-08
beta_first = 0.95
beta_second = 0.95
matrix_rate = 0.08
vector_rate = 0.3
rope_base = 10000.0
masked_score = -1e30
low = jnp.bfloat16
f32 = jnp.float32
VMEM_LIMIT = 56 * 1024 * 1024
GROUPS = 2
FEED_VMEM = 56 * 1024 * 1024
UPDATE_VMEM = 28 * 1024 * 1024


def swap(value, bit):
    axis, step = bit
    return lax.ppermute(value, axis, [(i, i ^ step) for i in range(lax.axis_size(axis))])


def mine(bit):
    axis, step = bit
    return lax.rem(lax.axis_index(axis) // step, 2)


def hold(*values):
    return lax.optimization_barrier(values)


def hold_lists(*lists):
    flat = iter(hold(*(value for values in lists for value in values)))
    return [[next(flat) for _ in values] for values in lists]


def swap_z(value, step):
    size = lax.axis_size("seq")
    return lax.ppermute(value, "seq", [(i, i ^ (2 * step)) for i in range(size)])


def gather_z(piece):
    return [piece] + [swap_z(piece, k) for k in range(1, lax.axis_size("seq") // 2)]


def gather_bit(value, bit, axis, absolute=False):
    got = swap(value, bit)
    if absolute:
        upper = mine(bit) == 1
        return jnp.stack([jnp.where(upper, got, value), jnp.where(upper, value, got)], axis=axis)
    return jnp.stack([value, got], axis=axis)


def split_bit(value, bit, axis):
    return lax.index_in_dim(value, 0, axis, keepdims=False), lax.index_in_dim(value, 1, axis, keepdims=False).astype(low)


def bit_names(axis, size):
    return [(axis, 1 << k) for k in range(size.bit_length() - 1)]


def moments(rotated, first, second):
    new_first = beta_first * first + (1.0 - beta_first) * rotated
    new_second = beta_second * second + (1.0 - beta_second) * rotated * rotated
    first_scale, second_scale = 1.0 / (1.0 - beta_first**STEP), 1.0 / (1.0 - beta_second**STEP)
    ratio = new_first * first_scale / (jnp.sqrt(new_second * second_scale) + adam_eps)
    return ratio, new_first, new_second


def adam_step(weight, grad, first, second):
    ratio, new_first, new_second = moments(grad, first, second)
    return (weight - vector_rate * ratio, new_first, new_second)


def attend(blocks, width, q_ref, do_ref, start_ref, cos_ref, sin_ref, kv_ref, context_ref, dq_ref, dkv_own_ref, dkv_ref):
    length = q_ref.shape[1]
    keys = blocks * length
    key_t = jnp.concatenate([kv_ref[k, :HEAD, :] for k in reversed(range(blocks))], axis=1)
    value_t = jnp.concatenate([kv_ref[k, HEAD:, :] for k in reversed(range(blocks))], axis=1)
    key = key_t.astype(f32).T.astype(low)
    value = value_t.astype(f32).T.astype(low)
    key_pos = lax.broadcasted_iota(jnp.int32, (keys, length), 0) - (blocks - 1) * length
    query_pos = lax.broadcasted_iota(jnp.int32, (keys, length), 1)
    allowed = (key_pos >= start_ref[0]) & (key_pos <= query_pos)
    bias = jnp.where(allowed, 0.0, masked_score)
    cosine, sine = cos_ref[...], sin_ref[...]
    d_key = jnp.zeros((keys, HEAD), f32)
    d_value = jnp.zeros((keys, HEAD), f32)
    last = (((1,), (1,)), ((), ()))
    for first in range(0, HEADS, width):
        heads = range(first, first + width)
        query = jnp.concatenate([q_ref[h * HEAD : (h + 1) * HEAD, :] for h in heads], axis=1)
        d_out = jnp.concatenate([do_ref[h * HEAD : (h + 1) * HEAD, :] for h in heads], axis=1)
        scores = jnp.dot(key, query, preferred_element_type=f32)
        scores = scores + jnp.concatenate([bias] * width, axis=1)
        weights = jnp.exp(scores - jnp.max(scores, axis=0, keepdims=True))
        probs = weights * (1.0 / jnp.sum(weights, axis=0, keepdims=True))
        probs_low = probs.astype(low)
        context_t = jnp.dot(value_t, probs_low, preferred_element_type=f32)
        d_probs = jnp.dot(value, d_out, preferred_element_type=f32)
        inner = jnp.sum(probs * d_probs, axis=0, keepdims=True)
        d_scores = (probs * (d_probs - inner)).astype(low)
        d_query = jnp.dot(key_t, d_scores, preferred_element_type=f32) * HEAD ** (-0.5)
        d_value = d_value + lax.dot_general(probs_low, d_out, last, preferred_element_type=f32)
        d_key = d_key + lax.dot_general(d_scores, query, last, preferred_element_type=f32)
        for k, h in enumerate(heads):
            lanes = slice(k * length, (k + 1) * length)
            part = d_query[:, lanes]
            a, b = part[: ROT // 2], part[ROT // 2 : ROT]
            turned = jnp.concatenate([a * cosine + b * sine, b * cosine - a * sine, part[ROT:]], axis=0)
            dq_ref[h * HEAD : (h + 1) * HEAD, :] = turned.astype(low)
        for k in range(0, width, 2):
            h = first + k
            two = jnp.concatenate(
                [context_t[:, k * length : (k + 1) * length], context_t[:, (k + 1) * length : (k + 2) * length]], axis=0
            )
            context_ref[:, h * HEAD : (h + 2) * HEAD] = two.T.astype(low)
    d_kv = jnp.concatenate([d_key, d_value], axis=1).T
    for k in range(blocks):
        part = d_kv[:, (blocks - 1 - k) * length : (blocks - k) * length]
        if k == 0:
            dkv_own_ref[...] = part
        else:
            dkv_ref[k - 1] = part.astype(low)
    for k in range(blocks, kv_ref.shape[0]):
        dkv_ref[k - 1] = jnp.zeros(dkv_ref.shape[1:], low)


def attention_kernel(counts, needed_ref, *refs):
    needed = needed_ref[pl.program_id(0)]
    for least, count in zip([0] + counts, counts):

        @pl.when((needed > least) & (needed <= count))
        def _():
            attend(count, HEADS, *refs)


def attention(q_t, do_t, start, cosine, sine, kv):
    rows, _, length = start.shape
    blocks = kv.shape[0]
    tokens = q_t.shape[1]
    by_row = lambda height: pl.BlockSpec((height, length), lambda r: (0, r))
    needed = 1 + jnp.clip((length - 1 - start[:, 0, 0]) // length, 0, blocks - 1).astype(jnp.int32)
    counts = list(range(1, blocks + 1)) if blocks <= 5 else [1, (blocks + 1) // 2, blocks]
    return pl.pallas_call(
        functools.partial(attention_kernel, counts),
        grid=(rows,),
        in_specs=[pl.BlockSpec(memory_space=pltpu.SMEM), by_row(D), by_row(D), pl.BlockSpec((1, 1, length), lambda r: (r, 0, 0)), by_row(ROT // 2), by_row(ROT // 2)]
        + [pl.BlockSpec((blocks, 2 * HEAD, length), lambda r: (0, 0, r))],
        out_specs=[
            pl.BlockSpec((length, D), lambda r: (r, 0)),
            by_row(D),
            by_row(2 * HEAD),
            pl.BlockSpec((blocks - 1, 2 * HEAD, length), lambda r: (0, 0, r)),
        ],
        out_shape=[
            jax.ShapeDtypeStruct((tokens, D), low),
            jax.ShapeDtypeStruct((D, tokens), low),
            jax.ShapeDtypeStruct((2 * HEAD, tokens), f32),
            jax.ShapeDtypeStruct((blocks - 1, 2 * HEAD, tokens), low),
        ],
        compiler_params=pltpu.CompilerParams(vmem_limit_bytes=VMEM_LIMIT),
        cost_estimate=pl.CostEstimate(
            flops=4 * 7 * tokens * HEADS * blocks * length * HEAD * 2, bytes_accessed=8 << 20, transcendentals=0
        ),
        name="attention",
    )(needed, q_t, do_t, start, cosine, sine, kv)


def gathered_parts(plane, refs, offset, rows):
    half = plane // 2
    out = []
    for end, ref in enumerate(refs):
        for j in range(half):
            out.append((0, end * half + j, ref.at[0, j, :, pl.ds(offset, rows)]))
            out.append((1, 2 * j + end, ref.at[1, j, :, pl.ds(offset, rows)]))
    return out


def feed_kernel(n_ref, dy_ref, first_far, last_far, first_near, last_near, bias_far_ref, bias_near_ref, *refs):
    far_refs, near_refs = (first_far, last_far), (first_near, last_near)
    before = refs[: len(refs) - 11]
    out_ref, dn_ref, far_grad_ref, near_grad_ref, bias_far_grad_ref, bias_near_grad_ref = refs[-11:-5]
    weights, far_sum, near_sum, held, sems = refs[-5:]
    plane = weights.shape[2]
    last = (((1,), (1,)), ((), ()))
    first = (((0,), (0,)), ((), ()))
    loads = [
        [
            pltpu.make_async_copy(source, weights.at[side, kind, k], sems.at[side, 2 * k + kind])
            for kind, k, source in gathered_parts(plane, refs_of, 0, weights.shape[4])
        ]
        for side, refs_of in enumerate((far_refs, near_refs))
    ]
    fetches = [pltpu.make_async_copy(ref, held.at[k], sems.at[2, k]) for k, ref in enumerate(before)]
    for copy in loads[0] + loads[1] + fetches:
        copy.start()
    normed, d_out = n_ref[...], dy_ref[...]
    units = far_sum.shape[1]
    out, d_normed = 0.0, 0.0
    stores = []
    for side, (bias_ref, bias_grad_ref, buffer, grad_ref) in enumerate(
        (
            (bias_far_ref, bias_far_grad_ref, far_sum, far_grad_ref),
            (bias_near_ref, bias_near_grad_ref, near_sum, near_grad_ref),
        )
    ):
        for copy in loads[side]:
            copy.wait()
        up, down = weights[side, 0].reshape(units, D), weights[side, 1].reshape(units, D)
        hidden = lax.dot_general(normed, up, last, preferred_element_type=f32) + bias_ref[...]
        share = 0.5 * (1.0 + lax.erf(hidden * (0.5**0.5)))
        slope = share + hidden * (jnp.exp(-0.5 * hidden * hidden) * (0.5 / 3.141592653589793) ** 0.5)
        active = (hidden * share).astype(low)
        d_active = lax.dot_general(d_out, down, last, preferred_element_type=f32)
        d_hidden = (d_active * slope).astype(low)
        for k, part in enumerate(
            (
                lax.dot_general(d_hidden, normed, first, preferred_element_type=f32),
                lax.dot_general(active, d_out, first, preferred_element_type=f32),
            )
        ):
            buffer[k] = part.astype(buffer.dtype)
            copy = pltpu.make_async_copy(buffer.at[k], grad_ref.at[k], sems.at[3, 2 * side + k])
            copy.start()
            stores.append(copy)
        bias_grad_ref[...] = jnp.sum(d_hidden.astype(f32), axis=0, keepdims=True)
        out = out + jnp.dot(active, down, preferred_element_type=f32)
        d_normed = d_normed + jnp.dot(d_hidden, up, preferred_element_type=f32)
    for copy in fetches:
        copy.wait()
    out_ref[...] = held[0] + out if before else out
    dn_ref[...] = held[1] + d_normed if before else d_normed
    for copy in stores:
        copy.wait()


def feed(normed, d_out, far, near, bias_far, bias_near, rows, before):
    tokens = normed.shape[0]
    plane, depth = 2 * far[0].shape[1], far[0].shape[2]
    units = plane * depth * rows
    before = before or []
    vmem, hbm = pl.BlockSpec(memory_space=pltpu.VMEM), pl.BlockSpec(memory_space=pl.ANY)
    return pl.pallas_call(
        feed_kernel,
        in_specs=[vmem, vmem, hbm, hbm, hbm, hbm, vmem, vmem] + [hbm] * len(before),
        out_specs=[vmem, vmem, hbm, hbm, vmem, vmem],
        out_shape=[
            jax.ShapeDtypeStruct((tokens, D), f32),
            jax.ShapeDtypeStruct((tokens, D), f32),
            jax.ShapeDtypeStruct((2, units, D), low),
            jax.ShapeDtypeStruct((2, units, D), f32),
            jax.ShapeDtypeStruct((1, units), f32),
            jax.ShapeDtypeStruct((1, units), f32),
        ],
        scratch_shapes=[
            pltpu.VMEM((2, 2, plane, depth, rows, D), low),
            pltpu.VMEM((2, units, D), low),
            pltpu.VMEM((2, units, D), f32),
            pltpu.VMEM((2, tokens, D), f32),
            pltpu.SemaphoreType.DMA((4, 2 * plane)),
        ],
        compiler_params=pltpu.CompilerParams(vmem_limit_bytes=FEED_VMEM),
        cost_estimate=pl.CostEstimate(flops=4 * 24 * tokens * units * D, bytes_accessed=8 << 20, transcendentals=0),
        name="feed",
    )(normed, d_out, *far, *near, bias_far, bias_near, *before)


def head_kernel(
    vec_len, offset, out_rows, device_ref, x_ref, first_near, last_near, first_far, last_far, cos_ref, sin_ref, n_one_ref,
    n_two_ref, q_ref, kv_ref, w_ref, gain_ref, bias_ref, *refs
):
    *bias_refs, out_ref, flat, units, held, pieces_of, outs_of, sems = refs if out_rows else (*refs[:-6], None, *refs[-6:])
    _, _, plane, depth, size, _ = held.shape
    copies = [
        pltpu.make_async_copy(source, held.at[side, kind, k], sems.at[side, 2 * k + kind])
        for side, refs_of in enumerate(((first_near, last_near), (first_far, last_far)))
        for kind, k, source in gathered_parts(plane, refs_of, offset, size)
    ]
    for copy in copies:
        copy.start()
    x = x_ref[...].astype(f32)
    center = x - jnp.mean(x, axis=-1, keepdims=True)
    xhat = center * lax.rsqrt(jnp.mean(center * center, axis=-1, keepdims=True) + layer_eps)
    for copy in copies:
        copy.wait()
    for side in range(2):
        for k in range(plane):
            for z in range(depth):
                number = device_ref[(side * plane + k) * depth + z]
                pieces_of[number] = held[side, 0, k, z].astype(f32)
                if out_rows:
                    outs_of[number] = held[side, 1, k, z][:out_rows].astype(f32)
    if out_rows:
        out_ref[...] = outs_of[...].reshape(out_ref.shape).astype(low)
    shards_of = (flat.shape[1]) // vec_len
    rows = (D + 2 * HEAD) // shards_of
    whole = pieces_of[...].reshape(shards_of, -1, D)
    for s in range(shards_of):
        left, row = vec_len, rows
        while left > 0:
            size = min(left, D)
            begin = s * vec_len + (row - rows) * D
            flat[:, begin : begin + size] = whole[s, row : row + 1, :size]
            left -= size
            row += 1
    vector = lambda begin, size: flat[:, begin : begin + size]
    gain_one, shift_one, gain_two, shift_two = [vector(k * D, D) for k in range(4)]
    gain_ref[0:1] = gain_one
    gain_ref[1:2] = gain_two
    qkv_bias = vector(4 * D, D + 2 * HEAD)
    start = 4 * D + D + 2 * HEAD
    bias_ref[...] = vector(start, D) + vector(start + D + FF, D)
    count, size_of = units.shape
    for k in range(count):
        units[k : k + 1, :] = vector(start + D + k * size_of, size_of)
    groups = len(bias_refs) // 2
    for k, ref in enumerate(bias_refs):
        side, g = k // groups, k % groups
        width = size_of // groups
        for i in range(count // 2):
            row = units[pl.ds(device_ref[side * (count // 2) + i], 1), :]
            ref[:, i * width : (i + 1) * width] = row[:, g * width : (g + 1) * width]
    n_one = (xhat * gain_one + shift_one).astype(low)
    n_one_ref[...] = n_one
    n_two_ref[...] = (xhat * gain_two + shift_two).astype(low)
    weight = whole[:, :rows].reshape(shards_of * rows, D).astype(low)
    w_ref[...] = weight
    column = jnp.broadcast_to(qkv_bias, (8, qkv_bias.shape[1])).T[:, 0:1]
    projected = lax.dot_general(weight, n_one, (((1,), (1,)), ((), ())), preferred_element_type=f32) + column
    cosine, sine = cos_ref[...], sin_ref[...]
    half = ROT // 2

    def turned(first):
        a, b = projected[first : first + half], projected[first + half : first + ROT]
        rest = projected[first + ROT : first + HEAD]
        return jnp.concatenate([a * cosine - b * sine, b * cosine + a * sine, rest], axis=0).astype(low)

    for h in range(HEADS):
        q_ref[h * HEAD : (h + 1) * HEAD, :] = turned(h * HEAD) * jnp.asarray(HEAD ** (-0.5), low)
    kv_ref[:HEAD, :] = turned(D)
    kv_ref[HEAD:, :] = projected[D + HEAD :].astype(low)


def head(device, x, near, far, offset, size, out_rows, cosine, sine, groups, vec_len, shards_of):
    tokens = x.shape[0]
    count = device.shape[0]
    plane, depth = 2 * near[0].shape[1], near[0].shape[2]
    vmem, hbm = pl.BlockSpec(memory_space=pltpu.VMEM), pl.BlockSpec(memory_space=pl.ANY)
    return pl.pallas_call(
        functools.partial(head_kernel, vec_len, offset, out_rows),
        in_specs=[pl.BlockSpec(memory_space=pltpu.SMEM), vmem, hbm, hbm, hbm, hbm, vmem, vmem],
        out_shape=[
            jax.ShapeDtypeStruct((tokens, D), low),
            jax.ShapeDtypeStruct((tokens, D), low),
            jax.ShapeDtypeStruct((D, tokens), low),
            jax.ShapeDtypeStruct((2 * HEAD, tokens), low),
            jax.ShapeDtypeStruct((D + 2 * HEAD, D), low),
            jax.ShapeDtypeStruct((2, D), f32),
            jax.ShapeDtypeStruct((1, D), f32),
        ]
        + [jax.ShapeDtypeStruct((1, FF // 2 // groups), f32)] * (2 * groups)
        + [jax.ShapeDtypeStruct((D, D), low)] * (out_rows > 0),
        scratch_shapes=[
            pltpu.VMEM((1, shards_of * vec_len), f32),
            pltpu.VMEM((count, FF // count), f32),
            pltpu.VMEM((2, 2, plane, depth, size, D), low),
            pltpu.VMEM((count, size, D), f32),
            pltpu.VMEM((count, max(out_rows, 8), D), f32),
            pltpu.SemaphoreType.DMA((2, 2 * plane)),
        ],
        compiler_params=pltpu.CompilerParams(vmem_limit_bytes=FEED_VMEM),
        cost_estimate=pl.CostEstimate(flops=4 * 2 * tokens * 896 * D, bytes_accessed=8 << 20, transcendentals=0),
        name="head",
    )(device, x, *near, *far, cosine, sine)


def tail_kernel(
    shards_of, entry_ref, x_ref, dy_ref, dq_ref, dkv_ref, cos_ref, sin_ref, w_ref, n_ref, context_ref, d_two_ref, gain_ref, *refs
):
    bias_refs, (in_grad_ref, qkv_ref, out_ref, flat, units) = refs[:-5], refs[-5:]
    d_kv = dkv_ref[...]
    a, b = d_kv[: ROT // 2], d_kv[ROT // 2 : ROT]
    cosine, sine = cos_ref[...], sin_ref[...]
    d_kv = jnp.concatenate([a * cosine + b * sine, b * cosine - a * sine, d_kv[ROT:]], axis=0).astype(low)
    d_proj = jnp.concatenate([dq_ref[...], d_kv], axis=0)
    first = (((0,), (0,)), ((), ()))
    qkv_grad = jnp.dot(d_proj, n_ref[...], preferred_element_type=f32)
    out_grad = lax.dot_general(dy_ref[...], context_ref[...], first, preferred_element_type=f32)
    d_one = lax.dot_general(d_proj, w_ref[...], first, preferred_element_type=f32)
    d_two = d_two_ref[...]
    x = x_ref[...].astype(f32)
    dy = dy_ref[...].astype(f32)
    center = x - jnp.mean(x, axis=-1, keepdims=True)
    inv_sigma = lax.rsqrt(jnp.mean(center * center, axis=-1, keepdims=True) + layer_eps)
    xhat = center * inv_sigma
    d_hat = d_one * gain_ref[0:1] + d_two * gain_ref[1:2]
    d_in = (
        d_hat - jnp.mean(d_hat, axis=-1, keepdims=True) - xhat * jnp.mean(d_hat * xhat, axis=-1, keepdims=True)
    ) * inv_sigma
    in_grad_ref[...] = (dy + d_in).astype(low)
    columns = lambda v: jnp.sum(v, axis=0, keepdims=True)
    dy_column = columns(dy)
    ones = jnp.ones((8, d_proj.shape[1]), low)
    proj_sum = lax.dot_general(ones, d_proj, (((1,), (1,)), ((), ())), preferred_element_type=f32)[0:1]
    pieces = [columns(d_one * xhat), columns(d_one), columns(d_two * xhat), columns(d_two)]
    pieces += [proj_sum, dy_column, None, dy_column]
    count, size = units.shape
    groups = len(bias_refs) // 2
    width = size // groups
    for k, ref in enumerate(bias_refs):
        side, g = k // groups, k % groups
        for i in range(count // 2):
            place = side * (count // 2) + i
            units[place : place + 1, g * width : (g + 1) * width] = ref[:, i * width : (i + 1) * width]
    offset = 0
    for piece in pieces:
        if piece is None:
            for k in range(count):
                flat[:, offset : offset + size] = units[pl.ds(entry_ref[k], 1), :]
                offset += size
        else:
            flat[:, offset : offset + piece.shape[1]] = piece
            offset += piece.shape[1]
    qkv_rows, vec_len = qkv_grad.shape[0] // shards_of, flat.shape[1] // shards_of
    to_shard = count // shards_of
    share = lambda k, total: [k // to_shard * total + min(-(-total // to_shard) * j, total) for j in (k % to_shard, k % to_shard + 1)]
    out_own = D // count
    vec_row = qkv_ref.shape[1] - 4
    for k in range(count):
        to = entry_ref[k]
        begin, end = share(k, qkv_rows)
        qkv_ref[to] = jnp.zeros(qkv_ref.shape[1:], f32)
        if end > begin:
            qkv_ref[to, : end - begin, :] = qkv_grad[begin:end]
        begin, end = share(k, vec_len)
        if end > begin:
            qkv_ref[to, vec_row : vec_row + 1, : end - begin] = flat[:, begin:end]
        out_ref[to] = jnp.zeros(out_ref.shape[1:], f32)
        out_ref[to, :out_own, :] = out_grad[k * out_own : (k + 1) * out_own]


def tail(entry, x, dy, dq_t, dkv, cosine, sine, weight, normed, context, d_two, gains, bias_grads, rows, shards_of, vec_len):
    tokens = x.shape[0]
    count = entry.shape[0]
    operands = (entry, x, dy, dq_t, dkv, cosine, sine, weight, normed, context, d_two, gains, *sum(bias_grads, []))
    return pl.pallas_call(
        functools.partial(tail_kernel, shards_of),
        in_specs=[pl.BlockSpec(memory_space=pltpu.SMEM)] + [pl.BlockSpec(memory_space=pltpu.VMEM)] * (len(operands) - 1),
        out_shape=[
            jax.ShapeDtypeStruct((tokens, D), low),
            jax.ShapeDtypeStruct((count, rows, D), f32),
            jax.ShapeDtypeStruct((count, rows, D), f32),
        ],
        scratch_shapes=[pltpu.VMEM((1, shards_of * vec_len), f32), pltpu.VMEM((count, FF // count), f32)],
        compiler_params=pltpu.CompilerParams(vmem_limit_bytes=VMEM_LIMIT),
        cost_estimate=pl.CostEstimate(flops=4 * 6 * tokens * 896 * D, bytes_accessed=8 << 20, transcendentals=0),
        name="tail",
    )(*operands)


def split_low(value):
    high = value.astype(low)
    return high, (value - high.astype(f32)).astype(low)


def update_step(across, grad, high, rest, w_ref, first_ref, second_ref, grad_ref, first_new_ref, second_new_ref, w_new_ref):
    rotated = jnp.dot(grad, high, preferred_element_type=f32) + jnp.dot(grad, rest, preferred_element_type=f32)
    grad = grad.astype(f32)
    if across:
        rotated, grad = rotated.T, grad.T
    grad_ref[...] = grad
    ratio, first_new, second_new = moments(rotated, first_ref[...], second_ref[...])
    first_new_ref[...] = first_new
    second_new_ref[...] = second_new
    r_high, r_rest = split_low(ratio)
    if across:
        product = lambda r, b: jnp.dot(b, r, preferred_element_type=f32)
    else:
        product = lambda r, b: lax.dot_general(r, b, (((1,), (1,)), ((), ())), preferred_element_type=f32)
    unrotated = product(r_high, high) + (product(r_high, rest) + product(r_rest, high))
    w_new_ref[...] = w_ref[...] - matrix_rate * unrotated


def update_kernel(across, grad_ref, high_ref, rest_ref, *refs):
    update_step(across, grad_ref[...], high_ref[...], rest_ref[...], *refs)


def update(grad, basis, weight, first, second, across=False):
    return pl.pallas_call(
        functools.partial(update_kernel, across),
        out_shape=[jax.ShapeDtypeStruct(weight.shape, f32)] * 4,
        compiler_params=pltpu.CompilerParams(vmem_limit_bytes=UPDATE_VMEM),
        cost_estimate=pl.CostEstimate(flops=10 * grad.shape[0] * D * D, bytes_accessed=8 << 20, transcendentals=0),
        name="update",
    )(grad, *basis, weight, first, second)


def outer_update_kernel(share, own, offset, g_ref, *refs):
    qkv_in, out_in, qkv_out, out_out, (qkv_rows, out_rows) = refs[:5], refs[5:10], refs[10:14], refs[14:18], refs[18:]
    for q in range(g_ref.shape[0]):
        part = g_ref[q].astype(f32)
        count = min(share, qkv_rows.shape[0] - q * share)
        if count > 0:
            qkv_rows[q * share : q * share + count, :] = part[:count]
        out_rows[q * own : (q + 1) * own, :] = part[offset : offset + own]
    for rows, (high_ref, rest_ref, *state), outs in ((qkv_rows, qkv_in, qkv_out), (out_rows, out_in, out_out)):
        update_step(False, rows[...].astype(low), high_ref[...], rest_ref[...], *state, *outs)


def outer_update(grads, share, own, offset, qkv, out):
    operands = [value for basis, *state in (qkv, out) for value in (*basis, *state)]
    shapes = [qkv[1].shape] * 4 + [out[1].shape] * 4
    new = pl.pallas_call(
        functools.partial(outer_update_kernel, share, own, offset),
        out_shape=[jax.ShapeDtypeStruct(shape, f32) for shape in shapes],
        scratch_shapes=[pltpu.VMEM(qkv[1].shape, f32), pltpu.VMEM(out[1].shape, f32)],
        compiler_params=pltpu.CompilerParams(vmem_limit_bytes=VMEM_LIMIT),
        cost_estimate=pl.CostEstimate(flops=10 * 208 * D * D, bytes_accessed=8 << 20, transcendentals=0),
        name="outer_update",
    )(grads, *operands)
    return new[:4], new[4:]


def shards(
    inputs,
    cotangent,
    doc_lengths,
    qkv_weight,
    out_weight,
    up_weight,
    down_weight,
    vectors,
    bases,
    qkv_first,
    out_first,
    up_first,
    down_first,
    vector_first,
    qkv_second,
    out_second,
    up_second,
    down_second,
    vector_second,
):
    seq_count, batch_count = lax.axis_size("seq"), lax.axis_size("batch")
    seq_index, batch_index = lax.axis_index("seq"), lax.axis_index("batch")
    row_count, shard_len = inputs.shape[:2]
    tokens = row_count * shard_len
    y_bit, *z_bits = bit_names("seq", seq_count)
    core_bit, *x_bits = bit_names("batch", batch_count)
    near = [core_bit] + x_bits[::-1] + [y_bit] + z_bits[::-1]
    depth = seq_count // 2
    plane = 2 ** (len(x_bits) + 1)
    x_low = inputs.reshape(tokens, D)
    dy = cotangent.reshape(tokens, D)

    first_pos = seq_index * shard_len
    query_pos = first_pos + jnp.arange(shard_len, dtype=jnp.int32)
    docs = doc_lengths.shape[1]
    earlier = jnp.arange(docs)[:, None] < jnp.arange(docs)[None, :]
    doc_starts = jnp.sum(jnp.where(earlier[None], doc_lengths[:, :, None], 0), axis=1)
    start = jnp.max(
        jnp.where(doc_starts[:, None, :] <= query_pos[None, :, None], doc_starts[:, None, :], 0), axis=-1
    )
    offsets = (query_pos[None, :] - start).reshape(tokens)
    inverse = 1.0 / rope_base ** (jnp.arange(0, ROT, 2).astype(f32) / ROT)
    angles = offsets.astype(f32)[None, :] * inverse[:, None]
    cosine, sine = jnp.cos(angles), jnp.sin(angles)
    start_here = (start - first_pos).astype(jnp.int32)[:, None, :]
    number = jnp.arange(seq_count * batch_count, dtype=jnp.int32)

    def bits_of(value, place_of):
        total = 0
        for k, (axis_name, step) in enumerate(near[::-1]):
            total = total + place_of(value, k, axis_name, step)
        return total

    differs = {"seq": (number // batch_count) ^ seq_index, "batch": (number % batch_count) ^ batch_index}
    entry = bits_of(number, lambda v, k, name, step: (differs[name] // step) % 2 << k).astype(jnp.int32)
    xor_of = lambda name: sum((number >> k) % 2 * step for k, (axis_name, step) in enumerate(near[::-1]) if axis_name == name)
    device = ((xor_of("seq") ^ seq_index) * batch_count + (xor_of("batch") ^ batch_index)).astype(jnp.int32)

    qkv_rows, out_rows, up_rows, vec_len = qkv_weight.shape[0], out_weight.shape[0], up_weight.shape[0], vectors.shape[0]
    vec_rows = -(-vec_len // D)
    used = qkv_rows + vec_rows
    head_rows = -(-used // (8 * batch_count)) * 8 * batch_count
    vec_pad = vec_rows * D - vec_len

    def own_part(rows):
        size = rows.shape[0] // batch_count
        return lax.dynamic_slice_in_dim(rows, batch_index * size, size, axis=0)

    head_shard = jnp.concatenate(
        [qkv_weight, jnp.pad(vectors, (0, vec_pad)).reshape(vec_rows, D), jnp.zeros((head_rows - used, D), f32)], axis=0
    ).astype(low)
    head_part_rows = head_rows // batch_count
    unit_rows = up_rows // batch_count // GROUPS
    out_own = out_rows // batch_count
    up_low, down_low = own_part(up_weight.astype(low)), own_part(down_weight.T.astype(low))
    outer = [
        own_part(head_shard),
        jnp.concatenate([own_part(out_weight.astype(low)), jnp.zeros((head_part_rows - out_own, D), low)], axis=0),
    ]
    parts_of = []
    for g in range(GROUPS):
        rows = slice(g * unit_rows, (g + 1) * unit_rows)
        pieces = [up_low[rows], outer[0], down_low[rows], outer[1]] if g == 0 else [up_low[rows], down_low[rows]]
        parts_of.append(jnp.concatenate(pieces, axis=0))

    def gather_first(parts):
        half = parts.shape[1] // 2
        up, down = parts[:, :half], parts[:, half:]
        for bit in x_bits[:-1]:
            down = gather_bit(down, bit, 0)
        return up, down, swap(up, y_bit), swap(down, x_bits[-1])

    def gather_second(up, down, up_got, down_got):
        up, down = jnp.stack([up, up_got]), jnp.stack([down, down_got])
        for bit in x_bits[:-1]:
            up = gather_bit(up, bit, 0)
        shape = (1, plane // 2, depth) + up.shape[-2:]
        return up, down, jnp.concatenate([up.reshape(shape), down.reshape(shape)], axis=0)

    def gather_last(up, down):
        return swap(up, x_bits[-1]), swap(down, y_bit)

    def joined(up, down):
        shape = (1, plane // 2, depth) + up.shape[-2:]
        return jnp.concatenate([up.reshape(shape), down.reshape(shape)], axis=0)

    z_zero = gather_z(parts_of[0])
    *z_zero, cosine, sine, start_here, entry, device, part_one = hold(
        *z_zero, cosine, sine, start_here, entry, device, parts_of[1]
    )
    up, down, up_got, down_got = gather_first(jnp.stack(z_zero))
    z_one = gather_z(part_one)
    up_got, down_got, z_one[1] = hold(up_got, down_got, z_one[1])
    up, down, first_zero = gather_second(up, down, up_got, down_got)
    up_got, down_got = gather_last(up, down)
    first_far_zero = swap(first_zero, core_bit)
    late_bases, up, down = hold(bases, up, down)
    split_bases = [part for k in range(4) for part in split_low(late_bases[k])]
    up_got, down_got, first_far_zero, *rest = hold(up_got, down_got, first_far_zero, *z_one[2:], *split_bases)
    z_one[2:], split_bases = rest[: len(z_one) - 2], rest[len(z_one) - 2 :]
    split_bases = [split_bases[2 * k : 2 * k + 2] for k in range(4)]
    last_zero = joined(up_got, down_got)
    last_far_zero = swap(last_zero, core_bit)

    aligned = unit_rows % 16 == 0 and head_part_rows % 16 == 0
    trim = lambda values, begin, end: values if aligned else tuple(v[..., begin:end, :] for v in values)
    near_zero, far_zero = (first_zero, last_zero), (first_far_zero, last_far_zero)
    end = unit_rows + head_part_rows

    inside = out_own % 8 == 0
    normed_one, normed_two, q_t, kv_own, qkv_full, gains, out_bias, *bias_rows = head(
        device, x_low, trim(near_zero, unit_rows, end), trim(far_zero, unit_rows, end), unit_rows if aligned else 0,
        head_part_rows, out_own if inside else 0, cosine, sine, GROUPS, vec_len, seq_count,
    )
    if inside:
        out_full = bias_rows.pop()
    else:
        chosen = (entry[:, None] == number[None, :]).astype(low)
        sides = []
        for pair in (near_zero, far_zero):
            along = [v[1, :, :, unit_rows : unit_rows + out_own] for v in pair]
            sides.append(jnp.stack(along, axis=1).reshape(-1, out_own * D))
        out_full = jnp.dot(chosen, jnp.concatenate(sides, axis=0), preferred_element_type=f32).astype(low).reshape(D, D)
    bias_rows = [bias_rows[:GROUPS], bias_rows[GROUPS:]]
    reach = seq_count // 2

    def shifted(value, step, back=False):
        pairs = [(j, j + step) for j in range(seq_count - step)]
        return lax.ppermute(value, "seq", [(b, a) for a, b in pairs] if back else pairs)

    farthest, pair = shifted(kv_own, reach), shifted(kv_own[None], 1)
    up, down, up_got, down_got = gather_first(jnp.stack(z_one))
    up_got, down_got, normed_two = hold(up_got, down_got, normed_two)
    up, down, first_one = gather_second(up, down, up_got, down_got)
    up_got, down_got = gather_last(up, down)
    first_far_one = swap(first_one, core_bit)

    last = (((1,), (1,)), ((), ()))
    bias_grads = [[], []]

    def feed_group(g, sums, normed, near, far, *beside):
        *sums, far_grad, near_grad, bias_far, bias_here = feed(
            normed, dy, trim(far, 0, unit_rows), trim(near, 0, unit_rows), bias_rows[1][g], bias_rows[0][g], unit_rows, sums
        )
        bias_grads[0].append(bias_here)
        bias_grads[1].append(bias_far)
        far_grad, *beside = hold(far_grad, *beside)
        shape = (2,) + (2,) * len(x_bits) + (2, depth, unit_rows, D)
        grad_sum = (near_grad + swap(far_grad, core_bit).astype(f32)).reshape(shape)
        return sums, grad_sum[0], grad_sum[1], *beside

    def sum_first(up, down):
        (up_kept, up_sent), (down_kept, down_sent) = split_bit(up, x_bits[-1], 0), split_bit(down, y_bit, len(x_bits))
        return up_kept, up_sent, down_kept, down_sent

    def send_first(sums):
        return swap(sums[1], x_bits[-1]), swap(sums[3], y_bit)

    def sum_second(sums, up_got, down_got):
        up = sums[0] + up_got.astype(f32)
        for bit in x_bits[-2::-1]:
            kept, sent = split_bit(up, bit, 0)
            up = kept + swap(sent, bit).astype(f32)
        down = sums[2] + down_got.astype(f32)
        (up_kept, up_sent), (down_kept, down_sent) = split_bit(up, y_bit, 0), split_bit(down, x_bits[-1], 0)
        return up_kept, up_sent, down_kept, down_sent

    def send_second(sums):
        return swap(sums[1], y_bit), swap(sums[3], x_bits[-1])

    def sum_third(up_kept, up_got, down_kept, down_got):
        up = up_kept + up_got.astype(f32)
        down = down_kept + down_got.astype(f32)
        for bit in x_bits[-2::-1]:
            kept, sent = split_bit(down, bit, 0)
            down = kept + swap(sent, bit).astype(f32)
        return jnp.concatenate([up, down], axis=1)

    def send_z(value):
        return [swap_z(value[k].astype(low), k) for k in range(1, depth)]

    def sum_z(value, got):
        return value[0] + sum(part.astype(f32) for part in got)

    def spread(part):
        value = part.astype(low)
        for bit in x_bits:
            value = gather_bit(value, bit, 0, True)
        return gather_bit(value, core_bit, len(x_bits), True).reshape(batch_count, -1, D)

    sums, up_sum, down_sum, up_got, down_got, farthest, pair = feed_group(
        0, None, normed_two, near_zero, far_zero, up_got, down_got, farthest, pair
    )
    kv = jnp.concatenate([kv_own[None], pair], axis=0)
    while kv.shape[0] < reach:
        kv = jnp.concatenate([kv, shifted(kv, kv.shape[0])], axis=0)
    kv = jnp.concatenate([kv, farthest[None]], axis=0)
    sum_zero = sum_first(up_sum, down_sum)
    *sum_zero, first_far_one, q_t = hold(*sum_zero, first_far_one, q_t)
    last_one = joined(up_got, down_got)
    last_far_one = swap(last_one, core_bit)

    do_t = lax.dot_general(out_full, dy, (((0,), (1,)), ((), ())), preferred_element_type=f32).astype(low)
    context, dq_t, dkv_own, dkv_sent = attention(q_t, do_t, start_here, cosine, sine, kv)
    sum_zero = sum_second(sum_zero, *send_first(sum_zero))
    last_far_one, dq_t, normed_late, *sum_zero = hold(last_far_one, dq_t, normed_two, *sum_zero)
    dkv_far = shifted(dkv_sent[reach - 1], reach, True)
    dkv = [dkv_own] + [dkv_sent[i] for i in range(reach - 1)]
    middle = reach // 2
    got = shifted(dkv_sent[middle - 1 : reach - 1], middle, True)
    up_got, down_got = send_second(sum_zero)
    (mlp_out, d_normed_two), up_sum, down_sum, up_got, down_got, dkv_far, got = feed_group(
        1, sums, normed_late, (first_one, last_one), (first_far_one, last_far_one), up_got, down_got, dkv_far, got
    )
    sum_zero = sum_third(sum_zero[0], up_got, sum_zero[2], down_got)
    dkv = [dkv[i].astype(f32) + got[i].astype(f32) for i in range(middle)]
    while middle > 1:
        middle //= 2
        got = shifted(jnp.stack([part.astype(low) for part in dkv[middle : 2 * middle]]), middle, True)
        dkv = [dkv[i] + got[i].astype(f32) for i in range(middle)]
    dkv = dkv[0] + dkv_far.astype(f32)
    qkv_share, vec_share = -(-qkv_rows // batch_count), -(-vec_len // batch_count)
    sum_one = sum_first(up_sum, down_sum)
    dkv, *sum_one = hold(dkv, *sum_one)
    up_got, down_got = send_first(sum_one)
    z_got = send_z(sum_zero)
    input_grad, qkv_part, out_part = tail(
        entry, x_low, dy, dq_t, dkv, cosine, sine, qkv_full, normed_one, context, d_normed_two, gains, bias_grads,
        head_part_rows, seq_count, vec_len,
    )
    qkv_part, up_got, down_got, *z_got = hold(qkv_part, up_got, down_got, *z_got)
    sum_one = sum_second(sum_one, up_got, down_got)
    one_got = send_second(sum_one)
    outer_shape = (2,) + (2,) * len(x_bits) + (2, depth, head_part_rows, D)
    qkv_part, out_part = qkv_part.reshape(outer_shape), out_part.reshape(outer_shape)
    got = swap(jnp.stack([qkv_part[1].astype(low), out_part[1].astype(low)]), core_bit)
    got, mlp_late, context_late, *one_got = hold(got, mlp_out, context, *one_got)
    sum_outer = sum_first(qkv_part[0] + got[0].astype(f32), out_part[0] + got[1].astype(f32))
    outer_got = send_first(sum_outer)
    sum_one = sum_third(sum_one[0], one_got[0], sum_one[2], one_got[1])
    one_got = send_z(sum_one)
    feed_zero = sum_z(sum_zero, z_got)
    attn_out = lax.dot_general(context_late, out_full, last, preferred_element_type=f32)
    outputs = (x_low.astype(f32) + attn_out + mlp_late + out_bias).astype(low)
    sum_outer = sum_second(sum_outer, *outer_got)
    outer_got = send_second(sum_outer)
    outer_got, one_got, (outputs,) = hold_lists(outer_got, one_got, [outputs])
    sum_outer = sum_third(sum_outer[0], outer_got[0], sum_outer[2], outer_got[1])
    outer_got = send_z(sum_outer)
    grads_feed = spread(jnp.concatenate([feed_zero, sum_z(sum_one, one_got)], axis=0))
    grads_feed = grads_feed.reshape(batch_count, GROUPS, 2, unit_rows, D).transpose(2, 0, 1, 3, 4).reshape(2, -1, D)
    (up_all, down_all), outer_got = hold_lists([grads_feed[0], grads_feed[1]], outer_got)
    up_out = update(up_all, split_bases[2], up_weight, up_first, up_second)
    grads_outer = spread(sum_z(sum_outer, outer_got))
    down_out = update(down_all, split_bases[3], down_weight, down_first, down_second, True)
    down_out, grads_outer = hold_lists(down_out, [grads_outer])
    grads_outer = grads_outer[0]
    (up_grad, *up_states), (down_grad, *down_states) = up_out, down_out
    (qkv_grad, *qkv_states), (out_grad, *out_states) = outer_update(
        grads_outer, qkv_share, out_own, head_part_rows,
        (split_bases[0], qkv_weight, qkv_first, qkv_second), (split_bases[1], out_weight, out_first, out_second),
    )
    vector_grad = grads_outer[:, head_part_rows - 4, :vec_share].astype(f32).reshape(-1)[:vec_len]
    vector_new, *vector_states = adam_step(vectors, vector_grad, vector_first, vector_second)
    states = (qkv_states, out_states, up_states, down_states, (*vector_states, vector_new))
    return (
        outputs.reshape(inputs.shape),
        input_grad.reshape(inputs.shape),
        qkv_grad,
        out_grad,
        up_grad,
        down_grad,
        vector_grad,
        *(state[0] for state in states),
        *(state[1] for state in states),
        *(state[2] for state in states),
    )


def solution(mesh):
    tokens = P("batch", "seq", None)
    rows, columns, flat = P("seq", None), P(None, "seq"), P("seq")
    params = (rows, rows, rows, columns, flat)
    return jax.shard_map(
        shards,
        mesh=mesh,
        in_specs=(tokens, tokens, P("batch", None)) + params + (P(),) + params + params,
        out_specs=(tokens, tokens) + params * 4,
        check_vma=False,
    )
```

```python
import functools

import jax
import jax.numpy as jnp
from jax import lax
from jax.experimental import pallas as pl
from jax.experimental.pallas import tpu as pltpu
from jax.sharding import PartitionSpec as P

D = 768
HEADS = 12
HEAD = 64
ROT = 16
FF = 3072
STEP = 10

layer_eps = 1e-05
adam_eps = 1e-08
beta_first = 0.95
beta_second = 0.95
matrix_rate = 0.08
vector_rate = 0.3
rope_base = 10000.0
masked_score = -1e30
low = jnp.bfloat16
f32 = jnp.float32
VMEM_LIMIT = 56 * 1024 * 1024
GROUPS = 2
FEED_VMEM = 56 * 1024 * 1024
UPDATE_VMEM = 28 * 1024 * 1024


def swap(value, bit):
    axis, step = bit
    return lax.ppermute(value, axis, [(i, i ^ step) for i in range(lax.axis_size(axis))])


def mine(bit):
    axis, step = bit
    return lax.rem(lax.axis_index(axis) // step, 2)


def hold(*values):
    return lax.optimization_barrier(values)


def hold_lists(*lists):
    flat = iter(hold(*(value for values in lists for value in values)))
    return [[next(flat) for _ in values] for values in lists]


def swap_z(value, step):
    size = lax.axis_size("seq")
    return lax.ppermute(value, "seq", [(i, i ^ (2 * step)) for i in range(size)])


def gather_z(piece):
    return [piece] + [swap_z(piece, k) for k in range(1, lax.axis_size("seq") // 2)]


def gather_bit(value, bit, axis, absolute=False):
    got = swap(value, bit)
    if absolute:
        upper = mine(bit) == 1
        return jnp.stack([jnp.where(upper, got, value), jnp.where(upper, value, got)], axis=axis)
    return jnp.stack([value, got], axis=axis)


def split_bit(value, bit, axis):
    return lax.index_in_dim(value, 0, axis, keepdims=False), lax.index_in_dim(value, 1, axis, keepdims=False).astype(low)


def bit_names(axis, size):
    return [(axis, 1 << k) for k in range(size.bit_length() - 1)]


def moments(rotated, first, second):
    new_first = beta_first * first + (1.0 - beta_first) * rotated
    new_second = beta_second * second + (1.0 - beta_second) * rotated * rotated
    first_scale, second_scale = 1.0 / (1.0 - beta_first**STEP), 1.0 / (1.0 - beta_second**STEP)
    ratio = new_first * first_scale / (jnp.sqrt(new_second * second_scale) + adam_eps)
    return ratio, new_first, new_second


def adam_step(weight, grad, first, second):
    ratio, new_first, new_second = moments(grad, first, second)
    return (weight - vector_rate * ratio, new_first, new_second)


def attend(blocks, width, q_ref, do_ref, start_ref, cos_ref, sin_ref, kv_ref, context_ref, dq_ref, dkv_own_ref, dkv_ref):
    length = q_ref.shape[1]
    keys = blocks * length
    key_t = jnp.concatenate([kv_ref[k, :HEAD, :] for k in reversed(range(blocks))], axis=1)
    value_t = jnp.concatenate([kv_ref[k, HEAD:, :] for k in reversed(range(blocks))], axis=1)
    key = key_t.astype(f32).T.astype(low)
    value = value_t.astype(f32).T.astype(low)
    key_pos = lax.broadcasted_iota(jnp.int32, (keys, length), 0) - (blocks - 1) * length
    query_pos = lax.broadcasted_iota(jnp.int32, (keys, length), 1)
    allowed = (key_pos >= start_ref[0]) & (key_pos <= query_pos)
    bias = jnp.where(allowed, 0.0, masked_score)
    cosine, sine = cos_ref[...], sin_ref[...]
    d_key = jnp.zeros((keys, HEAD), f32)
    d_value = jnp.zeros((keys, HEAD), f32)
    last = (((1,), (1,)), ((), ()))
    for first in range(0, HEADS, width):
        heads = range(first, first + width)
        query = jnp.concatenate([q_ref[h * HEAD : (h + 1) * HEAD, :] for h in heads], axis=1)
        d_out = jnp.concatenate([do_ref[h * HEAD : (h + 1) * HEAD, :] for h in heads], axis=1)
        scores = jnp.dot(key, query, preferred_element_type=f32)
        scores = scores + jnp.concatenate([bias] * width, axis=1)
        weights = jnp.exp(scores - jnp.max(scores, axis=0, keepdims=True))
        probs = weights * (1.0 / jnp.sum(weights, axis=0, keepdims=True))
        probs_low = probs.astype(low)
        context_t = jnp.dot(value_t, probs_low, preferred_element_type=f32)
        d_probs = jnp.dot(value, d_out, preferred_element_type=f32)
        inner = jnp.sum(probs * d_probs, axis=0, keepdims=True)
        d_scores = (probs * (d_probs - inner)).astype(low)
        d_query = jnp.dot(key_t, d_scores, preferred_element_type=f32) * HEAD ** (-0.5)
        d_value = d_value + lax.dot_general(probs_low, d_out, last, preferred_element_type=f32)
        d_key = d_key + lax.dot_general(d_scores, query, last, preferred_element_type=f32)
        for k, h in enumerate(heads):
            lanes = slice(k * length, (k + 1) * length)
            part = d_query[:, lanes]
            a, b = part[: ROT // 2], part[ROT // 2 : ROT]
            turned = jnp.concatenate([a * cosine + b * sine, b * cosine - a * sine, part[ROT:]], axis=0)
            dq_ref[h * HEAD : (h + 1) * HEAD, :] = turned.astype(low)
        for k in range(0, width, 2):
            h = first + k
            two = jnp.concatenate(
                [context_t[:, k * length : (k + 1) * length], context_t[:, (k + 1) * length : (k + 2) * length]], axis=0
            )
            context_ref[:, h * HEAD : (h + 2) * HEAD] = two.T.astype(low)
    d_kv = jnp.concatenate([d_key, d_value], axis=1).T
    for k in range(blocks):
        part = d_kv[:, (blocks - 1 - k) * length : (blocks - k) * length]
        if k == 0:
            dkv_own_ref[...] = part
        else:
            dkv_ref[k - 1] = part.astype(low)
    for k in range(blocks, kv_ref.shape[0]):
        dkv_ref[k - 1] = jnp.zeros(dkv_ref.shape[1:], low)


def attention_kernel(counts, needed_ref, *refs):
    needed = needed_ref[pl.program_id(0)]
    for least, count in zip([0] + counts, counts):

        @pl.when((needed > least) & (needed <= count))
        def _():
            attend(count, HEADS, *refs)


def attention(q_t, do_t, start, cosine, sine, kv):
    rows, _, length = start.shape
    blocks = kv.shape[0]
    tokens = q_t.shape[1]
    by_row = lambda height: pl.BlockSpec((height, length), lambda r: (0, r))
    needed = 1 + jnp.clip((length - 1 - start[:, 0, 0]) // length, 0, blocks - 1).astype(jnp.int32)
    counts = list(range(1, blocks + 1)) if blocks <= 5 else [1, (blocks + 1) // 2, blocks]
    return pl.pallas_call(
        functools.partial(attention_kernel, counts),
        grid=(rows,),
        in_specs=[pl.BlockSpec(memory_space=pltpu.SMEM), by_row(D), by_row(D), pl.BlockSpec((1, 1, length), lambda r: (r, 0, 0)), by_row(ROT // 2), by_row(ROT // 2)]
        + [pl.BlockSpec((blocks, 2 * HEAD, length), lambda r: (0, 0, r))],
        out_specs=[
            pl.BlockSpec((length, D), lambda r: (r, 0)),
            by_row(D),
            by_row(2 * HEAD),
            pl.BlockSpec((blocks - 1, 2 * HEAD, length), lambda r: (0, 0, r)),
        ],
        out_shape=[
            jax.ShapeDtypeStruct((tokens, D), low),
            jax.ShapeDtypeStruct((D, tokens), low),
            jax.ShapeDtypeStruct((2 * HEAD, tokens), f32),
            jax.ShapeDtypeStruct((blocks - 1, 2 * HEAD, tokens), low),
        ],
        compiler_params=pltpu.CompilerParams(vmem_limit_bytes=VMEM_LIMIT),
        cost_estimate=pl.CostEstimate(
            flops=4 * 7 * tokens * HEADS * blocks * length * HEAD * 2, bytes_accessed=8 << 20, transcendentals=0
        ),
        name="attention",
    )(needed, q_t, do_t, start, cosine, sine, kv)


def gathered_parts(plane, refs, offset, rows):
    half = plane // 2
    out = []
    for end, ref in enumerate(refs):
        for j in range(half):
            out.append((0, end * half + j, ref.at[0, j, :, pl.ds(offset, rows)]))
            out.append((1, 2 * j + end, ref.at[1, j, :, pl.ds(offset, rows)]))
    return out


def feed_kernel(n_ref, dy_ref, first_far, last_far, first_near, last_near, bias_far_ref, bias_near_ref, *refs):
    far_refs, near_refs = (first_far, last_far), (first_near, last_near)
    before = refs[: len(refs) - 11]
    out_ref, dn_ref, far_grad_ref, near_grad_ref, bias_far_grad_ref, bias_near_grad_ref = refs[-11:-5]
    weights, far_sum, near_sum, held, sems = refs[-5:]
    plane = weights.shape[2]
    last = (((1,), (1,)), ((), ()))
    first = (((0,), (0,)), ((), ()))
    loads = [
        [
            pltpu.make_async_copy(source, weights.at[side, kind, k], sems.at[side, 2 * k + kind])
            for kind, k, source in gathered_parts(plane, refs_of, 0, weights.shape[4])
        ]
        for side, refs_of in enumerate((far_refs, near_refs))
    ]
    fetches = [pltpu.make_async_copy(ref, held.at[k], sems.at[2, k]) for k, ref in enumerate(before)]
    for copy in loads[0] + loads[1] + fetches:
        copy.start()
    normed, d_out = n_ref[...], dy_ref[...]
    units = far_sum.shape[1]
    out, d_normed = 0.0, 0.0
    stores = []
    for side, (bias_ref, bias_grad_ref, buffer, grad_ref) in enumerate(
        (
            (bias_far_ref, bias_far_grad_ref, far_sum, far_grad_ref),
            (bias_near_ref, bias_near_grad_ref, near_sum, near_grad_ref),
        )
    ):
        for copy in loads[side]:
            copy.wait()
        up, down = weights[side, 0].reshape(units, D), weights[side, 1].reshape(units, D)
        hidden = lax.dot_general(normed, up, last, preferred_element_type=f32) + bias_ref[...]
        share = 0.5 * (1.0 + lax.erf(hidden * (0.5**0.5)))
        slope = share + hidden * (jnp.exp(-0.5 * hidden * hidden) * (0.5 / 3.141592653589793) ** 0.5)
        active = (hidden * share).astype(low)
        d_active = lax.dot_general(d_out, down, last, preferred_element_type=f32)
        d_hidden = (d_active * slope).astype(low)
        for k, part in enumerate(
            (
                lax.dot_general(d_hidden, normed, first, preferred_element_type=f32),
                lax.dot_general(active, d_out, first, preferred_element_type=f32),
            )
        ):
            buffer[k] = part.astype(buffer.dtype)
            copy = pltpu.make_async_copy(buffer.at[k], grad_ref.at[k], sems.at[3, 2 * side + k])
            copy.start()
            stores.append(copy)
        bias_grad_ref[...] = jnp.sum(d_hidden.astype(f32), axis=0, keepdims=True)
        out = out + jnp.dot(active, down, preferred_element_type=f32)
        d_normed = d_normed + jnp.dot(d_hidden, up, preferred_element_type=f32)
    for copy in fetches:
        copy.wait()
    out_ref[...] = held[0] + out if before else out
    dn_ref[...] = held[1] + d_normed if before else d_normed
    for copy in stores:
        copy.wait()


def feed(normed, d_out, far, near, bias_far, bias_near, rows, before):
    tokens = normed.shape[0]
    plane, depth = 2 * far[0].shape[1], far[0].shape[2]
    units = plane * depth * rows
    before = before or []
    vmem, hbm = pl.BlockSpec(memory_space=pltpu.VMEM), pl.BlockSpec(memory_space=pl.ANY)
    return pl.pallas_call(
        feed_kernel,
        in_specs=[vmem, vmem, hbm, hbm, hbm, hbm, vmem, vmem] + [hbm] * len(before),
        out_specs=[vmem, vmem, hbm, hbm, vmem, vmem],
        out_shape=[
            jax.ShapeDtypeStruct((tokens, D), f32),
            jax.ShapeDtypeStruct((tokens, D), f32),
            jax.ShapeDtypeStruct((2, units, D), low),
            jax.ShapeDtypeStruct((2, units, D), f32),
            jax.ShapeDtypeStruct((1, units), f32),
            jax.ShapeDtypeStruct((1, units), f32),
        ],
        scratch_shapes=[
            pltpu.VMEM((2, 2, plane, depth, rows, D), low),
            pltpu.VMEM((2, units, D), low),
            pltpu.VMEM((2, units, D), f32),
            pltpu.VMEM((2, tokens, D), f32),
            pltpu.SemaphoreType.DMA((4, 2 * plane)),
        ],
        compiler_params=pltpu.CompilerParams(vmem_limit_bytes=FEED_VMEM),
        cost_estimate=pl.CostEstimate(flops=4 * 24 * tokens * units * D, bytes_accessed=8 << 20, transcendentals=0),
        name="feed",
    )(normed, d_out, *far, *near, bias_far, bias_near, *before)


def head_kernel(
    vec_len, offset, out_rows, device_ref, x_ref, first_near, last_near, first_far, last_far, cos_ref, sin_ref, n_one_ref,
    n_two_ref, q_ref, kv_ref, w_ref, gain_ref, bias_ref, *refs
):
    *bias_refs, out_ref, flat, units, held, pieces_of, outs_of, sems = refs if out_rows else (*refs[:-6], None, *refs[-6:])
    _, _, plane, depth, size, _ = held.shape
    copies = [
        pltpu.make_async_copy(source, held.at[side, kind, k], sems.at[side, 2 * k + kind])
        for side, refs_of in enumerate(((first_near, last_near), (first_far, last_far)))
        for kind, k, source in gathered_parts(plane, refs_of, offset, size)
    ]
    for copy in copies:
        copy.start()
    x = x_ref[...].astype(f32)
    center = x - jnp.mean(x, axis=-1, keepdims=True)
    xhat = center * lax.rsqrt(jnp.mean(center * center, axis=-1, keepdims=True) + layer_eps)
    for copy in copies:
        copy.wait()
    for side in range(2):
        for k in range(plane):
            for z in range(depth):
                number = device_ref[(side * plane + k) * depth + z]
                pieces_of[number] = held[side, 0, k, z].astype(f32)
                if out_rows:
                    outs_of[number] = held[side, 1, k, z][:out_rows].astype(f32)
    if out_rows:
        out_ref[...] = outs_of[...].reshape(out_ref.shape).astype(low)
    shards_of = (flat.shape[1]) // vec_len
    rows = (D + 2 * HEAD) // shards_of
    whole = pieces_of[...].reshape(shards_of, -1, D)
    for s in range(shards_of):
        left, row = vec_len, rows
        while left > 0:
            size = min(left, D)
            begin = s * vec_len + (row - rows) * D
            flat[:, begin : begin + size] = whole[s, row : row + 1, :size]
            left -= size
            row += 1
    vector = lambda begin, size: flat[:, begin : begin + size]
    gain_one, shift_one, gain_two, shift_two = [vector(k * D, D) for k in range(4)]
    gain_ref[0:1] = gain_one
    gain_ref[1:2] = gain_two
    qkv_bias = vector(4 * D, D + 2 * HEAD)
    start = 4 * D + D + 2 * HEAD
    bias_ref[...] = vector(start, D) + vector(start + D + FF, D)
    count, size_of = units.shape
    for k in range(count):
        units[k : k + 1, :] = vector(start + D + k * size_of, size_of)
    groups = len(bias_refs) // 2
    for k, ref in enumerate(bias_refs):
        side, g = k // groups, k % groups
        width = size_of // groups
        for i in range(count // 2):
            row = units[pl.ds(device_ref[side * (count // 2) + i], 1), :]
            ref[:, i * width : (i + 1) * width] = row[:, g * width : (g + 1) * width]
    n_one = (xhat * gain_one + shift_one).astype(low)
    n_one_ref[...] = n_one
    n_two_ref[...] = (xhat * gain_two + shift_two).astype(low)
    weight = whole[:, :rows].reshape(shards_of * rows, D).astype(low)
    w_ref[...] = weight
    column = jnp.broadcast_to(qkv_bias, (8, qkv_bias.shape[1])).T[:, 0:1]
    projected = lax.dot_general(weight, n_one, (((1,), (1,)), ((), ())), preferred_element_type=f32) + column
    cosine, sine = cos_ref[...], sin_ref[...]
    half = ROT // 2

    def turned(first):
        a, b = projected[first : first + half], projected[first + half : first + ROT]
        rest = projected[first + ROT : first + HEAD]
        return jnp.concatenate([a * cosine - b * sine, b * cosine + a * sine, rest], axis=0).astype(low)

    for h in range(HEADS):
        q_ref[h * HEAD : (h + 1) * HEAD, :] = turned(h * HEAD) * jnp.asarray(HEAD ** (-0.5), low)
    kv_ref[:HEAD, :] = turned(D)
    kv_ref[HEAD:, :] = projected[D + HEAD :].astype(low)


def head(device, x, near, far, offset, size, out_rows, cosine, sine, groups, vec_len, shards_of):
    tokens = x.shape[0]
    count = device.shape[0]
    plane, depth = 2 * near[0].shape[1], near[0].shape[2]
    vmem, hbm = pl.BlockSpec(memory_space=pltpu.VMEM), pl.BlockSpec(memory_space=pl.ANY)
    return pl.pallas_call(
        functools.partial(head_kernel, vec_len, offset, out_rows),
        in_specs=[pl.BlockSpec(memory_space=pltpu.SMEM), vmem, hbm, hbm, hbm, hbm, vmem, vmem],
        out_shape=[
            jax.ShapeDtypeStruct((tokens, D), low),
            jax.ShapeDtypeStruct((tokens, D), low),
            jax.ShapeDtypeStruct((D, tokens), low),
            jax.ShapeDtypeStruct((2 * HEAD, tokens), low),
            jax.ShapeDtypeStruct((D + 2 * HEAD, D), low),
            jax.ShapeDtypeStruct((2, D), f32),
            jax.ShapeDtypeStruct((1, D), f32),
        ]
        + [jax.ShapeDtypeStruct((1, FF // 2 // groups), f32)] * (2 * groups)
        + [jax.ShapeDtypeStruct((D, D), low)] * (out_rows > 0),
        scratch_shapes=[
            pltpu.VMEM((1, shards_of * vec_len), f32),
            pltpu.VMEM((count, FF // count), f32),
            pltpu.VMEM((2, 2, plane, depth, size, D), low),
            pltpu.VMEM((count, size, D), f32),
            pltpu.VMEM((count, max(out_rows, 8), D), f32),
            pltpu.SemaphoreType.DMA((2, 2 * plane)),
        ],
        compiler_params=pltpu.CompilerParams(vmem_limit_bytes=FEED_VMEM),
        cost_estimate=pl.CostEstimate(flops=4 * 2 * tokens * 896 * D, bytes_accessed=8 << 20, transcendentals=0),
        name="head",
    )(device, x, *near, *far, cosine, sine)


def tail_kernel(
    shards_of, entry_ref, x_ref, dy_ref, dq_ref, dkv_ref, cos_ref, sin_ref, w_ref, n_ref, context_ref, d_two_ref, gain_ref, *refs
):
    bias_refs, (in_grad_ref, kept_ref, sent_ref, flat, units, tile) = refs[:-6], refs[-6:]
    d_kv = dkv_ref[...]
    a, b = d_kv[: ROT // 2], d_kv[ROT // 2 : ROT]
    cosine, sine = cos_ref[...], sin_ref[...]
    d_kv = jnp.concatenate([a * cosine + b * sine, b * cosine - a * sine, d_kv[ROT:]], axis=0).astype(low)
    d_proj = jnp.concatenate([dq_ref[...], d_kv], axis=0)
    first = (((0,), (0,)), ((), ()))
    qkv_grad = jnp.dot(d_proj, n_ref[...], preferred_element_type=f32)
    out_grad = lax.dot_general(dy_ref[...], context_ref[...], first, preferred_element_type=f32)
    d_one = lax.dot_general(d_proj, w_ref[...], first, preferred_element_type=f32)
    d_two = d_two_ref[...]
    x = x_ref[...].astype(f32)
    dy = dy_ref[...].astype(f32)
    center = x - jnp.mean(x, axis=-1, keepdims=True)
    inv_sigma = lax.rsqrt(jnp.mean(center * center, axis=-1, keepdims=True) + layer_eps)
    xhat = center * inv_sigma
    d_hat = d_one * gain_ref[0:1] + d_two * gain_ref[1:2]
    d_in = (
        d_hat - jnp.mean(d_hat, axis=-1, keepdims=True) - xhat * jnp.mean(d_hat * xhat, axis=-1, keepdims=True)
    ) * inv_sigma
    in_grad_ref[...] = (dy + d_in).astype(low)
    columns = lambda v: jnp.sum(v, axis=0, keepdims=True)
    dy_column = columns(dy)
    ones = jnp.ones((8, d_proj.shape[1]), low)
    proj_sum = lax.dot_general(ones, d_proj, (((1,), (1,)), ((), ())), preferred_element_type=f32)[0:1]
    pieces = [columns(d_one * xhat), columns(d_one), columns(d_two * xhat), columns(d_two)]
    pieces += [proj_sum, dy_column, None, dy_column]
    count, size = units.shape
    groups = len(bias_refs) // 2
    width = size // groups
    for k, ref in enumerate(bias_refs):
        side, g = k // groups, k % groups
        for i in range(count // 2):
            place = side * (count // 2) + i
            units[place : place + 1, g * width : (g + 1) * width] = ref[:, i * width : (i + 1) * width]
    offset = 0
    for piece in pieces:
        if piece is None:
            for k in range(count):
                flat[:, offset : offset + size] = units[pl.ds(entry_ref[k], 1), :]
                offset += size
        else:
            flat[:, offset : offset + piece.shape[1]] = piece
            offset += piece.shape[1]
    qkv_rows, vec_len = qkv_grad.shape[0] // shards_of, flat.shape[1] // shards_of
    to_shard = count // shards_of
    share = lambda k, total: [k // to_shard * total + min(-(-total // to_shard) * j, total) for j in (k % to_shard, k % to_shard + 1)]
    out_own = D // count
    half, rows = kept_ref.shape[1:3]
    vec_row = rows - 4

    def put(kind, to):
        @pl.when(to < half)
        def _():
            kept_ref[kind, to] = tile[...]

        @pl.when(to >= half)
        def _():
            sent_ref[kind, to - half] = tile[...].astype(low)

    tile[...] = jnp.zeros_like(tile)
    for k in range(count):
        begin, end = share(k, qkv_rows)
        first_end = end - begin
        if first_end < vec_row:
            tile[first_end:vec_row, :] = jnp.zeros((vec_row - first_end, D), f32)
        if end > begin:
            tile[:first_end, :] = qkv_grad[begin:end]
        begin, end = share(k, vec_len)
        tile[vec_row : vec_row + 1, :] = jnp.zeros((1, D), f32)
        if end > begin:
            tile[vec_row : vec_row + 1, : end - begin] = flat[:, begin:end]
        put(0, entry_ref[k])
    tile[...] = jnp.zeros_like(tile)
    for k in range(count):
        tile[:out_own, :] = out_grad[k * out_own : (k + 1) * out_own]
        put(1, entry_ref[k])


def tail(entry, x, dy, dq_t, dkv, cosine, sine, weight, normed, context, d_two, gains, bias_grads, rows, shards_of, vec_len):
    tokens = x.shape[0]
    count = entry.shape[0]
    operands = (entry, x, dy, dq_t, dkv, cosine, sine, weight, normed, context, d_two, gains, *sum(bias_grads, []))
    return pl.pallas_call(
        functools.partial(tail_kernel, shards_of),
        in_specs=[pl.BlockSpec(memory_space=pltpu.SMEM)] + [pl.BlockSpec(memory_space=pltpu.VMEM)] * (len(operands) - 1),
        out_shape=[
            jax.ShapeDtypeStruct((tokens, D), low),
            jax.ShapeDtypeStruct((2, count // 2, rows, D), f32),
            jax.ShapeDtypeStruct((2, count // 2, rows, D), low),
        ],
        scratch_shapes=[
            pltpu.VMEM((1, shards_of * vec_len), f32), pltpu.VMEM((count, FF // count), f32), pltpu.VMEM((rows, D), f32)
        ],
        compiler_params=pltpu.CompilerParams(vmem_limit_bytes=VMEM_LIMIT),
        cost_estimate=pl.CostEstimate(flops=4 * 6 * tokens * 896 * D, bytes_accessed=8 << 20, transcendentals=0),
        name="tail",
    )(*operands)


def split_low(value):
    high = value.astype(low)
    return high, (value - high.astype(f32)).astype(low)


def update_step(across, grad, high, rest, w_ref, first_ref, second_ref, grad_ref, first_new_ref, second_new_ref, w_new_ref):
    rotated = jnp.dot(grad, high, preferred_element_type=f32) + jnp.dot(grad, rest, preferred_element_type=f32)
    grad = grad.astype(f32)
    if across:
        rotated, grad = rotated.T, grad.T
    grad_ref[...] = grad
    ratio, first_new, second_new = moments(rotated, first_ref[...], second_ref[...])
    first_new_ref[...] = first_new
    second_new_ref[...] = second_new
    r_high, r_rest = split_low(ratio)
    if across:
        product = lambda r, b: jnp.dot(b, r, preferred_element_type=f32)
    else:
        product = lambda r, b: lax.dot_general(r, b, (((1,), (1,)), ((), ())), preferred_element_type=f32)
    unrotated = product(r_high, high) + (product(r_high, rest) + product(r_rest, high))
    w_new_ref[...] = w_ref[...] - matrix_rate * unrotated


def update_kernel(across, grad_ref, high_ref, rest_ref, *refs):
    update_step(across, grad_ref[...], high_ref[...], rest_ref[...], *refs)


def update(grad, basis, weight, first, second, across=False):
    return pl.pallas_call(
        functools.partial(update_kernel, across),
        out_shape=[jax.ShapeDtypeStruct(weight.shape, f32)] * 4,
        compiler_params=pltpu.CompilerParams(vmem_limit_bytes=UPDATE_VMEM),
        cost_estimate=pl.CostEstimate(flops=10 * grad.shape[0] * D * D, bytes_accessed=8 << 20, transcendentals=0),
        name="update",
    )(grad, *basis, weight, first, second)


def outer_update_kernel(share, own, offset, g_ref, *refs):
    qkv_in, out_in, qkv_out, out_out, (qkv_rows, out_rows) = refs[:5], refs[5:10], refs[10:14], refs[14:18], refs[18:]
    for q in range(g_ref.shape[0]):
        part = g_ref[q].astype(f32)
        count = min(share, qkv_rows.shape[0] - q * share)
        if count > 0:
            qkv_rows[q * share : q * share + count, :] = part[:count]
        out_rows[q * own : (q + 1) * own, :] = part[offset : offset + own]
    for rows, (high_ref, rest_ref, *state), outs in ((qkv_rows, qkv_in, qkv_out), (out_rows, out_in, out_out)):
        update_step(False, rows[...].astype(low), high_ref[...], rest_ref[...], *state, *outs)


def outer_update(grads, share, own, offset, qkv, out):
    operands = [value for basis, *state in (qkv, out) for value in (*basis, *state)]
    shapes = [qkv[1].shape] * 4 + [out[1].shape] * 4
    new = pl.pallas_call(
        functools.partial(outer_update_kernel, share, own, offset),
        out_shape=[jax.ShapeDtypeStruct(shape, f32) for shape in shapes],
        scratch_shapes=[pltpu.VMEM(qkv[1].shape, f32), pltpu.VMEM(out[1].shape, f32)],
        compiler_params=pltpu.CompilerParams(vmem_limit_bytes=VMEM_LIMIT),
        cost_estimate=pl.CostEstimate(flops=10 * 208 * D * D, bytes_accessed=8 << 20, transcendentals=0),
        name="outer_update",
    )(grads, *operands)
    return new[:4], new[4:]


def shards(
    inputs,
    cotangent,
    doc_lengths,
    qkv_weight,
    out_weight,
    up_weight,
    down_weight,
    vectors,
    bases,
    qkv_first,
    out_first,
    up_first,
    down_first,
    vector_first,
    qkv_second,
    out_second,
    up_second,
    down_second,
    vector_second,
):
    seq_count, batch_count = lax.axis_size("seq"), lax.axis_size("batch")
    seq_index, batch_index = lax.axis_index("seq"), lax.axis_index("batch")
    row_count, shard_len = inputs.shape[:2]
    tokens = row_count * shard_len
    y_bit, *z_bits = bit_names("seq", seq_count)
    core_bit, *x_bits = bit_names("batch", batch_count)
    near = [core_bit] + x_bits[::-1] + [y_bit] + z_bits[::-1]
    depth = seq_count // 2
    plane = 2 ** (len(x_bits) + 1)
    x_low = inputs.reshape(tokens, D)
    dy = cotangent.reshape(tokens, D)

    first_pos = seq_index * shard_len
    query_pos = first_pos + jnp.arange(shard_len, dtype=jnp.int32)
    docs = doc_lengths.shape[1]
    earlier = jnp.arange(docs)[:, None] < jnp.arange(docs)[None, :]
    doc_starts = jnp.sum(jnp.where(earlier[None], doc_lengths[:, :, None], 0), axis=1)
    start = jnp.max(
        jnp.where(doc_starts[:, None, :] <= query_pos[None, :, None], doc_starts[:, None, :], 0), axis=-1
    )
    offsets = (query_pos[None, :] - start).reshape(tokens)
    inverse = 1.0 / rope_base ** (jnp.arange(0, ROT, 2).astype(f32) / ROT)
    angles = offsets.astype(f32)[None, :] * inverse[:, None]
    cosine, sine = jnp.cos(angles), jnp.sin(angles)
    start_here = (start - first_pos).astype(jnp.int32)[:, None, :]
    number = jnp.arange(seq_count * batch_count, dtype=jnp.int32)

    def bits_of(value, place_of):
        total = 0
        for k, (axis_name, step) in enumerate(near[::-1]):
            total = total + place_of(value, k, axis_name, step)
        return total

    differs = {"seq": (number // batch_count) ^ seq_index, "batch": (number % batch_count) ^ batch_index}
    entry = bits_of(number, lambda v, k, name, step: (differs[name] // step) % 2 << k).astype(jnp.int32)
    xor_of = lambda name: sum((number >> k) % 2 * step for k, (axis_name, step) in enumerate(near[::-1]) if axis_name == name)
    device = ((xor_of("seq") ^ seq_index) * batch_count + (xor_of("batch") ^ batch_index)).astype(jnp.int32)

    qkv_rows, out_rows, up_rows, vec_len = qkv_weight.shape[0], out_weight.shape[0], up_weight.shape[0], vectors.shape[0]
    vec_rows = -(-vec_len // D)
    used = qkv_rows + vec_rows
    head_rows = -(-used // (8 * batch_count)) * 8 * batch_count
    vec_pad = vec_rows * D - vec_len

    def own_part(rows):
        size = rows.shape[0] // batch_count
        return lax.dynamic_slice_in_dim(rows, batch_index * size, size, axis=0)

    head_shard = jnp.concatenate(
        [qkv_weight, jnp.pad(vectors, (0, vec_pad)).reshape(vec_rows, D), jnp.zeros((head_rows - used, D), f32)], axis=0
    ).astype(low)
    head_part_rows = head_rows // batch_count
    unit_rows = up_rows // batch_count // GROUPS
    out_own = out_rows // batch_count
    up_low, down_low = own_part(up_weight.astype(low)), own_part(down_weight.T.astype(low))
    outer = [
        own_part(head_shard),
        jnp.concatenate([own_part(out_weight.astype(low)), jnp.zeros((head_part_rows - out_own, D), low)], axis=0),
    ]
    parts_of = []
    for g in range(GROUPS):
        rows = slice(g * unit_rows, (g + 1) * unit_rows)
        pieces = [up_low[rows], outer[0], down_low[rows], outer[1]] if g == 0 else [up_low[rows], down_low[rows]]
        parts_of.append(jnp.concatenate(pieces, axis=0))

    def gather_first(parts):
        half = parts.shape[1] // 2
        up, down = parts[:, :half], parts[:, half:]
        for bit in x_bits[:-1]:
            down = gather_bit(down, bit, 0)
        return up, down, swap(up, y_bit), swap(down, x_bits[-1])

    def gather_second(up, down, up_got, down_got):
        up, down = jnp.stack([up, up_got]), jnp.stack([down, down_got])
        for bit in x_bits[:-1]:
            up = gather_bit(up, bit, 0)
        shape = (1, plane // 2, depth) + up.shape[-2:]
        return up, down, jnp.concatenate([up.reshape(shape), down.reshape(shape)], axis=0)

    def gather_last(up, down):
        return swap(up, x_bits[-1]), swap(down, y_bit)

    def joined(up, down):
        shape = (1, plane // 2, depth) + up.shape[-2:]
        return jnp.concatenate([up.reshape(shape), down.reshape(shape)], axis=0)

    z_zero = gather_z(parts_of[0])
    *z_zero, cosine, sine, start_here, entry, device, part_one = hold(
        *z_zero, cosine, sine, start_here, entry, device, parts_of[1]
    )
    up, down, up_got, down_got = gather_first(jnp.stack(z_zero))
    z_one = gather_z(part_one)
    up_got, down_got, z_one[1] = hold(up_got, down_got, z_one[1])
    up, down, first_zero = gather_second(up, down, up_got, down_got)
    up_got, down_got = gather_last(up, down)
    first_far_zero = swap(first_zero, core_bit)
    late_bases, up, down = hold(bases, up, down)
    split_bases = [part for k in range(4) for part in split_low(late_bases[k])]
    up_got, down_got, first_far_zero, *rest = hold(up_got, down_got, first_far_zero, *z_one[2:], *split_bases)
    z_one[2:], split_bases = rest[: len(z_one) - 2], rest[len(z_one) - 2 :]
    split_bases = [split_bases[2 * k : 2 * k + 2] for k in range(4)]
    last_zero = joined(up_got, down_got)
    last_far_zero = swap(last_zero, core_bit)

    aligned = unit_rows % 16 == 0 and head_part_rows % 16 == 0
    trim = lambda values, begin, end: values if aligned else tuple(v[..., begin:end, :] for v in values)
    near_zero, far_zero = (first_zero, last_zero), (first_far_zero, last_far_zero)
    end = unit_rows + head_part_rows

    inside = out_own % 8 == 0
    normed_one, normed_two, q_t, kv_own, qkv_full, gains, out_bias, *bias_rows = head(
        device, x_low, trim(near_zero, unit_rows, end), trim(far_zero, unit_rows, end), unit_rows if aligned else 0,
        head_part_rows, out_own if inside else 0, cosine, sine, GROUPS, vec_len, seq_count,
    )
    if inside:
        out_full = bias_rows.pop()
    else:
        chosen = (entry[:, None] == number[None, :]).astype(low)
        sides = []
        for pair in (near_zero, far_zero):
            along = [v[1, :, :, unit_rows : unit_rows + out_own] for v in pair]
            sides.append(jnp.stack(along, axis=1).reshape(-1, out_own * D))
        out_full = jnp.dot(chosen, jnp.concatenate(sides, axis=0), preferred_element_type=f32).astype(low).reshape(D, D)
    bias_rows = [bias_rows[:GROUPS], bias_rows[GROUPS:]]
    reach = seq_count // 2

    def shifted(value, step, back=False):
        pairs = [(j, j + step) for j in range(seq_count - step)]
        return lax.ppermute(value, "seq", [(b, a) for a, b in pairs] if back else pairs)

    farthest, pair = shifted(kv_own, reach), shifted(kv_own[None], 1)
    up, down, up_got, down_got = gather_first(jnp.stack(z_one))
    up_got, down_got, normed_two = hold(up_got, down_got, normed_two)
    up, down, first_one = gather_second(up, down, up_got, down_got)
    up_got, down_got = gather_last(up, down)
    first_far_one = swap(first_one, core_bit)

    last = (((1,), (1,)), ((), ()))
    bias_grads = [[], []]

    def feed_group(g, sums, normed, near, far, *beside):
        *sums, far_grad, near_grad, bias_far, bias_here = feed(
            normed, dy, trim(far, 0, unit_rows), trim(near, 0, unit_rows), bias_rows[1][g], bias_rows[0][g], unit_rows, sums
        )
        bias_grads[0].append(bias_here)
        bias_grads[1].append(bias_far)
        far_grad, *beside = hold(far_grad, *beside)
        shape = (2,) + (2,) * len(x_bits) + (2, depth, unit_rows, D)
        grad_sum = (near_grad + swap(far_grad, core_bit).astype(f32)).reshape(shape)
        return sums, grad_sum[0], grad_sum[1], *beside

    def sum_first(up, down):
        (up_kept, up_sent), (down_kept, down_sent) = split_bit(up, x_bits[-1], 0), split_bit(down, y_bit, len(x_bits))
        return up_kept, up_sent, down_kept, down_sent

    def send_first(sums):
        return swap(sums[1], x_bits[-1]), swap(sums[3], y_bit)

    def sum_second(sums, up_got, down_got):
        up = sums[0] + up_got.astype(f32)
        for bit in x_bits[-2::-1]:
            kept, sent = split_bit(up, bit, 0)
            up = kept + swap(sent, bit).astype(f32)
        down = sums[2] + down_got.astype(f32)
        (up_kept, up_sent), (down_kept, down_sent) = split_bit(up, y_bit, 0), split_bit(down, x_bits[-1], 0)
        return up_kept, up_sent, down_kept, down_sent

    def send_second(sums):
        return swap(sums[1], y_bit), swap(sums[3], x_bits[-1])

    def sum_third(up_kept, up_got, down_kept, down_got):
        up = up_kept + up_got.astype(f32)
        down = down_kept + down_got.astype(f32)
        for bit in x_bits[-2::-1]:
            kept, sent = split_bit(down, bit, 0)
            down = kept + swap(sent, bit).astype(f32)
        return jnp.concatenate([up, down], axis=1)

    def send_z(value):
        return [swap_z(value[k].astype(low), k) for k in range(1, depth)]

    def sum_z(value, got):
        return value[0] + sum(part.astype(f32) for part in got)

    def spread(part):
        value = part.astype(low)
        for bit in x_bits:
            value = gather_bit(value, bit, 0, True)
        return gather_bit(value, core_bit, len(x_bits), True).reshape(batch_count, -1, D)

    sums, up_sum, down_sum, up_got, down_got, farthest, pair = feed_group(
        0, None, normed_two, near_zero, far_zero, up_got, down_got, farthest, pair
    )
    kv = jnp.concatenate([kv_own[None], pair], axis=0)
    while kv.shape[0] < reach:
        kv = jnp.concatenate([kv, shifted(kv, kv.shape[0])], axis=0)
    kv = jnp.concatenate([kv, farthest[None]], axis=0)
    sum_zero = sum_first(up_sum, down_sum)
    *sum_zero, first_far_one, q_t = hold(*sum_zero, first_far_one, q_t)
    last_one = joined(up_got, down_got)
    last_far_one = swap(last_one, core_bit)

    do_t = lax.dot_general(out_full, dy, (((0,), (1,)), ((), ())), preferred_element_type=f32).astype(low)
    context, dq_t, dkv_own, dkv_sent = attention(q_t, do_t, start_here, cosine, sine, kv)
    sum_zero = sum_second(sum_zero, *send_first(sum_zero))
    last_far_one, dq_t, normed_late, *sum_zero = hold(last_far_one, dq_t, normed_two, *sum_zero)
    dkv_far = shifted(dkv_sent[reach - 1], reach, True)
    dkv = [dkv_own] + [dkv_sent[i] for i in range(reach - 1)]
    middle = reach // 2
    got = shifted(dkv_sent[middle - 1 : reach - 1], middle, True)
    up_got, down_got = send_second(sum_zero)
    (mlp_out, d_normed_two), up_sum, down_sum, up_got, down_got, dkv_far, got = feed_group(
        1, sums, normed_late, (first_one, last_one), (first_far_one, last_far_one), up_got, down_got, dkv_far, got
    )
    sum_zero = sum_third(sum_zero[0], up_got, sum_zero[2], down_got)
    dkv = [dkv[i].astype(f32) + got[i].astype(f32) for i in range(middle)]
    while middle > 1:
        middle //= 2
        got = shifted(jnp.stack([part.astype(low) for part in dkv[middle : 2 * middle]]), middle, True)
        dkv = [dkv[i] + got[i].astype(f32) for i in range(middle)]
    dkv = dkv[0] + dkv_far.astype(f32)
    qkv_share, vec_share = -(-qkv_rows // batch_count), -(-vec_len // batch_count)
    sum_one = sum_first(up_sum, down_sum)
    dkv, *sum_one = hold(dkv, *sum_one)
    up_got, down_got = send_first(sum_one)
    z_got = send_z(sum_zero)
    input_grad, kept_part, sent_part = tail(
        entry, x_low, dy, dq_t, dkv, cosine, sine, qkv_full, normed_one, context, d_normed_two, gains, bias_grads,
        head_part_rows, seq_count, vec_len,
    )
    sent_part, up_got, down_got, *z_got = hold(sent_part, up_got, down_got, *z_got)
    sum_one = sum_second(sum_one, up_got, down_got)
    one_got = send_second(sum_one)
    got = swap(sent_part, core_bit)
    got, mlp_late, context_late, *one_got = hold(got, mlp_out, context, *one_got)
    outer = (kept_part + got.astype(f32)).reshape((2,) + (2,) * len(x_bits) + (2, depth, head_part_rows, D))
    sum_outer = sum_first(outer[0], outer[1])
    outer_got = send_first(sum_outer)
    sum_one = sum_third(sum_one[0], one_got[0], sum_one[2], one_got[1])
    one_got = send_z(sum_one)
    feed_zero = sum_z(sum_zero, z_got)
    attn_out = lax.dot_general(context_late, out_full, last, preferred_element_type=f32)
    outputs = (x_low.astype(f32) + attn_out + mlp_late + out_bias).astype(low)
    sum_outer = sum_second(sum_outer, *outer_got)
    outer_got = send_second(sum_outer)
    outer_got, one_got, (outputs,) = hold_lists(outer_got, one_got, [outputs])
    sum_outer = sum_third(sum_outer[0], outer_got[0], sum_outer[2], outer_got[1])
    outer_got = send_z(sum_outer)
    grads_feed = spread(jnp.concatenate([feed_zero, sum_z(sum_one, one_got)], axis=0))
    grads_feed = grads_feed.reshape(batch_count, GROUPS, 2, unit_rows, D).transpose(2, 0, 1, 3, 4).reshape(2, -1, D)
    (up_all, down_all), outer_got = hold_lists([grads_feed[0], grads_feed[1]], outer_got)
    up_out = update(up_all, split_bases[2], up_weight, up_first, up_second)
    grads_outer = spread(sum_z(sum_outer, outer_got))
    down_out = update(down_all, split_bases[3], down_weight, down_first, down_second, True)
    down_out, grads_outer = hold_lists(down_out, [grads_outer])
    grads_outer = grads_outer[0]
    (up_grad, *up_states), (down_grad, *down_states) = up_out, down_out
    (qkv_grad, *qkv_states), (out_grad, *out_states) = outer_update(
        grads_outer, qkv_share, out_own, head_part_rows,
        (split_bases[0], qkv_weight, qkv_first, qkv_second), (split_bases[1], out_weight, out_first, out_second),
    )
    vector_grad = grads_outer[:, head_part_rows - 4, :vec_share].astype(f32).reshape(-1)[:vec_len]
    vector_new, *vector_states = adam_step(vectors, vector_grad, vector_first, vector_second)
    states = (qkv_states, out_states, up_states, down_states, (*vector_states, vector_new))
    return (
        outputs.reshape(inputs.shape),
        input_grad.reshape(inputs.shape),
        qkv_grad,
        out_grad,
        up_grad,
        down_grad,
        vector_grad,
        *(state[0] for state in states),
        *(state[1] for state in states),
        *(state[2] for state in states),
    )


def solution(mesh):
    tokens = P("batch", "seq", None)
    rows, columns, flat = P("seq", None), P(None, "seq"), P("seq")
    params = (rows, rows, rows, columns, flat)
    return jax.shard_map(
        shards,
        mesh=mesh,
        in_specs=(tokens, tokens, P("batch", None)) + params + (P(),) + params + params,
        out_specs=(tokens, tokens) + params * 4,
        check_vma=False,
    )
```

```python
import functools

import jax
import jax.numpy as jnp
from jax import lax
from jax.experimental import pallas as pl
from jax.experimental.pallas import tpu as pltpu
from jax.sharding import PartitionSpec as P

D = 768
HEADS = 12
HEAD = 64
ROT = 16
FF = 3072
STEP = 10

layer_eps = 1e-05
adam_eps = 1e-08
beta_first = 0.95
beta_second = 0.95
matrix_rate = 0.08
vector_rate = 0.3
rope_base = 10000.0
masked_score = -1e30
low = jnp.bfloat16
f32 = jnp.float32
VMEM_LIMIT = 56 * 1024 * 1024
GROUPS = 2
FEED_VMEM = 56 * 1024 * 1024
UPDATE_VMEM = 28 * 1024 * 1024


def swap(value, bit):
    axis, step = bit
    return lax.ppermute(value, axis, [(i, i ^ step) for i in range(lax.axis_size(axis))])


def mine(bit):
    axis, step = bit
    return lax.rem(lax.axis_index(axis) // step, 2)


def hold(*values):
    return lax.optimization_barrier(values)


def hold_lists(*lists):
    flat = iter(hold(*(value for values in lists for value in values)))
    return [[next(flat) for _ in values] for values in lists]


def swap_z(value, step):
    size = lax.axis_size("seq")
    return lax.ppermute(value, "seq", [(i, i ^ (2 * step)) for i in range(size)])


def gather_z(piece):
    return [piece] + [swap_z(piece, k) for k in range(1, lax.axis_size("seq") // 2)]


def gather_bit(value, bit, axis, absolute=False):
    got = swap(value, bit)
    if absolute:
        upper = mine(bit) == 1
        return jnp.stack([jnp.where(upper, got, value), jnp.where(upper, value, got)], axis=axis)
    return jnp.stack([value, got], axis=axis)


def split_bit(value, bit, axis):
    return lax.index_in_dim(value, 0, axis, keepdims=False), lax.index_in_dim(value, 1, axis, keepdims=False).astype(low)


def bit_names(axis, size):
    return [(axis, 1 << k) for k in range(size.bit_length() - 1)]


def moments(rotated, first, second):
    new_first = beta_first * first + (1.0 - beta_first) * rotated
    new_second = beta_second * second + (1.0 - beta_second) * rotated * rotated
    first_scale, second_scale = 1.0 / (1.0 - beta_first**STEP), 1.0 / (1.0 - beta_second**STEP)
    ratio = new_first * first_scale / (jnp.sqrt(new_second * second_scale) + adam_eps)
    return ratio, new_first, new_second


def adam_step(weight, grad, first, second):
    ratio, new_first, new_second = moments(grad, first, second)
    return (weight - vector_rate * ratio, new_first, new_second)


def sent_place(sent_refs, k):
    rest, pair, far = sent_refs
    if k <= rest.shape[0]:
        return rest.at[k - 1]
    return pair.at[k - 1 - rest.shape[0]] if k <= rest.shape[0] + pair.shape[0] else far


def attend(blocks, width, q_ref, do_ref, start_ref, cos_ref, sin_ref, kv_ref, context_ref, dq_ref, dkv_own_ref, *sent_refs):
    length = q_ref.shape[1]
    keys = blocks * length
    key_t = jnp.concatenate([kv_ref[k, :HEAD, :] for k in reversed(range(blocks))], axis=1)
    value_t = jnp.concatenate([kv_ref[k, HEAD:, :] for k in reversed(range(blocks))], axis=1)
    key = key_t.astype(f32).T.astype(low)
    value = value_t.astype(f32).T.astype(low)
    key_pos = lax.broadcasted_iota(jnp.int32, (keys, length), 0) - (blocks - 1) * length
    query_pos = lax.broadcasted_iota(jnp.int32, (keys, length), 1)
    allowed = (key_pos >= start_ref[0]) & (key_pos <= query_pos)
    bias = jnp.where(allowed, 0.0, masked_score)
    cosine, sine = cos_ref[...], sin_ref[...]
    d_key = jnp.zeros((keys, HEAD), f32)
    d_value = jnp.zeros((keys, HEAD), f32)
    last = (((1,), (1,)), ((), ()))
    for first in range(0, HEADS, width):
        heads = range(first, first + width)
        query = jnp.concatenate([q_ref[h * HEAD : (h + 1) * HEAD, :] for h in heads], axis=1)
        d_out = jnp.concatenate([do_ref[h * HEAD : (h + 1) * HEAD, :] for h in heads], axis=1)
        scores = jnp.dot(key, query, preferred_element_type=f32)
        scores = scores + jnp.concatenate([bias] * width, axis=1)
        weights = jnp.exp(scores - jnp.max(scores, axis=0, keepdims=True))
        probs = weights * (1.0 / jnp.sum(weights, axis=0, keepdims=True))
        probs_low = probs.astype(low)
        context_t = jnp.dot(value_t, probs_low, preferred_element_type=f32)
        d_probs = jnp.dot(value, d_out, preferred_element_type=f32)
        inner = jnp.sum(probs * d_probs, axis=0, keepdims=True)
        d_scores = (probs * (d_probs - inner)).astype(low)
        d_query = jnp.dot(key_t, d_scores, preferred_element_type=f32) * HEAD ** (-0.5)
        d_value = d_value + lax.dot_general(probs_low, d_out, last, preferred_element_type=f32)
        d_key = d_key + lax.dot_general(d_scores, query, last, preferred_element_type=f32)
        for k, h in enumerate(heads):
            lanes = slice(k * length, (k + 1) * length)
            part = d_query[:, lanes]
            a, b = part[: ROT // 2], part[ROT // 2 : ROT]
            turned = jnp.concatenate([a * cosine + b * sine, b * cosine - a * sine, part[ROT:]], axis=0)
            dq_ref[h * HEAD : (h + 1) * HEAD, :] = turned.astype(low)
        for k in range(0, width, 2):
            h = first + k
            two = jnp.concatenate(
                [context_t[:, k * length : (k + 1) * length], context_t[:, (k + 1) * length : (k + 2) * length]], axis=0
            )
            context_ref[:, h * HEAD : (h + 2) * HEAD] = two.T.astype(low)
    d_kv = jnp.concatenate([d_key, d_value], axis=1).T
    for k in range(blocks):
        part = d_kv[:, (blocks - 1 - k) * length : (blocks - k) * length]
        if k == 0:
            dkv_own_ref[...] = part
        else:
            sent_place(sent_refs, k)[...] = part.astype(low)
    for k in range(blocks, kv_ref.shape[0]):
        sent_place(sent_refs, k)[...] = jnp.zeros((2 * HEAD, length), low)


def attention_kernel(counts, needed_ref, *refs):
    needed = needed_ref[pl.program_id(0)]
    for least, count in zip([0] + counts, counts):

        @pl.when((needed > least) & (needed <= count))
        def _():
            attend(count, HEADS, *refs)


def attention(q_t, do_t, start, cosine, sine, kv):
    rows, _, length = start.shape
    blocks = kv.shape[0]
    tokens = q_t.shape[1]
    middle = (blocks - 1) // 2
    by_row = lambda height: pl.BlockSpec((height, length), lambda r: (0, r))
    needed = 1 + jnp.clip((length - 1 - start[:, 0, 0]) // length, 0, blocks - 1).astype(jnp.int32)
    counts = list(range(1, blocks + 1)) if blocks <= 5 else [1, (blocks + 1) // 2, blocks]
    return pl.pallas_call(
        functools.partial(attention_kernel, counts),
        grid=(rows,),
        in_specs=[pl.BlockSpec(memory_space=pltpu.SMEM), by_row(D), by_row(D), pl.BlockSpec((1, 1, length), lambda r: (r, 0, 0)), by_row(ROT // 2), by_row(ROT // 2)]
        + [pl.BlockSpec((blocks, 2 * HEAD, length), lambda r: (0, 0, r))],
        out_specs=[
            pl.BlockSpec((length, D), lambda r: (r, 0)),
            by_row(D),
            by_row(2 * HEAD),
            pl.BlockSpec((middle - 1, 2 * HEAD, length), lambda r: (0, 0, r)),
            pl.BlockSpec((blocks - 1 - middle, 2 * HEAD, length), lambda r: (0, 0, r)),
            by_row(2 * HEAD),
        ],
        out_shape=[
            jax.ShapeDtypeStruct((tokens, D), low),
            jax.ShapeDtypeStruct((D, tokens), low),
            jax.ShapeDtypeStruct((2 * HEAD, tokens), f32),
            jax.ShapeDtypeStruct((middle - 1, 2 * HEAD, tokens), low),
            jax.ShapeDtypeStruct((blocks - 1 - middle, 2 * HEAD, tokens), low),
            jax.ShapeDtypeStruct((2 * HEAD, tokens), low),
        ],
        compiler_params=pltpu.CompilerParams(vmem_limit_bytes=VMEM_LIMIT),
        cost_estimate=pl.CostEstimate(
            flops=4 * 7 * tokens * HEADS * blocks * length * HEAD * 2, bytes_accessed=8 << 20, transcendentals=0
        ),
        name="attention",
    )(needed, q_t, do_t, start, cosine, sine, kv)


def gathered_parts(plane, refs, offset, rows):
    half = plane // 2
    out = []
    for end, ref in enumerate(refs):
        for j in range(half):
            out.append((0, end * half + j, ref.at[0, j, :, pl.ds(offset, rows)]))
            out.append((1, 2 * j + end, ref.at[1, j, :, pl.ds(offset, rows)]))
    return out


def feed_kernel(n_ref, dy_ref, first_far, last_far, first_near, last_near, bias_far_ref, bias_near_ref, *refs):
    far_refs, near_refs = (first_far, last_far), (first_near, last_near)
    before = refs[: len(refs) - 11]
    out_ref, dn_ref, far_grad_ref, near_grad_ref, bias_far_grad_ref, bias_near_grad_ref = refs[-11:-5]
    weights, far_sum, near_sum, held, sems = refs[-5:]
    plane = weights.shape[2]
    last = (((1,), (1,)), ((), ()))
    first = (((0,), (0,)), ((), ()))
    loads = [
        [
            pltpu.make_async_copy(source, weights.at[side, kind, k], sems.at[side, 2 * k + kind])
            for kind, k, source in gathered_parts(plane, refs_of, 0, weights.shape[4])
        ]
        for side, refs_of in enumerate((far_refs, near_refs))
    ]
    fetches = [pltpu.make_async_copy(ref, held.at[k], sems.at[2, k]) for k, ref in enumerate(before)]
    for copy in loads[0] + loads[1] + fetches:
        copy.start()
    normed, d_out = n_ref[...], dy_ref[...]
    units = far_sum.shape[1]
    out, d_normed = 0.0, 0.0
    stores = []
    for side, (bias_ref, bias_grad_ref, buffer, grad_ref) in enumerate(
        (
            (bias_far_ref, bias_far_grad_ref, far_sum, far_grad_ref),
            (bias_near_ref, bias_near_grad_ref, near_sum, near_grad_ref),
        )
    ):
        for copy in loads[side]:
            copy.wait()
        up, down = weights[side, 0].reshape(units, D), weights[side, 1].reshape(units, D)
        hidden = lax.dot_general(normed, up, last, preferred_element_type=f32) + bias_ref[...]
        share = 0.5 * (1.0 + lax.erf(hidden * (0.5**0.5)))
        slope = share + hidden * (jnp.exp(-0.5 * hidden * hidden) * (0.5 / 3.141592653589793) ** 0.5)
        active = (hidden * share).astype(low)
        d_active = lax.dot_general(d_out, down, last, preferred_element_type=f32)
        d_hidden = (d_active * slope).astype(low)
        for k, part in enumerate(
            (
                lax.dot_general(d_hidden, normed, first, preferred_element_type=f32),
                lax.dot_general(active, d_out, first, preferred_element_type=f32),
            )
        ):
            buffer[k] = part.astype(buffer.dtype)
            copy = pltpu.make_async_copy(buffer.at[k], grad_ref.at[k], sems.at[3, 2 * side + k])
            copy.start()
            stores.append(copy)
        bias_grad_ref[...] = jnp.sum(d_hidden.astype(f32), axis=0, keepdims=True)
        out = out + jnp.dot(active, down, preferred_element_type=f32)
        d_normed = d_normed + jnp.dot(d_hidden, up, preferred_element_type=f32)
    for copy in fetches:
        copy.wait()
    out_ref[...] = held[0] + out if before else out
    dn_ref[...] = held[1] + d_normed if before else d_normed
    for copy in stores:
        copy.wait()


def feed(normed, d_out, far, near, bias_far, bias_near, rows, before):
    tokens = normed.shape[0]
    plane, depth = 2 * far[0].shape[1], far[0].shape[2]
    units = plane * depth * rows
    before = before or []
    vmem, hbm = pl.BlockSpec(memory_space=pltpu.VMEM), pl.BlockSpec(memory_space=pl.ANY)
    return pl.pallas_call(
        feed_kernel,
        in_specs=[vmem, vmem, hbm, hbm, hbm, hbm, vmem, vmem] + [hbm] * len(before),
        out_specs=[vmem, vmem, hbm, hbm, vmem, vmem],
        out_shape=[
            jax.ShapeDtypeStruct((tokens, D), f32),
            jax.ShapeDtypeStruct((tokens, D), f32),
            jax.ShapeDtypeStruct((2, units, D), low),
            jax.ShapeDtypeStruct((2, units, D), f32),
            jax.ShapeDtypeStruct((1, units), f32),
            jax.ShapeDtypeStruct((1, units), f32),
        ],
        scratch_shapes=[
            pltpu.VMEM((2, 2, plane, depth, rows, D), low),
            pltpu.VMEM((2, units, D), low),
            pltpu.VMEM((2, units, D), f32),
            pltpu.VMEM((2, tokens, D), f32),
            pltpu.SemaphoreType.DMA((4, 2 * plane)),
        ],
        compiler_params=pltpu.CompilerParams(vmem_limit_bytes=FEED_VMEM),
        cost_estimate=pl.CostEstimate(flops=4 * 24 * tokens * units * D, bytes_accessed=8 << 20, transcendentals=0),
        name="feed",
    )(normed, d_out, *far, *near, bias_far, bias_near, *before)


def head_kernel(
    vec_len, offset, out_rows, device_ref, x_ref, first_near, last_near, first_far, last_far, cos_ref, sin_ref, n_one_ref,
    n_two_ref, q_ref, kv_ref, w_ref, gain_ref, bias_ref, *refs
):
    *bias_refs, out_ref, flat, units, held, pieces_of, outs_of, sems = refs if out_rows else (*refs[:-6], None, *refs[-6:])
    _, _, plane, depth, size, _ = held.shape
    copies = [
        pltpu.make_async_copy(source, held.at[side, kind, k], sems.at[side, 2 * k + kind])
        for side, refs_of in enumerate(((first_near, last_near), (first_far, last_far)))
        for kind, k, source in gathered_parts(plane, refs_of, offset, size)
    ]
    for copy in copies:
        copy.start()
    x = x_ref[...].astype(f32)
    center = x - jnp.mean(x, axis=-1, keepdims=True)
    xhat = center * lax.rsqrt(jnp.mean(center * center, axis=-1, keepdims=True) + layer_eps)
    for copy in copies:
        copy.wait()
    for side in range(2):
        for k in range(plane):
            for z in range(depth):
                number = device_ref[(side * plane + k) * depth + z]
                pieces_of[number] = held[side, 0, k, z].astype(f32)
                if out_rows:
                    outs_of[number] = held[side, 1, k, z][:out_rows].astype(f32)
    if out_rows:
        out_ref[...] = outs_of[...].reshape(out_ref.shape).astype(low)
    shards_of = (flat.shape[1]) // vec_len
    rows = (D + 2 * HEAD) // shards_of
    whole = pieces_of[...].reshape(shards_of, -1, D)
    for s in range(shards_of):
        left, row = vec_len, rows
        while left > 0:
            size = min(left, D)
            begin = s * vec_len + (row - rows) * D
            flat[:, begin : begin + size] = whole[s, row : row + 1, :size]
            left -= size
            row += 1
    vector = lambda begin, size: flat[:, begin : begin + size]
    gain_one, shift_one, gain_two, shift_two = [vector(k * D, D) for k in range(4)]
    gain_ref[0:1] = gain_one
    gain_ref[1:2] = gain_two
    qkv_bias = vector(4 * D, D + 2 * HEAD)
    start = 4 * D + D + 2 * HEAD
    bias_ref[...] = vector(start, D) + vector(start + D + FF, D)
    count, size_of = units.shape
    for k in range(count):
        units[k : k + 1, :] = vector(start + D + k * size_of, size_of)
    groups = len(bias_refs) // 2
    for k, ref in enumerate(bias_refs):
        side, g = k // groups, k % groups
        width = size_of // groups
        for i in range(count // 2):
            row = units[pl.ds(device_ref[side * (count // 2) + i], 1), :]
            ref[:, i * width : (i + 1) * width] = row[:, g * width : (g + 1) * width]
    n_one = (xhat * gain_one + shift_one).astype(low)
    n_one_ref[...] = n_one
    n_two_ref[...] = (xhat * gain_two + shift_two).astype(low)
    weight = whole[:, :rows].reshape(shards_of * rows, D).astype(low)
    w_ref[...] = weight
    column = jnp.broadcast_to(qkv_bias, (8, qkv_bias.shape[1])).T[:, 0:1]
    projected = lax.dot_general(weight, n_one, (((1,), (1,)), ((), ())), preferred_element_type=f32) + column
    cosine, sine = cos_ref[...], sin_ref[...]
    half = ROT // 2

    def turned(first):
        a, b = projected[first : first + half], projected[first + half : first + ROT]
        rest = projected[first + ROT : first + HEAD]
        return jnp.concatenate([a * cosine - b * sine, b * cosine + a * sine, rest], axis=0).astype(low)

    for h in range(HEADS):
        q_ref[h * HEAD : (h + 1) * HEAD, :] = turned(h * HEAD) * jnp.asarray(HEAD ** (-0.5), low)
    kv_ref[:HEAD, :] = turned(D)
    kv_ref[HEAD:, :] = projected[D + HEAD :].astype(low)


def head(device, x, near, far, offset, size, out_rows, cosine, sine, groups, vec_len, shards_of):
    tokens = x.shape[0]
    count = device.shape[0]
    plane, depth = 2 * near[0].shape[1], near[0].shape[2]
    vmem, hbm = pl.BlockSpec(memory_space=pltpu.VMEM), pl.BlockSpec(memory_space=pl.ANY)
    return pl.pallas_call(
        functools.partial(head_kernel, vec_len, offset, out_rows),
        in_specs=[pl.BlockSpec(memory_space=pltpu.SMEM), vmem, hbm, hbm, hbm, hbm, vmem, vmem],
        out_shape=[
            jax.ShapeDtypeStruct((tokens, D), low),
            jax.ShapeDtypeStruct((tokens, D), low),
            jax.ShapeDtypeStruct((D, tokens), low),
            jax.ShapeDtypeStruct((2 * HEAD, tokens), low),
            jax.ShapeDtypeStruct((D + 2 * HEAD, D), low),
            jax.ShapeDtypeStruct((2, D), f32),
            jax.ShapeDtypeStruct((1, D), f32),
        ]
        + [jax.ShapeDtypeStruct((1, FF // 2 // groups), f32)] * (2 * groups)
        + [jax.ShapeDtypeStruct((D, D), low)] * (out_rows > 0),
        scratch_shapes=[
            pltpu.VMEM((1, shards_of * vec_len), f32),
            pltpu.VMEM((count, FF // count), f32),
            pltpu.VMEM((2, 2, plane, depth, size, D), low),
            pltpu.VMEM((count, size, D), f32),
            pltpu.VMEM((count, max(out_rows, 8), D), f32),
            pltpu.SemaphoreType.DMA((2, 2 * plane)),
        ],
        compiler_params=pltpu.CompilerParams(vmem_limit_bytes=FEED_VMEM),
        cost_estimate=pl.CostEstimate(flops=4 * 2 * tokens * 896 * D, bytes_accessed=8 << 20, transcendentals=0),
        name="head",
    )(device, x, *near, *far, cosine, sine)


def tail_kernel(
    shards_of, entry_ref, x_ref, dy_ref, dq_ref, dkv_ref, cos_ref, sin_ref, w_ref, n_ref, context_ref, d_two_ref, gain_ref, *refs
):
    bias_refs, (in_grad_ref, kept_ref, sent_ref, flat, units, tile) = refs[:-6], refs[-6:]
    d_kv = dkv_ref[...]
    a, b = d_kv[: ROT // 2], d_kv[ROT // 2 : ROT]
    cosine, sine = cos_ref[...], sin_ref[...]
    d_kv = jnp.concatenate([a * cosine + b * sine, b * cosine - a * sine, d_kv[ROT:]], axis=0).astype(low)
    d_proj = jnp.concatenate([dq_ref[...], d_kv], axis=0)
    first = (((0,), (0,)), ((), ()))
    qkv_grad = jnp.dot(d_proj, n_ref[...], preferred_element_type=f32)
    out_grad = lax.dot_general(dy_ref[...], context_ref[...], first, preferred_element_type=f32)
    d_one = lax.dot_general(d_proj, w_ref[...], first, preferred_element_type=f32)
    d_two = d_two_ref[...]
    x = x_ref[...].astype(f32)
    dy = dy_ref[...].astype(f32)
    center = x - jnp.mean(x, axis=-1, keepdims=True)
    inv_sigma = lax.rsqrt(jnp.mean(center * center, axis=-1, keepdims=True) + layer_eps)
    xhat = center * inv_sigma
    d_hat = d_one * gain_ref[0:1] + d_two * gain_ref[1:2]
    d_in = (
        d_hat - jnp.mean(d_hat, axis=-1, keepdims=True) - xhat * jnp.mean(d_hat * xhat, axis=-1, keepdims=True)
    ) * inv_sigma
    in_grad_ref[...] = (dy + d_in).astype(low)
    columns = lambda v: jnp.sum(v, axis=0, keepdims=True)
    dy_column = columns(dy)
    ones = jnp.ones((8, d_proj.shape[1]), low)
    proj_sum = lax.dot_general(ones, d_proj, (((1,), (1,)), ((), ())), preferred_element_type=f32)[0:1]
    pieces = [columns(d_one * xhat), columns(d_one), columns(d_two * xhat), columns(d_two)]
    pieces += [proj_sum, dy_column, None, dy_column]
    count, size = units.shape
    groups = len(bias_refs) // 2
    width = size // groups
    for k, ref in enumerate(bias_refs):
        side, g = k // groups, k % groups
        for i in range(count // 2):
            place = side * (count // 2) + i
            units[place : place + 1, g * width : (g + 1) * width] = ref[:, i * width : (i + 1) * width]
    offset = 0
    for piece in pieces:
        if piece is None:
            for k in range(count):
                flat[:, offset : offset + size] = units[pl.ds(entry_ref[k], 1), :]
                offset += size
        else:
            flat[:, offset : offset + piece.shape[1]] = piece
            offset += piece.shape[1]
    qkv_rows, vec_len = qkv_grad.shape[0] // shards_of, flat.shape[1] // shards_of
    to_shard = count // shards_of
    share = lambda k, total: [k // to_shard * total + min(-(-total // to_shard) * j, total) for j in (k % to_shard, k % to_shard + 1)]
    out_own = D // count
    half, rows = kept_ref.shape[1:3]
    vec_row = rows - 4

    def put(kind, to):
        @pl.when(to < half)
        def _():
            kept_ref[kind, to] = tile[...]

        @pl.when(to >= half)
        def _():
            sent_ref[kind, to - half] = tile[...].astype(low)

    tile[...] = jnp.zeros_like(tile)
    for k in range(count):
        begin, end = share(k, qkv_rows)
        first_end = end - begin
        if first_end < vec_row:
            tile[first_end:vec_row, :] = jnp.zeros((vec_row - first_end, D), f32)
        if end > begin:
            tile[:first_end, :] = qkv_grad[begin:end]
        begin, end = share(k, vec_len)
        tile[vec_row : vec_row + 1, :] = jnp.zeros((1, D), f32)
        if end > begin:
            tile[vec_row : vec_row + 1, : end - begin] = flat[:, begin:end]
        put(0, entry_ref[k])
    tile[...] = jnp.zeros_like(tile)
    for k in range(count):
        tile[:out_own, :] = out_grad[k * out_own : (k + 1) * out_own]
        put(1, entry_ref[k])


def tail(entry, x, dy, dq_t, dkv, cosine, sine, weight, normed, context, d_two, gains, bias_grads, rows, shards_of, vec_len):
    tokens = x.shape[0]
    count = entry.shape[0]
    operands = (entry, x, dy, dq_t, dkv, cosine, sine, weight, normed, context, d_two, gains, *sum(bias_grads, []))
    return pl.pallas_call(
        functools.partial(tail_kernel, shards_of),
        in_specs=[pl.BlockSpec(memory_space=pltpu.SMEM)] + [pl.BlockSpec(memory_space=pltpu.VMEM)] * (len(operands) - 1),
        out_shape=[
            jax.ShapeDtypeStruct((tokens, D), low),
            jax.ShapeDtypeStruct((2, count // 2, rows, D), f32),
            jax.ShapeDtypeStruct((2, count // 2, rows, D), low),
        ],
        scratch_shapes=[
            pltpu.VMEM((1, shards_of * vec_len), f32), pltpu.VMEM((count, FF // count), f32), pltpu.VMEM((rows, D), f32)
        ],
        compiler_params=pltpu.CompilerParams(vmem_limit_bytes=VMEM_LIMIT),
        cost_estimate=pl.CostEstimate(flops=4 * 6 * tokens * 896 * D, bytes_accessed=8 << 20, transcendentals=0),
        name="tail",
    )(*operands)


def split_low(value):
    high = value.astype(low)
    return high, (value - high.astype(f32)).astype(low)


def update_step(across, grad, high, rest, w_ref, first_ref, second_ref, grad_ref, first_new_ref, second_new_ref, w_new_ref):
    rotated = jnp.dot(grad, high, preferred_element_type=f32) + jnp.dot(grad, rest, preferred_element_type=f32)
    grad = grad.astype(f32)
    if across:
        rotated, grad = rotated.T, grad.T
    grad_ref[...] = grad
    ratio, first_new, second_new = moments(rotated, first_ref[...], second_ref[...])
    first_new_ref[...] = first_new
    second_new_ref[...] = second_new
    r_high, r_rest = split_low(ratio)
    if across:
        product = lambda r, b: jnp.dot(b, r, preferred_element_type=f32)
    else:
        product = lambda r, b: lax.dot_general(r, b, (((1,), (1,)), ((), ())), preferred_element_type=f32)
    unrotated = product(r_high, high) + (product(r_high, rest) + product(r_rest, high))
    w_new_ref[...] = w_ref[...] - matrix_rate * unrotated


def update_kernel(across, grad_ref, high_ref, rest_ref, *refs):
    update_step(across, grad_ref[...], high_ref[...], rest_ref[...], *refs)


def update(grad, basis, weight, first, second, across=False):
    return pl.pallas_call(
        functools.partial(update_kernel, across),
        out_shape=[jax.ShapeDtypeStruct(weight.shape, f32)] * 4,
        compiler_params=pltpu.CompilerParams(vmem_limit_bytes=UPDATE_VMEM),
        cost_estimate=pl.CostEstimate(flops=10 * grad.shape[0] * D * D, bytes_accessed=8 << 20, transcendentals=0),
        name="update",
    )(grad, *basis, weight, first, second)


def outer_update_kernel(share, own, offset, g_ref, *refs):
    qkv_in, out_in, qkv_out, out_out, (qkv_rows, out_rows) = refs[:5], refs[5:10], refs[10:14], refs[14:18], refs[18:]
    for q in range(g_ref.shape[0]):
        part = g_ref[q].astype(f32)
        count = min(share, qkv_rows.shape[0] - q * share)
        if count > 0:
            qkv_rows[q * share : q * share + count, :] = part[:count]
        out_rows[q * own : (q + 1) * own, :] = part[offset : offset + own]
    for rows, (high_ref, rest_ref, *state), outs in ((qkv_rows, qkv_in, qkv_out), (out_rows, out_in, out_out)):
        update_step(False, rows[...].astype(low), high_ref[...], rest_ref[...], *state, *outs)


def outer_update(grads, share, own, offset, qkv, out):
    operands = [value for basis, *state in (qkv, out) for value in (*basis, *state)]
    shapes = [qkv[1].shape] * 4 + [out[1].shape] * 4
    new = pl.pallas_call(
        functools.partial(outer_update_kernel, share, own, offset),
        out_shape=[jax.ShapeDtypeStruct(shape, f32) for shape in shapes],
        scratch_shapes=[pltpu.VMEM(qkv[1].shape, f32), pltpu.VMEM(out[1].shape, f32)],
        compiler_params=pltpu.CompilerParams(vmem_limit_bytes=VMEM_LIMIT),
        cost_estimate=pl.CostEstimate(flops=10 * 208 * D * D, bytes_accessed=8 << 20, transcendentals=0),
        name="outer_update",
    )(grads, *operands)
    return new[:4], new[4:]


def shards(
    inputs,
    cotangent,
    doc_lengths,
    qkv_weight,
    out_weight,
    up_weight,
    down_weight,
    vectors,
    bases,
    qkv_first,
    out_first,
    up_first,
    down_first,
    vector_first,
    qkv_second,
    out_second,
    up_second,
    down_second,
    vector_second,
):
    seq_count, batch_count = lax.axis_size("seq"), lax.axis_size("batch")
    seq_index, batch_index = lax.axis_index("seq"), lax.axis_index("batch")
    row_count, shard_len = inputs.shape[:2]
    tokens = row_count * shard_len
    y_bit, *z_bits = bit_names("seq", seq_count)
    core_bit, *x_bits = bit_names("batch", batch_count)
    near = [core_bit] + x_bits[::-1] + [y_bit] + z_bits[::-1]
    depth = seq_count // 2
    plane = 2 ** (len(x_bits) + 1)
    x_low = inputs.reshape(tokens, D)
    dy = cotangent.reshape(tokens, D)

    first_pos = seq_index * shard_len
    query_pos = first_pos + jnp.arange(shard_len, dtype=jnp.int32)
    docs = doc_lengths.shape[1]
    earlier = jnp.arange(docs)[:, None] < jnp.arange(docs)[None, :]
    doc_starts = jnp.sum(jnp.where(earlier[None], doc_lengths[:, :, None], 0), axis=1)
    start = jnp.max(
        jnp.where(doc_starts[:, None, :] <= query_pos[None, :, None], doc_starts[:, None, :], 0), axis=-1
    )
    offsets = (query_pos[None, :] - start).reshape(tokens)
    inverse = 1.0 / rope_base ** (jnp.arange(0, ROT, 2).astype(f32) / ROT)
    angles = offsets.astype(f32)[None, :] * inverse[:, None]
    cosine, sine = jnp.cos(angles), jnp.sin(angles)
    start_here = (start - first_pos).astype(jnp.int32)[:, None, :]
    number = jnp.arange(seq_count * batch_count, dtype=jnp.int32)

    def bits_of(value, place_of):
        total = 0
        for k, (axis_name, step) in enumerate(near[::-1]):
            total = total + place_of(value, k, axis_name, step)
        return total

    differs = {"seq": (number // batch_count) ^ seq_index, "batch": (number % batch_count) ^ batch_index}
    entry = bits_of(number, lambda v, k, name, step: (differs[name] // step) % 2 << k).astype(jnp.int32)
    xor_of = lambda name: sum((number >> k) % 2 * step for k, (axis_name, step) in enumerate(near[::-1]) if axis_name == name)
    device = ((xor_of("seq") ^ seq_index) * batch_count + (xor_of("batch") ^ batch_index)).astype(jnp.int32)

    qkv_rows, out_rows, up_rows, vec_len = qkv_weight.shape[0], out_weight.shape[0], up_weight.shape[0], vectors.shape[0]
    vec_rows = -(-vec_len // D)
    used = qkv_rows + vec_rows
    head_rows = -(-used // (8 * batch_count)) * 8 * batch_count
    vec_pad = vec_rows * D - vec_len

    def own_part(rows):
        size = rows.shape[0] // batch_count
        return lax.dynamic_slice_in_dim(rows, batch_index * size, size, axis=0)

    head_shard = jnp.concatenate(
        [qkv_weight, jnp.pad(vectors, (0, vec_pad)).reshape(vec_rows, D), jnp.zeros((head_rows - used, D), f32)], axis=0
    ).astype(low)
    head_part_rows = head_rows // batch_count
    unit_rows = up_rows // batch_count // GROUPS
    out_own = out_rows // batch_count
    up_low, down_low = own_part(up_weight.astype(low)), own_part(down_weight.T.astype(low))
    outer = [
        own_part(head_shard),
        jnp.concatenate([own_part(out_weight.astype(low)), jnp.zeros((head_part_rows - out_own, D), low)], axis=0),
    ]
    parts_of = []
    for g in range(GROUPS):
        rows = slice(g * unit_rows, (g + 1) * unit_rows)
        pieces = [up_low[rows], outer[0], down_low[rows], outer[1]] if g == 0 else [up_low[rows], down_low[rows]]
        parts_of.append(jnp.concatenate(pieces, axis=0))

    def gather_first(parts):
        half = parts.shape[1] // 2
        up, down = parts[:, :half], parts[:, half:]
        for bit in x_bits[:-1]:
            down = gather_bit(down, bit, 0)
        return up, down, swap(up, y_bit), swap(down, x_bits[-1])

    def gather_second(up, down, up_got, down_got):
        up, down = jnp.stack([up, up_got]), jnp.stack([down, down_got])
        for bit in x_bits[:-1]:
            up = gather_bit(up, bit, 0)
        shape = (1, plane // 2, depth) + up.shape[-2:]
        return up, down, jnp.concatenate([up.reshape(shape), down.reshape(shape)], axis=0)

    def gather_last(up, down):
        return swap(up, x_bits[-1]), swap(down, y_bit)

    def joined(up, down):
        shape = (1, plane // 2, depth) + up.shape[-2:]
        return jnp.concatenate([up.reshape(shape), down.reshape(shape)], axis=0)

    z_zero = gather_z(parts_of[0])
    *z_zero, cosine, sine, start_here, entry, device, part_one = hold(
        *z_zero, cosine, sine, start_here, entry, device, parts_of[1]
    )
    up, down, up_got, down_got = gather_first(jnp.stack(z_zero))
    z_one = gather_z(part_one)
    up_got, down_got, z_one[1] = hold(up_got, down_got, z_one[1])
    up, down, first_zero = gather_second(up, down, up_got, down_got)
    up_got, down_got = gather_last(up, down)
    first_far_zero = swap(first_zero, core_bit)
    late_bases, up, down = hold(bases, up, down)
    split_bases = [part for k in range(4) for part in split_low(late_bases[k])]
    up_got, down_got, first_far_zero, *rest = hold(up_got, down_got, first_far_zero, *z_one[2:], *split_bases)
    z_one[2:], split_bases = rest[: len(z_one) - 2], rest[len(z_one) - 2 :]
    split_bases = [split_bases[2 * k : 2 * k + 2] for k in range(4)]
    last_zero = joined(up_got, down_got)
    last_far_zero = swap(last_zero, core_bit)

    aligned = unit_rows % 16 == 0 and head_part_rows % 16 == 0
    trim = lambda values, begin, end: values if aligned else tuple(v[..., begin:end, :] for v in values)
    near_zero, far_zero = (first_zero, last_zero), (first_far_zero, last_far_zero)
    end = unit_rows + head_part_rows

    inside = out_own % 8 == 0
    normed_one, normed_two, q_t, kv_own, qkv_full, gains, out_bias, *bias_rows = head(
        device, x_low, trim(near_zero, unit_rows, end), trim(far_zero, unit_rows, end), unit_rows if aligned else 0,
        head_part_rows, out_own if inside else 0, cosine, sine, GROUPS, vec_len, seq_count,
    )
    if inside:
        out_full = bias_rows.pop()
    else:
        chosen = (entry[:, None] == number[None, :]).astype(low)
        sides = []
        for pair in (near_zero, far_zero):
            along = [v[1, :, :, unit_rows : unit_rows + out_own] for v in pair]
            sides.append(jnp.stack(along, axis=1).reshape(-1, out_own * D))
        out_full = jnp.dot(chosen, jnp.concatenate(sides, axis=0), preferred_element_type=f32).astype(low).reshape(D, D)
    bias_rows = [bias_rows[:GROUPS], bias_rows[GROUPS:]]
    reach = seq_count // 2

    def shifted(value, step, back=False):
        pairs = [(j, j + step) for j in range(seq_count - step)]
        return lax.ppermute(value, "seq", [(b, a) for a, b in pairs] if back else pairs)

    farthest, pair = shifted(kv_own, reach), shifted(kv_own[None], 1)
    up, down, up_got, down_got = gather_first(jnp.stack(z_one))
    up_got, down_got, normed_two = hold(up_got, down_got, normed_two)
    up, down, first_one = gather_second(up, down, up_got, down_got)
    up_got, down_got = gather_last(up, down)
    first_far_one = swap(first_one, core_bit)

    last = (((1,), (1,)), ((), ()))
    bias_grads = [[], []]

    def feed_group(g, sums, normed, near, far, *beside):
        *sums, far_grad, near_grad, bias_far, bias_here = feed(
            normed, dy, trim(far, 0, unit_rows), trim(near, 0, unit_rows), bias_rows[1][g], bias_rows[0][g], unit_rows, sums
        )
        bias_grads[0].append(bias_here)
        bias_grads[1].append(bias_far)
        far_grad, *beside = hold(far_grad, *beside)
        shape = (2,) + (2,) * len(x_bits) + (2, depth, unit_rows, D)
        grad_sum = (near_grad + swap(far_grad, core_bit).astype(f32)).reshape(shape)
        return sums, grad_sum[0], grad_sum[1], *beside

    def sum_first(up, down):
        (up_kept, up_sent), (down_kept, down_sent) = split_bit(up, x_bits[-1], 0), split_bit(down, y_bit, len(x_bits))
        return up_kept, up_sent, down_kept, down_sent

    def send_first(sums):
        return swap(sums[1], x_bits[-1]), swap(sums[3], y_bit)

    def sum_second(sums, up_got, down_got):
        up = sums[0] + up_got.astype(f32)
        for bit in x_bits[-2::-1]:
            kept, sent = split_bit(up, bit, 0)
            up = kept + swap(sent, bit).astype(f32)
        down = sums[2] + down_got.astype(f32)
        (up_kept, up_sent), (down_kept, down_sent) = split_bit(up, y_bit, 0), split_bit(down, x_bits[-1], 0)
        return up_kept, up_sent, down_kept, down_sent

    def send_second(sums):
        return swap(sums[1], y_bit), swap(sums[3], x_bits[-1])

    def sum_third(up_kept, up_got, down_kept, down_got):
        up = up_kept + up_got.astype(f32)
        down = down_kept + down_got.astype(f32)
        for bit in x_bits[-2::-1]:
            kept, sent = split_bit(down, bit, 0)
            down = kept + swap(sent, bit).astype(f32)
        return jnp.concatenate([up, down], axis=1)

    def send_z(value):
        return [swap_z(value[k].astype(low), k) for k in range(1, depth)]

    def sum_z(value, got):
        return value[0] + sum(part.astype(f32) for part in got)

    def spread(part):
        value = part.astype(low)
        for bit in x_bits:
            value = gather_bit(value, bit, 0, True)
        return gather_bit(value, core_bit, len(x_bits), True).reshape(batch_count, -1, D)

    sums, up_sum, down_sum, up_got, down_got, farthest, pair = feed_group(
        0, None, normed_two, near_zero, far_zero, up_got, down_got, farthest, pair
    )
    kv = jnp.concatenate([kv_own[None], pair], axis=0)
    while kv.shape[0] < reach:
        kv = jnp.concatenate([kv, shifted(kv, kv.shape[0])], axis=0)
    kv = jnp.concatenate([kv, farthest[None]], axis=0)
    sum_zero = sum_first(up_sum, down_sum)
    *sum_zero, first_far_one, q_t = hold(*sum_zero, first_far_one, q_t)
    last_one = joined(up_got, down_got)
    last_far_one = swap(last_one, core_bit)

    do_t = lax.dot_general(out_full, dy, (((0,), (1,)), ((), ())), preferred_element_type=f32).astype(low)
    context, dq_t, dkv_own, dkv_rest, dkv_pair, dkv_end = attention(q_t, do_t, start_here, cosine, sine, kv)
    sum_zero = sum_second(sum_zero, *send_first(sum_zero))
    last_far_one, dq_t, normed_late, *sum_zero = hold(last_far_one, dq_t, normed_two, *sum_zero)
    dkv_far = shifted(dkv_end, reach, True)
    middle = reach // 2
    dkv = [dkv_own] + [dkv_rest[i] for i in range(middle - 1)]
    got = shifted(dkv_pair, middle, True)
    up_got, down_got = send_second(sum_zero)
    (mlp_out, d_normed_two), up_sum, down_sum, up_got, down_got, dkv_far, got = feed_group(
        1, sums, normed_late, (first_one, last_one), (first_far_one, last_far_one), up_got, down_got, dkv_far, got
    )
    sum_zero = sum_third(sum_zero[0], up_got, sum_zero[2], down_got)
    dkv = [dkv[i].astype(f32) + got[i].astype(f32) for i in range(middle)]
    while middle > 1:
        middle //= 2
        got = shifted(jnp.stack([part.astype(low) for part in dkv[middle : 2 * middle]]), middle, True)
        dkv = [dkv[i] + got[i].astype(f32) for i in range(middle)]
    dkv = dkv[0] + dkv_far.astype(f32)
    qkv_share, vec_share = -(-qkv_rows // batch_count), -(-vec_len // batch_count)
    sum_one = sum_first(up_sum, down_sum)
    dkv, *sum_one = hold(dkv, *sum_one)
    up_got, down_got = send_first(sum_one)
    z_got = send_z(sum_zero)
    input_grad, kept_part, sent_part = tail(
        entry, x_low, dy, dq_t, dkv, cosine, sine, qkv_full, normed_one, context, d_normed_two, gains, bias_grads,
        head_part_rows, seq_count, vec_len,
    )
    sent_part, up_got, down_got, *z_got = hold(sent_part, up_got, down_got, *z_got)
    sum_one = sum_second(sum_one, up_got, down_got)
    one_got = send_second(sum_one)
    got = swap(sent_part, core_bit)
    got, mlp_late, context_late, *one_got = hold(got, mlp_out, context, *one_got)
    outer = (kept_part + got.astype(f32)).reshape((2,) + (2,) * len(x_bits) + (2, depth, head_part_rows, D))
    sum_outer = sum_first(outer[0], outer[1])
    outer_got = send_first(sum_outer)
    sum_one = sum_third(sum_one[0], one_got[0], sum_one[2], one_got[1])
    one_got = send_z(sum_one)
    feed_zero = sum_z(sum_zero, z_got)
    attn_out = lax.dot_general(context_late, out_full, last, preferred_element_type=f32)
    outputs = (x_low.astype(f32) + attn_out + mlp_late + out_bias).astype(low)
    sum_outer = sum_second(sum_outer, *outer_got)
    outer_got = send_second(sum_outer)
    outer_got, one_got, (outputs,) = hold_lists(outer_got, one_got, [outputs])
    sum_outer = sum_third(sum_outer[0], outer_got[0], sum_outer[2], outer_got[1])
    outer_got = send_z(sum_outer)
    grads_feed = spread(jnp.concatenate([feed_zero, sum_z(sum_one, one_got)], axis=0))
    grads_feed = grads_feed.reshape(batch_count, GROUPS, 2, unit_rows, D).transpose(2, 0, 1, 3, 4).reshape(2, -1, D)
    (up_all, down_all), outer_got = hold_lists([grads_feed[0], grads_feed[1]], outer_got)
    up_out = update(up_all, split_bases[2], up_weight, up_first, up_second)
    grads_outer = spread(sum_z(sum_outer, outer_got))
    down_out = update(down_all, split_bases[3], down_weight, down_first, down_second, True)
    down_out, grads_outer = hold_lists(down_out, [grads_outer])
    grads_outer = grads_outer[0]
    (up_grad, *up_states), (down_grad, *down_states) = up_out, down_out
    (qkv_grad, *qkv_states), (out_grad, *out_states) = outer_update(
        grads_outer, qkv_share, out_own, head_part_rows,
        (split_bases[0], qkv_weight, qkv_first, qkv_second), (split_bases[1], out_weight, out_first, out_second),
    )
    vector_grad = grads_outer[:, head_part_rows - 4, :vec_share].astype(f32).reshape(-1)[:vec_len]
    vector_new, *vector_states = adam_step(vectors, vector_grad, vector_first, vector_second)
    states = (qkv_states, out_states, up_states, down_states, (*vector_states, vector_new))
    return (
        outputs.reshape(inputs.shape),
        input_grad.reshape(inputs.shape),
        qkv_grad,
        out_grad,
        up_grad,
        down_grad,
        vector_grad,
        *(state[0] for state in states),
        *(state[1] for state in states),
        *(state[2] for state in states),
    )


def solution(mesh):
    tokens = P("batch", "seq", None)
    rows, columns, flat = P("seq", None), P(None, "seq"), P("seq")
    params = (rows, rows, rows, columns, flat)
    return jax.shard_map(
        shards,
        mesh=mesh,
        in_specs=(tokens, tokens, P("batch", None)) + params + (P(),) + params + params,
        out_specs=(tokens, tokens) + params * 4,
        check_vma=False,
    )
```
